32 devices in a mesh: dp: 4 (over z), blk: 8 (over y, x, core).
Axes of the slice: x: 2, y: 2, z: 4, core: 2. Of those that a mesh axis runs over, the one named last changes fastest.
Arguments:
- tokens: bfloat16 [4096, 1536], P(('dp', 'blk')), may hold values from -6 to 6
- cotangent: bfloat16 [4096, 1536], P(('dp', 'blk')), may hold values from -6 to 6
- doc_table: int32 [4, 8], P('dp'), may hold values from 0 to 1, as said below
- gain_attn: bfloat16 [1536], P(('dp', 'blk')), may hold values from 0.5 to 1.5
- attn_in: bfloat16 [1536, 6144], P(('dp', 'blk')), may hold values from -0.15625 to 0.15625
- beta_proj: bfloat16 [1536, 12], P(('dp', 'blk')), may hold values from -0.625 to 0.625
- attn_out: bfloat16 [1536, 1536], P(('dp', 'blk')), may hold values from -1.25 to 1.25
- gain_ffn: bfloat16 [1536], P(('dp', 'blk')), may hold values from 0.5 to 1.5
- ffn_in: bfloat16 [1536, 8192], P(('dp', 'blk')), may hold values from -0.15625 to 0.15625
- ffn_down: bfloat16 [4096, 1536], P(('dp', 'blk')), may hold values from -0.09375 to 0.09375
Outputs:
- block_out: bfloat16 [4096, 1536], P(('dp', 'blk'))
- grad_tokens: float32 [4096, 1536], P(('dp', 'blk'))
- grad_gain_attn: float32 [1536], P(('dp', 'blk'))
- grad_attn_in: float32 [1536, 6144], P(('dp', 'blk'))
- grad_beta_proj: float32 [1536, 12], P(('dp', 'blk'))
- grad_attn_out: float32 [1536, 1536], P(('dp', 'blk'))
- grad_gain_ffn: float32 [1536], P(('dp', 'blk'))
- grad_ffn_in: float32 [1536, 8192], P(('dp', 'blk'))
- grad_ffn_down: float32 [4096, 1536], P(('dp', 'blk'))
The draws below stay inside these ranges and needn't reach their ends.
Inputs may be any that keep to these rules, and one draw needn't show every extreme that they name: `doc_table`: in each row either all 8 spans hold one sequence (id 0), or the first and second half each hold one sequence (ids 0 and 1); row 0 is always of the second kind.
All inputs are finite; a program needn't handle non-finite values.
Results may differ from the reference program's by a relative error of at most 0.017.
Values may be sent and summed in bfloat16 or wider, within the bound.
A program may use at most 448 MiB of HBM per device.

```python
import jax
import jax.numpy as jnp
from jax import lax

D = 1536
HEADS = 12
FF = 4096
TOKENS = 4096
N_DP = 4
N_BLK = 8


def draw_doc_table(key, part):
    flags = jax.random.randint(jax.random.fold_in(key, 7), (N_DP, 1), 0, 2)
    rows_idx = jnp.arange(N_DP, dtype=jnp.int32)[:, None]
    flags = jnp.where(rows_idx == 0, 0, flags)
    span_ids = jnp.arange(N_BLK, dtype=jnp.int32)[None, :]
    return jnp.where(flags == 1, 0, span_ids // (N_BLK // 2)).astype(jnp.int32)


def steps_of(rng, dims, split, smallest, largest):
    loudness = 1.0
    for axis_at, parts in split:
        draws = jax.random.uniform(jax.random.fold_in(jax.random.fold_in(rng, 6), axis_at), (parts,), jnp.float32, smallest / len(split), largest / len(split))
        loudness = loudness * jnp.repeat(jnp.exp(draws), dims[axis_at] // parts).reshape((-1,) + (1,) * (len(dims) - 1 - axis_at))
    return loudness


def scatter_about(rng, shape, width, limit, split=(), kind=jnp.bfloat16):
    entries = jax.random.normal(rng, shape, jnp.float32) * width
    if len(split) > 0:
        entries = steps_of(rng, shape, split, -0.22, 0.18) * entries
    return jnp.clip(entries, min=-limit, max=limit).astype(kind)


def setup_inputs(seed: int = 0) -> dict:
    keys = jax.random.split(jax.random.key(seed), 11)
    return {
        "tokens": scatter_about(keys[0], (TOKENS, D), 1.0, 6.0, ((0, 32),)),
        "cotangent": scatter_about(keys[1], (TOKENS, D), 1.0, 6.0, ((0, 32),)),
        "doc_table": draw_doc_table(jax.random.fold_in(keys[10], 71), 0),
        "gain_attn": jnp.clip(1.0 + 0.1 * jax.random.normal(keys[3], (D,), jnp.float32), 0.5, 1.5).astype(jnp.bfloat16),
        "attn_in": scatter_about(keys[4], (D, 4 * D), D ** -0.5, 0.15625, ((0, 32),)),
        "beta_proj": scatter_about(keys[5], (D, HEADS), (D // 16) ** -0.5, 0.625, ((0, 32),)),
        "attn_out": scatter_about(keys[6], (D, D), (D // 64) ** -0.5, 1.25, ((0, 32),)),
        "gain_ffn": jnp.clip(1.0 + 0.1 * jax.random.normal(keys[7], (D,), jnp.float32), 0.5, 1.5).astype(jnp.bfloat16),
        "ffn_in": scatter_about(keys[8], (D, 2 * FF), D ** -0.5, 0.15625, ((0, 32),)),
        "ffn_down": scatter_about(keys[9], (FF, D), FF ** -0.5, 0.09375, ((0, 32),)),
    }


HIGHEST = lax.Precision.HIGHEST
EPSILON = 1e-06

@jax.custom_vjp
def low(v):
    return lax.optimization_barrier(v.astype(jnp.bfloat16)).astype(jnp.float32)

@jax.custom_vjp
def low_back(v):
    return v

def low_keep(v):
    return (low(v), None)

def low_pass(kept, grad):
    return (grad,)

def back_keep(v):
    return (v, None)

def back_low(kept, grad):
    return (low(grad),)
low.defvjp(low_keep, low_pass)
low_back.defvjp(back_keep, back_low)

def matmul(left_part, right_part):
    return jnp.dot(left_part, right_part, precision=HIGHEST)

def rms_norm(values, gain):
    return values * lax.rsqrt(lax.optimization_barrier(jnp.mean(values * values, axis=-1, keepdims=True)) + EPSILON) * gain

def span_transform(queries, key_rows, direction_raw, strength):
    row_count = queries.shape[0]
    head_count = strength.shape[1]
    head_size = queries.shape[1] // head_count
    query_heads = queries.reshape(row_count, head_count, head_size).transpose(1, 0, 2)
    key_heads = key_rows.reshape(row_count, head_count, head_size).transpose(1, 0, 2)
    raw_heads = direction_raw.reshape(row_count, head_count, head_size).transpose(1, 0, 2)
    directions = raw_heads * lax.rsqrt(lax.optimization_barrier(jnp.sum(raw_heads * raw_heads, -1, keepdims=True)) + EPSILON)
    identity = jnp.eye(row_count, dtype=jnp.float32)
    lower_mask = jnp.tril(jnp.ones((row_count, row_count), jnp.float32))
    strict_mask = lower_mask - identity
    gram_matrix = jnp.einsum('hae,hbe->hab', directions, directions, precision=HIGHEST)
    system = gram_matrix * strict_mask + identity / strength.T[:, :, None]
    solved = lax.linalg.triangular_solve(system, jnp.broadcast_to(identity, system.shape), left_side=True, lower=True)
    query_dirs = jnp.einsum('hte,hae->hta', query_heads, directions, precision=HIGHEST) * lower_mask
    dirs_key = jnp.einsum('hbe,hse->hbs', directions, key_heads, precision=HIGHEST) * strict_mask
    left_part = jnp.einsum('hta,hab->htb', query_dirs, solved, precision=HIGHEST)
    right_part = jnp.einsum('hab,hbs->has', solved, dirs_key, precision=HIGHEST)
    score_scale = head_size ** (-0.5)
    plain = jnp.einsum('hte,hse->hts', query_heads, key_heads, precision=HIGHEST)
    scores = (plain - jnp.einsum('htb,hbs->hts', left_part, dirs_key, precision=HIGHEST)) * score_scale
    query_path = query_heads - jnp.einsum('htb,hbe->hte', left_part, directions, precision=HIGHEST)
    key_path = key_heads - jnp.einsum('has,hae->hse', right_part, directions, precision=HIGHEST)
    carry_map = jnp.eye(head_size, dtype=jnp.float32) - jnp.einsum('hae,hab,hbf->hef', directions, solved, directions, precision=HIGHEST)
    return (scores, query_path, key_path, carry_map)

def group_forward(inputs, doc_ids, gain_attn, attn_in, beta_proj, attn_out, gain_ffn, ffn_in, ffn_down):
    rows_all, model_width = inputs.shape
    blocks = doc_ids.shape[0]
    row_count = rows_all // blocks
    head_count = beta_proj.shape[1]
    head_size = model_width // head_count
    score_scale = head_size ** (-0.5)
    normed = low(rms_norm(inputs, gain_attn))
    project = low_back(matmul(normed, attn_in))
    strength_logit = low_back(matmul(normed, beta_proj))
    strength = 2.0 * jax.nn.sigmoid(strength_logit)
    queries = project[:, :model_width].reshape(blocks, row_count, model_width)
    key_rows = project[:, model_width:2 * model_width].reshape(blocks, row_count, model_width)
    value_rows = low(project[:, 2 * model_width:3 * model_width])
    value_rows = value_rows.reshape(blocks, row_count, head_count, head_size).transpose(0, 2, 1, 3)
    direction_raw = project[:, 3 * model_width:].reshape(blocks, row_count, model_width)
    strengths = strength.reshape(blocks, row_count, head_count)

    def local_piece(member):
        return span_transform(member[0], member[1], member[2], member[3])
    scores, query_path, key_path, carry_map = lax.map(jax.checkpoint(local_piece), (queries, key_rows, direction_raw, strengths))
    scores = low_back(scores)
    causal = jnp.tril(jnp.ones((row_count, row_count), dtype=bool))
    local_exp = jnp.where(causal, jnp.exp(scores), 0.0)
    totals = lax.optimization_barrier(jnp.sum(local_exp, -1))
    numerator = jnp.einsum('nhts,nhse->nhte', low(local_exp), value_rows, precision=HIGHEST)
    query_low = low(query_path)
    span_ids = jnp.arange(blocks, dtype=jnp.int32)

    def cycle_step(carry, distance):
        key_buf, value_buf, numer_now, totals_now = carry
        key_recv = jnp.concatenate([jnp.zeros_like(key_buf[:1]), key_buf[:-1]], 0)
        value_recv = jnp.concatenate([jnp.zeros_like(value_buf[:1]), value_buf[:-1]], 0)
        source = span_ids - distance
        source_doc = doc_ids[jnp.maximum(source, 0)]
        usable = ((source >= 0) & (source_doc == doc_ids)).astype(jnp.float32)
        cross_scores = jnp.einsum('nhte,nhse->nhts', query_low, low(key_recv), precision=HIGHEST) * score_scale
        cross_scores = low_back(cross_scores)
        block_exp = jnp.exp(cross_scores) * usable[:, None, None, None]
        totals_now = totals_now + lax.optimization_barrier(jnp.sum(block_exp, -1))
        numer_now = numer_now + jnp.einsum('nhts,nhse->nhte', low(block_exp), value_recv, precision=HIGHEST)
        key_next = jnp.einsum('nhse,nhfe->nhsf', key_recv, carry_map, precision=HIGHEST)
        return ((key_next, value_recv, numer_now, totals_now), None)
    distances = jnp.arange(1, blocks, dtype=jnp.int32)
    (key_end, value_end, numerator, totals), _ = lax.scan(jax.checkpoint(cycle_step), (key_path, value_rows, numerator, totals), distances)
    attended = low_back(numerator) / totals[..., None]
    attended = attended.transpose(0, 2, 1, 3).reshape(rows_all, model_width)
    branch_out = low_back(matmul(low(attended), attn_out))
    residual = inputs + branch_out
    normed_ffn = low(rms_norm(residual, gain_ffn))
    gate_up = low_back(matmul(normed_ffn, ffn_in))
    unit_count = ffn_down.shape[0]
    hidden = low(jax.nn.silu(gate_up[:, :unit_count]) * gate_up[:, unit_count:])
    return residual + matmul(hidden, ffn_down)

def reference(tokens, cotangent, doc_table, gain_attn, attn_in, beta_proj, attn_out, gain_ffn, ffn_in, ffn_down):
    weights = tuple((member.astype(jnp.float32) for member in (gain_attn, attn_in, beta_proj, attn_out, gain_ffn, ffn_in, ffn_down)))
    groups = doc_table.shape[0]
    model_width = tokens.shape[1]
    inputs = tokens.astype(jnp.float32).reshape(groups, -1, model_width)
    upstream = cotangent.astype(jnp.float32).reshape(groups, -1, model_width)

    def per_group(totals_all, member):
        group_in, group_up, doc_ids = member

        def forward(values, *params):
            return group_forward(values, doc_ids, *params)
        output, pullback = jax.vjp(forward, group_in, *weights)
        gradients = pullback(group_up)
        summed = tuple((total + grad_one for total, grad_one in zip(totals_all, gradients[1:])))
        return (summed, (output.astype(jnp.bfloat16), gradients[0]))
    start = tuple((jnp.zeros_like(member) for member in weights))
    totals_all, (outputs, input_grads) = lax.scan(per_group, start, (inputs, upstream, doc_table))
    return (outputs.reshape(-1, model_width), input_grads.reshape(-1, model_width), totals_all[0], totals_all[1], totals_all[2], totals_all[3], totals_all[4], totals_all[5], totals_all[6])
```

```python
import functools

import jax
import jax.numpy as jnp
from jax import lax
from jax.experimental import pallas as pl
from jax.experimental.pallas import tpu as pltpu
from jax.sharding import PartitionSpec as P

EPSILON = 1e-06
F32 = jnp.float32
BF16 = jnp.bfloat16

NN = (((1,), (0,)), ((), ()))
NT = (((1,), (1,)), ((), ()))
TN = (((0,), (0,)), ((), ()))


def dot(a, b, dims=NN):
    return lax.dot_general(a, b, dims, preferred_element_type=F32)


def halves(x):
    high = x.astype(BF16)
    return high, (x - high.astype(F32)).astype(BF16)


def dot3(a, b, dims=NN):
    (ah, al), (bh, bl) = a, b
    return dot(ah, bh, dims) + (dot(ah, bl, dims) + dot(al, bh, dims))


def both(parts, axis):
    return tuple(jnp.concatenate(p, axis) for p in zip(*parts))


def rms_norm(values, gain):
    return values * lax.rsqrt(jnp.mean(values * values, axis=-1, keepdims=True) + EPSILON) * gain


def rms_pull(values, gain, grad):
    scale = lax.rsqrt(jnp.mean(values * values, axis=-1, keepdims=True) + EPSILON)
    inner = grad * gain
    along = jnp.mean(inner * values, axis=-1, keepdims=True)
    return scale * inner - values * (scale * scale * scale) * along


def lanes(n):
    return lax.broadcasted_iota(jnp.int32, (n, n), 1)


def rows_of(n):
    return lax.broadcasted_iota(jnp.int32, (n, n), 0)


def inverses(grams, betas, span):
    r, c = rows_of(span), lanes(span)
    eye = r == c
    outs = []
    pair = (c + 1 == r) & (r % 2 == 1)
    for gram, beta in zip(grams, betas):
        below = jnp.where(pair, gram, 0.0) * beta * beta.T
        outs.append(jnp.where(eye, beta, 0.0) - below)
    size = 2
    while size < span:
        part = (r // (2 * size) == c // (2 * size)) & ((r // size) % 2 == 1) & ((c // size) % 2 == 0)
        sides = [halves(x) for x in outs]
        steps = [dot3(halves(jnp.where(part, g, 0.0)), x) for g, x in zip(grams, sides)]
        outs = [x - dot3(s, halves(t)) for x, s, t in zip(outs, sides, steps)]
        size *= 2
    return outs


def attention_forward_kernel(
    spans, span, doc_ref, proj_ref, logit_ref,
    att_ref, sum_ref, a1_ref, g_ref, y_ref, e0_ref, qp_ref, m_ref, kts_ref,
    kpt_ref, kt_ref,
):
    h = span
    scale = h ** -0.5
    r, c = rows_of(span), lanes(span)
    lower, strict, eye = c <= r, c < r, (c == r).astype(F32)
    at = [pl.ds(n * span, span) for n in range(spans)]
    group = 4
    for first in range(0, spans, group):
        members = range(first, min(first + group, spans))
        grams, betas, kept = [], [], []
        for n in members:
            q = proj_ref[at[n], 0:h]
            k = proj_ref[at[n], h : 2 * h]
            d = proj_ref[at[n], 3 * h : 4 * h]
            w = d * lax.rsqrt(jnp.sum(d * d, -1, keepdims=True) + EPSILON)
            qs, ks, ws = halves(q), halves(k), halves(w)
            z = dot3(both((qs, ws), 0), both((ws, ks), 0), NT)
            a1 = jnp.where(lower, z[:span, :span], 0.0)
            a1_ref[at[n], :] = a1
            b1 = jnp.where(strict, z[span:, span:], 0.0)
            grams.append(jnp.where(strict, z[span:, :span], 0.0))
            betas.append(2.0 / (1.0 + jnp.exp(-logit_ref[at[n], :])))
            kept.append((q, k, ws, halves(a1), halves(b1), z[:span, span:]))
        solved = inverses(grams, betas, span)
        for n, g, (q, k, ws, a1s, b1s, qk) in zip(members, solved, kept):
            g_ref[at[n], :] = g
            y = dot3(halves(g), both((ws, b1s), 1))
            y_ref[at[n], :] = y
            ys = halves(y)
            t = dot3(a1s, ys)
            u = dot3(ws, ys, TN)
            qp_ref[at[n], :] = (q - t[:, :h]).astype(BF16)
            local = (qk - t[:, h:]) * scale
            e0_ref[at[n], :] = jnp.where(lower, jnp.exp(local), 0.0)
            m_ref[at[n], :] = eye - u[:, :h]
            kpt_ref[:, at[n]] = k.T - u[:, h:]
    for n in range(spans):
        w = n * span
        e0 = e0_ref[at[n], :]
        total = jnp.sum(e0, -1, keepdims=True)
        numer = dot(e0.astype(BF16), proj_ref[at[n], 2 * h : 3 * h].astype(BF16))
        if n > 0:
            kt = kt_ref[:, :w]
            kts = halves(kt)
            kts_ref[0, n, :, :w] = kts[0]
            block = jnp.exp(dot(qp_ref[at[n], :], kts[0]) * scale)
            block = jnp.concatenate(
                [jnp.where(doc_ref[0, j] == doc_ref[0, n], block[:, j * span : (j + 1) * span], 0.0) for j in range(n)], 1
            )
            total = total + jnp.sum(block, -1, keepdims=True)
            numer = numer + dot(block.astype(BF16), proj_ref[:w, 2 * h : 3 * h].astype(BF16))
            if n < spans - 1:
                kt_ref[:, :w] = dot3(halves(m_ref[at[n], :]), kts)
        if n < spans - 1:
            kt_ref[:, at[n]] = kpt_ref[:, at[n]]
        att_ref[at[n], :] = numer / total
        sum_ref[at[n], :] = jnp.broadcast_to(total, (span, h))


def attention_backward_kernel(
    spans, span, doc_ref, proj_ref, logit_ref, datt_ref,
    att_ref, sum_ref, a1_ref, g_ref, y_ref, e0_ref, qp_ref, m_ref, kts_ref,
    dproj_ref, dlogit_ref,
    gkt_ref, dvt_ref, dqp_ref, dm_ref, dkpt_ref, ds_ref,
):
    h = span
    scale = h ** -0.5
    r, c = rows_of(span), lanes(span)
    lower, strict, same = c <= r, c < r, c == r
    at = [pl.ds(n * span, span) for n in range(spans)]
    dvt_ref[...] = jnp.zeros_like(dvt_ref)
    for n in reversed(range(spans)):
        w = n * span
        last = n == spans - 1
        datt, total = datt_ref[at[n], :], sum_ref[at[n], :]
        da = (datt / total).astype(BF16)
        delta = jnp.sum(datt * att_ref[at[n], :], -1, keepdims=True) / total
        e0 = e0_ref[at[n], :]
        mix = dot(da, proj_ref[at[n], 2 * h : 3 * h].astype(BF16), NT) - delta
        ds_ref[at[n], :] = (e0 * mix).astype(BF16).astype(F32) * scale
        dvt_ref[:, at[n]] += dot(da, e0.astype(BF16), TN)
        if n == 0:
            dqp_ref[at[n], :] = jnp.zeros((span, h), F32)
            dm_ref[at[n], :] = jnp.zeros((h, h), F32)
            dkpt_ref[:, at[n]] = gkt_ref[:, at[n]] if not last else jnp.zeros((h, span), F32)
            continue
        keys = kts_ref[0, n, :, :w]
        qp = qp_ref[at[n], :]
        block = jnp.exp(dot(qp, keys) * scale)
        block = jnp.concatenate(
            [jnp.where(doc_ref[0, j] == doc_ref[0, n], block[:, j * span : (j + 1) * span], 0.0) for j in range(n)], 1
        )
        wide = jnp.concatenate([delta] * n, 1)
        mix = dot(da, proj_ref[:w, 2 * h : 3 * h].astype(BF16), NT) - wide
        ds = (block * mix).astype(BF16)
        dqp_ref[at[n], :] = dot(ds, keys, NT) * scale
        pulled = dot(qp, ds, TN) * scale
        dvt_ref[:, :w] += dot(da, block.astype(BF16), TN)
        if last:
            dm_ref[at[n], :] = jnp.zeros((h, h), F32)
            dkpt_ref[:, at[n]] = jnp.zeros((h, span), F32)
            gkt_ref[:, :w] = pulled
        else:
            dkpt_ref[:, at[n]] = gkt_ref[:, at[n]]
            gs = halves(gkt_ref[:, :w])
            dm_ref[at[n], :] = dot(gs[0], keys, NT) + dot(gs[1], keys, NT)
            gkt_ref[:, :w] = pulled + dot3(halves(m_ref[at[n], :]), gs, TN)
    for n in range(spans):
        q = proj_ref[at[n], 0:h]
        k = proj_ref[at[n], h : 2 * h]
        d = proj_ref[at[n], 3 * h : 4 * h]
        inv = lax.rsqrt(jnp.sum(d * d, -1, keepdims=True) + EPSILON)
        w = d * inv
        beta = 2.0 / (1.0 + jnp.exp(-logit_ref[at[n], :]))
        qs, ks, ws = halves(q), halves(k), halves(w)
        dqp, ds, dkpt = dqp_ref[at[n], :], ds_ref[at[n], :], dkpt_ref[:, at[n]]
        ys = halves(y_ref[at[n], :])
        left = both((halves(dqp), halves(ds)), 1)
        mid = both((halves(dm_ref[at[n], :]), halves(dkpt)), 1)
        da1 = jnp.where(lower, -dot3(left, ys, NT), 0.0)
        dy = dot3(halves(a1_ref[at[n], :]), left, TN) + dot3(ws, mid)
        dx = -dot3(halves(g_ref[at[n], :]), halves(dy), TN)
        dl = -dot3(halves(dx), ys, NT)
        dw = dx[:, :h] - dot3(ys, mid, NT)
        pull = jnp.sum(jnp.where(same, dl, 0.0), -1, keepdims=True)
        dlogit_ref[at[n], :] = (-pull * (1.0 - 0.5 * beta) / jnp.maximum(beta, 1e-30)).astype(BF16)
        dz = jnp.concatenate(
            [
                jnp.concatenate([da1, ds], 1),
                jnp.concatenate([jnp.where(strict, dl, 0.0), jnp.where(strict, dx[:, h:], 0.0)], 1),
            ],
            0,
        )
        dzs = halves(dz)
        dp = dot3(dzs, both((ws, ks), 0))
        dr = dot3(dzs, both((qs, ws), 0), TN)
        dw = dw + dp[span:] + dr[:span]
        dproj_ref[at[n], 0:h] = (dqp + dp[:span]).astype(BF16)
        dproj_ref[at[n], h : 2 * h] = (dkpt.T + dr[span:]).astype(BF16)
        dproj_ref[at[n], 2 * h : 3 * h] = dvt_ref[:, at[n]].T.astype(BF16)
        dproj_ref[at[n], 3 * h : 4 * h] = (inv * (dw - w * jnp.sum(dw * w, -1, keepdims=True))).astype(BF16)


def head_specs(rows, h, spans):
    one = pl.BlockSpec((rows, h), lambda s: (0, s))
    two = pl.BlockSpec((rows, 2 * h), lambda s: (0, s))
    four = pl.BlockSpec((rows, 4 * h), lambda s: (0, s))
    keys = pl.BlockSpec((1, spans, h, rows), lambda s: (s, 0, 0, 0))
    docs = pl.BlockSpec(memory_space=pltpu.SMEM)
    return one, two, four, keys, docs


def attention_forward(docs, proj, logits, slots, span):
    rows = proj.shape[0]
    spans, h = rows // span, span
    one, two, four, keys, smem = head_specs(rows, h, spans)

    def full(width, dtype=F32):
        return jax.ShapeDtypeStruct((rows, slots * width), dtype)

    return pl.pallas_call(
        functools.partial(attention_forward_kernel, spans, span),
        grid=(slots,),
        in_specs=[smem, four, one],
        out_specs=[one, one, one, one, two, one, one, one, keys],
        out_shape=[
            full(h), full(h), full(h), full(h), full(2 * h), full(h), full(h, BF16), full(h),
            jax.ShapeDtypeStruct((slots, spans, h, rows), BF16),
        ],
        scratch_shapes=[pltpu.VMEM((h, rows), F32), pltpu.VMEM((h, rows), F32)],
        compiler_params=pltpu.CompilerParams(vmem_limit_bytes=60 * 1024 * 1024),
        name="attention_forward",
    )(docs, proj, logits)


def attention_backward(docs, proj, logits, datt, saved, slots, span):
    rows = proj.shape[0]
    spans, h = rows // span, span
    one, two, four, keys, smem = head_specs(rows, h, spans)
    wide, tall = pltpu.VMEM((h, rows), F32), pltpu.VMEM((rows, h), F32)
    return pl.pallas_call(
        functools.partial(attention_backward_kernel, spans, span),
        grid=(slots,),
        in_specs=[smem, four, one, one, one, one, one, one, two, one, one, one, keys],
        out_specs=[four, one],
        out_shape=[
            jax.ShapeDtypeStruct((rows, slots * 4 * h), BF16),
            jax.ShapeDtypeStruct((rows, slots * h), BF16),
        ],
        scratch_shapes=[wide, wide, tall, tall, wide, tall],
        compiler_params=pltpu.CompilerParams(vmem_limit_bytes=60 * 1024 * 1024),
        name="attention_backward",
    )(docs, proj, logits, datt, *saved)


def to_columns(value, axis="blk"):
    return lax.all_to_all(value, axis, split_axis=1, concat_axis=0, tiled=True)


def to_rows(value, axis="blk"):
    return lax.all_to_all(value, axis, split_axis=0, concat_axis=1, tiled=True)


def scatter_tokens(partial, peers):
    rows = partial.shape[0] // peers
    parts = lax.all_to_all(partial.astype(BF16), "blk", split_axis=0, concat_axis=0, tiled=True)
    return jnp.sum(parts.reshape(peers, rows, -1).astype(F32), 0)


def shards(
    tokens, cotangent, doc_table, gain_attn, attn_in, beta_proj, attn_out, gain_ffn, ffn_in, ffn_down
):
    rows, width = tokens.shape
    heads = beta_proj.shape[1]
    h = width // heads
    groups, peers = lax.axis_size("dp"), lax.axis_size("blk")
    slots = -(-heads // peers)
    padded = slots * peers
    share = attn_in.shape[0]
    units = ffn_down.shape[0]
    me = lax.axis_index("blk")
    by_head = attn_in.reshape(share, 4, heads, h).transpose(0, 2, 1, 3)
    by_head = jnp.pad(by_head, ((0, 0), (0, padded - heads), (0, 0), (0, 0)))
    strengths = jnp.pad(beta_proj, ((0, 0), (0, padded - heads))).reshape(share, peers, slots)
    gains = jnp.broadcast_to(jnp.stack([gain_attn, gain_ffn], -1)[:, None], (share, peers, 2))
    extra = jnp.pad(jnp.concatenate([strengths, gains], -1), ((0, 0), (0, 0), (0, h - slots - 2)))
    attn_slab = jnp.concatenate([by_head.reshape(share, peers, slots * 4 * h), extra], -1)
    attn_slab = to_columns(attn_slab.reshape(share, -1))
    attn_slab = lax.all_gather(attn_slab, "dp", axis=0, tiled=True)
    x_all = lax.all_gather(tokens, "blk", axis=0, tiled=True)
    out_full = lax.all_gather(attn_out, ("dp", "blk"), axis=0, tiled=True)
    ffn_slab = ffn_in.reshape(share, 2, groups, peers, units).transpose(0, 3, 1, 2, 4)
    ffn_slab = to_columns(ffn_slab.reshape(share, -1))
    ffn_slab = lax.all_gather(ffn_slab, "dp", axis=0, tiled=True)
    down_slab = lax.all_gather(ffn_down, "dp", axis=0, tiled=True)
    dy_all = lax.all_gather(cotangent, "blk", axis=0, tiled=True)

    attn_cols = slots * 4 * h
    w_attn = attn_slab[:, :attn_cols]
    w_beta = attn_slab[:, attn_cols : attn_cols + slots]
    gain_one = attn_slab[:, attn_cols + slots].astype(F32)
    gain_two = attn_slab[:, attn_cols + slots + 1].astype(F32)

    normed = rms_norm(x_all.astype(F32), gain_one).astype(BF16)
    proj = dot(normed, w_attn)
    logits = dot(normed, jnp.repeat(w_beta, h, axis=1))
    saved = attention_forward(doc_table, proj, logits, slots, rows)
    attended = saved[0].astype(BF16)
    attended_own = to_rows(attended)[:, :width]
    inputs = tokens.astype(F32)
    residual = inputs + dot(attended_own, out_full)
    normed_two = rms_norm(residual, gain_two).astype(BF16)
    normed_two_all = lax.all_gather(normed_two, "blk", axis=0, tiled=True)

    gate_up = dot(normed_two_all, ffn_slab)
    mine = gate_up.shape[1] // 2
    gate, up = gate_up[:, :mine], gate_up[:, mine:]
    sig = jax.nn.sigmoid(gate)
    hidden = (gate * sig * up).astype(BF16)
    dhidden = dot(dy_all, down_slab, NT)
    dgate = dhidden * up * (sig * (1.0 + gate * (1.0 - sig)))
    dup = dhidden * (gate * sig)
    dgate_up = jnp.concatenate([dgate, dup], 1).astype(BF16)
    dnormed_two = scatter_tokens(dot(dgate_up, ffn_slab, NT), peers)
    block_out = (residual + scatter_tokens(dot(hidden, down_slab), peers)).astype(BF16)
    grad_down = lax.psum_scatter(dot(hidden, dy_all, TN).astype(BF16), "dp", scatter_dimension=0, tiled=True)
    grad_ffn = lax.psum_scatter(dot(normed_two_all, dgate_up, TN).astype(BF16), "dp", scatter_dimension=0, tiled=True)

    dresidual = cotangent.astype(F32) + rms_pull(residual, gain_two, dnormed_two)
    dbranch_all = lax.all_gather(dresidual.astype(BF16), "blk", axis=0, tiled=True)
    out_rows = jnp.pad(out_full, ((0, (padded - heads) * h), (0, 0)))
    out_rows = lax.dynamic_slice_in_dim(out_rows, me * slots * h, slots * h, 0)
    datt = dot(dbranch_all, out_rows, NT)
    grad_out = to_columns(dot(attended, dbranch_all, TN).astype(BF16))[:width]
    grad_out = lax.psum_scatter(grad_out, "dp", scatter_dimension=0, tiled=True)

    dproj, dlogits = attention_backward(doc_table, proj, logits, datt, saved, slots, rows)
    dlogits = dlogits.reshape(-1, slots, h)[:, :, 0]
    dlogits = jnp.pad(dlogits, ((0, 0), (0, h - slots)))
    dslab = jnp.concatenate([dproj, dlogits], 1)
    grad_attn = lax.psum_scatter(dot(normed, dslab, TN).astype(BF16), "dp", scatter_dimension=0, tiled=True)
    dnormed = scatter_tokens(dot(dslab, attn_slab, NT), peers)
    grad_tokens = dresidual + rms_pull(inputs, gain_one, dnormed)

    grad_attn = to_rows(grad_attn).reshape(share, peers, -1).astype(F32)
    grad_beta = grad_attn[:, :, attn_cols : attn_cols + slots].reshape(share, padded)[:, :heads]
    grad_attn_in = grad_attn[:, :, :attn_cols].reshape(share, padded, 4, h)[:, :heads]
    grad_attn_in = grad_attn_in.transpose(0, 2, 1, 3).reshape(share, -1)
    grad_attn_out = to_rows(grad_out).astype(F32)
    grad_ffn_in = to_rows(grad_ffn).reshape(share, peers, 2, groups, units).astype(F32)
    grad_ffn_in = grad_ffn_in.transpose(0, 2, 3, 1, 4).reshape(share, -1)
    grad_gain_attn = (
        jnp.sum(grad_attn_in * attn_in.astype(F32), -1) + jnp.sum(grad_beta * beta_proj.astype(F32), -1)
    ) / gain_attn.astype(F32)
    grad_gain_ffn = jnp.sum(grad_ffn_in * ffn_in.astype(F32), -1) / gain_ffn.astype(F32)
    return (
        block_out, grad_tokens, grad_gain_attn, grad_attn_in, grad_beta, grad_attn_out,
        grad_gain_ffn, grad_ffn_in, grad_down.astype(F32),
    )


def solution(mesh):
    split, vector = P(("dp", "blk"), None), P(("dp", "blk"))
    in_specs = (split, split, P("dp", None), vector, split, split, split, vector, split, split)
    out_specs = (split, split, vector, split, split, split, vector, split, split)
    return jax.shard_map(shards, mesh=mesh, in_specs=in_specs, out_specs=out_specs, check_vma=False)
```

```python
import functools

import jax
import jax.numpy as jnp
from jax import lax
from jax.experimental import pallas as pl
from jax.experimental.pallas import tpu as pltpu
from jax.sharding import PartitionSpec as P

EPSILON = 1e-06
F32 = jnp.float32
BF16 = jnp.bfloat16

NN = (((1,), (0,)), ((), ()))
NT = (((1,), (1,)), ((), ()))
TN = (((0,), (0,)), ((), ()))


def dot(a, b, dims=NN):
    return lax.dot_general(a, b, dims, preferred_element_type=F32)


def halves(x):
    high = x.astype(BF16)
    return high, (x - high.astype(F32)).astype(BF16)


def dot3(a, b, dims=NN):
    (ah, al), (bh, bl) = a, b
    return dot(ah, bh, dims) + (dot(ah, bl, dims) + dot(al, bh, dims))


def both(parts, axis):
    return tuple(jnp.concatenate(p, axis) for p in zip(*parts))


def rms_norm(values, gain):
    return values * lax.rsqrt(jnp.mean(values * values, axis=-1, keepdims=True) + EPSILON) * gain


def rms_pull(values, gain, grad):
    scale = lax.rsqrt(jnp.mean(values * values, axis=-1, keepdims=True) + EPSILON)
    inner = grad * gain
    along = jnp.mean(inner * values, axis=-1, keepdims=True)
    return scale * inner - values * (scale * scale * scale) * along


def lanes(n):
    return lax.broadcasted_iota(jnp.int32, (n, n), 1)


def rows_of(n):
    return lax.broadcasted_iota(jnp.int32, (n, n), 0)


def inverses(grams, betas, span):
    r, c = rows_of(span), lanes(span)
    eye = r == c
    outs = []
    pair = (c + 1 == r) & (r % 2 == 1)
    for gram, beta in zip(grams, betas):
        below = jnp.where(pair, gram, 0.0) * beta * beta.T
        outs.append(jnp.where(eye, beta, 0.0) - below)
    size = 2
    while size < span:
        part = (r // (2 * size) == c // (2 * size)) & ((r // size) % 2 == 1) & ((c // size) % 2 == 0)
        sides = [halves(x) for x in outs]
        steps = [dot3(halves(jnp.where(part, g, 0.0)), x) for g, x in zip(grams, sides)]
        outs = [x - dot3(s, halves(t)) for x, s, t in zip(outs, sides, steps)]
        size *= 2
    return outs


def attention_forward_kernel(
    spans, span, doc_ref, proj_ref, logit_ref,
    low_ref, att_ref, sum_ref, a1_ref, g_ref, y_ref, e0_ref, qp_ref, m_ref, kts_ref,
    kpt_ref, kt_ref,
):
    h = span
    scale = h ** -0.5
    r, c = rows_of(span), lanes(span)
    lower, strict, eye = c <= r, c < r, (c == r).astype(F32)
    at = [pl.ds(n * span, span) for n in range(spans)]
    group = 4
    for first in range(0, spans, group):
        members = range(first, min(first + group, spans))
        grams, betas, kept = [], [], []
        for n in members:
            q = proj_ref[at[n], 0:h]
            k = proj_ref[at[n], h : 2 * h]
            d = proj_ref[at[n], 3 * h : 4 * h]
            w = d * lax.rsqrt(jnp.sum(d * d, -1, keepdims=True) + EPSILON)
            qs, ks, ws = halves(q), halves(k), halves(w)
            z = dot3(both((qs, ws), 0), both((ws, ks), 0), NT)
            a1 = jnp.where(lower, z[:span, :span], 0.0)
            a1_ref[at[n], :] = a1
            b1 = jnp.where(strict, z[span:, span:], 0.0)
            grams.append(jnp.where(strict, z[span:, :span], 0.0))
            betas.append(2.0 / (1.0 + jnp.exp(-logit_ref[at[n], :])))
            kept.append((q, k, ws, halves(a1), halves(b1), z[:span, span:]))
        solved = inverses(grams, betas, span)
        for n, g, (q, k, ws, a1s, b1s, qk) in zip(members, solved, kept):
            g_ref[at[n], :] = g
            y = dot3(halves(g), both((ws, b1s), 1))
            y_ref[at[n], :] = y
            ys = halves(y)
            t = dot3(a1s, ys)
            u = dot3(ws, ys, TN)
            qp_ref[at[n], :] = (q - t[:, :h]).astype(BF16)
            local = (qk - t[:, h:]) * scale
            e0_ref[at[n], :] = jnp.where(lower, jnp.exp(local), 0.0)
            m_ref[at[n], :] = eye - u[:, :h]
            kpt_ref[:, at[n]] = k.T - u[:, h:]
    for n in range(spans):
        w = n * span
        e0 = e0_ref[at[n], :]
        total = jnp.sum(e0, -1, keepdims=True)
        numer = dot(e0.astype(BF16), proj_ref[at[n], 2 * h : 3 * h].astype(BF16))
        if n > 0:
            kt = kt_ref[:, :w]
            kts = halves(kt)
            kts_ref[0, n, :, :w] = kts[0]
            block = jnp.exp(dot(qp_ref[at[n], :], kts[0]) * scale)
            block = jnp.concatenate(
                [jnp.where(doc_ref[0, j] == doc_ref[0, n], block[:, j * span : (j + 1) * span], 0.0) for j in range(n)], 1
            )
            total = total + jnp.sum(block, -1, keepdims=True)
            numer = numer + dot(block.astype(BF16), proj_ref[:w, 2 * h : 3 * h].astype(BF16))
            if n < spans - 1:
                kt_ref[:, :w] = dot3(halves(m_ref[at[n], :]), kts)
        if n < spans - 1:
            kt_ref[:, at[n]] = kpt_ref[:, at[n]]
        attended = numer / total
        att_ref[at[n], :] = attended
        low_ref[at[n], :] = attended.astype(BF16)
        sum_ref[at[n], :] = jnp.broadcast_to(total, (span, h))


def attention_backward_kernel(
    spans, span, doc_ref, proj_ref, logit_ref, datt_ref,
    att_ref, sum_ref, a1_ref, g_ref, y_ref, e0_ref, qp_ref, m_ref, kts_ref,
    dproj_ref, dlogit_ref,
    gkt_ref, dvt_ref, dqp_ref, dm_ref, dkpt_ref, ds_ref,
):
    h = span
    scale = h ** -0.5
    r, c = rows_of(span), lanes(span)
    lower, strict, same = c <= r, c < r, c == r
    at = [pl.ds(n * span, span) for n in range(spans)]
    slot = pl.program_id(0)
    dvt_ref[...] = jnp.zeros_like(dvt_ref)
    for n in reversed(range(spans)):
        w = n * span
        last = n == spans - 1
        datt, total = datt_ref[at[n], :], sum_ref[at[n], :]
        da = (datt / total).astype(BF16)
        delta = jnp.sum(datt * att_ref[at[n], :], -1, keepdims=True) / total
        e0 = e0_ref[at[n], :]
        mix = dot(da, proj_ref[at[n], 2 * h : 3 * h].astype(BF16), NT) - delta
        ds_ref[at[n], :] = (e0 * mix).astype(BF16).astype(F32) * scale
        dvt_ref[:, at[n]] += dot(da, e0.astype(BF16), TN)
        if n == 0:
            dqp_ref[at[n], :] = jnp.zeros((span, h), F32)
            dm_ref[at[n], :] = jnp.zeros((h, h), F32)
            dkpt_ref[:, at[n]] = gkt_ref[:, at[n]] if not last else jnp.zeros((h, span), F32)
            continue
        keys = kts_ref[0, n, :, :w]
        qp = qp_ref[at[n], :]
        block = jnp.exp(dot(qp, keys) * scale)
        block = jnp.concatenate(
            [jnp.where(doc_ref[0, j] == doc_ref[0, n], block[:, j * span : (j + 1) * span], 0.0) for j in range(n)], 1
        )
        wide = jnp.concatenate([delta] * n, 1)
        mix = dot(da, proj_ref[:w, 2 * h : 3 * h].astype(BF16), NT) - wide
        ds = (block * mix).astype(BF16)
        dqp_ref[at[n], :] = dot(ds, keys, NT) * scale
        pulled = dot(qp, ds, TN) * scale
        dvt_ref[:, :w] += dot(da, block.astype(BF16), TN)
        if last:
            dm_ref[at[n], :] = jnp.zeros((h, h), F32)
            dkpt_ref[:, at[n]] = jnp.zeros((h, span), F32)
            gkt_ref[:, :w] = pulled
        else:
            dkpt_ref[:, at[n]] = gkt_ref[:, at[n]]
            gs = halves(gkt_ref[:, :w])
            dm_ref[at[n], :] = dot(gs[0], keys, NT) + dot(gs[1], keys, NT)
            gkt_ref[:, :w] = pulled + dot3(halves(m_ref[at[n], :]), gs, TN)
    for n in range(spans):
        q = proj_ref[at[n], 0:h]
        k = proj_ref[at[n], h : 2 * h]
        d = proj_ref[at[n], 3 * h : 4 * h]
        inv = lax.rsqrt(jnp.sum(d * d, -1, keepdims=True) + EPSILON)
        w = d * inv
        beta = 2.0 / (1.0 + jnp.exp(-logit_ref[at[n], :]))
        qs, ks, ws = halves(q), halves(k), halves(w)
        dqp, ds, dkpt = dqp_ref[at[n], :], ds_ref[at[n], :], dkpt_ref[:, at[n]]
        ys = halves(y_ref[at[n], :])
        left = both((halves(dqp), halves(ds)), 1)
        mid = both((halves(dm_ref[at[n], :]), halves(dkpt)), 1)
        da1 = jnp.where(lower, -dot3(left, ys, NT), 0.0)
        dy = dot3(halves(a1_ref[at[n], :]), left, TN) + dot3(ws, mid)
        dx = -dot3(halves(g_ref[at[n], :]), halves(dy), TN)
        dl = -dot3(halves(dx), ys, NT)
        dw = dx[:, :h] - dot3(ys, mid, NT)
        pull = jnp.sum(jnp.where(same, dl, 0.0), -1, keepdims=True)
        dlogit = -pull * (1.0 - 0.5 * beta) / jnp.maximum(beta, 1e-30)
        before = jnp.where(slot == 0, 0.0, dlogit_ref[at[n], :].astype(F32))
        dlogit_ref[at[n], :] = jnp.where(c == slot, dlogit, before).astype(BF16)
        dz = jnp.concatenate(
            [
                jnp.concatenate([da1, ds], 1),
                jnp.concatenate([jnp.where(strict, dl, 0.0), jnp.where(strict, dx[:, h:], 0.0)], 1),
            ],
            0,
        )
        dzs = halves(dz)
        dp = dot3(dzs, both((ws, ks), 0))
        dr = dot3(dzs, both((qs, ws), 0), TN)
        dw = dw + dp[span:] + dr[:span]
        dproj_ref[at[n], 0:h] = (dqp + dp[:span]).astype(BF16)
        dproj_ref[at[n], h : 2 * h] = (dkpt.T + dr[span:]).astype(BF16)
        dproj_ref[at[n], 2 * h : 3 * h] = dvt_ref[:, at[n]].T.astype(BF16)
        dproj_ref[at[n], 3 * h : 4 * h] = (inv * (dw - w * jnp.sum(dw * w, -1, keepdims=True))).astype(BF16)


def head_specs(rows, h, spans):
    one = pl.BlockSpec((rows, h), lambda s: (0, s))
    two = pl.BlockSpec((rows, 2 * h), lambda s: (0, s))
    four = pl.BlockSpec((rows, 4 * h), lambda s: (0, s))
    keys = pl.BlockSpec((1, spans, h, rows), lambda s: (s, 0, 0, 0))
    docs = pl.BlockSpec(memory_space=pltpu.SMEM)
    return one, two, four, keys, docs


def attention_forward(docs, proj, logits, slots, span):
    rows = proj.shape[0]
    spans, h = rows // span, span
    one, two, four, keys, smem = head_specs(rows, h, spans)

    def full(width, dtype=F32):
        return jax.ShapeDtypeStruct((rows, slots * width), dtype)

    return pl.pallas_call(
        functools.partial(attention_forward_kernel, spans, span),
        grid=(slots,),
        in_specs=[smem, four, one],
        out_specs=[one, one, one, one, one, two, one, one, one, keys],
        out_shape=[
            full(h, BF16), full(h), full(h), full(h), full(h), full(2 * h), full(h), full(h, BF16), full(h),
            jax.ShapeDtypeStruct((slots, spans, h, rows), BF16),
        ],
        scratch_shapes=[pltpu.VMEM((h, rows), F32), pltpu.VMEM((h, rows), F32)],
        compiler_params=pltpu.CompilerParams(vmem_limit_bytes=60 * 1024 * 1024),
        name="attention_forward",
    )(docs, proj, logits)


def attention_backward(docs, proj, logits, datt, saved, slots, span):
    rows = proj.shape[0]
    spans, h = rows // span, span
    one, two, four, keys, smem = head_specs(rows, h, spans)
    wide, tall = pltpu.VMEM((h, rows), F32), pltpu.VMEM((rows, h), F32)
    return pl.pallas_call(
        functools.partial(attention_backward_kernel, spans, span),
        grid=(slots,),
        in_specs=[smem, four, one, one, one, one, one, one, two, one, one, one, keys],
        out_specs=[four, pl.BlockSpec((rows, h), lambda s: (0, 0))],
        out_shape=[
            jax.ShapeDtypeStruct((rows, slots * 4 * h), BF16),
            jax.ShapeDtypeStruct((rows, h), BF16),
        ],
        scratch_shapes=[wide, wide, tall, tall, wide, tall],
        compiler_params=pltpu.CompilerParams(vmem_limit_bytes=60 * 1024 * 1024),
        name="attention_backward",
    )(docs, proj, logits, datt, *saved)


MESH = pl.DeviceIdType.MESH


def send(src, dst, send_sem, recv_sem, **device):
    return pltpu.make_async_remote_copy(
        src_ref=src, dst_ref=dst, send_sem=send_sem, recv_sem=recv_sem, device_id=device, device_id_type=MESH
    )


def greet(peers, groups=0):
    barrier = pltpu.get_barrier_semaphore()
    me = lax.axis_index("blk")
    for k in range(1, peers):
        pl.semaphore_signal(barrier, inc=1, device_id={"blk": (me + k) % peers}, device_id_type=MESH)
    if groups:
        at = lax.axis_index("dp")

        @pl.when(at + 1 < groups)
        def _():
            pl.semaphore_signal(barrier, inc=1, device_id={"dp": at + 1}, device_id_type=MESH)

        @pl.when(at > 0)
        def _():
            pl.semaphore_signal(barrier, inc=1, device_id={"dp": at - 1}, device_id_type=MESH)

        @pl.when((at > 0) & (at + 1 < groups))
        def _():
            pl.semaphore_wait(barrier, peers + 1)

        @pl.when((at == 0) | (at + 1 == groups))
        def _():
            pl.semaphore_wait(barrier, peers)
    else:
        pl.semaphore_wait(barrier, peers - 1)


class Spread:
    def __init__(self, peers, src, pick, sems, recvs):
        me = lax.axis_index("blk")
        self.chips = peers // 2
        sibling = me + 1 - 2 * (me % 2)
        self.first = [send(src, pick(me), sems.at[0], recvs.at[0], blk=sibling)]
        self.second = []
        for k in range(1, self.chips):
            self.first.append(send(src, pick(me), sems.at[k], recvs.at[k], blk=(me + 2 * k) % peers))
            origin = pick((me + peers - 2 * k) % peers)
            at = self.chips + k - 1
            self.second.append(send(origin, origin, sems.at[at], recvs.at[at], blk=sibling))

    def start(self):
        for copy in self.first[1:] + self.first[:1]:
            copy.start()

    def forward(self):
        for copy, onward in zip(self.first[1:], self.second):
            copy.wait_recv()
            onward.start()

    def finish(self):
        for copy in self.first:
            copy.wait_send()
        self.first[0].wait_recv()
        for copy in self.second:
            copy.wait()


class Line:
    def __init__(self, groups, pick, sems, recvs):
        self.groups, self.pick, self.sems, self.recvs = groups, pick, sems, recvs
        self.at = lax.axis_index("dp")

    def copies(self, step):
        at, n = self.at, self.groups
        up, down = at - (step - 1), at + (step - 1)
        i = 2 * (step - 1)
        above = send(self.pick(up), self.pick(up), self.sems.at[i], self.recvs.at[i], dp=at + 1)
        below = send(self.pick(down), self.pick(down), self.sems.at[i + 1], self.recvs.at[i + 1], dp=at - 1)
        return above, below

    def start(self, step):
        at, n = self.at, self.groups
        above, below = self.copies(step)
        pl.when((at + 1 < n) & (at - (step - 1) >= 0))(above.start)
        pl.when((at - 1 >= 0) & (at + (step - 1) < n))(below.start)

    def arrive(self, step):
        at, n = self.at, self.groups
        i = 2 * (step - 1)
        pick = self.pick

        @pl.when(at - step >= 0)
        def _():
            send(pick(at - step), pick(at - step), self.sems.at[i], self.recvs.at[i], dp=at - 1).wait_recv()

        @pl.when(at + step < n)
        def _():
            send(pick(at + step), pick(at + step), self.sems.at[i + 1], self.recvs.at[i + 1], dp=at + 1).wait_recv()

    def finish(self):
        at, n = self.at, self.groups
        for step in range(1, n):
            above, below = self.copies(step)
            pl.when((at + 1 < n) & (at - (step - 1) >= 0))(above.wait_send)
            pl.when((at - 1 >= 0) & (at + (step - 1) < n))(below.wait_send)


def gather_kernel(
    groups, peers, attn_ref, ffn_ref, tok_ref, dy_ref, out_ref,
    attn_all, ffn_all, tok_all, dy_all, out_all,
    local, a_s, a_r, f_s, f_r, t_s, t_r, d_s, d_r, o_s, o_r, al_s, al_r, ol_s, ol_r,
):
    me, at = lax.axis_index("blk"), lax.axis_index("dp")
    own = [
        pltpu.make_async_copy(attn_ref.at[me], attn_all.at[at, me], local.at[0]),
        pltpu.make_async_copy(ffn_ref.at[me], ffn_all.at[me], local.at[1]),
        pltpu.make_async_copy(tok_ref, tok_all.at[me], local.at[2]),
        pltpu.make_async_copy(dy_ref, dy_all.at[me], local.at[3]),
        pltpu.make_async_copy(out_ref, out_all.at[at, me], local.at[4]),
    ]
    for copy in own:
        copy.start()
    greet(peers, groups)
    attn = [
        send(attn_ref.at[(me + k) % peers], attn_all.at[at, me], a_s.at[k], a_r.at[k], blk=(me + k) % peers)
        for k in range(1, peers)
    ]
    ffn = [
        send(ffn_ref.at[(me + k) % peers], ffn_all.at[me], f_s.at[k], f_r.at[k], blk=(me + k) % peers)
        for k in range(1, peers)
    ]
    for copy in attn:
        copy.start()
    tok = Spread(peers, tok_ref, lambda b: tok_all.at[b], t_s, t_r)
    dys = Spread(peers, dy_ref, lambda b: dy_all.at[b], d_s, d_r)
    out = Spread(peers, out_all.at[:, me], lambda b: out_all.at[:, b], o_s, o_r)
    attn_line = Line(groups, lambda d: attn_all.at[d], al_s, al_r)
    out_line = Line(groups, lambda d: out_all.at[d, me], ol_s, ol_r)
    tok.start()
    own[4].wait()
    out_line.start(1)
    for copy in attn:
        copy.wait_recv()
    own[0].wait()
    attn_line.start(1)
    for copy in ffn:
        copy.start()
    out_line.arrive(1)
    for step in range(2, groups):
        out_line.start(step)
        out_line.arrive(step)
    tok.forward()
    out.start()
    for step in range(2, groups):
        attn_line.arrive(step - 1)
        attn_line.start(step)
    out.forward()
    dys.start()
    dys.forward()
    attn_line.arrive(groups - 1)
    for copy in ffn:
        copy.wait_recv()
    for copy in attn + ffn:
        copy.wait_send()
    for spread in (tok, out, dys):
        spread.finish()
    attn_line.finish()
    out_line.finish()
    for i in (1, 2, 3):
        own[i].wait()


def gather_all(groups, peers, attn, ffn, tok, dy, out):
    def shape(*dims):
        return jax.ShapeDtypeStruct(dims, BF16)

    dma = pltpu.SemaphoreType.DMA
    hbm = pl.BlockSpec(memory_space=pl.ANY)
    return pl.pallas_call(
        functools.partial(gather_kernel, groups, peers),
        in_specs=[hbm] * 5,
        out_specs=[hbm] * 5,
        out_shape=[
            shape(groups, *attn.shape), shape(*ffn.shape), shape(peers, *tok.shape), shape(peers, *dy.shape),
            shape(groups, peers, *out.shape),
        ],
        scratch_shapes=[dma((5,))] + [dma((peers,))] * 10 + [dma((2 * groups,))] * 4,
        compiler_params=pltpu.CompilerParams(collective_id=1, has_side_effects=True),
        name="gather_all",
    )(attn, ffn, tok, dy, out)


def branch_kernel(
    peers, pieces, att_ref, out_ref, tok_ref, gain_ref, res_ref, n2_all,
    got, low, local, a_s, a_r, n_s, n_r,
):
    me = lax.axis_index("blk")
    rows, width = tok_ref.shape
    own = pltpu.make_async_copy(att_ref.at[pl.ds(pl.multiple_of(me * rows, rows), rows)], got.at[me], local.at[0])
    own.start()
    greet(peers)
    moves = []
    for k in range(1, peers):
        p = (me + k) % peers
        moves.append(send(att_ref.at[pl.ds(pl.multiple_of(p * rows, rows), rows)], got.at[me], a_s.at[k], a_r.at[k], blk=p))
    for copy in moves:
        copy.start()
    for copy in moves:
        copy.wait_recv()
    own.wait()
    attended = jnp.concatenate([got[b] for b in range(pieces)], 1)[:, :width]
    square = jnp.zeros((rows, 1), F32)
    tile = 256
    for j in range(0, width, tile):
        part = tok_ref[:, j : j + tile].astype(F32) + dot(attended, out_ref[:, j : j + tile])
        res_ref[:, j : j + tile] = part
        square = square + jnp.sum(part * part, -1, keepdims=True)
    low[...] = (res_ref[...] * lax.rsqrt(square / width + EPSILON) * gain_ref[...]).astype(BF16)
    keep = pltpu.make_async_copy(low, n2_all.at[me], local.at[1])
    keep.start()
    spread = Spread(peers, low, lambda b: n2_all.at[b], n_s, n_r)
    spread.start()
    spread.forward()
    spread.finish()
    for copy in moves:
        copy.wait_send()
    keep.wait()


def branch(peers, att, out_full, tok, gain):
    rows, width = tok.shape
    pieces = -(-width // att.shape[1])
    dma = pltpu.SemaphoreType.DMA
    vmem, hbm = pl.BlockSpec(memory_space=pltpu.VMEM), pl.BlockSpec(memory_space=pl.ANY)
    return pl.pallas_call(
        functools.partial(branch_kernel, peers, pieces),
        in_specs=[vmem] * 4,
        out_specs=[vmem, hbm],
        out_shape=[jax.ShapeDtypeStruct((rows, width), F32), jax.ShapeDtypeStruct((peers, rows, width), BF16)],
        scratch_shapes=[
            pltpu.VMEM((peers, rows, att.shape[1]), BF16), pltpu.VMEM((rows, width), BF16),
            dma((2,)), dma((peers,)), dma((peers,)), dma((peers,)), dma((peers,)),
        ],
        compiler_params=pltpu.CompilerParams(
            collective_id=2, has_side_effects=True, vmem_limit_bytes=48 * 1024 * 1024
        ),
        name="branch_and_norm",
    )(att, out_full, tok, gain)


class Reduce:
    def __init__(self, peers, part, half, mine, got, sems, recvs):
        me = lax.axis_index("blk")
        self.chips = peers // 2
        self.core, self.chip = me % 2, me // 2
        sibling = me + 1 - 2 * self.core
        self.part, self.half, self.mine, self.got = part, half, mine, got
        self.inner, self.outer = [], []
        for k in range(self.chips):
            to = (self.chip + k) % self.chips
            self.inner.append(send(part.at[2 * to + 1 - self.core], half.at[to], sems.at[k], recvs.at[k], blk=sibling))
        for k in range(1, self.chips):
            to = (self.chip + k) % self.chips
            at = self.chips + k
            self.outer.append(send(mine.at[k], got.at[k], sems.at[at], recvs.at[at], blk=2 * to + self.core))

    def order(self):
        return [k for k in range(1, self.chips)] + [0]

    def start(self):
        for k in self.order():
            self.inner[k].start()

    def pair(self):
        for k in self.order():
            self.inner[k].wait_recv()
            to = (self.chip + k) % self.chips
            both_cores = self.part[2 * to + self.core].astype(F32) + self.half[to].astype(F32)
            self.mine[k] = both_cores.astype(BF16)
            if k > 0:
                self.outer[k - 1].start()

    def total(self):
        total = self.mine[0].astype(F32)
        for k in range(1, self.chips):
            self.outer[k - 1].wait_recv()
            total = total + self.got[k].astype(F32)
        return total

    def finish(self):
        for copy in self.inner + self.outer:
            copy.wait_send()

    @staticmethod
    def scratch(peers, rows, width):
        block = pltpu.VMEM((peers // 2, rows, width), BF16)
        return [block, block, block, pltpu.SemaphoreType.DMA((peers,)), pltpu.SemaphoreType.DMA((peers,))]


def residual_kernel(
    peers, part_ref, res_ref, dy_ref, gain_ref, dres_ref, db_all, low, local, half, mine, got, r_s, r_r, n_s, n_r
):
    me = lax.axis_index("blk")
    greet(peers)
    reduce = Reduce(peers, part_ref, half, mine, got, r_s, r_r)
    reduce.start()
    reduce.pair()
    dres_ref[...] = dy_ref[...].astype(F32) + rms_pull(res_ref[...], gain_ref[...], reduce.total())
    low[...] = dres_ref[...].astype(BF16)
    keep = pltpu.make_async_copy(low, db_all.at[me], local.at[0])
    keep.start()
    spread = Spread(peers, low, lambda b: db_all.at[b], n_s, n_r)
    spread.start()
    spread.forward()
    spread.finish()
    reduce.finish()
    keep.wait()


def residual_gradient(peers, part, res, dy, gain):
    rows, width = res.shape
    dma = pltpu.SemaphoreType.DMA
    vmem, hbm = pl.BlockSpec(memory_space=pltpu.VMEM), pl.BlockSpec(memory_space=pl.ANY)
    return pl.pallas_call(
        functools.partial(residual_kernel, peers),
        in_specs=[vmem] * 4,
        out_specs=[vmem, hbm],
        out_shape=[jax.ShapeDtypeStruct((rows, width), F32), jax.ShapeDtypeStruct((peers, rows, width), BF16)],
        scratch_shapes=[pltpu.VMEM((rows, width), BF16), dma((1,))]
        + Reduce.scratch(peers, rows, width)
        + [dma((peers,)), dma((peers,))],
        compiler_params=pltpu.CompilerParams(
            collective_id=3, has_side_effects=True, vmem_limit_bytes=48 * 1024 * 1024
        ),
        name="residual_gradient",
    )(part, res, dy, gain)


def final_kernel(
    groups, peers, grad_ref, part_ref, outp_ref, tok_ref, gain_ref, dres_ref, res_ref,
    dtok_ref, block_ref, rows_ref,
    up_got, dn_got, up_out, dn_out, fin,
    l_s, l_r, w_s, w_r, local, half, mine, got, r_s, r_r, half2, mine2, got2, q_s, q_r,
):
    me, at = lax.axis_index("blk"), lax.axis_index("dp")
    greet(peers, groups)
    n = groups

    def stage(out, chunk, arrived):
        def body(j, carry):
            out[j] = (grad_ref[chunk, j].astype(F32) + arrived[j].astype(F32)).astype(BF16)
            return carry

        lax.fori_loop(0, peers, body, 0)

    def up_from(i, src):
        return send(src, up_got.at[i], l_s.at[2 * i], l_r.at[2 * i], dp=at + 1)

    def down_from(i, src):
        return send(src, dn_got.at[i], l_s.at[2 * i + 1], l_r.at[2 * i + 1], dp=at - 1)

    def step(i):
        far = n - 1 - i

        @pl.when((at + far < n) & (at == 0))
        def _():
            up_from(i, grad_ref.at[at + far]).start()

        @pl.when((at + far < n) & (at > 0))
        def _():
            send(up_out.at[0], up_got.at[i - 1], l_s.at[2 * i - 2], l_r.at[2 * i - 2], dp=at - 1).wait_recv()
            stage(up_out.at[i], at + far, up_got.at[i - 1])
            up_from(i, up_out.at[i]).start()

        @pl.when((at - far >= 0) & (at == n - 1))
        def _():
            down_from(i, grad_ref.at[at - far]).start()

        @pl.when((at - far >= 0) & (at < n - 1))
        def _():
            send(dn_out.at[0], dn_got.at[i - 1], l_s.at[2 * i - 1], l_r.at[2 * i - 1], dp=at + 1).wait_recv()
            stage(dn_out.at[i], at - far, dn_got.at[i - 1])
            down_from(i, dn_out.at[i]).start()

    reduce = Reduce(peers, part_ref, half, mine, got, r_s, r_r)
    reduce2 = Reduce(peers, outp_ref, half2, mine2, got2, q_s, q_r)
    reduce.start()
    step(0)
    reduce2.start()
    reduce.pair()
    step(1) if n > 2 else None
    reduce2.pair()
    for i in range(2, n - 1):
        step(i)
    dtok_ref[...] = dres_ref[...] + rms_pull(tok_ref[...].astype(F32), gain_ref[...], reduce.total())
    block_ref[...] = (res_ref[...] + reduce2.total()).astype(BF16)
    i = n - 2

    @pl.when(at > 0)
    def _():
        send(up_out.at[0], up_got.at[i], l_s.at[2 * i], l_r.at[2 * i], dp=at - 1).wait_recv()
        stage(fin, at, up_got.at[i])

    @pl.when(at == 0)
    def _():
        send(dn_out.at[0], dn_got.at[i], l_s.at[2 * i + 1], l_r.at[2 * i + 1], dp=at + 1).wait_recv()
        stage(fin, at, dn_got.at[i])

    @pl.when((at > 0) & (at < n - 1))
    def _():
        send(dn_out.at[0], dn_got.at[i], l_s.at[2 * i + 1], l_r.at[2 * i + 1], dp=at + 1).wait_recv()

        def body(j, carry):
            fin[j] = (fin[j].astype(F32) + dn_got[i, j].astype(F32)).astype(BF16)
            return carry

        lax.fori_loop(0, peers, body, 0)

    own = pltpu.make_async_copy(fin.at[me], rows_ref.at[me], local.at[0])
    own.start()
    moves = [
        send(fin.at[(me + k) % peers], rows_ref.at[me], w_s.at[k], w_r.at[k], blk=(me + k) % peers)
        for k in range(1, peers)
    ]
    for copy in moves:
        copy.start()
    for copy in moves:
        copy.wait()
    own.wait()
    reduce.finish()
    reduce2.finish()
    for i in range(n - 1):
        far = n - 1 - i
        pl.when(at + far < n)(up_from(i, up_out.at[i]).wait_send)
        pl.when(at - far >= 0)(down_from(i, dn_out.at[i]).wait_send)


def final_sums(groups, peers, grad, part, outp, tok, gain, dres, res):
    rows, width = tok.shape
    share, cols = grad.shape[2:]
    dma = pltpu.SemaphoreType.DMA
    vmem, hbm = pl.BlockSpec(memory_space=pltpu.VMEM), pl.BlockSpec(memory_space=pl.ANY)
    hop = pltpu.VMEM((groups - 1, peers, share, cols), BF16)
    return pl.pallas_call(
        functools.partial(final_kernel, groups, peers),
        in_specs=[vmem] * 7,
        out_specs=[vmem, vmem, hbm],
        out_shape=[
            jax.ShapeDtypeStruct((rows, width), F32),
            jax.ShapeDtypeStruct((rows, width), BF16),
            jax.ShapeDtypeStruct((peers, share, cols), BF16),
        ],
        scratch_shapes=[hop, hop, hop, hop, pltpu.VMEM((peers, share, cols), BF16)]
        + [dma((2 * groups,)), dma((2 * groups,)), dma((peers,)), dma((peers,)), dma((1,))]
        + Reduce.scratch(peers, rows, width) * 2,
        compiler_params=pltpu.CompilerParams(
            collective_id=4, has_side_effects=True, vmem_limit_bytes=60 * 1024 * 1024
        ),
        name="final_sums",
    )(grad, part, outp, tok, gain, dres, res)


def to_rows(value, axis="blk"):
    return lax.all_to_all(value, axis, split_axis=0, concat_axis=1, tiled=True)


def shards(
    tokens, cotangent, doc_table, gain_attn, attn_in, beta_proj, attn_out, gain_ffn, ffn_in, ffn_down
):
    rows, width = tokens.shape
    heads = beta_proj.shape[1]
    h = width // heads
    groups, peers = lax.axis_size("dp"), lax.axis_size("blk")
    slots = -(-heads // peers)
    padded = slots * peers
    share = attn_in.shape[0]
    units = ffn_down.shape[0]
    me = lax.axis_index("blk")
    by_head = attn_in.reshape(share, 4, heads, h).transpose(2, 0, 1, 3)
    by_head = jnp.pad(by_head, ((0, padded - heads), (0, 0), (0, 0), (0, 0)))
    by_head = by_head.reshape(peers, slots, share, 4 * h).transpose(0, 2, 1, 3).reshape(peers, share, slots * 4 * h)
    strengths = jnp.pad(beta_proj, ((0, 0), (0, padded - heads))).reshape(share, peers, slots).transpose(1, 0, 2)
    gains = jnp.broadcast_to(jnp.stack([gain_attn, gain_ffn], -1)[None], (peers, share, 2))
    extra = jnp.pad(jnp.concatenate([strengths, gains], -1), ((0, 0), (0, 0), (0, h - slots - 2)))
    attn_parts = jnp.concatenate([by_head, extra], -1)
    ffn_parts = ffn_in.reshape(share, 2, groups, peers, units).transpose(3, 0, 1, 2, 4).reshape(peers, share, -1)
    attn_slab, ffn_part, x_all, dy_all, out_full = gather_all(
        groups, peers, attn_parts, ffn_parts, tokens, cotangent, attn_out
    )
    attn_slab = attn_slab.reshape(width, -1)
    ffn_part = ffn_part.reshape(peers * share, -1)
    x_all, dy_all = x_all.reshape(peers * rows, width), dy_all.reshape(peers * rows, width)
    out_full = out_full.reshape(width, width)
    ffn_slab = lax.all_gather(ffn_part, "dp", axis=0, tiled=True)
    down_slab = lax.all_gather(ffn_down, "dp", axis=0, tiled=True)

    attn_cols = slots * 4 * h
    w_attn = attn_slab[:, :attn_cols]
    w_beta = attn_slab[:, attn_cols : attn_cols + slots]
    gain_one = attn_slab[:, attn_cols + slots].astype(F32)[None]
    gain_two = attn_slab[:, attn_cols + slots + 1].astype(F32)[None]

    normed = rms_norm(x_all.astype(F32), gain_one).astype(BF16)
    proj = dot(normed, w_attn)
    logits = dot(normed, jnp.repeat(w_beta, h, axis=1))
    attended, *saved = attention_forward(doc_table, proj, logits, slots, rows)
    residual, normed_two_all = branch(peers, attended, out_full, tokens, gain_two)
    normed_two_all = normed_two_all.reshape(peers * rows, width)
    attended_all = lax.all_gather(attended, "blk", axis=1, tiled=True)[:, :width]

    gate_up = dot(normed_two_all, ffn_slab)
    mine = gate_up.shape[1] // 2
    gate, up = gate_up[:, :mine], gate_up[:, mine:]
    sig = jax.nn.sigmoid(gate)
    hidden = (gate * sig * up).astype(BF16)
    dhidden = dot(dy_all, down_slab, NT)
    dgate = dhidden * up * (sig * (1.0 + gate * (1.0 - sig)))
    dup = dhidden * (gate * sig)
    dgate_up = jnp.concatenate([dgate, dup], 1).astype(BF16)
    ffn_pull = dot(dgate_up, ffn_slab, NT).astype(BF16).reshape(peers, rows, width)
    dresidual, dbranch_all = residual_gradient(peers, ffn_pull, residual, cotangent, gain_two)
    dbranch_all = dbranch_all.reshape(peers * rows, width)
    out_part = dot(hidden, down_slab).astype(BF16).reshape(peers, rows, width)
    grad_ffn = lax.psum_scatter(dot(normed_two_all, dgate_up, TN).astype(BF16), "dp", scatter_dimension=0, tiled=True)
    grad_down = lax.psum_scatter(dot(hidden, dy_all, TN).astype(BF16), "dp", scatter_dimension=0, tiled=True)

    out_rows = jnp.pad(out_full, ((0, (padded - heads) * h), (0, 0)))
    out_rows = lax.dynamic_slice_in_dim(out_rows, me * slots * h, slots * h, 0)
    datt = dot(dbranch_all, out_rows, NT)
    dproj, dlogits = attention_backward(doc_table, proj, logits, datt, saved, slots, rows)
    dslab = jnp.concatenate([dproj, dlogits], 1)
    part = width // peers
    dbranch_cols = lax.dynamic_slice_in_dim(dbranch_all, me * part, part, 1)
    grad_out = lax.psum_scatter(
        dot(attended_all, dbranch_cols, TN).astype(BF16), "dp", scatter_dimension=0, tiled=True
    )
    attn_pull = dot(dslab, attn_slab, NT).astype(BF16).reshape(peers, rows, width)
    grad_attn = dot(normed, dslab, TN).astype(BF16).reshape(groups, peers, share, -1)
    grad_tokens, block_out, grad_attn = final_sums(
        groups, peers, grad_attn, attn_pull, out_part, tokens, gain_one, dresidual, residual
    )

    grad_attn = grad_attn.astype(F32)
    grad_beta = grad_attn[:, :, attn_cols : attn_cols + slots].transpose(1, 0, 2).reshape(share, padded)[:, :heads]
    grad_attn_in = grad_attn[:, :, :attn_cols].reshape(peers, share, slots, 4, h)
    grad_attn_in = grad_attn_in.transpose(1, 3, 0, 2, 4).reshape(share, 4, padded, h)[:, :, :heads].reshape(share, -1)
    grad_attn_out = to_rows(grad_out).astype(F32)
    grad_ffn_in = to_rows(grad_ffn).reshape(share, peers, 2, groups, units).astype(F32)
    grad_ffn_in = grad_ffn_in.transpose(0, 2, 3, 1, 4).reshape(share, -1)
    grad_gain_attn = (
        jnp.sum(grad_attn_in * attn_in.astype(F32), -1) + jnp.sum(grad_beta * beta_proj.astype(F32), -1)
    ) / gain_attn.astype(F32)
    grad_gain_ffn = jnp.sum(grad_ffn_in * ffn_in.astype(F32), -1) / gain_ffn.astype(F32)
    return (
        block_out, grad_tokens, grad_gain_attn, grad_attn_in, grad_beta, grad_attn_out,
        grad_gain_ffn, grad_ffn_in, grad_down.astype(F32),
    )


def solution(mesh):
    split, vector = P(("dp", "blk"), None), P(("dp", "blk"))
    in_specs = (split, split, P("dp", None), vector, split, split, split, vector, split, split)
    out_specs = (split, split, vector, split, split, split, vector, split, split)
    return jax.shard_map(shards, mesh=mesh, in_specs=in_specs, out_specs=out_specs, check_vma=False)
```

```python
import functools

import jax
import jax.numpy as jnp
from jax import lax
from jax.experimental import pallas as pl
from jax.experimental.pallas import tpu as pltpu
from jax.sharding import PartitionSpec as P

EPSILON = 1e-06
F32 = jnp.float32
BF16 = jnp.bfloat16

NN = (((1,), (0,)), ((), ()))
NT = (((1,), (1,)), ((), ()))
TN = (((0,), (0,)), ((), ()))


def dot(a, b, dims=NN):
    return lax.dot_general(a, b, dims, preferred_element_type=F32)


def halves(x):
    high = x.astype(BF16)
    return high, (x - high.astype(F32)).astype(BF16)


def dot3(a, b, dims=NN):
    (ah, al), (bh, bl) = a, b
    return dot(ah, bh, dims) + (dot(ah, bl, dims) + dot(al, bh, dims))


def both(parts, axis):
    return tuple(jnp.concatenate(p, axis) for p in zip(*parts))


def rms_norm(values, gain):
    return values * lax.rsqrt(jnp.mean(values * values, axis=-1, keepdims=True) + EPSILON) * gain


def rms_pull(values, gain, grad):
    scale = lax.rsqrt(jnp.mean(values * values, axis=-1, keepdims=True) + EPSILON)
    inner = grad * gain
    along = jnp.mean(inner * values, axis=-1, keepdims=True)
    return scale * inner - values * (scale * scale * scale) * along


def lanes(n):
    return lax.broadcasted_iota(jnp.int32, (n, n), 1)


def rows_of(n):
    return lax.broadcasted_iota(jnp.int32, (n, n), 0)


def inverses(grams, betas, span):
    r, c = rows_of(span), lanes(span)
    eye = r == c
    outs = []
    pair = (c + 1 == r) & (r % 2 == 1)
    for gram, beta in zip(grams, betas):
        below = jnp.where(pair, gram, 0.0) * beta * beta.T
        outs.append(jnp.where(eye, beta, 0.0) - below)
    size = 2
    while size < span:
        part = (r // (2 * size) == c // (2 * size)) & ((r // size) % 2 == 1) & ((c // size) % 2 == 0)
        sides = [halves(x) for x in outs]
        steps = [dot3(halves(jnp.where(part, g, 0.0)), x) for g, x in zip(grams, sides)]
        outs = [x - dot3(s, halves(t)) for x, s, t in zip(outs, sides, steps)]
        size *= 2
    return outs


MESH = pl.DeviceIdType.MESH


def send(src, dst, send_sem, recv_sem, **device):
    return pltpu.make_async_remote_copy(
        src_ref=src, dst_ref=dst, send_sem=send_sem, recv_sem=recv_sem, device_id=device, device_id_type=MESH
    )


def greet(peers, groups=0):
    barrier = pltpu.get_barrier_semaphore()
    me = lax.axis_index("blk")
    for k in range(1, peers):
        pl.semaphore_signal(barrier, inc=1, device_id={"blk": (me + k) % peers}, device_id_type=MESH)
    if groups:
        at = lax.axis_index("dp")

        @pl.when(at + 1 < groups)
        def _():
            pl.semaphore_signal(barrier, inc=1, device_id={"dp": at + 1}, device_id_type=MESH)

        @pl.when(at > 0)
        def _():
            pl.semaphore_signal(barrier, inc=1, device_id={"dp": at - 1}, device_id_type=MESH)

        @pl.when((at > 0) & (at + 1 < groups))
        def _():
            pl.semaphore_wait(barrier, peers + 1)

        @pl.when((at == 0) | (at + 1 == groups))
        def _():
            pl.semaphore_wait(barrier, peers)
    else:
        pl.semaphore_wait(barrier, peers - 1)


class Spread:
    def __init__(self, peers, source, pick, sems, recvs):
        me = lax.axis_index("blk")
        self.chips = peers // 2
        sibling = me + 1 - 2 * (me % 2)
        self.first = [send(source(me // 2), pick(me), sems.at[0], recvs.at[0], blk=sibling)]
        self.second = []
        for k in range(1, self.chips):
            to = (me + 2 * k) % peers
            self.first.append(send(source(to // 2), pick(me), sems.at[k], recvs.at[k], blk=to))
            origin = pick((me + peers - 2 * k) % peers)
            at = self.chips + k - 1
            self.second.append(send(origin, origin, sems.at[at], recvs.at[at], blk=sibling))

    def start(self):
        for copy in self.first[1:] + self.first[:1]:
            copy.start()

    def forward(self):
        for copy, onward in zip(self.first[1:], self.second):
            copy.wait_recv()
            onward.start()

    def finish(self):
        for copy in self.first:
            copy.wait_send()
        self.first[0].wait_recv()
        for copy in self.second:
            copy.wait()


class Line:
    def __init__(self, groups, pick, sems, recvs):
        self.groups, self.pick, self.sems, self.recvs = groups, pick, sems, recvs
        self.at = lax.axis_index("dp")

    def up(self, step, to, block):
        i = 2 * (step - 1)
        return send(self.pick(block), self.pick(block), self.sems.at[i], self.recvs.at[i], dp=to)

    def down(self, step, to, block):
        i = 2 * (step - 1) + 1
        return send(self.pick(block), self.pick(block), self.sems.at[i], self.recvs.at[i], dp=to)

    def start(self, step):
        at, n = self.at, self.groups

        @pl.when((at + 1 < n) & (at - (step - 1) >= 0))
        def _():
            self.up(step, at + 1, at - (step - 1)).start()

        @pl.when((at - 1 >= 0) & (at + (step - 1) < n))
        def _():
            self.down(step, at - 1, at + (step - 1)).start()

    def arrive(self, step, then=None):
        at, n = self.at, self.groups

        @pl.when(at - step >= 0)
        def _():
            self.up(step, at - 1, at - step).wait_recv()
            if then is not None:
                then(at - step).start()

        @pl.when(at + step < n)
        def _():
            self.down(step, at + 1, at + step).wait_recv()
            if then is not None:
                then(at + step).start()

    def finish(self):
        at, n = self.at, self.groups
        for step in range(1, n):

            @pl.when((at + 1 < n) & (at - (step - 1) >= 0))
            def _():
                self.up(step, at + 1, at - (step - 1)).wait_send()

            @pl.when((at - 1 >= 0) & (at + (step - 1) < n))
            def _():
                self.down(step, at - 1, at + (step - 1)).wait_send()


class LineSum:
    def __init__(self, groups, pick, up_got, dn_got, up_out, dn_out, sems, recvs):
        self.n, self.pick = groups, pick
        self.up_got, self.dn_got, self.up_out, self.dn_out = up_got, dn_got, up_out, dn_out
        self.sems, self.recvs = sems, recvs
        self.at = lax.axis_index("dp")

    @staticmethod
    def scratch(groups, *block):
        hop = pltpu.VMEM((groups - 1, *block), BF16)
        return [hop] * 4 + [pltpu.SemaphoreType.DMA((2 * groups,))] * 2

    def up(self, i, src, to):
        return send(src, self.up_got.at[i], self.sems.at[2 * i], self.recvs.at[2 * i], dp=to)

    def down(self, i, src, to):
        return send(src, self.dn_got.at[i], self.sems.at[2 * i + 1], self.recvs.at[2 * i + 1], dp=to)

    def add(self, out, one, other):
        def body(j, carry):
            out[j] = (one[j].astype(F32) + other[j].astype(F32)).astype(out.dtype)
            return carry

        lax.fori_loop(0, out.shape[0], body, 0)

    def step(self, i):
        at, n = self.at, self.n
        far = n - 1 - i

        @pl.when((at + far < n) & (at == 0))
        def _():
            self.up(i, self.pick(at + far), at + 1).start()

        @pl.when((at - far >= 0) & (at == n - 1))
        def _():
            self.down(i, self.pick(at - far), at - 1).start()

        if i > 0:

            @pl.when((at + far < n) & (at > 0))
            def _():
                self.up(i - 1, self.up_out.at[i - 1], at - 1).wait_recv()
                self.add(self.up_out.at[i], self.pick(at + far), self.up_got.at[i - 1])
                self.up(i, self.up_out.at[i], at + 1).start()

            @pl.when((at - far >= 0) & (at < n - 1))
            def _():
                self.down(i - 1, self.dn_out.at[i - 1], at + 1).wait_recv()
                self.add(self.dn_out.at[i], self.pick(at - far), self.dn_got.at[i - 1])
                self.down(i, self.dn_out.at[i], at - 1).start()

    def total(self, out):
        at, n, i = self.at, self.n, self.n - 2

        @pl.when(at > 0)
        def _():
            self.up(i, self.up_out.at[i], at - 1).wait_recv()
            self.add(out, self.pick(at), self.up_got.at[i])

        @pl.when(at == 0)
        def _():
            self.down(i, self.dn_out.at[i], at + 1).wait_recv()
            self.add(out, self.pick(at), self.dn_got.at[i])

        @pl.when((at > 0) & (at < n - 1))
        def _():
            self.down(i, self.dn_out.at[i], at + 1).wait_recv()
            self.add(out, out, self.dn_got.at[i])

    def finish(self):
        at, n = self.at, self.n
        for i in range(n - 1):
            far = n - 1 - i

            @pl.when(at + far < n)
            def _():
                self.up(i, self.up_out.at[i], at + 1).wait_send()

            @pl.when(at - far >= 0)
            def _():
                self.down(i, self.dn_out.at[i], at - 1).wait_send()


class Reduce:
    def __init__(self, peers, part, half, mine, got, sems, recvs, place=None):
        me = lax.axis_index("blk")
        self.chips = peers // 2
        self.core, self.chip = me % 2, me // 2
        sibling = me + 1 - 2 * self.core
        self.part, self.half, self.mine, self.got = part, half, mine, got
        self.inner, self.outer = [], []
        for k in range(self.chips):
            to = (self.chip + k) % self.chips
            self.inner.append(send(part.at[2 * to + 1 - self.core], half.at[k], sems.at[k], recvs.at[k], blk=sibling))
        for k in range(1, self.chips):
            to = (self.chip + k) % self.chips
            at = self.chips + k
            arrival = got.at[k] if place is None else place
            self.outer.append(send(mine.at[k], arrival, sems.at[at], recvs.at[at], blk=2 * to + self.core))

    def order(self):
        return [k for k in range(1, self.chips)] + [0]

    def start(self):
        for k in self.order():
            self.inner[k].start()

    def pair(self):
        for k in self.order():
            self.inner[k].wait_recv()
            to = (self.chip + k) % self.chips
            both_cores = self.part[2 * to + self.core].astype(F32) + self.half[k].astype(F32)
            self.mine[k] = both_cores.astype(BF16)
            if k > 0:
                self.outer[k - 1].start()

    def total(self):
        total = self.mine[0].astype(F32)
        for k in range(1, self.chips):
            self.outer[k - 1].wait_recv()
            total = total + self.got[k].astype(F32)
        return total

    def finish(self):
        for copy in self.inner + self.outer:
            copy.wait_send()

    @staticmethod
    def scratch(peers, rows, width):
        block = pltpu.VMEM((peers // 2, rows, width), BF16)
        return [block, block, block, pltpu.SemaphoreType.DMA((peers,)), pltpu.SemaphoreType.DMA((peers,))]


def fanout(peers, source, dst, sems, recvs):
    me = lax.axis_index("blk")
    copies = []
    for k in range(1, peers):
        p = (me + k) % peers
        copies.append(send(source(p), dst(p), sems.at[k], recvs.at[k], blk=p))
    return copies


def attention_forward_kernel(
    peers, spans, span, doc_ref, on_ref, head_ref, x_ref, gain_ref, w_ref, ext_ref, dy_ref,
    norm_ref, dy_all, proj_ref, logit_ref,
    low_ref, att_ref, sum_ref, a1_ref, g_ref, y_ref, e0_ref, qp_ref, m_ref, kts_ref,
    kpt_ref, kt_ref, keep_sem, d_s, d_r,
):
    h = span
    scale = h ** -0.5
    slot, me = pl.program_id(0), lax.axis_index("blk")
    tall = 2 * span

    def dy_copies():
        keep = pltpu.make_async_copy(dy_ref, dy_all.at[me], keep_sem.at[0])
        return keep, Spread(peers, lambda c: dy_ref, lambda b: dy_all.at[b], d_s, d_r)

    @pl.when(slot == 0)
    def _():
        greet(peers)
        keep, spread = dy_copies()
        keep.start()
        spread.start()

        def normalize(i, carry):
            rows = pl.ds(pl.multiple_of(i * tall, tall), tall)
            norm_ref[rows, :] = rms_norm(x_ref[rows, :].astype(F32), gain_ref[...]).astype(BF16)
            return carry

        lax.fori_loop(0, spans // 2, normalize, 0)

    def project(i, carry):
        rows = pl.ds(pl.multiple_of(i * tall, tall), tall)
        normed = norm_ref[rows, :]
        proj_ref[rows, :] = dot(normed, w_ref[...])
        every = dot(normed, ext_ref[...], NT)
        lane = lax.broadcasted_iota(jnp.int32, every.shape, 1)
        mine = jnp.sum(jnp.where(lane == head_ref[slot], every, 0.0), -1, keepdims=True)
        logit_ref[rows, :] = jnp.broadcast_to(mine, (tall, h))
        return carry

    lax.fori_loop(0, spans // 2, project, 0)
    r, c = rows_of(span), lanes(span)
    lower, strict, eye = c <= r, c < r, (c == r).astype(F32)
    at = [pl.ds(n * span, span) for n in range(spans)]
    group = 4
    for first in range(0, spans, group):
        members = range(first, min(first + group, spans))
        grams, betas, kept = [], [], []
        for n in members:
            q = proj_ref[at[n], 0:h]
            k = proj_ref[at[n], h : 2 * h]
            d = proj_ref[at[n], 3 * h : 4 * h]
            w = d * lax.rsqrt(jnp.sum(d * d, -1, keepdims=True) + EPSILON)
            qs, ks, ws = halves(q), halves(k), halves(w)
            z = dot3(both((qs, ws), 0), both((ws, ks), 0), NT)
            a1 = jnp.where(lower, z[:span, :span], 0.0)
            a1_ref[at[n], :] = a1
            b1 = jnp.where(strict, z[span:, span:], 0.0)
            grams.append(jnp.where(strict, z[span:, :span], 0.0))
            betas.append(2.0 / (1.0 + jnp.exp(-logit_ref[at[n], :])))
            kept.append((q, k, ws, halves(a1), halves(b1), z[:span, span:]))
        solved = inverses(grams, betas, span)
        for n, g, (q, k, ws, a1s, b1s, qk) in zip(members, solved, kept):
            g_ref[at[n], :] = g
            y = dot3(halves(g), both((ws, b1s), 1))
            y_ref[at[n], :] = y
            ys = halves(y)
            t = dot3(a1s, ys)
            u = dot3(ws, ys, TN)
            qp_ref[at[n], :] = (q - t[:, :h]).astype(BF16)
            local = (qk - t[:, h:]) * scale
            e0_ref[at[n], :] = jnp.where(lower, jnp.exp(local), 0.0)
            m_ref[at[n], :] = eye - u[:, :h]
            kpt_ref[:, at[n]] = k.T - u[:, h:]
    for n in range(spans):
        w = n * span
        e0 = e0_ref[at[n], :]
        total = jnp.sum(e0, -1, keepdims=True)
        numer = dot(e0.astype(BF16), proj_ref[at[n], 2 * h : 3 * h].astype(BF16))
        if n > 0:
            kt = kt_ref[:, :w]
            kts = halves(kt)
            kts_ref[0, n, :, :w] = kts[0]
            block = jnp.exp(dot(qp_ref[at[n], :], kts[0]) * scale)
            block = jnp.concatenate(
                [jnp.where(doc_ref[0, j] == doc_ref[0, n], block[:, j * span : (j + 1) * span], 0.0) for j in range(n)], 1
            )
            total = total + jnp.sum(block, -1, keepdims=True)
            numer = numer + dot(block.astype(BF16), proj_ref[:w, 2 * h : 3 * h].astype(BF16))
            if n < spans - 1:
                kt_ref[:, :w] = dot3(halves(m_ref[at[n], :]), kts)
        if n < spans - 1:
            kt_ref[:, at[n]] = kpt_ref[:, at[n]]
        attended = numer / total
        att_ref[at[n], :] = attended
        low_ref[at[n], :] = jnp.where(on_ref[slot] > 0, attended, 0.0).astype(BF16)
        sum_ref[at[n], :] = jnp.broadcast_to(total, (span, h))

    @pl.when(slot == 0)
    def _():
        dy_copies()[1].forward()

    @pl.when(slot == pl.num_programs(0) - 1)
    def _():
        keep, spread = dy_copies()
        spread.finish()
        keep.wait()


def attention_backward_kernel(
    peers, spans, span, doc_ref, on_ref, head_ref, outp_ref, res_ref, proj_ref, logit_ref, datt_ref,
    att_ref, sum_ref, a1_ref, g_ref, y_ref, e0_ref, qp_ref, m_ref, kts_ref,
    dproj_ref, dlogit_ref, block_ref,
    gkt_ref, dvt_ref, dqp_ref, dm_ref, dkpt_ref, ds_ref, half, mine, got, r_s, r_r,
):
    h = span
    scale = h ** -0.5
    r, c = rows_of(span), lanes(span)
    lower, strict, same = c <= r, c < r, c == r
    at = [pl.ds(n * span, span) for n in range(spans)]
    slot = pl.program_id(0)

    def reduce():
        return Reduce(peers, outp_ref, half, mine, got, r_s, r_r)

    @pl.when(slot == 0)
    def _():
        greet(peers)
        reduce().start()

    dvt_ref[...] = jnp.zeros_like(dvt_ref)
    for n in reversed(range(spans)):
        w = n * span
        last = n == spans - 1
        datt, total = jnp.where(on_ref[slot] > 0, datt_ref[at[n], :], 0.0), sum_ref[at[n], :]
        da = (datt / total).astype(BF16)
        delta = jnp.sum(datt * att_ref[at[n], :], -1, keepdims=True) / total
        e0 = e0_ref[at[n], :]
        mix = dot(da, proj_ref[at[n], 2 * h : 3 * h].astype(BF16), NT) - delta
        ds_ref[at[n], :] = (e0 * mix).astype(BF16).astype(F32) * scale
        dvt_ref[:, at[n]] += dot(da, e0.astype(BF16), TN)
        if n == 0:
            dqp_ref[at[n], :] = jnp.zeros((span, h), F32)
            dm_ref[at[n], :] = jnp.zeros((h, h), F32)
            dkpt_ref[:, at[n]] = gkt_ref[:, at[n]] if not last else jnp.zeros((h, span), F32)
            continue
        keys = kts_ref[0, n, :, :w]
        qp = qp_ref[at[n], :]
        block = jnp.exp(dot(qp, keys) * scale)
        block = jnp.concatenate(
            [jnp.where(doc_ref[0, j] == doc_ref[0, n], block[:, j * span : (j + 1) * span], 0.0) for j in range(n)], 1
        )
        wide = jnp.concatenate([delta] * n, 1)
        mix = dot(da, proj_ref[:w, 2 * h : 3 * h].astype(BF16), NT) - wide
        ds = (block * mix).astype(BF16)
        dqp_ref[at[n], :] = dot(ds, keys, NT) * scale
        pulled = dot(qp, ds, TN) * scale
        dvt_ref[:, :w] += dot(da, block.astype(BF16), TN)
        if last:
            dm_ref[at[n], :] = jnp.zeros((h, h), F32)
            dkpt_ref[:, at[n]] = jnp.zeros((h, span), F32)
            gkt_ref[:, :w] = pulled
        else:
            dkpt_ref[:, at[n]] = gkt_ref[:, at[n]]
            gs = halves(gkt_ref[:, :w])
            dm_ref[at[n], :] = dot(gs[0], keys, NT) + dot(gs[1], keys, NT)
            gkt_ref[:, :w] = pulled + dot3(halves(m_ref[at[n], :]), gs, TN)

    @pl.when(slot == 0)
    def _():
        reduce().pair()

    for n in range(spans):
        q = proj_ref[at[n], 0:h]
        k = proj_ref[at[n], h : 2 * h]
        d = proj_ref[at[n], 3 * h : 4 * h]
        inv = lax.rsqrt(jnp.sum(d * d, -1, keepdims=True) + EPSILON)
        w = d * inv
        beta = 2.0 / (1.0 + jnp.exp(-logit_ref[at[n], :]))
        qs, ks, ws = halves(q), halves(k), halves(w)
        dqp, ds, dkpt = dqp_ref[at[n], :], ds_ref[at[n], :], dkpt_ref[:, at[n]]
        ys = halves(y_ref[at[n], :])
        left = both((halves(dqp), halves(ds)), 1)
        mid = both((halves(dm_ref[at[n], :]), halves(dkpt)), 1)
        da1 = jnp.where(lower, -dot3(left, ys, NT), 0.0)
        dy = dot3(halves(a1_ref[at[n], :]), left, TN) + dot3(ws, mid)
        dx = -dot3(halves(g_ref[at[n], :]), halves(dy), TN)
        dl = -dot3(halves(dx), ys, NT)
        dw = dx[:, :h] - dot3(ys, mid, NT)
        pull = jnp.sum(jnp.where(same, dl, 0.0), -1, keepdims=True)
        dlogit = -pull * (1.0 - 0.5 * beta) / jnp.maximum(beta, 1e-30)
        before = jnp.where(slot == 0, 0.0, dlogit_ref[at[n], :].astype(F32))
        dlogit_ref[at[n], :] = jnp.where(c == head_ref[slot], dlogit, before).astype(BF16)
        dz = jnp.concatenate(
            [
                jnp.concatenate([da1, ds], 1),
                jnp.concatenate([jnp.where(strict, dl, 0.0), jnp.where(strict, dx[:, h:], 0.0)], 1),
            ],
            0,
        )
        dzs = halves(dz)
        dp = dot3(dzs, both((ws, ks), 0))
        dr = dot3(dzs, both((qs, ws), 0), TN)
        dw = dw + dp[span:] + dr[:span]
        dproj_ref[at[n], 0:h] = (dqp + dp[:span]).astype(BF16)
        dproj_ref[at[n], h : 2 * h] = (dkpt.T + dr[span:]).astype(BF16)
        dproj_ref[at[n], 2 * h : 3 * h] = dvt_ref[:, at[n]].T.astype(BF16)
        dproj_ref[at[n], 3 * h : 4 * h] = (inv * (dw - w * jnp.sum(dw * w, -1, keepdims=True))).astype(BF16)

    @pl.when(slot == pl.num_programs(0) - 1)
    def _():
        last = reduce()
        block_ref[...] = (res_ref[...] + last.total()).astype(BF16)
        last.finish()


def head_specs(rows, h, spans):
    one = pl.BlockSpec((rows, h), lambda s: (0, s))
    two = pl.BlockSpec((rows, 2 * h), lambda s: (0, s))
    four = pl.BlockSpec((rows, 4 * h), lambda s: (0, s))
    keys = pl.BlockSpec((1, spans, h, rows), lambda s: (s, 0, 0, 0))
    docs = pl.BlockSpec(memory_space=pltpu.SMEM)
    return one, two, four, keys, docs


def attention_forward(docs, on, heads, x_all, gain, w, ext, dy, peers, slots, span):
    rows, width = x_all.shape
    spans, h = rows // span, span
    one, two, four, keys, smem = head_specs(rows, h, spans)
    dma = pltpu.SemaphoreType.DMA
    vmem, hbm = pl.BlockSpec(memory_space=pltpu.VMEM), pl.BlockSpec(memory_space=pl.ANY)

    def full(columns, dtype=F32):
        return jax.ShapeDtypeStruct((rows, slots * columns), dtype)

    return pl.pallas_call(
        functools.partial(attention_forward_kernel, peers, spans, span),
        grid=(slots,),
        in_specs=[smem, smem, smem, vmem, vmem, pl.BlockSpec((width, 4 * h), lambda s: (0, s)), vmem, vmem],
        out_specs=[pl.BlockSpec((rows, width), lambda s: (0, 0)), hbm, four, one, one, one, one, one, one, two, one, one, one, keys],
        out_shape=[
            jax.ShapeDtypeStruct((rows, width), BF16), jax.ShapeDtypeStruct((peers, *dy.shape), BF16),
            full(4 * h), full(h),
            full(h, BF16), full(h), full(h), full(h), full(h), full(2 * h), full(h), full(h, BF16), full(h),
            jax.ShapeDtypeStruct((slots, spans, h, rows), BF16),
        ],
        scratch_shapes=[
            pltpu.VMEM((h, rows), F32), pltpu.VMEM((h, rows), F32), dma((1,)), dma((peers,)), dma((peers,))
        ],
        compiler_params=pltpu.CompilerParams(
            collective_id=5, has_side_effects=True, vmem_limit_bytes=60 * 1024 * 1024
        ),
        name="attention_forward",
    )(docs, on, heads, x_all, gain, w, ext, dy)


def attention_backward(docs, on, heads, outp, res, proj, logits, datt, saved, peers, slots, span):
    rows = proj.shape[0]
    spans, h = rows // span, span
    one, two, four, keys, smem = head_specs(rows, h, spans)
    wide, tall = pltpu.VMEM((h, rows), F32), pltpu.VMEM((rows, h), F32)
    vmem = pl.BlockSpec(memory_space=pltpu.VMEM)
    return pl.pallas_call(
        functools.partial(attention_backward_kernel, peers, spans, span),
        grid=(slots,),
        in_specs=[smem, smem, smem, vmem, vmem, four, one, one, one, one, one, one, two, one, one, one, keys],
        out_specs=[four, pl.BlockSpec((rows, h), lambda s: (0, 0)), pl.BlockSpec(res.shape, lambda s: (0, 0))],
        out_shape=[
            jax.ShapeDtypeStruct((rows, slots * 4 * h), BF16),
            jax.ShapeDtypeStruct((rows, h), BF16),
            jax.ShapeDtypeStruct(res.shape, BF16),
        ],
        scratch_shapes=[wide, wide, tall, tall, wide, tall] + Reduce.scratch(peers, *res.shape),
        compiler_params=pltpu.CompilerParams(
            collective_id=6, has_side_effects=True, vmem_limit_bytes=60 * 1024 * 1024
        ),
        name="attention_backward",
    )(docs, on, heads, outp, res, proj, logits, datt, *saved)


def gather_kernel(
    groups, peers, own_cols, aligned, own_ref, mix_ref, ffn_ref, tok_ref, out_ref, ext_ref,
    w_all, ffn_all, tok_all, out_all, ext_all, out_z,
    local, a_s, a_r, m_s, m_r, f_s, f_r, t_s, t_r, o_s, o_r, e_s, e_r, s_s, s_r,
    al_s, al_r, ml_s, ml_r, ol_s, ol_r, el_s, el_r,
):
    me, at = lax.axis_index("blk"), lax.axis_index("dp")
    core = me % 2
    sibling = me + 1 - 2 * core
    cols = w_all.shape[3]
    shared = cols > own_cols
    quarter = (cols - own_cols) // 2

    def side(device):
        return pl.ds(pl.multiple_of(own_cols + quarter * (device % 2), 128), quarter)

    own = [
        pltpu.make_async_copy(ext_ref, ext_all.at[at, me], local.at[0]),
        pltpu.make_async_copy(out_ref, out_z.at[at], local.at[1]),
        pltpu.make_async_copy(own_ref.at[me], w_all.at[at, me, :, pl.ds(0, own_cols)], local.at[2]),
        pltpu.make_async_copy(ffn_ref.at[me], ffn_all.at[me], local.at[3]),
        pltpu.make_async_copy(tok_ref, tok_all.at[me], local.at[4]),
    ]
    if shared:
        own.append(pltpu.make_async_copy(mix_ref.at[me], w_all.at[at, me, :, side(me)], local.at[5]))
    for copy in own:
        copy.start()
    greet(peers, groups)
    moves = fanout(peers, lambda p: own_ref.at[p], lambda p: w_all.at[at, me, :, pl.ds(0, own_cols)], a_s, a_r)
    if shared:
        moves += fanout(peers, lambda p: mix_ref.at[p], lambda p: w_all.at[at, me, :, side(p)], m_s, m_r)
    exts = fanout(peers, lambda p: ext_ref, lambda p: ext_all.at[at, me], e_s, e_r)
    ffn = fanout(peers, lambda p: ffn_ref.at[p], lambda p: ffn_all.at[me], f_s, f_r)
    for copy in moves + exts:
        copy.start()
    out_line = Line(groups, lambda d: out_z.at[d], ol_s, ol_r)
    own[1].wait()
    out_line.start(1)
    tok = Spread(peers, lambda c: tok_ref, lambda b: tok_all.at[b], t_s, t_r)
    if aligned:
        out = Spread(peers, lambda c: out_z.at[c], lambda b: out_all.at[b], o_s, o_r)
    else:
        out = Spread(peers, lambda c: out_z, lambda b: out_all.at[:, b], o_s, o_r)
    lines = [Line(groups, lambda d: w_all.at[d, :, :, pl.ds(0, own_cols)], al_s, al_r)]
    if shared:
        mix_line = Line(groups, lambda d: w_all.at[d, :, :, side(me)], ml_s, ml_r)
    ext_line = Line(groups, lambda d: ext_all.at[d], el_s, el_r)

    def across(d):
        block = w_all.at[d, :, :, side(me)]
        return send(block, block, s_s.at[d], s_r.at[d], blk=sibling)

    out_line.arrive(1)
    if groups > 2:
        out_line.start(2)
    for copy in moves:
        copy.wait_recv()
    for copy in own[2:3] + own[5:]:
        copy.wait()
    lines[0].start(1)
    if shared:
        mix_line.start(1)
        across(at).start()
    tok.start()
    for copy in exts:
        copy.wait_recv()
    own[0].wait()
    ext_line.start(1)
    for copy in ffn:
        copy.start()
    for step in range(3, groups):
        out_line.arrive(step - 1)
        out_line.start(step)
    if groups > 2:
        out_line.arrive(groups - 1)
    out.start()
    if aligned:
        mine = pltpu.make_async_copy(out_z.at[me // 2], out_all.at[me], local.at[7])
    else:
        mine = pltpu.make_async_copy(out_z, out_all.at[:, me], local.at[7])
    mine.start()
    for step in range(2, groups):
        lines[0].arrive(step - 1)
        lines[0].start(step)
        if shared:
            mix_line.arrive(step - 1, across)
            mix_line.start(step)
        ext_line.arrive(step - 1)
        ext_line.start(step)
        if step == 2:
            tok.forward()
    out.forward()
    lines[0].arrive(groups - 1)
    if shared:
        mix_line.arrive(groups - 1, across)
    ext_line.arrive(groups - 1)
    for copy in ffn:
        copy.wait_recv()
    for copy in moves + exts + ffn:
        copy.wait_send()
    for spread in (tok, out):
        spread.finish()
    lines[0].finish()
    if shared:
        mix_line.finish()
        for d in range(groups):
            across(d).wait()
    ext_line.finish()
    out_line.finish()
    mine.wait()
    for i in (3, 4):
        own[i].wait()


def gather_all(groups, peers, aligned, own, mix, ffn, tok, out, ext):
    def shape(*dims):
        return jax.ShapeDtypeStruct(dims, BF16)

    dma = pltpu.SemaphoreType.DMA
    vmem, hbm = pl.BlockSpec(memory_space=pltpu.VMEM), pl.BlockSpec(memory_space=pl.ANY)
    share, own_cols = own.shape[1:]
    cols = own_cols if mix is None else own_cols + 2 * mix.shape[2]
    inputs = [own, own if mix is None else mix, ffn, tok, out, ext]
    return pl.pallas_call(
        functools.partial(gather_kernel, groups, peers, own_cols, aligned),
        in_specs=[vmem] * 6,
        out_specs=[hbm] * 5,
        out_shape=[
            shape(groups, peers, share, cols), shape(*ffn.shape), shape(peers, *tok.shape),
            shape(peers, *out.shape) if aligned else shape(groups, peers, *out.shape),
            shape(groups, peers, *ext.shape),
        ],
        scratch_shapes=[pltpu.VMEM((groups, *out.shape), BF16), dma((8,))] + [dma((peers,))] * 12 + [dma((groups,))] * 2 + [dma((2 * groups,))] * 8,
        compiler_params=pltpu.CompilerParams(
            collective_id=1, has_side_effects=True, vmem_limit_bytes=32 * 1024 * 1024
        ),
        name="gather_all",
    )(*inputs)


def branch_kernel(
    groups, peers, att_ref, out_ref, tok_ref, gain_ref, down_ref, res_ref, n2_all, down_all,
    part, low, local, half, mine, got, r_s, r_r, n_s, n_r, dl_s, dl_r,
):
    me, at = lax.axis_index("blk"), lax.axis_index("dp")
    rows, width = tok_ref.shape
    own_down = pltpu.make_async_copy(down_ref, down_all.at[at], local.at[0])
    own_down.start()
    greet(peers, groups)
    own_down.wait()
    down_line = Line(groups, lambda d: down_all.at[d], dl_s, dl_r)
    down_line.start(1)
    reduce = Reduce(peers, part, half, mine, got, r_s, r_r)

    def fill(b):
        block = att_ref[pl.ds(pl.multiple_of(b * rows, rows), rows), :]
        part[b] = dot(block, out_ref[...]).astype(BF16)

    for k in reduce.order():
        to = (me // 2 + k) % (peers // 2)
        fill(2 * to + 1 - me % 2)
        reduce.inner[k].start()
    for k in reduce.order():
        to = (me // 2 + k) % (peers // 2)
        fill(2 * to + me % 2)
    reduce.pair()
    res_ref[...] = tok_ref[...].astype(F32) + reduce.total()
    low[...] = rms_norm(res_ref[...], gain_ref[...]).astype(BF16)
    keep = pltpu.make_async_copy(low, n2_all.at[me], local.at[1])
    keep.start()
    spread = Spread(peers, lambda c: low, lambda b: n2_all.at[b], n_s, n_r)
    spread.start()
    for step in range(2, groups):
        down_line.arrive(step - 1)
        down_line.start(step)
    spread.forward()
    down_line.arrive(groups - 1)
    spread.finish()
    reduce.finish()
    down_line.finish()
    keep.wait()


def branch(groups, peers, att, out, tok, gain, down):
    rows, width = tok.shape
    dma = pltpu.SemaphoreType.DMA
    vmem, hbm = pl.BlockSpec(memory_space=pltpu.VMEM), pl.BlockSpec(memory_space=pl.ANY)
    return pl.pallas_call(
        functools.partial(branch_kernel, groups, peers),
        in_specs=[vmem] * 5,
        out_specs=[vmem, hbm, hbm],
        out_shape=[
            jax.ShapeDtypeStruct((rows, width), F32),
            jax.ShapeDtypeStruct((peers, rows, width), BF16),
            jax.ShapeDtypeStruct((groups, *down.shape), BF16),
        ],
        scratch_shapes=[pltpu.VMEM((peers, rows, width), BF16), pltpu.VMEM((rows, width), BF16), dma((2,))]
        + Reduce.scratch(peers, rows, width)
        + [dma((peers,)), dma((peers,)), dma((2 * groups,)), dma((2 * groups,))],
        compiler_params=pltpu.CompilerParams(
            collective_id=2, has_side_effects=True, vmem_limit_bytes=48 * 1024 * 1024
        ),
        name="branch_and_norm",
    )(att, out, tok, gain, down)


def residual_kernel(
    peers, part_ref, res_ref, dy_ref, gain_ref, dres_ref, db_all, low, local, half, mine, got, r_s, r_r, n_s, n_r
):
    me = lax.axis_index("blk")
    greet(peers)
    reduce = Reduce(peers, part_ref, half, mine, got, r_s, r_r)
    reduce.start()
    reduce.pair()
    dres_ref[...] = dy_ref[...].astype(F32) + rms_pull(res_ref[...], gain_ref[...], reduce.total())
    low[...] = dres_ref[...].astype(BF16)
    keep = pltpu.make_async_copy(low, db_all.at[me], local.at[0])
    keep.start()
    spread = Spread(peers, lambda c: low, lambda b: db_all.at[b], n_s, n_r)
    spread.start()
    spread.forward()
    spread.finish()
    reduce.finish()
    keep.wait()


def residual_gradient(peers, part, res, dy, gain):
    rows, width = res.shape
    dma = pltpu.SemaphoreType.DMA
    vmem, hbm = pl.BlockSpec(memory_space=pltpu.VMEM), pl.BlockSpec(memory_space=pl.ANY)
    return pl.pallas_call(
        functools.partial(residual_kernel, peers),
        in_specs=[vmem] * 4,
        out_specs=[vmem, hbm],
        out_shape=[jax.ShapeDtypeStruct((rows, width), F32), jax.ShapeDtypeStruct((peers, rows, width), BF16)],
        scratch_shapes=[pltpu.VMEM((rows, width), BF16), dma((1,))]
        + Reduce.scratch(peers, rows, width)
        + [dma((peers,)), dma((peers,))],
        compiler_params=pltpu.CompilerParams(
            collective_id=3, has_side_effects=True, vmem_limit_bytes=48 * 1024 * 1024
        ),
        name="residual_gradient",
    )(part, res, dy, gain)


def final_kernel(
    groups, peers, own_cols, quarter, aligned,
    g_ref, part_ref, gout_ref, ffn_ref, tok_ref, gain_ref, dres_ref,
    dtok_ref, own_rows, mix_rows, ffn_rows, gout_fin, beta_fin,
    local, half, mine, got, r_s, r_r,
    oug, odg, ouo, odo, ol_s, ol_r, own_fin, w_s, w_r, f_s, f_r,
    beta_got, beta_sum, b_s, b_r, bug, bdg, buo, bdo, bl_s, bl_r,
    *extra,
):
    me = lax.axis_index("blk")
    core, chip = me % 2, me // 2
    chips = peers // 2
    sibling = me + 1 - 2 * core
    shared = quarter > 0
    extra = list(extra)
    if shared:
        mix_half, mix_sum, mug, mdg, muo, mdo, ml_s, ml_r, mix_fin, x_s, x_r, mw_s, mw_r = extra[:13]
        extra = extra[13:]
    if aligned:
        go_half, go_mine, go_all, g_s, g_r, gug, gdg, guo, gdo, gl_s, gl_r = extra
    beta_at = own_cols + 2 * quarter
    greet(peers, groups)
    own = LineSum(groups, lambda d: g_ref.at[d, :, :, pl.ds(0, own_cols)], oug, odg, ouo, odo, ol_s, ol_r)
    own.step(0)
    if shared:
        theirs = pl.ds(pl.multiple_of(own_cols + quarter * (1 - core), 128), quarter)
        ours = pl.ds(pl.multiple_of(own_cols + quarter * core, 128), quarter)
        swap = send(g_ref.at[:, :, :, theirs], mix_half, x_s.at[0], x_r.at[0], blk=sibling)
        swap.start()
    reduce = Reduce(peers, part_ref, half, mine, got, r_s, r_r)
    reduce.start()
    betas = fanout(
        peers, lambda p: g_ref.at[:, p, :, pl.ds(beta_at, 128)], lambda p: beta_got.at[me], b_s, b_r
    )
    for copy in betas:
        copy.start()
    ffn_own = pltpu.make_async_copy(ffn_ref.at[me], ffn_rows.at[me], local.at[0])
    ffn_own.start()
    if shared:
        swap.wait_recv()
        mix = LineSum(groups, lambda d: mix_sum.at[d], mug, mdg, muo, mdo, ml_s, ml_r)
        for d in range(groups):

            def body(j, carry):
                mix_sum[d, j] = (g_ref[d, j, :, ours].astype(F32) + mix_half[d, j].astype(F32)).astype(BF16)
                return carry

            lax.fori_loop(0, peers, body, 0)
        mix.step(0)
    reduce.pair()
    if aligned:
        gout = Reduce(peers, gout_ref, go_half, go_mine, go_all, g_s, g_r, go_all.at[chip, 0])
        gout.start()
        gout.pair()
        go_all[chip, 0] = go_mine[0]
    beta_got[me] = g_ref[:, me, :, pl.ds(beta_at, 128)]
    for copy in betas:
        copy.wait_recv()
    summed = beta_got[0].astype(F32)
    for b in range(1, peers):
        summed = summed + beta_got[b].astype(F32)
    beta_sum[:, 0] = summed.astype(BF16)
    beta = LineSum(groups, lambda d: beta_sum.at[d], bug, bdg, buo, bdo, bl_s, bl_r)
    if aligned:
        for copy in gout.outer:
            copy.wait_recv()
        outs = LineSum(groups, lambda d: go_all.at[d], gug, gdg, guo, gdo, gl_s, gl_r)
    sums = [own] + ([mix] if shared else [])
    late = ([outs] if aligned else []) + [beta]
    for i in range(1, groups - 1):
        for item in sums:
            item.step(i)
        for item in late:
            item.step(i - 1)
    ffn = fanout(peers, lambda p: ffn_ref.at[p], lambda p: ffn_rows.at[me], f_s, f_r)
    for copy in ffn:
        copy.start()
    for item in late:
        item.step(groups - 2)
    dtok_ref[...] = dres_ref[...] + rms_pull(tok_ref[...].astype(F32), gain_ref[...], reduce.total())
    own.total(own_fin)
    moves = fanout(peers, lambda p: own_fin.at[p], lambda p: own_rows.at[me], w_s, w_r)
    keeps = [pltpu.make_async_copy(own_fin.at[me], own_rows.at[me], local.at[1])]
    if shared:
        mix.total(mix_fin)
        moves += fanout(peers, lambda p: mix_fin.at[p], lambda p: mix_rows.at[me], mw_s, mw_r)
        keeps.append(pltpu.make_async_copy(mix_fin.at[me], mix_rows.at[me], local.at[2]))
    for copy in moves + keeps:
        copy.start()
    if aligned:
        outs.total(gout_fin)
    beta.total(beta_fin)
    for copy in moves + ffn:
        copy.wait()
    for copy in keeps:
        copy.wait()
    ffn_own.wait()
    reduce.finish()
    for copy in betas:
        copy.wait_send()
    if shared:
        swap.wait_send()
    if aligned:
        gout.finish()
    for item in sums + late:
        item.finish()


def final_sums(groups, peers, own_cols, quarter, aligned, g, part, gout, ffn, tok, gain, dres):
    rows, width = tok.shape
    share = g.shape[2]
    dma = pltpu.SemaphoreType.DMA
    vmem, hbm = pl.BlockSpec(memory_space=pltpu.VMEM), pl.BlockSpec(memory_space=pl.ANY)

    def block(*dims):
        return pltpu.VMEM(dims, BF16)

    def shape(*dims, dtype=BF16):
        return jax.ShapeDtypeStruct(dims, dtype)

    pair = [dma((peers,))] * 2
    scratch = [dma((3,))] + Reduce.scratch(peers, rows, width)
    scratch += LineSum.scratch(groups, peers, share, own_cols) + [block(peers, share, own_cols)] + pair + pair
    scratch += [block(peers, groups, share, 128), block(groups, 1, share, 128)] + pair
    scratch += LineSum.scratch(groups, 1, share, 128)
    if quarter:
        scratch += [block(groups, peers, share, quarter)] * 2 + LineSum.scratch(groups, peers, share, quarter)
        scratch += [block(peers, share, quarter), dma((1,)), dma((1,))] + pair
    if aligned:
        half = block(peers // 2, share, width)
        scratch += [half, half, block(groups, 1, share, width)] + pair + LineSum.scratch(groups, 1, share, width)
    return pl.pallas_call(
        functools.partial(final_kernel, groups, peers, own_cols, quarter, aligned),
        in_specs=[vmem] * 7,
        out_specs=[vmem, hbm, hbm, hbm, vmem, vmem],
        out_shape=[
            shape(rows, width, dtype=F32),
            shape(peers, share, own_cols),
            shape(peers, share, max(quarter, 128)),
            shape(*ffn.shape),
            shape(1, share, width, dtype=F32),
            shape(1, share, 128, dtype=F32),
        ],
        scratch_shapes=scratch,
        compiler_params=pltpu.CompilerParams(
            collective_id=4, has_side_effects=True, vmem_limit_bytes=60 * 1024 * 1024
        ),
        name="final_sums",
    )(g, part, gout, ffn, tok, gain, dres)


def finish_kernel(
    peers, groups, heads, own, shared, own_ref, mix_ref, beta_ref, ffn_ref, w_ref, wb_ref, wf_ref, ga_ref, gf_ref,
    grad_ref, ffn_out_ref, gain_ref, gain_ffn_ref,
):
    share = w_ref.shape[0]
    width = w_ref.shape[1] // 4
    h = width // heads
    hc = 2 * own + shared
    gain = beta_ref[0] * wb_ref[...].astype(F32)

    def put(acc, rows, head, part):
        at = part * width + head * h
        value = rows.astype(F32)
        grad_ref[:, at : at + h] = value
        return acc + value * w_ref[:, at : at + h].astype(F32)

    for b in range(peers):
        chip, core = b // 2, b % 2
        for s in range(own):
            head = chip * hc + core * (own + shared) + s
            if head < heads:
                for part in range(4):
                    gain = put(gain, own_ref[b, :, (4 * s + part) * h : (4 * s + part + 1) * h], head, part)
        if shared:
            for i in range(2):
                gain = put(gain, mix_ref[b, :, i * h : (i + 1) * h], chip * hc + own, 2 * core + i)
    gain_ref[...] = jnp.broadcast_to(jnp.sum(gain, -1, keepdims=True), gain.shape) / ga_ref[...]
    units = wf_ref.shape[1] // (2 * groups * peers)
    tile = min(units, 128)
    total = jnp.zeros((share, 1), F32)
    for b in range(peers):
        for part in range(2):
            for d in range(groups):
                src = (part * groups + d) * units
                at = ((part * groups + d) * peers + b) * units
                value = ffn_ref[b, :, src : src + units].astype(F32)
                ffn_out_ref[:, at : at + units] = value
                total = total + jnp.sum(value * wf_ref[:, at : at + units].astype(F32), -1, keepdims=True)
    gain_ffn_ref[...] = jnp.broadcast_to(total, (share, 128)) / gf_ref[...]


def finish(peers, groups, heads, own, shared, *args):
    share = args[4].shape[0]
    vmem = pl.BlockSpec(memory_space=pltpu.VMEM)
    vector = jax.ShapeDtypeStruct((share, 128), F32)
    return pl.pallas_call(
        functools.partial(finish_kernel, peers, groups, heads, own, shared),
        in_specs=[vmem] * len(args),
        out_specs=[vmem] * 4,
        out_shape=[
            jax.ShapeDtypeStruct(args[4].shape, F32), jax.ShapeDtypeStruct(args[6].shape, F32), vector, vector
        ],
        compiler_params=pltpu.CompilerParams(vmem_limit_bytes=48 * 1024 * 1024),
        name="finish",
    )(*args)


def shards(
    tokens, cotangent, doc_table, gain_attn, attn_in, beta_proj, attn_out, gain_ffn, ffn_in, ffn_down
):
    rows, width = tokens.shape
    heads = beta_proj.shape[1]
    h = width // heads
    groups, peers = lax.axis_size("dp"), lax.axis_size("blk")
    chips = peers // 2
    hc = -(-heads // chips)
    own, shared = hc // 2, hc % 2
    slots, padded = own + shared, hc * chips
    own_cols, quarter = own * 4 * h, shared * 2 * h
    share, units = attn_in.shape[0], ffn_down.shape[0]
    aligned = chips == groups and padded == heads
    me = lax.axis_index("blk")
    chip, core = me // 2, me % 2
    by_chip = attn_in.reshape(share, 4, heads, h).transpose(2, 0, 1, 3)
    by_chip = jnp.pad(by_chip, ((0, padded - heads), (0, 0), (0, 0), (0, 0))).reshape(chips, hc, share, 4, h)
    own_parts = jnp.stack([by_chip[:, :own], by_chip[:, own + shared :]], 1)
    own_parts = own_parts.transpose(0, 1, 3, 2, 4, 5).reshape(peers, share, own_cols)
    mix_parts = None
    if shared:
        mix_parts = by_chip[:, own].reshape(chips, share, 2, 2 * h).transpose(0, 2, 1, 3).reshape(peers, share, 2 * h)
    ffn_parts = ffn_in.reshape(share, 2, groups, peers, units).transpose(3, 0, 1, 2, 4).reshape(peers, share, -1)
    ext = jnp.concatenate([beta_proj.T, gain_attn[None], gain_ffn[None]], 0)
    ext_rows = -(-(heads + 2) // 16) * 16
    ext = jnp.pad(ext, ((0, ext_rows - heads - 2), (0, 128 - share)))
    w2, ffn_part, x_all, out_all, ext_all = gather_all(
        groups, peers, aligned, own_parts, mix_parts, ffn_parts, tokens, attn_out, ext
    )
    w2 = w2.reshape(width, -1)
    ffn_part = ffn_part.reshape(peers * share, -1)
    x_all = x_all.reshape(peers * rows, width)
    ext_all = ext_all[..., :share].transpose(2, 0, 1, 3).reshape(ext_rows, width)
    out_rows = out_all.reshape(-1, width)
    if not aligned:
        out_rows = jnp.pad(out_rows, ((0, (padded - heads) * h), (0, 0)))
        out_rows = lax.dynamic_slice_in_dim(out_rows, chip * hc * h, hc * h, 0)
    out2 = lax.dynamic_slice_in_dim(out_rows, core * (own + shared) * h, own * h, 0)
    if shared:
        out2 = jnp.concatenate([out2, out_rows[own * h : (own + 1) * h]], 0)
    ffn_slab = lax.all_gather(ffn_part, "dp", axis=0, tiled=True)

    first = chip * hc + core * (own + shared)
    my_heads = jnp.stack([first + s for s in range(own)] + [chip * hc + own] * shared).astype(jnp.int32)
    on = jnp.stack([jnp.int32(1)] * own + [1 - core] * shared).astype(jnp.int32)
    gain_one = ext_all[heads][None].astype(F32)
    gain_two = ext_all[heads + 1][None].astype(F32)

    normed, dy_all, proj, logits, attended, *saved = attention_forward(
        doc_table, on, my_heads, x_all, gain_one, w2, ext_all, cotangent, peers, slots, rows
    )
    dy_all = dy_all.reshape(peers * rows, width)
    residual, normed_two_all, down_all = branch(groups, peers, attended, out2, tokens, gain_two, ffn_down)
    normed_two_all = normed_two_all.reshape(peers * rows, width)
    down_slab = down_all.reshape(-1, width)

    gate_up = dot(normed_two_all, ffn_slab)
    mine = gate_up.shape[1] // 2
    gate, up = gate_up[:, :mine], gate_up[:, mine:]
    sig = jax.nn.sigmoid(gate)
    hidden = (gate * sig * up).astype(BF16)
    dhidden = dot(dy_all, down_slab, NT)
    dgate = dhidden * up * (sig * (1.0 + gate * (1.0 - sig)))
    dup = dhidden * (gate * sig)
    dgate_up = jnp.concatenate([dgate, dup], 1).astype(BF16)
    ffn_pull = dot(dgate_up, ffn_slab, NT).astype(BF16).reshape(peers, rows, width)
    dresidual, dbranch_all = residual_gradient(peers, ffn_pull, residual, cotangent, gain_two)
    dbranch_all = dbranch_all.reshape(peers * rows, width)
    out_part = dot(hidden, down_slab).astype(BF16).reshape(peers, rows, width)
    grad_ffn = lax.psum_scatter(dot(normed_two_all, dgate_up, TN).astype(BF16), "dp", scatter_dimension=0, tiled=True)
    grad_down = lax.psum_scatter(dot(hidden, dy_all, TN).astype(BF16), "dp", scatter_dimension=0, tiled=True)

    datt = dot(dbranch_all, out2, NT)
    gout = dot(attended, dbranch_all, TN)
    gout_own, gout_mix = gout[: own * h], gout[own * h :]
    gout = jnp.concatenate([jnp.where(core == 0, gout_own, 0.0), gout_mix, jnp.where(core == 1, gout_own, 0.0)], 0)
    gout = gout.astype(BF16)
    dproj, dlogits, block_out = attention_backward(
        doc_table, on, my_heads, out_part, residual, proj, logits, datt, saved, peers, slots, rows
    )
    pull = dot(dproj, w2, NT) + dot(dlogits[:, :ext_rows], ext_all * (jnp.arange(ext_rows) < heads)[:, None].astype(BF16))
    attn_pull = pull.astype(BF16).reshape(peers, rows, width)
    grad_attn = dot(normed, jnp.concatenate([dproj, dlogits], 1), TN).astype(BF16).reshape(groups, peers, share, -1)
    gout_parts = gout.reshape(peers, share, width) if aligned else gout[:16]
    grad_tokens, own_rows, mix_rows, ffn_rows, grad_attn_out, grad_beta = final_sums(
        groups, peers, own_cols, quarter, aligned, grad_attn, attn_pull, gout_parts,
        grad_ffn.reshape(peers, share, -1), tokens, gain_one, dresidual,
    )
    if aligned:
        grad_attn_out = grad_attn_out[0]
    else:
        whole = jnp.zeros((padded * h, width), F32)
        whole = lax.dynamic_update_slice_in_dim(whole, gout.astype(F32), chip * hc * h, 0)[: heads * h]
        grad_attn_out = lax.psum_scatter(whole, ("dp", "blk"), scatter_dimension=0, tiled=True)
    wide_beta = jnp.pad(beta_proj, ((0, 0), (0, 128 - heads)))
    grad_attn_in, grad_ffn_in, grad_gain_attn, grad_gain_ffn = finish(
        peers, groups, heads, own, shared, own_rows, mix_rows, grad_beta, ffn_rows, attn_in, wide_beta, ffn_in,
        jnp.broadcast_to(gain_attn.astype(F32)[:, None], (share, 128)),
        jnp.broadcast_to(gain_ffn.astype(F32)[:, None], (share, 128)),
    )
    return (
        block_out, grad_tokens, grad_gain_attn[:, 0], grad_attn_in, grad_beta[0, :, :heads], grad_attn_out,
        grad_gain_ffn[:, 0], grad_ffn_in, grad_down.astype(F32),
    )


def solution(mesh):
    split, vector = P(("dp", "blk"), None), P(("dp", "blk"))
    in_specs = (split, split, P("dp", None), vector, split, split, split, vector, split, split)
    out_specs = (split, split, vector, split, split, split, vector, split, split)
    return jax.shard_map(shards, mesh=mesh, in_specs=in_specs, out_specs=out_specs, check_vma=False)
```

```python
import functools

import jax
import jax.numpy as jnp
from jax import lax
from jax.experimental import pallas as pl
from jax.experimental.pallas import tpu as pltpu
from jax.sharding import PartitionSpec as P

EPSILON = 1e-06
F32 = jnp.float32
BF16 = jnp.bfloat16

NN = (((1,), (0,)), ((), ()))
NT = (((1,), (1,)), ((), ()))
TN = (((0,), (0,)), ((), ()))


def dot(a, b, dims=NN):
    return lax.dot_general(a, b, dims, preferred_element_type=F32)


def halves(x):
    high = x.astype(BF16)
    return high, (x - high.astype(F32)).astype(BF16)


def dot3(a, b, dims=NN):
    (ah, al), (bh, bl) = a, b
    ka, kb = dims[0][0][0], dims[0][1][0]
    deep, wide = ah.shape[ka], bh.shape[1 - kb]
    if deep <= 128:
        left = jnp.concatenate([ah, al], ka)
        if wide <= 128:
            below = jnp.concatenate([bh, jnp.zeros_like(bh)], 1 - kb)
            both_parts = dot(left, jnp.concatenate([jnp.concatenate([bh, bl], 1 - kb), below], kb), dims)
            return both_parts[:, :wide] + both_parts[:, wide:]
        return dot(left, jnp.concatenate([bh, bh], kb), dims) + dot(ah, bl, dims)
    if wide <= 128:
        both_parts = dot(ah, jnp.concatenate([bh, bl], 1 - kb), dims)
        return both_parts[:, :wide] + (both_parts[:, wide:] + dot(al, bh, dims))
    return dot(ah, bh, dims) + (dot(ah, bl, dims) + dot(al, bh, dims))


def both(parts, axis):
    return tuple(jnp.concatenate(p, axis) for p in zip(*parts))


def rms_norm(values, gain):
    return values * lax.rsqrt(jnp.mean(values * values, axis=-1, keepdims=True) + EPSILON) * gain


def rms_pull(values, gain, grad):
    scale = lax.rsqrt(jnp.mean(values * values, axis=-1, keepdims=True) + EPSILON)
    inner = grad * gain
    along = jnp.mean(inner * values, axis=-1, keepdims=True)
    return scale * inner - values * (scale * scale * scale) * along


def lanes(n):
    return lax.broadcasted_iota(jnp.int32, (n, n), 1)


def rows_of(n):
    return lax.broadcasted_iota(jnp.int32, (n, n), 0)


def inverses(grams, betas, span):
    r, c = rows_of(span), lanes(span)
    eye = r == c
    outs = []
    pair = (c + 1 == r) & (r % 2 == 1)
    for gram, beta in zip(grams, betas):
        below = jnp.where(pair, gram, 0.0) * beta * beta.T
        outs.append(jnp.where(eye, beta, 0.0) - below)
    size = 2
    while size < span:
        part = (r // (2 * size) == c // (2 * size)) & ((r // size) % 2 == 1) & ((c // size) % 2 == 0)
        sides = [halves(x) for x in outs]
        steps = [dot3(halves(jnp.where(part, g, 0.0)), x) for g, x in zip(grams, sides)]
        outs = [x - dot3(s, halves(t)) for x, s, t in zip(outs, sides, steps)]
        size *= 2
    return outs


MESH = pl.DeviceIdType.MESH


def send(src, dst, send_sem, recv_sem, **device):
    return pltpu.make_async_remote_copy(
        src_ref=src, dst_ref=dst, send_sem=send_sem, recv_sem=recv_sem, device_id=device, device_id_type=MESH
    )


def greet(peers, groups=0):
    barrier = pltpu.get_barrier_semaphore()
    me = lax.axis_index("blk")
    for k in range(1, peers):
        pl.semaphore_signal(barrier, inc=1, device_id={"blk": (me + k) % peers}, device_id_type=MESH)
    if groups:
        at = lax.axis_index("dp")

        @pl.when(at + 1 < groups)
        def _():
            pl.semaphore_signal(barrier, inc=1, device_id={"dp": at + 1}, device_id_type=MESH)

        @pl.when(at > 0)
        def _():
            pl.semaphore_signal(barrier, inc=1, device_id={"dp": at - 1}, device_id_type=MESH)

        @pl.when((at > 0) & (at + 1 < groups))
        def _():
            pl.semaphore_wait(barrier, peers + 1)

        @pl.when((at == 0) | (at + 1 == groups))
        def _():
            pl.semaphore_wait(barrier, peers)
    else:
        pl.semaphore_wait(barrier, peers - 1)


def square(chips, chip):
    return chip + 1 - 2 * (chip % 2), (chip + 2) % chips, chips - 1 - chip


class Spread:
    def __init__(self, peers, source, pick, sems, recvs, halved=False):
        me = lax.axis_index("blk")
        self.chips = peers // 2
        core, chip = me % 2, me // 2
        sibling = me + 1 - 2 * core
        self.halved = halved and self.chips == 4

        def copy(i, src, dst, to):
            return send(src, dst, sems.at[i], recvs.at[i], blk=to)

        self.first = [copy(0, source(chip), pick(me), sibling)]
        self.second, self.cross = [], []
        if self.halved:
            x, y, far = (2 * c + core for c in square(self.chips, chip))
            half = pick(me).shape[0] // 2
            low, high = pl.ds(0, half), pl.ds(half, half)
            for i, to in enumerate((x, y)):
                self.first.append(copy(1 + i, source(to // 2), pick(me), to))
                self.second.append(copy(3 + i, pick(to), pick(to), sibling))
            self.cross = [
                copy(5, pick(x).at[low], pick(x).at[low], y),
                copy(6, pick(y).at[high], pick(y).at[high], x),
            ]
            self.last = [
                copy(7 + i, pick(far).at[rows], pick(far).at[rows], sibling) for i, rows in enumerate((low, high))
            ]
            return
        for k in range(1, self.chips):
            to = (me + 2 * k) % peers
            self.first.append(copy(k, source(to // 2), pick(me), to))
            origin = pick((me + peers - 2 * k) % peers)
            self.second.append(copy(self.chips + k - 1, origin, origin, sibling))

    def start(self):
        for copy in self.first[1:] + self.first[:1]:
            copy.start()

    def forward(self):
        for i, (copy, onward) in enumerate(zip(self.first[1:], self.second)):
            copy.wait_recv()
            if self.halved:
                self.cross[i].start()
            onward.start()
        if self.halved:
            for copy, onward in zip(self.cross, self.last):
                copy.wait_recv()
                onward.start()

    def finish(self):
        for copy in self.first + self.cross:
            copy.wait_send()
        self.first[0].wait_recv()
        for copy in self.second + (self.last if self.halved else []):
            copy.wait()


class Line:
    def __init__(self, groups, pick, sems, recvs):
        self.groups, self.pick, self.sems, self.recvs = groups, pick, sems, recvs
        self.at = lax.axis_index("dp")

    def up(self, step, to, block):
        i = 2 * (step - 1)
        return send(self.pick(block), self.pick(block), self.sems.at[i], self.recvs.at[i], dp=to)

    def down(self, step, to, block):
        i = 2 * (step - 1) + 1
        return send(self.pick(block), self.pick(block), self.sems.at[i], self.recvs.at[i], dp=to)

    def start(self, step):
        at, n = self.at, self.groups

        @pl.when((at + 1 < n) & (at - (step - 1) >= 0))
        def _():
            self.up(step, at + 1, at - (step - 1)).start()

        @pl.when((at - 1 >= 0) & (at + (step - 1) < n))
        def _():
            self.down(step, at - 1, at + (step - 1)).start()

    def arrive(self, step, then=None):
        at, n = self.at, self.groups

        @pl.when(at - step >= 0)
        def _():
            self.up(step, at - 1, at - step).wait_recv()
            if then is not None:
                then(at - step).start()

        @pl.when(at + step < n)
        def _():
            self.down(step, at + 1, at + step).wait_recv()
            if then is not None:
                then(at + step).start()

    def finish(self):
        at, n = self.at, self.groups
        for step in range(1, n):

            @pl.when((at + 1 < n) & (at - (step - 1) >= 0))
            def _():
                self.up(step, at + 1, at - (step - 1)).wait_send()

            @pl.when((at - 1 >= 0) & (at + (step - 1) < n))
            def _():
                self.down(step, at - 1, at + (step - 1)).wait_send()


class LineSum:
    def __init__(self, groups, pick, up_got, dn_got, up_out, dn_out, sems, recvs, arrived=None, base=0):
        self.n, self.pick, self.arrived, self.base = groups, pick, arrived, base
        self.up_got, self.dn_got, self.up_out, self.dn_out = up_got, dn_got, up_out, dn_out
        self.sems, self.recvs = sems, recvs
        self.at = lax.axis_index("dp")

    @staticmethod
    def scratch(groups, *block, steps=None):
        hop = pltpu.VMEM((steps or groups - 1, *block), BF16)
        return [hop] * 4 + [pltpu.SemaphoreType.DMA((2 * groups,))] * 2

    def up(self, i, src, to):
        return send(src, self.up_got.at[i - self.base], self.sems.at[2 * i], self.recvs.at[2 * i], dp=to)

    def down(self, i, src, to):
        return send(src, self.dn_got.at[i - self.base], self.sems.at[2 * i + 1], self.recvs.at[2 * i + 1], dp=to)

    def add(self, out, one, other):
        def body(j, carry):
            out[j] = (one[j].astype(F32) + other[j].astype(F32)).astype(out.dtype)
            return carry

        lax.fori_loop(0, out.shape[0], body, 0)

    def step(self, i):
        at, n = self.at, self.n
        far = n - 1 - i

        @pl.when((at + far < n) & (at == 0))
        def _():
            self.up(i, self.pick(far), at + 1).start()

        @pl.when((at - far >= 0) & (at == n - 1))
        def _():
            self.down(i, self.pick(-far), at - 1).start()

        if i > 0:

            @pl.when((at + far < n) & (at > 0))
            def _():
                if self.arrived is None:
                    self.up(i - 1, self.up_out.at[max(i - 1 - self.base, 0)], at - 1).wait_recv()
                before = self.up_got.at[max(i - 1 - self.base, 0)] if self.arrived is None else self.arrived[0]
                self.add(self.up_out.at[i - self.base], self.pick(far), before)
                self.up(i, self.up_out.at[i - self.base], at + 1).start()

            @pl.when((at - far >= 0) & (at < n - 1))
            def _():
                if self.arrived is None:
                    self.down(i - 1, self.dn_out.at[max(i - 1 - self.base, 0)], at + 1).wait_recv()
                before = self.dn_got.at[max(i - 1 - self.base, 0)] if self.arrived is None else self.arrived[1]
                self.add(self.dn_out.at[i - self.base], self.pick(-far), before)
                self.down(i, self.dn_out.at[i - self.base], at - 1).start()

    def arrive(self, i, up, down):
        at, n = self.at, self.n
        far = n - 1 - i
        some_up, some_down = (at > 0) & (at - 1 + far < n), (at < n - 1) & (at + 1 - far >= 0)

        @pl.when(some_up)
        def _():
            self.up(i, self.up_out.at[i - self.base], at - 1).wait_recv()
            up[...] = self.up_got[i - self.base]

        @pl.when(some_down)
        def _():
            self.down(i, self.dn_out.at[i - self.base], at + 1).wait_recv()
            down[...] = self.dn_got[i - self.base]

        @pl.when(jnp.logical_not(some_up))
        def _():
            up[...] = jnp.zeros_like(up)

        @pl.when(jnp.logical_not(some_down))
        def _():
            down[...] = jnp.zeros_like(down)

    def total(self, out):
        at, n, i = self.at, self.n, self.n - 2

        @pl.when(at > 0)
        def _():
            self.up(i, self.up_out.at[i - self.base], at - 1).wait_recv()
            self.add(out, self.pick(0), self.up_got.at[i - self.base])

        @pl.when(at == 0)
        def _():
            self.down(i, self.dn_out.at[i - self.base], at + 1).wait_recv()
            self.add(out, self.pick(0), self.dn_got.at[i - self.base])

        @pl.when((at > 0) & (at < n - 1))
        def _():
            self.down(i, self.dn_out.at[i - self.base], at + 1).wait_recv()
            self.add(out, out, self.dn_got.at[i - self.base])

    def finish(self, steps=None):
        at, n = self.at, self.n
        for i in range(n - 1) if steps is None else steps:
            far = n - 1 - i

            @pl.when(at + far < n)
            def _():
                self.up(i, self.up_out.at[i - self.base], at + 1).wait_send()

            @pl.when(at - far >= 0)
            def _():
                self.down(i, self.dn_out.at[i - self.base], at - 1).wait_send()


class Reduce:
    def __init__(self, peers, part, half, mine, got, sems, recvs, place=None, halved=False):
        me = lax.axis_index("blk")
        self.chips = peers // 2
        self.core, self.chip = me % 2, me // 2
        sibling = me + 1 - 2 * self.core
        self.part, self.half, self.mine, self.got = part, half, mine, got
        self.halved = halved and self.chips == 4

        def copy(i, src, dst, to):
            return send(src, dst, sems.at[i], recvs.at[i], blk=to)

        if self.halved:
            self.to = [self.chip, *square(self.chips, self.chip)]
        else:
            self.to = [(self.chip + k) % self.chips for k in range(self.chips)]
        self.inner = [copy(k, part.at[2 * to + 1 - self.core], half.at[k], sibling) for k, to in enumerate(self.to)]
        self.outer = []
        if self.halved:
            x, y, far = (2 * c + self.core for c in self.to[1:])
            middle = mine.shape[1] // 2
            self.low, self.high = pl.ds(0, middle), pl.ds(middle, middle)
            self.cross = [
                copy(6, mine.at[3, self.low], got.at[3, self.low], x),
                copy(7, mine.at[3, self.high], got.at[3, self.high], y),
            ]
            self.outer = [copy(4, mine.at[1], got.at[1], x), copy(5, mine.at[2], got.at[2], y)]
            return
        for k in range(1, self.chips):
            arrival = got.at[k] if place is None else place
            self.outer.append(copy(self.chips + k, mine.at[k], arrival, 2 * self.to[k] + self.core))

    def order(self):
        return list(range(self.chips - 1, -1, -1)) if self.halved else list(range(1, self.chips)) + [0]

    def start(self):
        for k in self.order():
            self.inner[k].start()

    def pair(self):
        for k in self.order():
            self.inner[k].wait_recv()
            both_cores = self.part[2 * self.to[k] + self.core].astype(F32) + self.half[k].astype(F32)
            self.mine[k] = both_cores.astype(BF16)
            if self.halved:
                if k == 3:
                    for copy in self.cross:
                        copy.start()
            elif k > 0:
                self.outer[k - 1].start()
        if self.halved:
            for copy, rows, k in ((self.cross[0], self.low, 2), (self.cross[1], self.high, 1)):
                copy.wait_recv()
                summed = self.mine[k, rows].astype(F32) + self.got[3, rows].astype(F32)
                self.mine[k, rows] = summed.astype(BF16)
                self.outer[k - 1].start()

    def total(self):
        total = self.mine[0].astype(F32)
        for k, copy in enumerate(self.outer):
            copy.wait_recv()
            total = total + self.got[k + 1].astype(F32)
        return total

    def finish(self):
        for copy in self.inner + self.outer + (self.cross if self.halved else []):
            copy.wait_send()

    @staticmethod
    def scratch(peers, rows, width):
        block = pltpu.VMEM((peers // 2, rows, width), BF16)
        return [block, block, block, pltpu.SemaphoreType.DMA((peers,)), pltpu.SemaphoreType.DMA((peers,))]


def fanout(peers, source, dst, sems, recvs):
    me = lax.axis_index("blk")
    copies = []
    for k in range(1, peers):
        p = (me + k) % peers
        copies.append(send(source(p), dst(p), sems.at[k], recvs.at[k], blk=p))
    return copies


def attention_forward_kernel(
    peers, spans, span, doc_ref, on_ref, head_ref, x_ref, gain_ref, w_ref, ext_ref, dy_ref,
    norm_ref, dy_all, proj_ref, logit_ref,
    low_ref, att_ref, sum_ref, a1_ref, g_ref, y_ref, e0_ref, qp_ref, m_ref, kts_ref,
    kpt_ref, kt_ref, keep_sem, d_s, d_r,
):
    h = span
    scale = h ** -0.5
    slot, me = pl.program_id(0), lax.axis_index("blk")
    tall = 2 * span

    def dy_copies():
        keep = pltpu.make_async_copy(dy_ref, dy_all.at[me], keep_sem.at[0])
        return keep, Spread(peers, lambda c: dy_ref, lambda b: dy_all.at[b], d_s, d_r, True)

    @pl.when(slot == 0)
    def _():
        greet(peers)
        keep, spread = dy_copies()
        keep.start()
        spread.start()

        def normalize(i, carry):
            rows = pl.ds(pl.multiple_of(i * tall, tall), tall)
            norm_ref[rows, :] = rms_norm(x_ref[rows, :].astype(F32), gain_ref[...]).astype(BF16)
            return carry

        lax.fori_loop(0, spans // 2, normalize, 0)

    def project(i, carry):
        rows = pl.ds(pl.multiple_of(i * tall, tall), tall)
        normed = norm_ref[rows, :]
        proj_ref[rows, :] = dot(normed, w_ref[...])
        every = dot(normed, ext_ref[...], NT)
        lane = lax.broadcasted_iota(jnp.int32, every.shape, 1)
        mine = jnp.sum(jnp.where(lane == head_ref[slot], every, 0.0), -1, keepdims=True)
        logit_ref[rows, :] = jnp.broadcast_to(mine, (tall, h))
        return carry

    lax.fori_loop(0, spans // 2, project, 0)
    r, c = rows_of(span), lanes(span)
    lower, strict, eye = c <= r, c < r, (c == r).astype(F32)
    at = [pl.ds(n * span, span) for n in range(spans)]
    group = 4
    for first in range(0, spans, group):
        members = range(first, min(first + group, spans))
        grams, betas, kept = [], [], []
        for n in members:
            q = proj_ref[at[n], 0:h]
            k = proj_ref[at[n], h : 2 * h]
            d = proj_ref[at[n], 3 * h : 4 * h]
            w = d * lax.rsqrt(jnp.sum(d * d, -1, keepdims=True) + EPSILON)
            qs, ks, ws = halves(q), halves(k), halves(w)
            z = dot3(both((qs, ws), 0), both((ws, ks), 0), NT)
            a1 = jnp.where(lower, z[:span, :span], 0.0)
            a1_ref[at[n], :] = a1
            b1 = jnp.where(strict, z[span:, span:], 0.0)
            grams.append(jnp.where(strict, z[span:, :span], 0.0))
            betas.append(2.0 / (1.0 + jnp.exp(-logit_ref[at[n], :])))
            kept.append((q, k, ws, halves(a1), halves(b1), z[:span, span:]))
        solved = inverses(grams, betas, span)
        for n, g, (q, k, ws, a1s, b1s, qk) in zip(members, solved, kept):
            g_ref[at[n], :] = g
            y = dot3(halves(g), both((ws, b1s), 1))
            y_ref[at[n], :] = y
            ys = halves(y)
            t = dot3(a1s, ys)
            u = dot3(ws, ys, TN)
            qp_ref[at[n], :] = (q - t[:, :h]).astype(BF16)
            local = (qk - t[:, h:]) * scale
            e0_ref[at[n], :] = jnp.where(lower, jnp.exp(local), 0.0)
            m_ref[at[n], :] = eye - u[:, :h]
            kpt_ref[:, at[n]] = k.T - u[:, h:]
    for n in range(spans):
        w = n * span
        e0 = e0_ref[at[n], :]
        total = jnp.sum(e0, -1, keepdims=True)
        numer = dot(e0.astype(BF16), proj_ref[at[n], 2 * h : 3 * h].astype(BF16))
        if n > 0:
            kt = kt_ref[:, :w]
            kts = halves(kt)
            kts_ref[0, n, :, :w] = kts[0]
            block = jnp.exp(dot(qp_ref[at[n], :], kts[0]) * scale)
            block = jnp.concatenate(
                [jnp.where(doc_ref[0, j] == doc_ref[0, n], block[:, j * span : (j + 1) * span], 0.0) for j in range(n)], 1
            )
            total = total + jnp.sum(block, -1, keepdims=True)
            numer = numer + dot(block.astype(BF16), proj_ref[:w, 2 * h : 3 * h].astype(BF16))
            if n < spans - 1:
                kt_ref[:, :w] = dot3(halves(m_ref[at[n], :]), kts)
        if n < spans - 1:
            kt_ref[:, at[n]] = kpt_ref[:, at[n]]
        attended = numer / total
        att_ref[at[n], :] = attended
        low_ref[at[n], :] = jnp.where(on_ref[slot] > 0, attended, 0.0).astype(BF16)
        sum_ref[at[n], :] = jnp.broadcast_to(total, (span, h))

    @pl.when(slot == 0)
    def _():
        dy_copies()[1].forward()

    @pl.when(slot == pl.num_programs(0) - 1)
    def _():
        keep, spread = dy_copies()
        spread.finish()
        keep.wait()


def attention_backward_kernel(
    groups, peers, spans, span, doc_ref, on_ref, head_ref, outp_ref, res_ref, gi_all, up_ref, dn_ref, gd_ref, db_ref, out_ref,
    proj_ref, logit_ref, att_ref, sum_ref, a1_ref, g_ref, y_ref, e0_ref, qp_ref, m_ref, kts_ref,
    dproj_ref, dlogit_ref, block_ref, rows_ref, dup_ref, ddn_ref,
    gkt_ref, dvt_ref, dqp_ref, dm_ref, dkpt_ref, ds_ref, datt_ref, half, mine, got, r_s, r_r, gi_ref, local,
    ug, dg, uo, do, l_s, l_r, vg, wg, vo, wo, m_s, m_r,
):
    h = span
    scale = h ** -0.5
    r, c = rows_of(span), lanes(span)
    lower, strict, same = c <= r, c < r, c == r
    at = [pl.ds(n * span, span) for n in range(spans)]
    slot = pl.program_id(0)

    def reduce():
        return Reduce(peers, outp_ref, half, mine, got, r_s, r_r, halved=True)

    place = {1: 0, -1: 1, 0: 2}
    line = LineSum(groups, lambda r: gi_ref.at[place[r]], ug, dg, uo, do, l_s, l_r, (up_ref, dn_ref), groups - 2)
    at_dp = line.at
    down = LineSum(groups, lambda r: gd_ref.at[at_dp + r], vg, wg, vo, wo, m_s, m_r)

    @pl.when(slot == 0)
    def _():
        loads = [
            pltpu.make_async_copy(gi_all.at[(at_dp + groups + r) % groups], gi_ref.at[i], local.at[i])
            for r, i in place.items()
        ]
        for copy in loads:
            copy.start()
        greet(peers, groups)
        reduce().start()
        for copy in loads:
            copy.wait()
        line.step(groups - 2)
        down.step(0)

    def pull_back(i, carry):
        rows = pl.ds(pl.multiple_of(i * 2 * span, span), 2 * span)
        datt_ref[rows, :] = dot(db_ref[rows, :], out_ref[...], NT)
        return carry

    lax.fori_loop(0, spans // 2, pull_back, 0)
    dvt_ref[...] = jnp.zeros_like(dvt_ref)
    for n in reversed(range(spans)):
        w = n * span
        last = n == spans - 1
        datt, total = jnp.where(on_ref[slot] > 0, datt_ref[at[n], :], 0.0), sum_ref[at[n], :]
        da = (datt / total).astype(BF16)
        delta = jnp.sum(datt * att_ref[at[n], :], -1, keepdims=True) / total
        e0 = e0_ref[at[n], :]
        mix = dot(da, proj_ref[at[n], 2 * h : 3 * h].astype(BF16), NT) - delta
        ds_ref[at[n], :] = (e0 * mix).astype(BF16).astype(F32) * scale
        dvt_ref[:, at[n]] += dot(da, e0.astype(BF16), TN)
        if n == 0:
            dqp_ref[at[n], :] = jnp.zeros((span, h), F32)
            dm_ref[at[n], :] = jnp.zeros((h, h), F32)
            dkpt_ref[:, at[n]] = gkt_ref[:, at[n]] if not last else jnp.zeros((h, span), F32)
            continue
        keys = kts_ref[0, n, :, :w]
        qp = qp_ref[at[n], :]
        block = jnp.exp(dot(qp, keys) * scale)
        block = jnp.concatenate(
            [jnp.where(doc_ref[0, j] == doc_ref[0, n], block[:, j * span : (j + 1) * span], 0.0) for j in range(n)], 1
        )
        wide = jnp.concatenate([delta] * n, 1)
        mix = dot(da, proj_ref[:w, 2 * h : 3 * h].astype(BF16), NT) - wide
        ds = (block * mix).astype(BF16)
        dqp_ref[at[n], :] = dot(ds, keys, NT) * scale
        pulled = dot(qp, ds, TN) * scale
        dvt_ref[:, :w] += dot(da, block.astype(BF16), TN)
        if last:
            dm_ref[at[n], :] = jnp.zeros((h, h), F32)
            dkpt_ref[:, at[n]] = jnp.zeros((h, span), F32)
            gkt_ref[:, :w] = pulled
        else:
            dkpt_ref[:, at[n]] = gkt_ref[:, at[n]]
            gs = halves(gkt_ref[:, :w])
            dm_ref[at[n], :] = dot(gs[0], keys, NT) + dot(gs[1], keys, NT)
            gkt_ref[:, :w] = pulled + dot3(halves(m_ref[at[n], :]), gs, TN)

    @pl.when(slot == 0)
    def _():
        reduce().pair()

    for n in range(spans):
        q = proj_ref[at[n], 0:h]
        k = proj_ref[at[n], h : 2 * h]
        d = proj_ref[at[n], 3 * h : 4 * h]
        inv = lax.rsqrt(jnp.sum(d * d, -1, keepdims=True) + EPSILON)
        w = d * inv
        beta = 2.0 / (1.0 + jnp.exp(-logit_ref[at[n], :]))
        qs, ks, ws = halves(q), halves(k), halves(w)
        dqp, ds, dkpt = dqp_ref[at[n], :], ds_ref[at[n], :], dkpt_ref[:, at[n]]
        ys = halves(y_ref[at[n], :])
        left = both((halves(dqp), halves(ds)), 1)
        mid = both((halves(dm_ref[at[n], :]), halves(dkpt)), 1)
        da1 = jnp.where(lower, -dot3(left, ys, NT), 0.0)
        dy = dot3(halves(a1_ref[at[n], :]), left, TN) + dot3(ws, mid)
        dx = -dot3(halves(g_ref[at[n], :]), halves(dy), TN)
        dl = -dot3(halves(dx), ys, NT)
        dw = dx[:, :h] - dot3(ys, mid, NT)
        pull = jnp.sum(jnp.where(same, dl, 0.0), -1, keepdims=True)
        dlogit = -pull * (1.0 - 0.5 * beta) / jnp.maximum(beta, 1e-30)
        before = jnp.where(slot == 0, 0.0, dlogit_ref[at[n], :].astype(F32))
        dlogit_ref[at[n], :] = jnp.where(c == head_ref[slot], dlogit, before).astype(BF16)
        dz = jnp.concatenate(
            [
                jnp.concatenate([da1, ds], 1),
                jnp.concatenate([jnp.where(strict, dl, 0.0), jnp.where(strict, dx[:, h:], 0.0)], 1),
            ],
            0,
        )
        dzs = halves(dz)
        dp = dot3(dzs, both((ws, ks), 0))
        dr = dot3(dzs, both((qs, ws), 0), TN)
        dw = dw + dp[span:] + dr[:span]
        dproj_ref[at[n], 0:h] = (dqp + dp[:span]).astype(BF16)
        dproj_ref[at[n], h : 2 * h] = (dkpt.T + dr[span:]).astype(BF16)
        dproj_ref[at[n], 2 * h : 3 * h] = dvt_ref[:, at[n]].T.astype(BF16)
        dproj_ref[at[n], 3 * h : 4 * h] = (inv * (dw - w * jnp.sum(dw * w, -1, keepdims=True))).astype(BF16)

    @pl.when(slot == 0)
    def _():
        for i in range(1, groups - 2):
            down.step(i)

    @pl.when(slot == pl.num_programs(0) - 1)
    def _():
        last = reduce()
        block_ref[...] = (res_ref[...] + last.total()).astype(BF16)
        last.finish()
        line.total(rows_ref)
        line.finish([groups - 2])
        down.arrive(groups - 3, dup_ref, ddn_ref)
        down.finish(range(groups - 2))


def head_specs(rows, h, spans, slots):
    mode = {"pipeline_mode": pl.Buffered(1)} if slots == 1 else {}
    one = pl.BlockSpec((rows, h), lambda s: (0, s), **mode)
    two = pl.BlockSpec((rows, 2 * h), lambda s: (0, s), **mode)
    four = pl.BlockSpec((rows, 4 * h), lambda s: (0, s), **mode)
    keys = pl.BlockSpec((1, spans, h, rows), lambda s: (s, 0, 0, 0), **mode)
    docs = pl.BlockSpec(memory_space=pltpu.SMEM)
    return one, two, four, keys, docs


def attention_forward(docs, on, heads, x_all, gain, w, ext, dy, peers, slots, span):
    rows, width = x_all.shape
    spans, h = rows // span, span
    one, two, four, keys, smem = head_specs(rows, h, spans, slots)
    dma = pltpu.SemaphoreType.DMA
    vmem, hbm = pl.BlockSpec(memory_space=pltpu.VMEM), pl.BlockSpec(memory_space=pl.ANY)

    def full(columns, dtype=F32):
        return jax.ShapeDtypeStruct((rows, slots * columns), dtype)

    return pl.pallas_call(
        functools.partial(attention_forward_kernel, peers, spans, span),
        grid=(slots,),
        in_specs=[smem, smem, smem, vmem, vmem, pl.BlockSpec((width, 4 * h), lambda s: (0, s)), vmem, vmem],
        out_specs=[pl.BlockSpec((rows, width), lambda s: (0, 0)), hbm, four, one, one, one, one, one, one, two, one, one, one, keys],
        out_shape=[
            jax.ShapeDtypeStruct((rows, width), BF16), jax.ShapeDtypeStruct((peers, *dy.shape), BF16),
            full(4 * h), full(h),
            full(h, BF16), full(h), full(h), full(h), full(h), full(2 * h), full(h), full(h, BF16), full(h),
            jax.ShapeDtypeStruct((slots, spans, h, rows), BF16),
        ],
        scratch_shapes=[
            pltpu.VMEM((h, rows), F32), pltpu.VMEM((h, rows), F32), dma((1,)), dma((2 * peers,)), dma((2 * peers,))
        ],
        compiler_params=pltpu.CompilerParams(
            collective_id=5, has_side_effects=True, vmem_limit_bytes=60 * 1024 * 1024
        ),
        name="attention_forward",
    )(docs, on, heads, x_all, gain, w, ext, dy)


def attention_backward(
    docs, on, heads, outp, res, gi, up, dn, gd, db_all, out2, proj, logits, saved, groups, peers, slots, span
):
    rows = proj.shape[0]
    spans, h = rows // span, span
    one, two, four, keys, smem = head_specs(rows, h, spans, slots)
    wide, tall = pltpu.VMEM((h, rows), F32), pltpu.VMEM((rows, h), F32)
    vmem = pl.BlockSpec(memory_space=pltpu.VMEM)
    block = pl.BlockSpec(gd.shape[1:], lambda s: (0, 0, 0))
    return pl.pallas_call(
        functools.partial(attention_backward_kernel, groups, peers, spans, span),
        grid=(slots,),
        in_specs=[smem, smem, smem, vmem, vmem, pl.BlockSpec(memory_space=pl.ANY)] + [vmem] * 4 + [pl.BlockSpec((h, db_all.shape[1]), lambda s: (s, 0))]
        + [four, one, one, one, one, one, two, one, one, one, keys],
        out_specs=[
            four, pl.BlockSpec((rows, h), lambda s: (0, 0)), pl.BlockSpec(res.shape, lambda s: (0, 0)),
            pl.BlockSpec(up.shape, lambda s: (0, 0, 0)), block, block,
        ],
        out_shape=[
            jax.ShapeDtypeStruct((rows, slots * 4 * h), BF16),
            jax.ShapeDtypeStruct((rows, h), BF16),
            jax.ShapeDtypeStruct(res.shape, BF16),
            jax.ShapeDtypeStruct(up.shape, BF16),
            jax.ShapeDtypeStruct(gd.shape[1:], BF16),
            jax.ShapeDtypeStruct(gd.shape[1:], BF16),
        ],
        scratch_shapes=[wide, wide, tall, tall, wide, tall, tall] + Reduce.scratch(peers, *res.shape)
        + [pltpu.VMEM((3, *up.shape), BF16), pltpu.SemaphoreType.DMA((3,))]
        + LineSum.scratch(groups, *up.shape, steps=1) + LineSum.scratch(groups, *gd.shape[1:], steps=groups - 2),
        compiler_params=pltpu.CompilerParams(
            collective_id=6, has_side_effects=True, vmem_limit_bytes=62 * 1024 * 1024
        ),
        name="attention_backward",
    )(docs, on, heads, outp, res, gi, up, dn, gd, db_all, out2, proj, logits, *saved)


def gather_kernel(
    groups, peers, own_cols, aligned, own_ref, mix_ref, ffn_ref, tok_ref, out_ref, ext_ref,
    w_all, ffn_all, tok_all, out_all, ext_all, out_z,
    local, a_s, a_r, m_s, m_r, f_s, f_r, t_s, t_r, o_s, o_r, e_s, e_r, s_s, s_r,
    al_s, al_r, ml_s, ml_r, ol_s, ol_r, el_s, el_r,
):
    me, at = lax.axis_index("blk"), lax.axis_index("dp")
    core = me % 2
    sibling = me + 1 - 2 * core
    cols = w_all.shape[3]
    shared = cols > own_cols
    quarter = (cols - own_cols) // 2

    def side(device):
        return pl.ds(pl.multiple_of(own_cols + quarter * (device % 2), 128), quarter)

    own = [
        pltpu.make_async_copy(ext_ref, ext_all.at[at, me], local.at[0]),
        pltpu.make_async_copy(out_ref, out_z.at[at], local.at[1]),
        pltpu.make_async_copy(own_ref.at[me], w_all.at[at, me, :, pl.ds(0, own_cols)], local.at[2]),
        pltpu.make_async_copy(ffn_ref.at[me], ffn_all.at[me], local.at[3]),
        pltpu.make_async_copy(tok_ref, tok_all.at[me], local.at[4]),
    ]
    if shared:
        own.append(pltpu.make_async_copy(mix_ref.at[me], w_all.at[at, me, :, side(me)], local.at[5]))
    for copy in own:
        copy.start()
    greet(peers, groups)
    moves = fanout(peers, lambda p: own_ref.at[p], lambda p: w_all.at[at, me, :, pl.ds(0, own_cols)], a_s, a_r)
    if shared:
        moves += fanout(peers, lambda p: mix_ref.at[p], lambda p: w_all.at[at, me, :, side(p)], m_s, m_r)
    exts = fanout(peers, lambda p: ext_ref, lambda p: ext_all.at[at, me], e_s, e_r)
    ffn = fanout(peers, lambda p: ffn_ref.at[p], lambda p: ffn_all.at[me], f_s, f_r)
    for copy in moves + exts:
        copy.start()
    out_line = Line(groups, lambda d: out_z.at[d], ol_s, ol_r)
    own[1].wait()
    out_line.start(1)
    tok = Spread(peers, lambda c: tok_ref, lambda b: tok_all.at[b], t_s, t_r, True)
    if aligned:
        out = Spread(peers, lambda c: out_z.at[c], lambda b: out_all.at[b], o_s, o_r)
    else:
        out = Spread(peers, lambda c: out_z, lambda b: out_all.at[:, b], o_s, o_r)
    lines = [Line(groups, lambda d: w_all.at[d, :, :, pl.ds(0, own_cols)], al_s, al_r)]
    if shared:
        mix_line = Line(groups, lambda d: w_all.at[d, :, :, side(me)], ml_s, ml_r)
    ext_line = Line(groups, lambda d: ext_all.at[d], el_s, el_r)

    def across(d):
        block = w_all.at[d, :, :, side(me)]
        return send(block, block, s_s.at[d], s_r.at[d], blk=sibling)

    out_line.arrive(1)
    if groups > 2:
        out_line.start(2)
    for copy in moves:
        copy.wait_recv()
    for copy in own[2:3] + own[5:]:
        copy.wait()
    lines[0].start(1)
    if shared:
        mix_line.start(1)
        across(at).start()
    tok.start()
    for copy in exts:
        copy.wait_recv()
    own[0].wait()
    ext_line.start(1)
    for copy in ffn:
        copy.start()
    for step in range(3, groups):
        out_line.arrive(step - 1)
        out_line.start(step)
    if groups > 2:
        out_line.arrive(groups - 1)
    out.start()
    if aligned:
        mine = pltpu.make_async_copy(out_z.at[me // 2], out_all.at[me], local.at[7])
    else:
        mine = pltpu.make_async_copy(out_z, out_all.at[:, me], local.at[7])
    mine.start()
    for step in range(2, groups):
        lines[0].arrive(step - 1)
        lines[0].start(step)
        if shared:
            mix_line.arrive(step - 1, across)
            mix_line.start(step)
        ext_line.arrive(step - 1)
        ext_line.start(step)
        if step == 2:
            tok.forward()
    out.forward()
    lines[0].arrive(groups - 1)
    if shared:
        mix_line.arrive(groups - 1, across)
    ext_line.arrive(groups - 1)
    for copy in ffn:
        copy.wait_recv()
    for copy in moves + exts + ffn:
        copy.wait_send()
    for spread in (tok, out):
        spread.finish()
    lines[0].finish()
    if shared:
        mix_line.finish()
        for d in range(groups):
            across(d).wait()
    ext_line.finish()
    out_line.finish()
    mine.wait()
    for i in (3, 4):
        own[i].wait()


def gather_all(groups, peers, aligned, own, mix, ffn, tok, out, ext):
    def shape(*dims):
        return jax.ShapeDtypeStruct(dims, BF16)

    dma = pltpu.SemaphoreType.DMA
    vmem, hbm = pl.BlockSpec(memory_space=pltpu.VMEM), pl.BlockSpec(memory_space=pl.ANY)
    share, own_cols = own.shape[1:]
    cols = own_cols if mix is None else own_cols + 2 * mix.shape[2]
    inputs = [own, own if mix is None else mix, ffn, tok, out, ext]
    return pl.pallas_call(
        functools.partial(gather_kernel, groups, peers, own_cols, aligned),
        in_specs=[vmem] * 6,
        out_specs=[hbm] * 5,
        out_shape=[
            shape(groups, peers, share, cols), shape(*ffn.shape), shape(peers, *tok.shape),
            shape(peers, *out.shape) if aligned else shape(groups, peers, *out.shape),
            shape(groups, peers, *ext.shape),
        ],
        scratch_shapes=[pltpu.VMEM((groups, *out.shape), BF16), dma((8,))] + [dma((2 * peers,))] * 12 + [dma((groups,))] * 2 + [dma((2 * groups,))] * 8,
        compiler_params=pltpu.CompilerParams(
            collective_id=1, has_side_effects=True, vmem_limit_bytes=32 * 1024 * 1024
        ),
        name="gather_all",
    )(*inputs)


def branch_kernel(
    groups, peers, att_ref, out_ref, tok_ref, gain_ref, down_ref, res_ref, n2_all, down_all,
    part, low, local, half, mine, got, r_s, r_r, n_s, n_r, dl_s, dl_r,
):
    me, at = lax.axis_index("blk"), lax.axis_index("dp")
    rows, width = tok_ref.shape
    own_down = pltpu.make_async_copy(down_ref, down_all.at[at], local.at[0])
    own_down.start()
    greet(peers, groups)
    own_down.wait()
    down_line = Line(groups, lambda d: down_all.at[d], dl_s, dl_r)
    down_line.start(1)
    reduce = Reduce(peers, part, half, mine, got, r_s, r_r, halved=True)

    def fill(b):
        block = att_ref[pl.ds(pl.multiple_of(b * rows, rows), rows), :]
        part[b] = dot(block, out_ref[...]).astype(BF16)

    for k in reduce.order():
        fill(2 * reduce.to[k] + 1 - me % 2)
        reduce.inner[k].start()
    for k in reduce.order():
        fill(2 * reduce.to[k] + me % 2)
    reduce.pair()
    res_ref[...] = tok_ref[...].astype(F32) + reduce.total()
    low[...] = rms_norm(res_ref[...], gain_ref[...]).astype(BF16)
    keep = pltpu.make_async_copy(low, n2_all.at[me], local.at[1])
    keep.start()
    spread = Spread(peers, lambda c: low, lambda b: n2_all.at[b], n_s, n_r, True)
    spread.start()
    for step in range(2, groups):
        down_line.arrive(step - 1)
        down_line.start(step)
    spread.forward()
    down_line.arrive(groups - 1)
    spread.finish()
    reduce.finish()
    down_line.finish()
    keep.wait()


def branch(groups, peers, att, out, tok, gain, down):
    rows, width = tok.shape
    dma = pltpu.SemaphoreType.DMA
    vmem, hbm = pl.BlockSpec(memory_space=pltpu.VMEM), pl.BlockSpec(memory_space=pl.ANY)
    return pl.pallas_call(
        functools.partial(branch_kernel, groups, peers),
        in_specs=[vmem] * 5,
        out_specs=[vmem, hbm, hbm],
        out_shape=[
            jax.ShapeDtypeStruct((rows, width), F32),
            jax.ShapeDtypeStruct((peers, rows, width), BF16),
            jax.ShapeDtypeStruct((groups, *down.shape), BF16),
        ],
        scratch_shapes=[pltpu.VMEM((peers, rows, width), BF16), pltpu.VMEM((rows, width), BF16), dma((2,))]
        + Reduce.scratch(peers, rows, width)
        + [dma((2 * peers,)), dma((2 * peers,)), dma((2 * groups,)), dma((2 * groups,))],
        compiler_params=pltpu.CompilerParams(
            collective_id=2, has_side_effects=True, vmem_limit_bytes=48 * 1024 * 1024
        ),
        name="branch_and_norm",
    )(att, out, tok, gain, down)


def feed_forward_kernel(
    groups, peers, n2_ref, w_ref, down_ref, dy_ref, res_ref, gain_ref,
    dres_ref, db_all, outp_all, gd_all, gi_all, up_ref, dn_ref,
    part, hidden, pulled, low, outp_ref, gd_ref, gi_ref, local, half, mine, got, r_s, r_r, n_s, n_r, ug, dg, uo, do, l_s, l_r,
):
    me = lax.axis_index("blk")
    rows, width = res_ref.shape
    cols = w_ref.shape[1]
    units = cols // 2
    share = gi_ref.shape[2]
    slab = peers * share
    greet(peers, groups)
    reduce = Reduce(peers, part, half, mine, got, r_s, r_r, halved=True)

    def block(ref, b, count=1):
        return ref.at[pl.ds(pl.multiple_of(b * rows, rows), count * rows)]

    for k in reduce.order():
        chip = reduce.to[k]
        normed = block(n2_ref, 2 * chip, 2)[...]
        gate_up = dot(normed, w_ref[...])
        gate, up = gate_up[:, :units], gate_up[:, units:]
        sig = 1.0 / (1.0 + jnp.exp(-gate))
        silu = gate * sig
        block(hidden, 2 * chip, 2)[...] = (silu * up).astype(BF16)
        dhidden = dot(block(dy_ref, 2 * chip, 2)[...], down_ref[...], NT)
        dgate = dhidden * up * (sig + silu * (1.0 - sig))
        both_pulled = jnp.concatenate([dgate, dhidden * silu], 1).astype(BF16)
        block(pulled, 2 * chip, 2)[...] = both_pulled
        pull = dot(both_pulled, w_ref[...], NT).astype(BF16)
        part[2 * chip] = pull[:rows]
        part[2 * chip + 1] = pull[rows:]
        reduce.inner[k].start()
    line = LineSum(groups, lambda r: gi_ref.at[line.at + r], ug, dg, uo, do, l_s, l_r)
    upper = line.at >= groups // 2

    def chunk(i):
        d = jnp.where(upper, i, groups - 1 - i)
        cols_at = pl.ds(pl.multiple_of(d * slab, 128), slab)
        value = dot(n2_ref[:, cols_at], pulled[...], TN).astype(BF16)
        gi_ref[d] = value.reshape(peers, share, cols)

    chunk(0)
    line.step(0)
    reduce.pair()
    for i in range(1, groups):
        chunk(i)
    out_copies = [pltpu.make_async_copy(gi_ref, gi_all, local.at[1])]
    out_copies[0].start()
    dres_ref[...] = block(dy_ref, me)[...].astype(F32) + rms_pull(res_ref[...], gain_ref[...], reduce.total())
    low[...] = dres_ref[...].astype(BF16)
    keep = pltpu.make_async_copy(low, db_all.at[me], local.at[0])
    keep.start()
    spread = Spread(peers, lambda c: low, lambda b: db_all.at[b], n_s, n_r, True)
    spread.start()
    gd_ref[...] = dot(hidden[...], dy_ref[...], TN).astype(BF16).reshape(gd_ref.shape)
    out_copies.append(pltpu.make_async_copy(gd_ref, gd_all, local.at[2]))
    out_copies[1].start()
    steps = range(max(groups - 2, 1))
    for i in steps[1:]:
        line.step(i)
    spread.forward()

    def out(i, carry):
        at = pl.ds(pl.multiple_of(i * 2 * rows, rows), 2 * rows)
        value = dot(hidden[at, :], down_ref[...]).astype(BF16)
        outp_ref[2 * i] = value[:rows]
        outp_ref[2 * i + 1] = value[rows:]
        return carry

    lax.fori_loop(0, peers // 2, out, 0)
    out_copies.append(pltpu.make_async_copy(outp_ref, outp_all, local.at[3]))
    out_copies[2].start()
    spread.finish()
    reduce.finish()
    line.arrive(steps[-1], up_ref, dn_ref)
    line.finish(steps)
    for copy in [keep] + out_copies:
        copy.wait()


def feed_forward(groups, peers, n2_all, w, down, dy_all, res, gain):
    rows, width = res.shape
    tokens, cols = n2_all.shape[0], w.shape[1]
    share = width // (groups * peers)
    units = cols // (2 * groups)
    tall = 16 if units % 16 == 0 else units
    down_shape = (groups, units // tall, tall, width)
    dma = pltpu.SemaphoreType.DMA
    vmem, hbm = pl.BlockSpec(memory_space=pltpu.VMEM), pl.BlockSpec(memory_space=pl.ANY)

    def shape(*dims, dtype=BF16):
        return jax.ShapeDtypeStruct(dims, dtype)

    return pl.pallas_call(
        functools.partial(feed_forward_kernel, groups, peers),
        in_specs=[vmem] * 6,
        out_specs=[vmem, hbm, hbm, hbm, hbm, vmem, vmem],
        out_shape=[
            shape(rows, width, dtype=F32), shape(peers, rows, width), shape(peers, rows, width),
            shape(*down_shape), shape(groups, peers, share, cols),
            shape(peers, share, cols), shape(peers, share, cols),
        ],
        scratch_shapes=[
            pltpu.VMEM((peers, rows, width), BF16), pltpu.VMEM((tokens, cols // 2), BF16),
            pltpu.VMEM((tokens, cols), BF16), pltpu.VMEM((rows, width), BF16),
            pltpu.VMEM((peers, rows, width), BF16), pltpu.VMEM(down_shape, BF16),
            pltpu.VMEM((groups, peers, share, cols), BF16), dma((4,)),
        ]
        + Reduce.scratch(peers, rows, width)
        + [dma((2 * peers,)), dma((2 * peers,))]
        + LineSum.scratch(groups, peers, share, cols, steps=groups - 2),
        compiler_params=pltpu.CompilerParams(
            collective_id=3, has_side_effects=True, vmem_limit_bytes=62 * 1024 * 1024
        ),
        name="feed_forward",
    )(n2_all, w, down, dy_all, res, gain)


def final_kernel(
    groups, peers, heads, own, shared, aligned,
    norm_ref, dproj_ref, dlogit_ref, w_ref, ext_ref, att_ref, db_ref, ffn_ref, tok_ref, gain_ref, dres_ref,
    gd_ref, dup_ref, ddn_ref, wa_ref, wb_ref, wf_ref, ga_ref, gf_ref,
    dtok_ref, grad_ref, beta_fin, gout_fin, ffn_out, down_fin, gain_out, gain_ffn_out,
    g_ref, beta_ref, part, half, mine, got, r_s, r_r,
    oug, odg, ouo, odo, ol_s, ol_r, own_fin, own_rows, w_s, w_r, ffn_rows, f_s, f_r,
    beta_got, beta_sum, b_s, b_r, bug, bdg, buo, bdo, bl_s, bl_r,
    vg, wg, vo, wo, m_s, m_r,
    *extra,
):
    me, at = lax.axis_index("blk"), lax.axis_index("dp")
    core, chip = me % 2, me // 2
    sibling = me + 1 - 2 * core
    rows, width = tok_ref.shape
    h = width // heads
    share = g_ref.shape[2]
    slab = peers * share
    own_cols, quarter = own * 4 * h, shared * 2 * h
    cols = own_cols + 2 * quarter
    extra = list(extra)
    if shared:
        mix_half, mix_sum, mug, mdg, muo, mdo, ml_s, ml_r, mix_fin, mix_rows, x_s, x_r, mw_s, mw_r = extra[:14]
        extra = extra[14:]
    if aligned:
        go_part, go_half, go_mine, go_all, g_s, g_r, gug, gdg, guo, gdo, gl_s, gl_r = extra
    greet(peers, groups)
    down = LineSum(groups, lambda r: gd_ref.at[at + r], vg, wg, vo, wo, m_s, m_r, (dup_ref, ddn_ref), groups - 2)
    down.step(groups - 2)
    own_line = LineSum(groups, lambda r: g_ref.at[at + r, :, :, pl.ds(0, own_cols)], oug, odg, ouo, odo, ol_s, ol_r)
    upper = at >= groups // 2
    if shared:
        theirs = pl.ds(pl.multiple_of(own_cols + quarter * (1 - core), 128), quarter)
        ours = pl.ds(pl.multiple_of(own_cols + quarter * core, 128), quarter)
        mix = LineSum(groups, lambda r: mix_sum.at[at + r], mug, mdg, muo, mdo, ml_s, ml_r)

        def swap(d):
            return send(g_ref.at[d, :, :, theirs], mix_half.at[d], x_s.at[d], x_r.at[d], blk=sibling)

    def nth(i):
        return jnp.where(upper, i, groups - 1 - i)

    for i in range(groups):
        d = nth(i)
        normed = norm_ref[:, pl.ds(pl.multiple_of(d * slab, 128), slab)]
        g_ref[d] = dot(normed, dproj_ref[...], TN).astype(BF16).reshape(peers, share, cols)
        beta_ref[d] = dot(normed, dlogit_ref[...], TN).astype(BF16).reshape(peers, share, 128)
        if i == 0:
            own_line.step(0)
        if shared:
            swap(d).start()
    ffn = fanout(peers, lambda p: ffn_ref.at[p], lambda p: ffn_rows.at[me], f_s, f_r)
    reduce = Reduce(peers, part, half, mine, got, r_s, r_r, halved=True)
    for k in reduce.order():
        to = 2 * reduce.to[k]
        two = pl.ds(pl.multiple_of(to * rows, rows), 2 * rows)
        pull = dot(dproj_ref[two, :], w_ref[...], NT) + dot(dlogit_ref[two, :], ext_ref[...])
        pull = pull.astype(BF16)
        part[to] = pull[:rows]
        part[to + 1] = pull[rows:]
        reduce.inner[k].start()
        if shared and k == reduce.order()[0]:
            for i in range(groups):
                d = nth(i)
                swap(d).wait_recv()

                def body(j, carry):
                    mix_sum[d, j] = (g_ref[d, j, :, ours].astype(F32) + mix_half[d, j].astype(F32)).astype(BF16)
                    return carry

                lax.fori_loop(0, peers, body, 0)
                if i == 0:
                    mix.step(0)
    betas = fanout(peers, lambda p: beta_ref.at[:, p], lambda p: beta_got.at[me], b_s, b_r)
    for copy in betas:
        copy.start()
    sums = [own_line] + ([mix] if shared else [])
    reduce.pair()
    own_line.step(1)
    if aligned:
        att = att_ref[...]
        mine_att, zero = att[:, : own * h], jnp.zeros((att.shape[0], own * h), BF16)
        wide = jnp.concatenate(
            [jnp.where(core == 0, mine_att, zero), att[:, own * h :], jnp.where(core == 1, mine_att, zero)], 1
        )
        tile = width // 3
        for j in range(0, width, tile):
            value = dot(wide, db_ref[:, j : j + tile], TN).astype(BF16)
            go_part[:, :, j : j + tile] = value.reshape(peers, share, tile)
        gout = Reduce(peers, go_part, go_half, go_mine, go_all, g_s, g_r, go_all.at[chip, 0])
        gout.start()
    if shared:
        mix.step(1)
    if aligned:
        gout.pair()
        go_all[chip, 0] = go_mine[0]
    for copy in ffn:
        copy.start()
    ffn_rows[me] = ffn_ref[me]
    beta_got[me] = beta_ref[:, me]
    for copy in betas:
        copy.wait_recv()
    summed = beta_got[0].astype(F32)
    for b in range(1, peers):
        summed = summed + beta_got[b].astype(F32)
    beta_sum[:, 0] = summed.astype(BF16)
    late = [LineSum(groups, lambda r: beta_sum.at[at + r], bug, bdg, buo, bdo, bl_s, bl_r)]
    if aligned:
        for copy in gout.outer:
            copy.wait_recv()
        late.append(LineSum(groups, lambda r: go_all.at[at + r], gug, gdg, guo, gdo, gl_s, gl_r))
    for item in late:
        item.step(0)
    dtok_ref[...] = dres_ref[...] + rms_pull(tok_ref[...].astype(F32), gain_ref[...], reduce.total())
    for i in range(2, groups - 1):
        for item in sums:
            item.step(i)
        for item in late:
            item.step(i - 1)
    down.total(down_fin)
    for item in late:
        item.step(groups - 2)
    for copy in ffn:
        copy.wait_recv()
    units = wf_ref.shape[1] // (2 * groups * peers)
    total = jnp.zeros((share, 1), F32)
    for b in range(peers):
        for side in range(2):
            for d in range(groups):
                src = (side * groups + d) * units
                to = ((side * groups + d) * peers + b) * units
                value = ffn_rows[b, :, src : src + units].astype(F32)
                ffn_out[:, to : to + units] = value
                total = total + jnp.sum(value * wf_ref[:, to : to + units].astype(F32), -1, keepdims=True)
    gain_ffn_out[...] = jnp.broadcast_to(total, (share, 128)) / gf_ref[...]
    own_line.total(own_fin)
    moves = fanout(peers, lambda p: own_fin.at[p], lambda p: own_rows.at[me], w_s, w_r)
    for copy in moves:
        copy.start()
    own_rows[me] = own_fin[me]
    if shared:
        mix.total(mix_fin)
        mix_moves = fanout(peers, lambda p: mix_fin.at[p], lambda p: mix_rows.at[me], mw_s, mw_r)
        for copy in mix_moves:
            copy.start()
        mix_rows[me] = mix_fin[me]
        moves += mix_moves
    late[0].total(beta_fin)
    if aligned:
        late[1].total(gout_fin)
    for copy in moves:
        copy.wait_recv()
    gain = beta_fin[0] * wb_ref[...].astype(F32)
    hc = 2 * own + shared

    def put(acc, value, head, side):
        to = side * width + head * h
        value = value.astype(F32)
        grad_ref[:, to : to + h] = value
        return acc + value * wa_ref[:, to : to + h].astype(F32)

    for b in range(peers):
        for s in range(own):
            head = (b // 2) * hc + (b % 2) * (own + shared) + s
            if head < heads:
                for side in range(4):
                    gain = put(gain, own_rows[b, :, (4 * s + side) * h : (4 * s + side + 1) * h], head, side)
        if shared:
            for i in range(2):
                gain = put(gain, mix_rows[b, :, i * h : (i + 1) * h], (b // 2) * hc + own, 2 * (b % 2) + i)
    gain_out[...] = jnp.broadcast_to(jnp.sum(gain, -1, keepdims=True), gain.shape) / ga_ref[...]
    reduce.finish()
    for copy in betas + ffn + moves:
        copy.wait_send()
    if shared:
        for i in range(groups):
            swap(nth(i)).wait_send()
    if aligned:
        gout.finish()
    for item in sums + late:
        item.finish()
    down.finish([groups - 2])


def final_sums(groups, peers, heads, own, shared, aligned, *args):
    normed, dproj, dlogits, w, ext, att, db, ffn, tok = args[:9]
    gd, wa, wf = args[11], args[14], args[16]
    rows, width = tok.shape
    h, share = width // heads, wa.shape[0]
    own_cols, quarter, cols = own * 4 * h, shared * 2 * h, w.shape[1]
    dma = pltpu.SemaphoreType.DMA
    vmem = pl.BlockSpec(memory_space=pltpu.VMEM)

    def block(*dims):
        return pltpu.VMEM(dims, BF16)

    def shape(*dims, dtype=F32):
        return jax.ShapeDtypeStruct(dims, dtype)

    pair = [dma((peers,))] * 2
    scratch = [block(groups, peers, share, cols), block(groups, peers, share, 128), block(peers, rows, width)]
    scratch += Reduce.scratch(peers, rows, width)
    scratch += LineSum.scratch(groups, peers, share, own_cols) + [block(peers, share, own_cols)] * 2 + pair
    scratch += [block(*ffn.shape)] + pair
    scratch += [block(peers, groups, share, 128), block(groups, 1, share, 128)] + pair
    scratch += LineSum.scratch(groups, 1, share, 128) + LineSum.scratch(groups, *gd.shape[1:], steps=1)
    if shared:
        scratch += [block(groups, peers, share, quarter)] * 2 + LineSum.scratch(groups, peers, share, quarter)
        scratch += [block(peers, share, quarter)] * 2 + [dma((groups,)), dma((groups,))] + pair
    if aligned:
        half = block(peers // 2, share, width)
        scratch += [block(peers, share, width), half, half, block(groups, 1, share, width)] + pair
        scratch += LineSum.scratch(groups, 1, share, width)
    return pl.pallas_call(
        functools.partial(final_kernel, groups, peers, heads, own, shared, aligned),
        in_specs=[vmem] * len(args),
        out_specs=[vmem] * 8,
        out_shape=[
            shape(rows, width), shape(*wa.shape), shape(1, share, 128), shape(1, share, width), shape(*wf.shape),
            shape(*gd.shape[1:]), shape(share, 128), shape(share, 128),
        ],
        scratch_shapes=scratch,
        compiler_params=pltpu.CompilerParams(
            collective_id=4, has_side_effects=True, vmem_limit_bytes=63 * 1024 * 1024
        ),
        name="final_sums",
    )(*args)


def shards(
    tokens, cotangent, doc_table, gain_attn, attn_in, beta_proj, attn_out, gain_ffn, ffn_in, ffn_down
):
    rows, width = tokens.shape
    heads = beta_proj.shape[1]
    h = width // heads
    groups, peers = lax.axis_size("dp"), lax.axis_size("blk")
    chips = peers // 2
    hc = -(-heads // chips)
    own, shared = hc // 2, hc % 2
    slots, padded = own + shared, hc * chips
    own_cols, quarter = own * 4 * h, shared * 2 * h
    share, units = attn_in.shape[0], ffn_down.shape[0]
    aligned = chips == groups and padded == heads
    me = lax.axis_index("blk")
    chip, core = me // 2, me % 2
    by_chip = attn_in.reshape(share, 4, heads, h).transpose(2, 0, 1, 3)
    by_chip = jnp.pad(by_chip, ((0, padded - heads), (0, 0), (0, 0), (0, 0))).reshape(chips, hc, share, 4, h)
    own_parts = jnp.stack([by_chip[:, :own], by_chip[:, own + shared :]], 1)
    own_parts = own_parts.transpose(0, 1, 3, 2, 4, 5).reshape(peers, share, own_cols)
    mix_parts = None
    if shared:
        mix_parts = by_chip[:, own].reshape(chips, share, 2, 2 * h).transpose(0, 2, 1, 3).reshape(peers, share, 2 * h)
    ffn_parts = ffn_in.reshape(share, 2, groups, peers, units).transpose(3, 0, 1, 2, 4).reshape(peers, share, -1)
    ext = jnp.concatenate([beta_proj.T, gain_attn[None], gain_ffn[None]], 0)
    ext_rows = -(-(heads + 2) // 16) * 16
    ext = jnp.pad(ext, ((0, ext_rows - heads - 2), (0, 128 - share)))
    w2, ffn_part, x_all, out_all, ext_all = gather_all(
        groups, peers, aligned, own_parts, mix_parts, ffn_parts, tokens, attn_out, ext
    )
    w2 = w2.reshape(width, -1)
    ffn_part = ffn_part.reshape(peers * share, -1)
    x_all = x_all.reshape(peers * rows, width)
    ext_all = ext_all[..., :share].transpose(2, 0, 1, 3).reshape(ext_rows, width)
    out_rows = out_all.reshape(-1, width)
    if not aligned:
        out_rows = jnp.pad(out_rows, ((0, (padded - heads) * h), (0, 0)))
        out_rows = lax.dynamic_slice_in_dim(out_rows, chip * hc * h, hc * h, 0)
    out2 = lax.dynamic_slice_in_dim(out_rows, core * (own + shared) * h, own * h, 0)
    if shared:
        out2 = jnp.concatenate([out2, out_rows[own * h : (own + 1) * h]], 0)
    ffn_slab = lax.all_gather(ffn_part, "dp", axis=0, tiled=True)

    first = chip * hc + core * (own + shared)
    my_heads = jnp.stack([first + s for s in range(own)] + [chip * hc + own] * shared).astype(jnp.int32)
    on = jnp.stack([jnp.int32(1)] * own + [1 - core] * shared).astype(jnp.int32)
    gain_one = ext_all[heads][None].astype(F32)
    gain_two = ext_all[heads + 1][None].astype(F32)

    normed, dy_all, proj, logits, attended, *saved = attention_forward(
        doc_table, on, my_heads, x_all, gain_one, w2, ext_all, cotangent, peers, slots, rows
    )
    dy_all = dy_all.reshape(peers * rows, width)
    residual, normed_two_all, down_all = branch(groups, peers, attended, out2, tokens, gain_two, ffn_down)
    normed_two_all = normed_two_all.reshape(peers * rows, width)
    down_slab = down_all.reshape(-1, width)

    dresidual, dbranch_all, out_part, grad_down, grad_ffn, up, down = feed_forward(
        groups, peers, normed_two_all, ffn_slab, down_slab, dy_all, residual, gain_two
    )
    dbranch_all = dbranch_all.reshape(peers * rows, width)
    dproj, dlogits, block_out, grad_ffn, down_up, down_dn = attention_backward(
        doc_table, on, my_heads, out_part, residual, grad_ffn, up, down, grad_down, dbranch_all, out2,
        proj, logits, saved, groups, peers, slots, rows,
    )
    grad_tokens, grad_attn_in, grad_beta, grad_attn_out, grad_ffn_in, grad_down, grad_gain_attn, grad_gain_ffn = final_sums(
        groups, peers, heads, own, shared, aligned,
        normed, dproj, dlogits, w2, jnp.pad(ext_all[:heads], ((0, 128 - heads), (0, 0))), attended, dbranch_all, grad_ffn,
        tokens, gain_one, dresidual, grad_down, down_up, down_dn,
        attn_in, jnp.pad(beta_proj, ((0, 0), (0, 128 - heads))), ffn_in,
        jnp.broadcast_to(gain_attn.astype(F32)[:, None], (share, 128)),
        jnp.broadcast_to(gain_ffn.astype(F32)[:, None], (share, 128)),
    )
    if aligned:
        grad_attn_out = grad_attn_out[0]
    else:
        gout = dot(attended, dbranch_all, TN)
        first = chip * hc + core * (own + shared)
        whole = jnp.zeros((padded * h, width), F32)
        whole = lax.dynamic_update_slice_in_dim(whole, gout, first * h, 0)[: heads * h]
        grad_attn_out = lax.psum_scatter(whole, ("dp", "blk"), scatter_dimension=0, tiled=True)
    return (
        block_out, grad_tokens, grad_gain_attn[:, 0], grad_attn_in, grad_beta[0, :, :heads], grad_attn_out,
        grad_gain_ffn[:, 0], grad_ffn_in, grad_down.reshape(units, width),
    )


def solution(mesh):
    split, vector = P(("dp", "blk"), None), P(("dp", "blk"))
    in_specs = (split, split, P("dp", None), vector, split, split, split, vector, split, split)
    out_specs = (split, split, vector, split, split, split, vector, split, split)
    return jax.shard_map(shards, mesh=mesh, in_specs=in_specs, out_specs=out_specs, check_vma=False)
```

```python
import functools

import jax
import jax.numpy as jnp
from jax import lax
from jax.experimental import pallas as pl
from jax.experimental.pallas import tpu as pltpu
from jax.sharding import PartitionSpec as P

EPSILON = 1e-06
F32 = jnp.float32
BF16 = jnp.bfloat16

NN = (((1,), (0,)), ((), ()))
NT = (((1,), (1,)), ((), ()))
TN = (((0,), (0,)), ((), ()))


def dot(a, b, dims=NN):
    return lax.dot_general(a, b, dims, preferred_element_type=F32)


def halves(x):
    high = x.astype(BF16)
    return high, (x - high.astype(F32)).astype(BF16)


def dot3(a, b, dims=NN):
    (ah, al), (bh, bl) = a, b
    ka, kb = dims[0][0][0], dims[0][1][0]
    deep, wide = ah.shape[ka], bh.shape[1 - kb]
    if deep <= 128:
        left = jnp.concatenate([ah, al], ka)
        if wide <= 128:
            below = jnp.concatenate([bh, jnp.zeros_like(bh)], 1 - kb)
            both_parts = dot(left, jnp.concatenate([jnp.concatenate([bh, bl], 1 - kb), below], kb), dims)
            return both_parts[:, :wide] + both_parts[:, wide:]
        return dot(left, jnp.concatenate([bh, bh], kb), dims) + dot(ah, bl, dims)
    if wide <= 128:
        both_parts = dot(ah, jnp.concatenate([bh, bl], 1 - kb), dims)
        return both_parts[:, :wide] + (both_parts[:, wide:] + dot(al, bh, dims))
    return dot(ah, bh, dims) + (dot(ah, bl, dims) + dot(al, bh, dims))


def both(parts, axis):
    return tuple(jnp.concatenate(p, axis) for p in zip(*parts))


def rms_norm(values, gain):
    return values * lax.rsqrt(jnp.mean(values * values, axis=-1, keepdims=True) + EPSILON) * gain


def rms_pull(values, gain, grad):
    scale = lax.rsqrt(jnp.mean(values * values, axis=-1, keepdims=True) + EPSILON)
    inner = grad * gain
    along = jnp.mean(inner * values, axis=-1, keepdims=True)
    return scale * inner - values * (scale * scale * scale) * along


def lanes(n):
    return lax.broadcasted_iota(jnp.int32, (n, n), 1)


def rows_of(n):
    return lax.broadcasted_iota(jnp.int32, (n, n), 0)


def inverses(grams, betas, span):
    r, c = rows_of(span), lanes(span)
    eye = r == c
    outs = []
    pair = (c + 1 == r) & (r % 2 == 1)
    for gram, beta in zip(grams, betas):
        below = jnp.where(pair, gram, 0.0) * beta * beta.T
        outs.append(jnp.where(eye, beta, 0.0) - below)
    size = 2
    while size < span:
        part = (r // (2 * size) == c // (2 * size)) & ((r // size) % 2 == 1) & ((c // size) % 2 == 0)
        sides = [halves(x) for x in outs]
        steps = [dot3(halves(jnp.where(part, g, 0.0)), x) for g, x in zip(grams, sides)]
        outs = [x - dot3(s, halves(t)) for x, s, t in zip(outs, sides, steps)]
        size *= 2
    return outs


MESH = pl.DeviceIdType.MESH


def send(src, dst, send_sem, recv_sem, **device):
    return pltpu.make_async_remote_copy(
        src_ref=src, dst_ref=dst, send_sem=send_sem, recv_sem=recv_sem, device_id=device, device_id_type=MESH
    )


def greet(peers, groups=0):
    barrier = pltpu.get_barrier_semaphore()
    me = lax.axis_index("blk")
    for k in range(1, peers):
        pl.semaphore_signal(barrier, inc=1, device_id={"blk": (me + k) % peers}, device_id_type=MESH)
    if groups:
        at = lax.axis_index("dp")

        @pl.when(at + 1 < groups)
        def _():
            pl.semaphore_signal(barrier, inc=1, device_id={"dp": at + 1}, device_id_type=MESH)

        @pl.when(at > 0)
        def _():
            pl.semaphore_signal(barrier, inc=1, device_id={"dp": at - 1}, device_id_type=MESH)

        @pl.when((at > 0) & (at + 1 < groups))
        def _():
            pl.semaphore_wait(barrier, peers + 1)

        @pl.when((at == 0) | (at + 1 == groups))
        def _():
            pl.semaphore_wait(barrier, peers)
    else:
        pl.semaphore_wait(barrier, peers - 1)


def square(chips, chip):
    return chip + 1 - 2 * (chip % 2), (chip + 2) % chips, chips - 1 - chip


class Spread:
    def __init__(self, peers, source, pick, sems, recvs, halved=False):
        me = lax.axis_index("blk")
        self.chips = peers // 2
        core, chip = me % 2, me // 2
        sibling = me + 1 - 2 * core
        self.halved = halved and self.chips == 4

        def copy(i, src, dst, to):
            return send(src, dst, sems.at[i], recvs.at[i], blk=to)

        self.first = [copy(0, source(chip), pick(me), sibling)]
        self.second, self.cross = [], []
        if self.halved:
            x, y, far = (2 * c + core for c in square(self.chips, chip))
            half = pick(me).shape[0] // 2
            low, high = pl.ds(0, half), pl.ds(half, half)
            for i, to in enumerate((x, y)):
                self.first.append(copy(1 + i, source(to // 2), pick(me), to))
                self.second.append(copy(3 + i, pick(to), pick(to), sibling))
            self.cross = [
                copy(5, pick(x).at[low], pick(x).at[low], y),
                copy(6, pick(y).at[high], pick(y).at[high], x),
            ]
            self.last = [
                copy(7 + i, pick(far).at[rows], pick(far).at[rows], sibling) for i, rows in enumerate((low, high))
            ]
            return
        for k in range(1, self.chips):
            to = (me + 2 * k) % peers
            self.first.append(copy(k, source(to // 2), pick(me), to))
            origin = pick((me + peers - 2 * k) % peers)
            self.second.append(copy(self.chips + k - 1, origin, origin, sibling))

    def start(self):
        for copy in self.first[1:] + self.first[:1]:
            copy.start()

    def forward(self):
        for i, (copy, onward) in enumerate(zip(self.first[1:], self.second)):
            copy.wait_recv()
            if self.halved:
                self.cross[i].start()
            onward.start()
        if self.halved:
            for copy, onward in zip(self.cross, self.last):
                copy.wait_recv()
                onward.start()

    def finish(self):
        for copy in self.first + self.cross:
            copy.wait_send()
        self.first[0].wait_recv()
        for copy in self.second + (self.last if self.halved else []):
            copy.wait()


class Line:
    def __init__(self, groups, pick, sems, recvs):
        self.groups, self.pick, self.sems, self.recvs = groups, pick, sems, recvs
        self.at = lax.axis_index("dp")

    def up(self, step, to, block):
        i = 2 * (step - 1)
        return send(self.pick(block), self.pick(block), self.sems.at[i], self.recvs.at[i], dp=to)

    def down(self, step, to, block):
        i = 2 * (step - 1) + 1
        return send(self.pick(block), self.pick(block), self.sems.at[i], self.recvs.at[i], dp=to)

    def start(self, step):
        at, n = self.at, self.groups

        @pl.when((at + 1 < n) & (at - (step - 1) >= 0))
        def _():
            self.up(step, at + 1, at - (step - 1)).start()

        @pl.when((at - 1 >= 0) & (at + (step - 1) < n))
        def _():
            self.down(step, at - 1, at + (step - 1)).start()

    def arrive(self, step, then=None):
        at, n = self.at, self.groups

        @pl.when(at - step >= 0)
        def _():
            self.up(step, at - 1, at - step).wait_recv()
            if then is not None:
                then(at - step).start()

        @pl.when(at + step < n)
        def _():
            self.down(step, at + 1, at + step).wait_recv()
            if then is not None:
                then(at + step).start()

    def finish(self, steps):
        at, n = self.at, self.groups
        for step in steps:

            @pl.when((at + 1 < n) & (at - (step - 1) >= 0))
            def _():
                self.up(step, at + 1, at - (step - 1)).wait_send()

            @pl.when((at - 1 >= 0) & (at + (step - 1) < n))
            def _():
                self.down(step, at - 1, at + (step - 1)).wait_send()


class LineSum:
    def __init__(self, groups, pick, up_got, dn_got, up_out, dn_out, sems, recvs, arrived=None, base=0):
        self.n, self.pick, self.arrived, self.base = groups, pick, arrived, base
        self.up_got, self.dn_got, self.up_out, self.dn_out = up_got, dn_got, up_out, dn_out
        self.sems, self.recvs = sems, recvs
        self.at = lax.axis_index("dp")

    @staticmethod
    def scratch(groups, *block, steps=None):
        hop = pltpu.VMEM((steps or groups - 1, *block), BF16)
        return [hop] * 4 + [pltpu.SemaphoreType.DMA((2 * groups,))] * 2

    def up(self, i, src, to):
        return send(src, self.up_got.at[i - self.base], self.sems.at[2 * i], self.recvs.at[2 * i], dp=to)

    def down(self, i, src, to):
        return send(src, self.dn_got.at[i - self.base], self.sems.at[2 * i + 1], self.recvs.at[2 * i + 1], dp=to)

    def add(self, out, one, other):
        def body(j, carry):
            out[j] = (one[j].astype(F32) + other[j].astype(F32)).astype(out.dtype)
            return carry

        lax.fori_loop(0, out.shape[0], body, 0)

    def step(self, i):
        at, n = self.at, self.n
        far = n - 1 - i

        @pl.when((at + far < n) & (at == 0))
        def _():
            self.up(i, self.pick(far), at + 1).start()

        @pl.when((at - far >= 0) & (at == n - 1))
        def _():
            self.down(i, self.pick(-far), at - 1).start()

        if i > 0:

            @pl.when((at + far < n) & (at > 0))
            def _():
                if self.arrived is None:
                    self.up(i - 1, self.up_out.at[max(i - 1 - self.base, 0)], at - 1).wait_recv()
                before = self.up_got.at[max(i - 1 - self.base, 0)] if self.arrived is None else self.arrived[0]
                self.add(self.up_out.at[i - self.base], self.pick(far), before)
                self.up(i, self.up_out.at[i - self.base], at + 1).start()

            @pl.when((at - far >= 0) & (at < n - 1))
            def _():
                if self.arrived is None:
                    self.down(i - 1, self.dn_out.at[max(i - 1 - self.base, 0)], at + 1).wait_recv()
                before = self.dn_got.at[max(i - 1 - self.base, 0)] if self.arrived is None else self.arrived[1]
                self.add(self.dn_out.at[i - self.base], self.pick(-far), before)
                self.down(i, self.dn_out.at[i - self.base], at - 1).start()

    def arrive(self, i, up, down):
        at, n = self.at, self.n
        far = n - 1 - i
        some_up, some_down = (at > 0) & (at - 1 + far < n), (at < n - 1) & (at + 1 - far >= 0)

        @pl.when(some_up)
        def _():
            self.up(i, self.up_out.at[i - self.base], at - 1).wait_recv()
            up[...] = self.up_got[i - self.base]

        @pl.when(some_down)
        def _():
            self.down(i, self.dn_out.at[i - self.base], at + 1).wait_recv()
            down[...] = self.dn_got[i - self.base]

        @pl.when(jnp.logical_not(some_up))
        def _():
            up[...] = jnp.zeros_like(up)

        @pl.when(jnp.logical_not(some_down))
        def _():
            down[...] = jnp.zeros_like(down)

    def total(self, out):
        at, n, i = self.at, self.n, self.n - 2

        @pl.when(at > 0)
        def _():
            self.up(i, self.up_out.at[i - self.base], at - 1).wait_recv()
            self.add(out, self.pick(0), self.up_got.at[i - self.base])

        @pl.when(at == 0)
        def _():
            self.down(i, self.dn_out.at[i - self.base], at + 1).wait_recv()
            self.add(out, self.pick(0), self.dn_got.at[i - self.base])

        @pl.when((at > 0) & (at < n - 1))
        def _():
            self.down(i, self.dn_out.at[i - self.base], at + 1).wait_recv()
            self.add(out, out, self.dn_got.at[i - self.base])

    def finish(self, steps=None):
        at, n = self.at, self.n
        for i in range(n - 1) if steps is None else steps:
            far = n - 1 - i

            @pl.when(at + far < n)
            def _():
                self.up(i, self.up_out.at[i - self.base], at + 1).wait_send()

            @pl.when(at - far >= 0)
            def _():
                self.down(i, self.dn_out.at[i - self.base], at - 1).wait_send()


class Reduce:
    def __init__(self, peers, part, half, mine, got, sems, recvs, place=None, halved=False):
        me = lax.axis_index("blk")
        self.chips = peers // 2
        self.core, self.chip = me % 2, me // 2
        sibling = me + 1 - 2 * self.core
        self.part, self.half, self.mine, self.got = part, half, mine, got
        self.halved = halved and self.chips == 4

        def copy(i, src, dst, to):
            return send(src, dst, sems.at[i], recvs.at[i], blk=to)

        if self.halved:
            self.to = [self.chip, *square(self.chips, self.chip)]
        else:
            self.to = [(self.chip + k) % self.chips for k in range(self.chips)]
        self.inner = [copy(k, part.at[2 * to + 1 - self.core], half.at[k], sibling) for k, to in enumerate(self.to)]
        self.outer = []
        if self.halved:
            x, y, far = (2 * c + self.core for c in self.to[1:])
            middle = mine.shape[1] // 2
            self.low, self.high = pl.ds(0, middle), pl.ds(middle, middle)
            self.cross = [
                copy(6, mine.at[3, self.low], got.at[3, self.low], x),
                copy(7, mine.at[3, self.high], got.at[3, self.high], y),
            ]
            self.outer = [copy(4, mine.at[1], got.at[1], x), copy(5, mine.at[2], got.at[2], y)]
            return
        for k in range(1, self.chips):
            arrival = got.at[k] if place is None else place
            self.outer.append(copy(self.chips + k, mine.at[k], arrival, 2 * self.to[k] + self.core))

    def order(self):
        return list(range(self.chips - 1, -1, -1)) if self.halved else list(range(1, self.chips)) + [0]

    def start(self):
        for k in self.order():
            self.inner[k].start()

    def chip_sums(self):
        for k in self.order():
            self.inner[k].wait_recv()
            both_cores = self.part[2 * self.to[k] + self.core].astype(F32) + self.half[k].astype(F32)
            self.mine[k] = both_cores.astype(BF16)
            if self.halved:
                if k == 3:
                    for copy in self.cross:
                        copy.start()
            elif k > 0:
                self.outer[k - 1].start()

    def pair(self):
        self.chip_sums()
        self.cross_sums()

    def cross_sums(self):
        if self.halved:
            for copy, rows, k in ((self.cross[0], self.low, 2), (self.cross[1], self.high, 1)):
                copy.wait_recv()
                summed = self.mine[k, rows].astype(F32) + self.got[3, rows].astype(F32)
                self.mine[k, rows] = summed.astype(BF16)
                self.outer[k - 1].start()

    def total(self):
        total = self.mine[0].astype(F32)
        for k, copy in enumerate(self.outer):
            copy.wait_recv()
            total = total + self.got[k + 1].astype(F32)
        return total

    def finish(self):
        for copy in self.inner + self.outer + (self.cross if self.halved else []):
            copy.wait_send()

    @staticmethod
    def scratch(peers, rows, width):
        block = pltpu.VMEM((peers // 2, rows, width), BF16)
        return [block, block, block, pltpu.SemaphoreType.DMA((peers,)), pltpu.SemaphoreType.DMA((peers,))]


def fanout(peers, source, dst, sems, recvs):
    me = lax.axis_index("blk")
    copies = []
    for k in range(1, peers):
        p = (me + k) % peers
        copies.append(send(source(p), dst(p), sems.at[k], recvs.at[k], blk=p))
    return copies


def attention_forward_kernel(
    groups, peers, heads, share, spans, span, doc_ref, on_ref, head_ref, x_all, w_ref, pieces_ref, dy_ref, ffn_ref,
    norm_ref, dy_all, ext_ref, ffn_all, proj_ref, logit_ref,
    low_ref, att_ref, sum_ref, a1_ref, g_ref, y_ref, e0_ref, qp_ref, m_ref, kts_ref,
    kpt_ref, kt_ref, x_ref, keep_sem, x_sem, d_s, d_r, l_s, l_r,
):
    h = span
    scale = h ** -0.5
    slot, me = pl.program_id(0), lax.axis_index("blk")
    tall = 2 * span

    def dy_copies():
        keep = pltpu.make_async_copy(dy_ref, dy_all.at[me], keep_sem.at[0])
        return keep, Spread(peers, lambda c: dy_ref, lambda b: dy_all.at[b], d_s, d_r, True)

    at_dp = lax.axis_index("dp")
    ffn_line = Line(groups, lambda d: ffn_all.at[d], l_s, l_r)

    @pl.when(slot == 0)
    def _():
        own_ffn = pltpu.make_async_copy(ffn_ref, ffn_all.at[at_dp], keep_sem.at[1])
        own_ffn.start()
        loads = [
            pltpu.make_async_copy(x_all.at[pl.ds(i * tall, tall)], x_ref.at[pl.ds(i * tall, tall)], x_sem.at[i])
            for i in range(spans // 2)
        ]
        for copy in loads:
            copy.start()
        greet(peers, groups)
        keep, spread = dy_copies()
        keep.start()
        spread.start()
        own_ffn.wait()
        ffn_line.start(1)
        lanes_in, slab = peers * 128, peers * share
        source = lax.broadcasted_iota(jnp.int32, (lanes_in, slab), 0)
        target = lax.broadcasted_iota(jnp.int32, (lanes_in, slab), 1)
        place = (source // 128 * share + source % 128 == target) & (source % 128 < share)
        place = jnp.where(place, 1.0, 0.0).astype(BF16)
        for d in range(groups):
            pieces = jnp.concatenate([pieces_ref[d, b] for b in range(peers)], 1)
            ext_ref[:, d * slab : (d + 1) * slab] = dot(pieces, place).astype(BF16)
        gain = ext_ref[...].astype(F32)[heads : heads + 1]
        for i, copy in enumerate(loads):
            copy.wait()
            rows = pl.ds(i * tall, tall)
            norm_ref[rows, :] = rms_norm(x_ref[rows, :].astype(F32), gain).astype(BF16)

    def project(i, carry):
        rows = pl.ds(pl.multiple_of(i * tall, tall), tall)
        normed = norm_ref[rows, :]
        proj_ref[rows, :] = dot(normed, w_ref[...])
        every = dot(normed, ext_ref[...], NT)
        lane = lax.broadcasted_iota(jnp.int32, every.shape, 1)
        mine = jnp.sum(jnp.where(lane == head_ref[slot], every, 0.0), -1, keepdims=True)
        logit_ref[rows, :] = jnp.broadcast_to(mine, (tall, h))
        return carry

    lax.fori_loop(0, spans // 2, project, 0)
    r, c = rows_of(span), lanes(span)
    lower, strict, eye = c <= r, c < r, (c == r).astype(F32)
    at = [pl.ds(n * span, span) for n in range(spans)]
    group = 4
    for first in range(0, spans, group):
        members = range(first, min(first + group, spans))
        grams, betas, kept = [], [], []
        for n in members:
            q = proj_ref[at[n], 0:h]
            k = proj_ref[at[n], h : 2 * h]
            d = proj_ref[at[n], 3 * h : 4 * h]
            w = d * lax.rsqrt(jnp.sum(d * d, -1, keepdims=True) + EPSILON)
            qs, ks, ws = halves(q), halves(k), halves(w)
            z = dot3(both((qs, ws), 0), both((ws, ks), 0), NT)
            a1 = jnp.where(lower, z[:span, :span], 0.0)
            a1_ref[at[n], :] = a1
            b1 = jnp.where(strict, z[span:, span:], 0.0)
            grams.append(jnp.where(strict, z[span:, :span], 0.0))
            betas.append(2.0 / (1.0 + jnp.exp(-logit_ref[at[n], :])))
            kept.append((q, k, ws, halves(a1), halves(b1), z[:span, span:]))
        solved = inverses(grams, betas, span)
        for n, g, (q, k, ws, a1s, b1s, qk) in zip(members, solved, kept):
            g_ref[at[n], :] = g
            y = dot3(halves(g), both((ws, b1s), 1))
            y_ref[at[n], :] = y
            ys = halves(y)
            t = dot3(a1s, ys)
            u = dot3(ws, ys, TN)
            qp_ref[at[n], :] = (q - t[:, :h]).astype(BF16)
            local = (qk - t[:, h:]) * scale
            e0_ref[at[n], :] = jnp.where(lower, jnp.exp(local), 0.0)
            m_ref[at[n], :] = eye - u[:, :h]
            kpt_ref[:, at[n]] = k.T - u[:, h:]
    for n in range(spans):
        w = n * span
        e0 = e0_ref[at[n], :]
        total = jnp.sum(e0, -1, keepdims=True)
        numer = dot(e0.astype(BF16), proj_ref[at[n], 2 * h : 3 * h].astype(BF16))
        if n > 0:
            kt = kt_ref[:, :w]
            kts = halves(kt)
            kts_ref[0, n, :, :w] = kts[0]
            block = jnp.exp(dot(qp_ref[at[n], :], kts[0]) * scale)
            block = jnp.concatenate(
                [jnp.where(doc_ref[0, j] == doc_ref[0, n], block[:, j * span : (j + 1) * span], 0.0) for j in range(n)], 1
            )
            total = total + jnp.sum(block, -1, keepdims=True)
            numer = numer + dot(block.astype(BF16), proj_ref[:w, 2 * h : 3 * h].astype(BF16))
            if n < spans - 1:
                kt_ref[:, :w] = dot3(halves(m_ref[at[n], :]), kts)
        if n < spans - 1:
            kt_ref[:, at[n]] = kpt_ref[:, at[n]]
        attended = numer / total
        att_ref[at[n], :] = attended
        low_ref[at[n], :] = jnp.where(on_ref[slot] > 0, attended, 0.0).astype(BF16)
        sum_ref[at[n], :] = jnp.broadcast_to(total, (span, h))

    @pl.when(slot == 0)
    def _():
        dy_copies()[1].forward()
        ffn_line.arrive(1)
        ffn_line.start(2)

    @pl.when(slot == pl.num_programs(0) - 1)
    def _():
        keep, spread = dy_copies()
        for step in range(3, groups - 1):
            ffn_line.arrive(step - 1)
            ffn_line.start(step)
        spread.finish()
        keep.wait()
        ffn_line.arrive(groups - 2)
        ffn_line.finish(range(1, groups - 1))


def attention_backward_kernel(
    groups, peers, spans, span, doc_ref, on_ref, head_ref, outp_ref, res_ref, gi_all, up_ref, dn_ref, gd_ref, db_ref, out_ref,
    proj_ref, logit_ref, att_ref, sum_ref, a1_ref, g_ref, y_ref, e0_ref, qp_ref, m_ref, kts_ref,
    dproj_ref, dlogit_ref, block_ref, rows_ref, dup_ref, ddn_ref,
    gkt_ref, dvt_ref, dqp_ref, dm_ref, dkpt_ref, ds_ref, datt_ref, half, mine, got, r_s, r_r, gi_ref, local,
    ug, dg, uo, do, l_s, l_r, vg, wg, vo, wo, m_s, m_r,
):
    h = span
    scale = h ** -0.5
    r, c = rows_of(span), lanes(span)
    lower, strict, same = c <= r, c < r, c == r
    at = [pl.ds(n * span, span) for n in range(spans)]
    slot = pl.program_id(0)

    def reduce():
        return Reduce(peers, outp_ref, half, mine, got, r_s, r_r, halved=True)

    place = {1: 0, -1: 1, 0: 2}
    line = LineSum(groups, lambda r: gi_ref.at[place[r]], ug, dg, uo, do, l_s, l_r, (up_ref, dn_ref), groups - 2)
    at_dp = line.at
    down = LineSum(groups, lambda r: gd_ref.at[at_dp + r], vg, wg, vo, wo, m_s, m_r)

    @pl.when(slot == 0)
    def _():
        loads = [
            pltpu.make_async_copy(gi_all.at[(at_dp + groups + r) % groups], gi_ref.at[i], local.at[i])
            for r, i in place.items()
        ]
        for copy in loads:
            copy.start()
        greet(peers, groups)
        reduce().start()
        for copy in loads:
            copy.wait()
        line.step(groups - 2)
        down.step(0)

    def pull_back(i, carry):
        rows = pl.ds(pl.multiple_of(i * 2 * span, span), 2 * span)
        datt_ref[rows, :] = dot(db_ref[rows, :], out_ref[...], NT)
        return carry

    lax.fori_loop(0, spans // 2, pull_back, 0)
    dvt_ref[...] = jnp.zeros_like(dvt_ref)
    for n in reversed(range(spans)):
        w = n * span
        last = n == spans - 1
        datt, total = jnp.where(on_ref[slot] > 0, datt_ref[at[n], :], 0.0), sum_ref[at[n], :]
        da = (datt / total).astype(BF16)
        delta = jnp.sum(datt * att_ref[at[n], :], -1, keepdims=True) / total
        e0 = e0_ref[at[n], :]
        mix = dot(da, proj_ref[at[n], 2 * h : 3 * h].astype(BF16), NT) - delta
        ds_ref[at[n], :] = (e0 * mix).astype(BF16).astype(F32) * scale
        dvt_ref[:, at[n]] += dot(da, e0.astype(BF16), TN)
        if n == 0:
            dqp_ref[at[n], :] = jnp.zeros((span, h), F32)
            dm_ref[at[n], :] = jnp.zeros((h, h), F32)
            dkpt_ref[:, at[n]] = gkt_ref[:, at[n]] if not last else jnp.zeros((h, span), F32)
            continue
        keys = kts_ref[0, n, :, :w]
        qp = qp_ref[at[n], :]
        block = jnp.exp(dot(qp, keys) * scale)
        block = jnp.concatenate(
            [jnp.where(doc_ref[0, j] == doc_ref[0, n], block[:, j * span : (j + 1) * span], 0.0) for j in range(n)], 1
        )
        wide = jnp.concatenate([delta] * n, 1)
        mix = dot(da, proj_ref[:w, 2 * h : 3 * h].astype(BF16), NT) - wide
        ds = (block * mix).astype(BF16)
        dqp_ref[at[n], :] = dot(ds, keys, NT) * scale
        pulled = dot(qp, ds, TN) * scale
        dvt_ref[:, :w] += dot(da, block.astype(BF16), TN)
        if last:
            dm_ref[at[n], :] = jnp.zeros((h, h), F32)
            dkpt_ref[:, at[n]] = jnp.zeros((h, span), F32)
            gkt_ref[:, :w] = pulled
        else:
            dkpt_ref[:, at[n]] = gkt_ref[:, at[n]]
            gs = halves(gkt_ref[:, :w])
            dm_ref[at[n], :] = dot(gs[0], keys, NT) + dot(gs[1], keys, NT)
            gkt_ref[:, :w] = pulled + dot3(halves(m_ref[at[n], :]), gs, TN)

    @pl.when(slot == 0)
    def _():
        reduce().pair()

    for n in range(spans):
        q = proj_ref[at[n], 0:h]
        k = proj_ref[at[n], h : 2 * h]
        d = proj_ref[at[n], 3 * h : 4 * h]
        inv = lax.rsqrt(jnp.sum(d * d, -1, keepdims=True) + EPSILON)
        w = d * inv
        beta = 2.0 / (1.0 + jnp.exp(-logit_ref[at[n], :]))
        qs, ks, ws = halves(q), halves(k), halves(w)
        dqp, ds, dkpt = dqp_ref[at[n], :], ds_ref[at[n], :], dkpt_ref[:, at[n]]
        ys = halves(y_ref[at[n], :])
        left = both((halves(dqp), halves(ds)), 1)
        mid = both((halves(dm_ref[at[n], :]), halves(dkpt)), 1)
        da1 = jnp.where(lower, -dot3(left, ys, NT), 0.0)
        dy = dot3(halves(a1_ref[at[n], :]), left, TN) + dot3(ws, mid)
        dx = -dot3(halves(g_ref[at[n], :]), halves(dy), TN)
        dl = -dot3(halves(dx), ys, NT)
        dw = dx[:, :h] - dot3(ys, mid, NT)
        pull = jnp.sum(jnp.where(same, dl, 0.0), -1, keepdims=True)
        dlogit = -pull * (1.0 - 0.5 * beta) / jnp.maximum(beta, 1e-30)
        before = jnp.where(slot == 0, 0.0, dlogit_ref[at[n], :].astype(F32))
        dlogit_ref[at[n], :] = jnp.where(c == head_ref[slot], dlogit, before).astype(BF16)
        dz = jnp.concatenate(
            [
                jnp.concatenate([da1, ds], 1),
                jnp.concatenate([jnp.where(strict, dl, 0.0), jnp.where(strict, dx[:, h:], 0.0)], 1),
            ],
            0,
        )
        dzs = halves(dz)
        dp = dot3(dzs, both((ws, ks), 0))
        dr = dot3(dzs, both((qs, ws), 0), TN)
        dw = dw + dp[span:] + dr[:span]
        dproj_ref[at[n], 0:h] = (dqp + dp[:span]).astype(BF16)
        dproj_ref[at[n], h : 2 * h] = (dkpt.T + dr[span:]).astype(BF16)
        dproj_ref[at[n], 2 * h : 3 * h] = dvt_ref[:, at[n]].T.astype(BF16)
        dproj_ref[at[n], 3 * h : 4 * h] = (inv * (dw - w * jnp.sum(dw * w, -1, keepdims=True))).astype(BF16)

    @pl.when(slot == 0)
    def _():
        for i in range(1, groups - 2):
            down.step(i)

    @pl.when(slot == pl.num_programs(0) - 1)
    def _():
        last = reduce()
        block_ref[...] = (res_ref[...] + last.total()).astype(BF16)
        last.finish()
        line.total(rows_ref)
        line.finish([groups - 2])
        down.arrive(groups - 3, dup_ref, ddn_ref)
        down.finish(range(groups - 2))


def head_specs(rows, h, spans, slots):
    mode = {"pipeline_mode": pl.Buffered(1)} if slots == 1 else {}
    one = pl.BlockSpec((rows, h), lambda s: (0, s), **mode)
    two = pl.BlockSpec((rows, 2 * h), lambda s: (0, s), **mode)
    four = pl.BlockSpec((rows, 4 * h), lambda s: (0, s), **mode)
    keys = pl.BlockSpec((1, spans, h, rows), lambda s: (s, 0, 0, 0), **mode)
    docs = pl.BlockSpec(memory_space=pltpu.SMEM)
    return one, two, four, keys, docs


def attention_forward(docs, on, my_heads, x_all, w, ext, dy, ffn, groups, peers, heads, slots, span):
    rows, width = x_all.shape
    spans, h = rows // span, span
    one, two, four, keys, smem = head_specs(rows, h, spans, slots)
    dma = pltpu.SemaphoreType.DMA
    vmem, hbm = pl.BlockSpec(memory_space=pltpu.VMEM), pl.BlockSpec(memory_space=pl.ANY)
    ext_rows = ext.shape[2]

    def full(columns, dtype=F32):
        return jax.ShapeDtypeStruct((rows, slots * columns), dtype)

    return pl.pallas_call(
        functools.partial(attention_forward_kernel, groups, peers, heads, width // (groups * peers), spans, span),
        grid=(slots,),
        in_specs=[smem, smem, smem, hbm, pl.BlockSpec((width, 4 * h), lambda s: (0, s)), vmem, vmem, vmem],
        out_specs=[
            pl.BlockSpec((rows, width), lambda s: (0, 0)), hbm, pl.BlockSpec((ext_rows, width), lambda s: (0, 0)), hbm,
            four, one, one, one, one, one, one, two, one, one, one, keys,
        ],
        out_shape=[
            jax.ShapeDtypeStruct((rows, width), BF16), jax.ShapeDtypeStruct((peers, *dy.shape), BF16),
            jax.ShapeDtypeStruct((ext_rows, width), BF16), jax.ShapeDtypeStruct((groups, *ffn.shape), BF16),
            full(4 * h), full(h),
            full(h, BF16), full(h), full(h), full(h), full(h), full(2 * h), full(h), full(h, BF16), full(h),
            jax.ShapeDtypeStruct((slots, spans, h, rows), BF16),
        ],
        scratch_shapes=[
            pltpu.VMEM((h, rows), F32), pltpu.VMEM((h, rows), F32), pltpu.VMEM((rows, width), BF16),
            dma((2,)), dma((spans // 2,)), dma((2 * peers,)), dma((2 * peers,)), dma((2 * groups,)), dma((2 * groups,)),
        ],
        compiler_params=pltpu.CompilerParams(
            collective_id=5, has_side_effects=True, vmem_limit_bytes=63 * 1024 * 1024
        ),
        name="attention_forward",
    )(docs, on, my_heads, x_all, w, ext, dy, ffn)


def attention_backward(
    docs, on, heads, outp, res, gi, up, dn, gd, db_all, out2, proj, logits, saved, groups, peers, slots, span
):
    rows = proj.shape[0]
    spans, h = rows // span, span
    one, two, four, keys, smem = head_specs(rows, h, spans, slots)
    wide, tall = pltpu.VMEM((h, rows), F32), pltpu.VMEM((rows, h), F32)
    vmem = pl.BlockSpec(memory_space=pltpu.VMEM)
    block = pl.BlockSpec(gd.shape[1:], lambda s: (0, 0, 0))
    return pl.pallas_call(
        functools.partial(attention_backward_kernel, groups, peers, spans, span),
        grid=(slots,),
        in_specs=[smem, smem, smem, vmem, vmem, pl.BlockSpec(memory_space=pl.ANY)] + [vmem] * 4 + [pl.BlockSpec((h, db_all.shape[1]), lambda s: (s, 0))]
        + [four, one, one, one, one, one, two, one, one, one, keys],
        out_specs=[
            four, pl.BlockSpec((rows, h), lambda s: (0, 0)), pl.BlockSpec(res.shape, lambda s: (0, 0)),
            pl.BlockSpec(up.shape, lambda s: (0, 0, 0)), block, block,
        ],
        out_shape=[
            jax.ShapeDtypeStruct((rows, slots * 4 * h), BF16),
            jax.ShapeDtypeStruct((rows, h), BF16),
            jax.ShapeDtypeStruct(res.shape, BF16),
            jax.ShapeDtypeStruct(up.shape, BF16),
            jax.ShapeDtypeStruct(gd.shape[1:], BF16),
            jax.ShapeDtypeStruct(gd.shape[1:], BF16),
        ],
        scratch_shapes=[wide, wide, tall, tall, wide, tall, tall] + Reduce.scratch(peers, *res.shape)
        + [pltpu.VMEM((3, *up.shape), BF16), pltpu.SemaphoreType.DMA((3,))]
        + LineSum.scratch(groups, *up.shape, steps=1) + LineSum.scratch(groups, *gd.shape[1:], steps=groups - 2),
        compiler_params=pltpu.CompilerParams(
            collective_id=6, has_side_effects=True, vmem_limit_bytes=62 * 1024 * 1024
        ),
        name="attention_backward",
    )(docs, on, heads, outp, res, gi, up, dn, gd, db_all, out2, proj, logits, *saved)


def gather_kernel(
    groups, peers, own_cols, aligned, own_ref, mix_ref, ffn_ref, tok_ref, out_ref, ext_ref, down_ref,
    w_all, ffn_all, tok_all, out_all, ext_all, down_all, out_z,
    local, a_s, a_r, m_s, m_r, f_s, f_r, t_s, t_r, o_s, o_r, e_s, e_r, s_s, s_r,
    al_s, al_r, ml_s, ml_r, ol_s, ol_r, el_s, el_r, dl_s, dl_r,
):
    me, at = lax.axis_index("blk"), lax.axis_index("dp")
    core = me % 2
    sibling = me + 1 - 2 * core
    cols = w_all.shape[3]
    shared = cols > own_cols
    quarter = (cols - own_cols) // 2

    def side(device):
        return pl.ds(pl.multiple_of(own_cols + quarter * (device % 2), 128), quarter)

    own = [
        pltpu.make_async_copy(ext_ref, ext_all.at[at, me], local.at[0]),
        pltpu.make_async_copy(out_ref, out_z.at[at], local.at[1]),
        pltpu.make_async_copy(own_ref.at[me], w_all.at[at, me, :, pl.ds(0, own_cols)], local.at[2]),
        pltpu.make_async_copy(ffn_ref.at[me], ffn_all.at[me], local.at[3]),
        pltpu.make_async_copy(tok_ref, tok_all.at[me], local.at[4]),
    ]
    if shared:
        own.append(pltpu.make_async_copy(mix_ref.at[me], w_all.at[at, me, :, side(me)], local.at[5]))
    own_down = pltpu.make_async_copy(down_ref, down_all.at[at], local.at[6])
    for copy in own + [own_down]:
        copy.start()
    greet(peers, groups)
    moves = fanout(peers, lambda p: own_ref.at[p], lambda p: w_all.at[at, me, :, pl.ds(0, own_cols)], a_s, a_r)
    if shared:
        moves += fanout(peers, lambda p: mix_ref.at[p], lambda p: w_all.at[at, me, :, side(p)], m_s, m_r)
    exts = fanout(peers, lambda p: ext_ref, lambda p: ext_all.at[at, me], e_s, e_r)
    ffn = fanout(peers, lambda p: ffn_ref.at[p], lambda p: ffn_all.at[me], f_s, f_r)
    for copy in moves + exts:
        copy.start()
    out_line = Line(groups, lambda d: out_z.at[d], ol_s, ol_r)
    down_line = Line(groups, lambda d: down_all.at[d], dl_s, dl_r)
    own[1].wait()
    out_line.start(1)
    own_down.wait()
    down_line.start(1)
    tok = Spread(peers, lambda c: tok_ref, lambda b: tok_all.at[b], t_s, t_r, True)
    if aligned:
        out = Spread(peers, lambda c: out_z.at[c], lambda b: out_all.at[b], o_s, o_r)
    else:
        out = Spread(peers, lambda c: out_z, lambda b: out_all.at[:, b], o_s, o_r)
    lines = [Line(groups, lambda d: w_all.at[d, :, :, pl.ds(0, own_cols)], al_s, al_r)]
    if shared:
        mix_line = Line(groups, lambda d: w_all.at[d, :, :, side(me)], ml_s, ml_r)
    ext_line = Line(groups, lambda d: ext_all.at[d], el_s, el_r)

    def across(d):
        block = w_all.at[d, :, :, side(me)]
        return send(block, block, s_s.at[d], s_r.at[d], blk=sibling)

    out_line.arrive(1)
    if groups > 2:
        out_line.start(2)
    for copy in moves:
        copy.wait_recv()
    for copy in own[2:3] + own[5:]:
        copy.wait()
    lines[0].start(1)
    if shared:
        mix_line.start(1)
        across(at).start()
    tok.start()
    for copy in exts:
        copy.wait_recv()
    own[0].wait()
    ext_line.start(1)
    for copy in ffn:
        copy.start()
    for step in range(3, groups):
        out_line.arrive(step - 1)
        out_line.start(step)
    if groups > 2:
        out_line.arrive(groups - 1)
    out.start()
    if aligned:
        mine = pltpu.make_async_copy(out_z.at[me // 2], out_all.at[me], local.at[7])
    else:
        mine = pltpu.make_async_copy(out_z, out_all.at[:, me], local.at[7])
    mine.start()
    for step in range(2, groups):
        lines[0].arrive(step - 1)
        lines[0].start(step)
        if shared:
            mix_line.arrive(step - 1, across)
            mix_line.start(step)
        ext_line.arrive(step - 1)
        ext_line.start(step)
        if step == 2:
            tok.forward()
    out.forward()
    lines[0].arrive(groups - 1)
    if shared:
        mix_line.arrive(groups - 1, across)
    ext_line.arrive(groups - 1)
    down_line.arrive(1)
    down_line.finish([1])
    for copy in ffn:
        copy.wait_recv()
    for copy in moves + exts + ffn:
        copy.wait_send()
    for spread in (tok, out):
        spread.finish()
    lines[0].finish(range(1, groups))
    if shared:
        mix_line.finish(range(1, groups))
        for d in range(groups):
            across(d).wait()
    ext_line.finish(range(1, groups))
    out_line.finish(range(1, groups))
    mine.wait()
    for i in (3, 4):
        own[i].wait()


def gather_all(groups, peers, aligned, own, mix, ffn, tok, out, ext, down):
    def shape(*dims):
        return jax.ShapeDtypeStruct(dims, BF16)

    dma = pltpu.SemaphoreType.DMA
    vmem, hbm = pl.BlockSpec(memory_space=pltpu.VMEM), pl.BlockSpec(memory_space=pl.ANY)
    share, own_cols = own.shape[1:]
    cols = own_cols if mix is None else own_cols + 2 * mix.shape[2]
    inputs = [own, own if mix is None else mix, ffn, tok, out, ext, down]
    return pl.pallas_call(
        functools.partial(gather_kernel, groups, peers, own_cols, aligned),
        in_specs=[vmem] * 7,
        out_specs=[hbm] * 6,
        out_shape=[
            shape(groups, peers, share, cols), shape(*ffn.shape), shape(peers, *tok.shape),
            shape(peers, *out.shape) if aligned else shape(groups, peers, *out.shape),
            shape(groups, peers, *ext.shape), shape(groups, *down.shape),
        ],
        scratch_shapes=[pltpu.VMEM((groups, *out.shape), BF16), dma((8,))] + [dma((2 * peers,))] * 12 + [dma((groups,))] * 2 + [dma((2 * groups,))] * 10,
        compiler_params=pltpu.CompilerParams(
            collective_id=1, has_side_effects=True, vmem_limit_bytes=63 * 1024 * 1024
        ),
        name="gather_all",
    )(*inputs)


def branch_kernel(
    groups, peers, heads, att_ref, out_ref, tok_ref, ext_ref, down_in, ffn_ref, res_ref, n2_all, down_all, far_all,
    part, low, local, half, mine, got, r_s, r_r, n_s, n_r, dl_s, dl_r, h_s, h_r,
):
    me, at = lax.axis_index("blk"), lax.axis_index("dp")
    rows, width = tok_ref.shape
    greet(peers, groups)
    down_line = Line(groups, lambda d: down_all.at[d], dl_s, dl_r)

    def hop(i, block, to):
        return send(ffn_ref.at[block], far_all, h_s.at[i], h_r.at[i], dp=to)

    @pl.when(at == groups - 2)
    def _():
        hop(0, 0, at + 1).start()

    @pl.when(at == 1)
    def _():
        hop(1, groups - 1, at - 1).start()

    down_line.start(2)
    reduce = Reduce(peers, part, half, mine, got, r_s, r_r, halved=True)

    def fill(b):
        block = att_ref[pl.ds(pl.multiple_of(b * rows, rows), rows), :]
        part[b] = dot(block, out_ref[...]).astype(BF16)

    for k in reduce.order():
        fill(2 * reduce.to[k] + 1 - me % 2)
        reduce.inner[k].start()
    for k in reduce.order():
        fill(2 * reduce.to[k] + me % 2)
    reduce.pair()
    res_ref[...] = tok_ref[...].astype(F32) + reduce.total()
    low[...] = rms_norm(res_ref[...], ext_ref[...].astype(F32)[heads + 1 : heads + 2]).astype(BF16)
    keep = pltpu.make_async_copy(low, n2_all.at[me], local.at[1])
    keep.start()
    spread = Spread(peers, lambda c: low, lambda b: n2_all.at[b], n_s, n_r, True)
    spread.start()
    for step in range(3, groups):
        down_line.arrive(step - 1)
        down_line.start(step)
    spread.forward()
    down_line.arrive(groups - 1)
    spread.finish()
    reduce.finish()
    down_line.finish(range(2, groups))
    keep.wait()

    @pl.when(at == groups - 1)
    def _():
        hop(0, 0, at - 1).wait_recv()

    @pl.when(at == 0)
    def _():
        hop(1, groups - 1, at + 1).wait_recv()

    @pl.when(at == groups - 2)
    def _():
        hop(0, 0, at + 1).wait_send()

    @pl.when(at == 1)
    def _():
        hop(1, groups - 1, at - 1).wait_send()


def branch(groups, peers, heads, att, out, tok, ext, down, ffn):
    rows, width = tok.shape
    dma = pltpu.SemaphoreType.DMA
    vmem, hbm = pl.BlockSpec(memory_space=pltpu.VMEM), pl.BlockSpec(memory_space=pl.ANY)
    return pl.pallas_call(
        functools.partial(branch_kernel, groups, peers, heads),
        in_specs=[vmem] * 4 + [hbm, hbm],
        out_specs=[vmem, hbm, hbm, hbm],
        input_output_aliases={4: 2},
        out_shape=[
            jax.ShapeDtypeStruct((rows, width), F32),
            jax.ShapeDtypeStruct((peers, rows, width), BF16),
            jax.ShapeDtypeStruct(down.shape, BF16),
            jax.ShapeDtypeStruct(ffn.shape[1:], BF16),
        ],
        scratch_shapes=[pltpu.VMEM((peers, rows, width), BF16), pltpu.VMEM((rows, width), BF16), dma((2,))]
        + Reduce.scratch(peers, rows, width)
        + [dma((2 * peers,)), dma((2 * peers,)), dma((2 * groups,)), dma((2 * groups,)), dma((2,)), dma((2,))],
        compiler_params=pltpu.CompilerParams(
            collective_id=2, has_side_effects=True, vmem_limit_bytes=63 * 1024 * 1024
        ),
        name="branch_and_norm",
    )(att, out, tok, ext, down, ffn)


def slab_order(groups, slab):
    if slab % 128:
        return list(range(groups))
    upper = lax.axis_index("dp") >= groups // 2
    return [jnp.where(upper, i, groups - 1 - i) for i in range(groups)]


def slab_of(ref, d, slab):
    if slab % 128:
        return ref[:, d * slab : (d + 1) * slab]
    return ref[:, pl.ds(pl.multiple_of(d * slab, 128), slab)]


def feed_forward_kernel(
    groups, peers, heads, n2_ref, ffn_all, far_all, down_ref, dy_ref, res_ref, ext_ref,
    dres_ref, db_all, outp_all, gd_all, gi_all, up_ref, dn_ref,
    w_ref, w_sem, part, hidden, pulled, low, outp_ref, gd_ref, gi_ref, local, half, mine, got, r_s, r_r, n_s, n_r, ug, dg, uo, do, l_s, l_r,
):
    me = lax.axis_index("blk")
    rows, width = res_ref.shape
    cols = w_ref.shape[1]
    units = cols // 2
    share = gi_ref.shape[2]
    slab = peers * share
    at_dp = lax.axis_index("dp")
    loads = []
    for d in range(groups):
        gap = at_dp - d
        remote = (gap == groups - 1) | (gap == 1 - groups)
        into = w_ref.at[pl.ds(d * slab, slab)]
        loads.append(pltpu.make_async_copy(ffn_all.at[d], into, w_sem.at[d]))
        pl.when(remote)(pltpu.make_async_copy(far_all, into, w_sem.at[d]).start)
        pl.when(jnp.logical_not(remote))(loads[d].start)
    greet(peers, groups)
    for copy in loads:
        copy.wait()
    reduce = Reduce(peers, part, half, mine, got, r_s, r_r, halved=True)

    def block(ref, b, count=1):
        return ref.at[pl.ds(pl.multiple_of(b * rows, rows), count * rows)]

    for k in reduce.order():
        chip = reduce.to[k]
        normed = block(n2_ref, 2 * chip, 2)[...]
        gate_up = dot(normed, w_ref[...])
        gate, up = gate_up[:, :units], gate_up[:, units:]
        sig = 1.0 / (1.0 + jnp.exp(-gate))
        silu = gate * sig
        block(hidden, 2 * chip, 2)[...] = (silu * up).astype(BF16)
        dhidden = dot(block(dy_ref, 2 * chip, 2)[...], down_ref[...], NT)
        dgate = dhidden * up * (sig + silu * (1.0 - sig))
        both_pulled = jnp.concatenate([dgate, dhidden * silu], 1).astype(BF16)
        block(pulled, 2 * chip, 2)[...] = both_pulled
        pull = dot(both_pulled, w_ref[...], NT).astype(BF16)
        part[2 * chip] = pull[:rows]
        part[2 * chip + 1] = pull[rows:]
        reduce.inner[k].start()
    line = LineSum(groups, lambda r: gi_ref.at[line.at + r], ug, dg, uo, do, l_s, l_r)

    def chunk(d):
        gi_ref[d] = dot(slab_of(n2_ref, d, slab), pulled[...], TN).astype(BF16).reshape(peers, share, cols)

    order = slab_order(groups, slab)
    early = 1 if slab % 128 == 0 else groups
    for d in order[:early]:
        chunk(d)
    line.step(0)
    reduce.pair()
    for d in order[early:]:
        chunk(d)
    out_copies = [pltpu.make_async_copy(gi_ref, gi_all, local.at[1])]
    out_copies[0].start()
    dres_ref[...] = block(dy_ref, me)[...].astype(F32) + rms_pull(
        res_ref[...], ext_ref[...].astype(F32)[heads + 1 : heads + 2], reduce.total()
    )
    low[...] = dres_ref[...].astype(BF16)
    keep = pltpu.make_async_copy(low, db_all.at[me], local.at[0])
    keep.start()
    spread = Spread(peers, lambda c: low, lambda b: db_all.at[b], n_s, n_r, True)
    spread.start()
    gd_ref[...] = dot(hidden[...], dy_ref[...], TN).astype(BF16).reshape(gd_ref.shape)
    out_copies.append(pltpu.make_async_copy(gd_ref, gd_all, local.at[2]))
    out_copies[1].start()
    steps = range(max(groups - 2, 1))
    for i in steps[1:]:
        line.step(i)
    spread.forward()

    def out(i, carry):
        at = pl.ds(pl.multiple_of(i * 2 * rows, rows), 2 * rows)
        value = dot(hidden[at, :], down_ref[...]).astype(BF16)
        outp_ref[2 * i] = value[:rows]
        outp_ref[2 * i + 1] = value[rows:]
        return carry

    lax.fori_loop(0, peers // 2, out, 0)
    out_copies.append(pltpu.make_async_copy(outp_ref, outp_all, local.at[3]))
    out_copies[2].start()
    spread.finish()
    reduce.finish()
    line.arrive(steps[-1], up_ref, dn_ref)
    line.finish(steps)
    for copy in [keep] + out_copies:
        copy.wait()


def feed_forward(groups, peers, heads, n2_all, ffn, far, down, dy_all, res, ext):
    rows, width = res.shape
    tokens, cols = n2_all.shape[0], ffn.shape[2]
    share = width // (groups * peers)
    units = cols // (2 * groups)
    tall = 16 if units % 16 == 0 else units
    down_shape = (groups, units // tall, tall, width)
    dma = pltpu.SemaphoreType.DMA
    vmem, hbm = pl.BlockSpec(memory_space=pltpu.VMEM), pl.BlockSpec(memory_space=pl.ANY)

    def shape(*dims, dtype=BF16):
        return jax.ShapeDtypeStruct(dims, dtype)

    return pl.pallas_call(
        functools.partial(feed_forward_kernel, groups, peers, heads),
        in_specs=[vmem, hbm, hbm, vmem, vmem, vmem, vmem],
        out_specs=[vmem, hbm, hbm, hbm, hbm, vmem, vmem],
        out_shape=[
            shape(rows, width, dtype=F32), shape(peers, rows, width), shape(peers, rows, width),
            shape(*down_shape), shape(groups, peers, share, cols),
            shape(peers, share, cols), shape(peers, share, cols),
        ],
        scratch_shapes=[
            pltpu.VMEM((width, cols), BF16), dma((groups,)),
            pltpu.VMEM((peers, rows, width), BF16), pltpu.VMEM((tokens, cols // 2), BF16),
            pltpu.VMEM((tokens, cols), BF16), pltpu.VMEM((rows, width), BF16),
            pltpu.VMEM((peers, rows, width), BF16), pltpu.VMEM(down_shape, BF16),
            pltpu.VMEM((groups, peers, share, cols), BF16), dma((4,)),
        ]
        + Reduce.scratch(peers, rows, width)
        + [dma((2 * peers,)), dma((2 * peers,))]
        + LineSum.scratch(groups, peers, share, cols, steps=groups - 2),
        compiler_params=pltpu.CompilerParams(
            collective_id=3, has_side_effects=True, vmem_limit_bytes=62 * 1024 * 1024
        ),
        name="feed_forward",
    )(n2_all, ffn, far, down, dy_all, res, ext)


def final_kernel(
    groups, peers, heads, own, shared, aligned,
    norm_ref, dproj_ref, dlogit_ref, w_ref, ext_ref, att_ref, db_ref, ffn_ref, tok_ref, dres_ref,
    gd_ref, dup_ref, ddn_ref, wa_ref, wb_ref, wf_ref, ga_ref, gf_ref,
    dtok_ref, grad_ref, beta_fin, gout_fin, ffn_out, down_fin, gain_out, gain_ffn_out,
    g_ref, beta_ref, part, half, mine, got, r_s, r_r,
    oug, odg, ouo, odo, ol_s, ol_r, own_fin, own_rows, w_s, w_r, ffn_rows, f_s, f_r,
    beta_got, beta_sum, b_s, b_r, bug, bdg, buo, bdo, bl_s, bl_r,
    vg, wg, vo, wo, m_s, m_r,
    *extra,
):
    me, at = lax.axis_index("blk"), lax.axis_index("dp")
    core, chip = me % 2, me // 2
    sibling = me + 1 - 2 * core
    rows, width = tok_ref.shape
    h = width // heads
    share = g_ref.shape[2]
    slab = peers * share
    own_cols, quarter = own * 4 * h, shared * 2 * h
    cols = own_cols + 2 * quarter
    extra = list(extra)
    if shared:
        mix_half, mix_sum, mug, mdg, muo, mdo, ml_s, ml_r, mix_fin, mix_rows, x_s, x_r, mw_s, mw_r = extra[:14]
        extra = extra[14:]
    if aligned:
        go_part, go_half, go_mine, go_all, g_s, g_r, gug, gdg, guo, gdo, gl_s, gl_r = extra
    greet(peers, groups)
    down = LineSum(groups, lambda r: gd_ref.at[at + r], vg, wg, vo, wo, m_s, m_r, (dup_ref, ddn_ref), groups - 2)
    own_line = LineSum(groups, lambda r: g_ref.at[at + r, :, :, pl.ds(0, own_cols)], oug, odg, ouo, odo, ol_s, ol_r)
    if shared:
        theirs = pl.ds(pl.multiple_of(own_cols + quarter * (1 - core), 128), quarter)
        ours = pl.ds(pl.multiple_of(own_cols + quarter * core, 128), quarter)
        mix = LineSum(groups, lambda r: mix_sum.at[at + r], mug, mdg, muo, mdo, ml_s, ml_r)

        def swap(d):
            return send(g_ref.at[d, :, :, theirs], mix_half.at[d], x_s.at[d], x_r.at[d], blk=sibling)

    order = slab_order(groups, slab)
    for i, d in enumerate(order):
        normed = slab_of(norm_ref, d, slab)
        g_ref[d] = dot(normed, dproj_ref[...], TN).astype(BF16).reshape(peers, share, cols)
        if i == (0 if slab % 128 == 0 else groups - 1):
            own_line.step(0)
        if shared:
            swap(d).start()
        beta_ref[d] = dot(normed, dlogit_ref[...], TN).astype(BF16).reshape(peers, share, 128)
    betas = fanout(peers, lambda p: beta_ref.at[:, p], lambda p: beta_got.at[me], b_s, b_r)
    ffn = fanout(peers, lambda p: ffn_ref.at[p], lambda p: ffn_rows.at[me], f_s, f_r)
    if shared:
        for i, d in enumerate(order):
            swap(d).wait_recv()

            def body(j, carry):
                mix_sum[d, j] = (g_ref[d, j, :, ours].astype(F32) + mix_half[d, j].astype(F32)).astype(BF16)
                return carry

            lax.fori_loop(0, peers, body, 0)
            if i == 0:
                mix.step(0)
    reduce = Reduce(peers, part, half, mine, got, r_s, r_r, halved=True)
    small = ext_ref[...].astype(F32)
    gain_row = small[heads : heads + 1]
    row = lax.broadcasted_iota(jnp.int32, small.shape, 0)
    small = jnp.where(row < heads, small, 0.0).astype(BF16)
    small = jnp.concatenate([small, jnp.zeros((128 - small.shape[0], width), BF16)], 0)

    def pull(k):
        to = 2 * reduce.to[k]
        two = pl.ds(pl.multiple_of(to * rows, rows), 2 * rows)
        value = (dot(dproj_ref[two, :], w_ref[...], NT) + dot(dlogit_ref[two, :], small)).astype(BF16)
        part[to] = value[:rows]
        part[to + 1] = value[rows:]
        reduce.inner[k].start()

    pulls = reduce.order()
    pull(pulls[0])
    own_line.step(1)
    for k in pulls[1:]:
        pull(k)
    if shared:
        mix.step(1)
    reduce.chip_sums()
    for copy in betas:
        copy.start()
    if aligned:
        att = att_ref[...]
        mine_att, zero = att[:, : own * h], jnp.zeros((att.shape[0], own * h), BF16)
        wide = jnp.concatenate(
            [jnp.where(core == 0, mine_att, zero), att[:, own * h :], jnp.where(core == 1, mine_att, zero)], 1
        )
        tile = width // 3
        for j in range(0, width, tile):
            value = dot(wide, db_ref[:, j : j + tile], TN).astype(BF16)
            go_part[:, :, j : j + tile] = value.reshape(peers, share, tile)
        gout = Reduce(peers, go_part, go_half, go_mine, go_all, g_s, g_r, go_all.at[chip, 0])
        gout.start()
    reduce.cross_sums()
    sums = [own_line] + ([mix] if shared else [])
    for i in range(2, groups - 1):
        for item in sums:
            item.step(i)
    if aligned:
        gout.pair()
        go_all[chip, 0] = go_mine[0]
    for copy in ffn:
        copy.start()
    ffn_rows[me] = ffn_ref[me]
    beta_got[me] = beta_ref[:, me]
    for copy in betas:
        copy.wait_recv()
    summed = beta_got[0].astype(F32)
    for b in range(1, peers):
        summed = summed + beta_got[b].astype(F32)
    beta_sum[:, 0] = summed.astype(BF16)
    late = [LineSum(groups, lambda r: beta_sum.at[at + r], bug, bdg, buo, bdo, bl_s, bl_r)]
    if aligned:
        for copy in gout.outer:
            copy.wait_recv()
        late.append(LineSum(groups, lambda r: go_all.at[at + r], gug, gdg, guo, gdo, gl_s, gl_r))
    for item in late:
        item.step(0)
    own_line.total(own_fin)
    moves = fanout(peers, lambda p: own_fin.at[p], lambda p: own_rows.at[me], w_s, w_r)
    for copy in moves:
        copy.start()
    down.step(groups - 2)
    own_rows[me] = own_fin[me]
    if shared:
        mix.total(mix_fin)
        mix_moves = fanout(peers, lambda p: mix_fin.at[p], lambda p: mix_rows.at[me], mw_s, mw_r)
        for copy in mix_moves:
            copy.start()
        mix_rows[me] = mix_fin[me]
        moves += mix_moves
    for item in late:
        item.step(1)
    dtok_ref[...] = dres_ref[...] + rms_pull(tok_ref[...].astype(F32), gain_row, reduce.total())

    def row_sums(wide):
        high = wide.astype(BF16)
        low = (wide - high.astype(F32)).astype(BF16)
        ones = jnp.ones((8, wide.shape[1]), BF16)
        return (dot(ones, high, NT) + dot(ones, low, NT))[:1]

    for copy in ffn:
        copy.wait_recv()
    units = wf_ref.shape[1] // (2 * groups * peers)
    total = jnp.zeros((share, units), F32)
    for b in range(peers):
        for side in range(2):
            for d in range(groups):
                src = (side * groups + d) * units
                to = ((side * groups + d) * peers + b) * units
                value = ffn_rows[b, :, src : src + units].astype(F32)
                ffn_out[:, to : to + units] = value
                total = total + value * wf_ref[:, to : to + units].astype(F32)
    gain_ffn_out[...] = row_sums(total) / gf_ref[...].astype(F32)
    for i in range(2, groups - 1):
        for item in late:
            item.step(i)
    down.total(down_fin)
    late[0].total(beta_fin)
    for copy in moves:
        copy.wait_recv()
    gain = beta_fin[0] * wb_ref[...].astype(F32)
    hc = 2 * own + shared

    def put(acc, value, head, side):
        to = side * width + head * h
        value = value.astype(F32)
        grad_ref[:, to : to + h] = value
        return acc + value * wa_ref[:, to : to + h].astype(F32)

    for b in range(peers):
        for s in range(own):
            head = (b // 2) * hc + (b % 2) * (own + shared) + s
            if head < heads:
                for side in range(4):
                    gain = put(gain, own_rows[b, :, (4 * s + side) * h : (4 * s + side + 1) * h], head, side)
        if shared:
            for i in range(2):
                gain = put(gain, mix_rows[b, :, i * h : (i + 1) * h], (b // 2) * hc + own, 2 * (b % 2) + i)
    gain_out[...] = row_sums(gain) / ga_ref[...].astype(F32)
    if aligned:
        late[1].total(gout_fin)
    reduce.finish()
    for copy in betas + ffn + moves:
        copy.wait_send()
    if shared:
        for d in range(groups):
            swap(d).wait_send()
    if aligned:
        gout.finish()
    for item in sums + late:
        item.finish()
    down.finish([groups - 2])


def final_sums(groups, peers, heads, own, shared, aligned, *args):
    normed, dproj, dlogits, w, ext, att, db, ffn, tok = args[:9]
    gd, wa, wf = args[10], args[13], args[15]
    rows, width = tok.shape
    h, share = width // heads, wa.shape[0]
    own_cols, quarter, cols = own * 4 * h, shared * 2 * h, w.shape[1]
    dma = pltpu.SemaphoreType.DMA
    vmem = pl.BlockSpec(memory_space=pltpu.VMEM)

    def block(*dims):
        return pltpu.VMEM(dims, BF16)

    def shape(*dims, dtype=F32):
        return jax.ShapeDtypeStruct(dims, dtype)

    pair = [dma((peers,))] * 2
    scratch = [block(groups, peers, share, cols), block(groups, peers, share, 128), block(peers, rows, width)]
    scratch += Reduce.scratch(peers, rows, width)
    scratch += LineSum.scratch(groups, peers, share, own_cols) + [block(peers, share, own_cols)] * 2 + pair
    scratch += [block(*ffn.shape)] + pair
    scratch += [block(peers, groups, share, 128), block(groups, 1, share, 128)] + pair
    scratch += LineSum.scratch(groups, 1, share, 128) + LineSum.scratch(groups, *gd.shape[1:], steps=1)
    if shared:
        scratch += [block(groups, peers, share, quarter)] * 2 + LineSum.scratch(groups, peers, share, quarter)
        scratch += [block(peers, share, quarter)] * 2 + [dma((groups,)), dma((groups,))] + pair
    if aligned:
        half = block(peers // 2, share, width)
        scratch += [block(peers, share, width), half, half, block(groups, 1, share, width)] + pair
        scratch += LineSum.scratch(groups, 1, share, width)
    return pl.pallas_call(
        functools.partial(final_kernel, groups, peers, heads, own, shared, aligned),
        in_specs=[vmem] * len(args),
        out_specs=[vmem] * 8,
        out_shape=[
            shape(rows, width), shape(*wa.shape), shape(1, share, 128), shape(1, share, width), shape(*wf.shape),
            shape(*gd.shape[1:]), shape(1, share), shape(1, share),
        ],
        scratch_shapes=scratch,
        compiler_params=pltpu.CompilerParams(
            collective_id=4, has_side_effects=True, vmem_limit_bytes=63 * 1024 * 1024
        ),
        name="final_sums",
    )(*args)


def hand_over_kernel(*refs):
    count = (len(refs) - 2) // 3
    given, out, held, sems = refs[:count], refs[count : 2 * count], refs[2 * count : 3 * count], refs[3 * count :]
    loads = [pltpu.make_async_copy(given[i], held[i], sems[0].at[i]) for i in range(count)]
    stores = [pltpu.make_async_copy(held[i], out[i], sems[1].at[i]) for i in range(count)]
    for load in loads:
        load.start()
    for load, store in zip(loads, stores):
        load.wait()
        store.start()
    for store in stores:
        store.wait()


def hand_over(*results):
    dma = pltpu.SemaphoreType.DMA((len(results),))
    hbm = pl.BlockSpec(memory_space=pl.ANY)
    return pl.pallas_call(
        hand_over_kernel,
        in_specs=[hbm] * len(results),
        out_specs=[hbm] * len(results),
        out_shape=[jax.ShapeDtypeStruct(x.shape, x.dtype) for x in results],
        scratch_shapes=[pltpu.VMEM(x.shape, x.dtype) for x in results] + [dma, dma],
        compiler_params=pltpu.CompilerParams(vmem_limit_bytes=63 * 1024 * 1024),
        name="hand_over",
    )(*results)


def shards(
    tokens, cotangent, doc_table, gain_attn, attn_in, beta_proj, attn_out, gain_ffn, ffn_in, ffn_down
):
    rows, width = tokens.shape
    heads = beta_proj.shape[1]
    h = width // heads
    groups, peers = lax.axis_size("dp"), lax.axis_size("blk")
    chips = peers // 2
    hc = -(-heads // chips)
    own, shared = hc // 2, hc % 2
    slots, padded = own + shared, hc * chips
    own_cols, quarter = own * 4 * h, shared * 2 * h
    share, units = attn_in.shape[0], ffn_down.shape[0]
    aligned = chips == groups and padded == heads
    me = lax.axis_index("blk")
    chip, core = me // 2, me % 2
    by_chip = attn_in.reshape(share, 4, heads, h).transpose(2, 0, 1, 3)
    by_chip = jnp.pad(by_chip, ((0, padded - heads), (0, 0), (0, 0), (0, 0))).reshape(chips, hc, share, 4, h)
    own_parts = jnp.stack([by_chip[:, :own], by_chip[:, own + shared :]], 1)
    own_parts = own_parts.transpose(0, 1, 3, 2, 4, 5).reshape(peers, share, own_cols)
    mix_parts = None
    if shared:
        mix_parts = by_chip[:, own].reshape(chips, share, 2, 2 * h).transpose(0, 2, 1, 3).reshape(peers, share, 2 * h)
    ffn_parts = ffn_in.reshape(share, 2, groups, peers, units).transpose(3, 0, 1, 2, 4).reshape(peers, share, -1)
    ext = jnp.concatenate([beta_proj.T, gain_attn[None], gain_ffn[None]], 0)
    ext_rows = -(-(heads + 2) // 16) * 16
    ext = jnp.pad(ext, ((0, ext_rows - heads - 2), (0, 128 - share)))
    w2, ffn_part, x_all, out_all, ext_all, down_part = gather_all(
        groups, peers, aligned, own_parts, mix_parts, ffn_parts, tokens, attn_out, ext, ffn_down
    )
    w2 = w2.reshape(width, -1)
    x_all = x_all.reshape(peers * rows, width)
    out_rows = out_all.reshape(-1, width)
    if not aligned:
        out_rows = jnp.pad(out_rows, ((0, (padded - heads) * h), (0, 0)))
        out_rows = lax.dynamic_slice_in_dim(out_rows, chip * hc * h, hc * h, 0)
    out2 = lax.dynamic_slice_in_dim(out_rows, core * (own + shared) * h, own * h, 0)
    if shared:
        out2 = jnp.concatenate([out2, out_rows[own * h : (own + 1) * h]], 0)

    first = chip * hc + core * (own + shared)
    my_heads = jnp.stack([first + s for s in range(own)] + [chip * hc + own] * shared).astype(jnp.int32)
    on = jnp.stack([jnp.int32(1)] * own + [1 - core] * shared).astype(jnp.int32)
    normed, dy_all, ext_all, ffn_all, proj, logits, attended, *saved = attention_forward(
        doc_table, on, my_heads, x_all, w2, ext_all, cotangent, ffn_part,
        groups, peers, heads, slots, rows,
    )
    dy_all = dy_all.reshape(peers * rows, width)
    residual, normed_two_all, down_all, ffn_far = branch(
        groups, peers, heads, attended, out2, tokens, ext_all, down_part, ffn_all
    )
    normed_two_all = normed_two_all.reshape(peers * rows, width)
    down_slab = down_all.reshape(-1, width)

    dresidual, dbranch_all, out_part, grad_down, grad_ffn, up, down = feed_forward(
        groups, peers, heads, normed_two_all, ffn_all.reshape(groups, peers * share, -1), ffn_far.reshape(peers * share, -1),
        down_slab, dy_all, residual, ext_all,
    )
    dbranch_all = dbranch_all.reshape(peers * rows, width)
    dproj, dlogits, block_out, grad_ffn, down_up, down_dn = attention_backward(
        doc_table, on, my_heads, out_part, residual, grad_ffn, up, down, grad_down, dbranch_all, out2,
        proj, logits, saved, groups, peers, slots, rows,
    )
    grad_tokens, grad_attn_in, grad_beta, grad_attn_out, grad_ffn_in, grad_down, grad_gain_attn, grad_gain_ffn = final_sums(
        groups, peers, heads, own, shared, aligned,
        normed, dproj, dlogits, w2, ext_all, attended, dbranch_all, grad_ffn, tokens, dresidual, grad_down, down_up, down_dn,
        attn_in, jnp.pad(beta_proj, ((0, 0), (0, 128 - heads))), ffn_in,
        gain_attn[None], gain_ffn[None],
    )
    if aligned:
        grad_attn_out = grad_attn_out[0]
    else:
        gout = dot(attended, dbranch_all, TN)
        first = chip * hc + core * (own + shared)
        whole = jnp.zeros((padded * h, width), F32)
        whole = lax.dynamic_update_slice_in_dim(whole, gout, first * h, 0)[: heads * h]
        grad_attn_out = lax.psum_scatter(whole, ("dp", "blk"), scatter_dimension=0, tiled=True)
    block_out, grad_tokens, grad_gain_attn, grad_attn_in, grad_beta, grad_attn_out, grad_gain_ffn, grad_ffn_in, grad_down = hand_over(
        block_out, grad_tokens, grad_gain_attn, grad_attn_in, grad_beta[0], grad_attn_out,
        grad_gain_ffn, grad_ffn_in, grad_down.reshape(units, width),
    )
    return (
        block_out, grad_tokens, grad_gain_attn[0], grad_attn_in, grad_beta[:, :heads], grad_attn_out,
        grad_gain_ffn[0], grad_ffn_in, grad_down,
    )


def solution(mesh):
    split, vector = P(("dp", "blk"), None), P(("dp", "blk"))
    in_specs = (split, split, P("dp", None), vector, split, split, split, vector, split, split)
    out_specs = (split, split, vector, split, split, split, vector, split, split)
    return jax.shard_map(shards, mesh=mesh, in_specs=in_specs, out_specs=out_specs, check_vma=False)
```

```python
import functools

import jax
import jax.numpy as jnp
from jax import lax
from jax.experimental import pallas as pl
from jax.experimental.pallas import tpu as pltpu
from jax.sharding import PartitionSpec as P

EPSILON = 1e-06
F32 = jnp.float32
BF16 = jnp.bfloat16

NN = (((1,), (0,)), ((), ()))
NT = (((1,), (1,)), ((), ()))
TN = (((0,), (0,)), ((), ()))


def dot(a, b, dims=NN):
    return lax.dot_general(a, b, dims, preferred_element_type=F32)


def halves(x):
    high = x.astype(BF16)
    return high, (x - high.astype(F32)).astype(BF16)


def dot3(a, b, dims=NN):
    (ah, al), (bh, bl) = a, b
    ka, kb = dims[0][0][0], dims[0][1][0]
    deep, wide = ah.shape[ka], bh.shape[1 - kb]
    if deep <= 128:
        left = jnp.concatenate([ah, al], ka)
        if wide <= 128:
            below = jnp.concatenate([bh, jnp.zeros_like(bh)], 1 - kb)
            both_parts = dot(left, jnp.concatenate([jnp.concatenate([bh, bl], 1 - kb), below], kb), dims)
            return both_parts[:, :wide] + both_parts[:, wide:]
        return dot(left, jnp.concatenate([bh, bh], kb), dims) + dot(ah, bl, dims)
    if wide <= 128:
        both_parts = dot(ah, jnp.concatenate([bh, bl], 1 - kb), dims)
        return both_parts[:, :wide] + (both_parts[:, wide:] + dot(al, bh, dims))
    return dot(ah, bh, dims) + (dot(ah, bl, dims) + dot(al, bh, dims))


def both(parts, axis):
    return tuple(jnp.concatenate(p, axis) for p in zip(*parts))


def rms_norm(values, gain):
    return values * lax.rsqrt(jnp.mean(values * values, axis=-1, keepdims=True) + EPSILON) * gain


def rms_pull(values, gain, grad):
    scale = lax.rsqrt(jnp.mean(values * values, axis=-1, keepdims=True) + EPSILON)
    inner = grad * gain
    along = jnp.mean(inner * values, axis=-1, keepdims=True)
    return scale * inner - values * (scale * scale * scale) * along


def lanes(n):
    return lax.broadcasted_iota(jnp.int32, (n, n), 1)


def rows_of(n):
    return lax.broadcasted_iota(jnp.int32, (n, n), 0)


def inverses(grams, betas, span):
    r, c = rows_of(span), lanes(span)
    eye = r == c
    outs = []
    pair = (c + 1 == r) & (r % 2 == 1)
    for gram, beta in zip(grams, betas):
        below = jnp.where(pair, gram, 0.0) * beta * beta.T
        outs.append(jnp.where(eye, beta, 0.0) - below)
    size = 2
    while size < span:
        part = (r // (2 * size) == c // (2 * size)) & ((r // size) % 2 == 1) & ((c // size) % 2 == 0)
        sides = [halves(x) for x in outs]
        steps = [dot3(halves(jnp.where(part, g, 0.0)), x) for g, x in zip(grams, sides)]
        outs = [x - dot3(s, halves(t)) for x, s, t in zip(outs, sides, steps)]
        size *= 2
    return outs


MESH = pl.DeviceIdType.MESH


def fetch(pairs, sems):
    copies = [pltpu.make_async_copy(src, dst, sems.at[i]) for i, (src, dst) in enumerate(pairs)]
    for copy in copies:
        copy.start()
    return copies


def send(src, dst, send_sem, recv_sem, **device):
    return pltpu.make_async_remote_copy(
        src_ref=src, dst_ref=dst, send_sem=send_sem, recv_sem=recv_sem, device_id=device, device_id_type=MESH
    )


def greet(peers, groups=0):
    barrier = pltpu.get_barrier_semaphore()
    me = lax.axis_index("blk")
    for k in range(1, peers):
        pl.semaphore_signal(barrier, inc=1, device_id={"blk": (me + k) % peers}, device_id_type=MESH)
    if groups:
        at = lax.axis_index("dp")

        @pl.when(at + 1 < groups)
        def _():
            pl.semaphore_signal(barrier, inc=1, device_id={"dp": at + 1}, device_id_type=MESH)

        @pl.when(at > 0)
        def _():
            pl.semaphore_signal(barrier, inc=1, device_id={"dp": at - 1}, device_id_type=MESH)

        @pl.when((at > 0) & (at + 1 < groups))
        def _():
            pl.semaphore_wait(barrier, peers + 1)

        @pl.when((at == 0) | (at + 1 == groups))
        def _():
            pl.semaphore_wait(barrier, peers)
    else:
        pl.semaphore_wait(barrier, peers - 1)


def square(chips, chip):
    return chip + 1 - 2 * (chip % 2), (chip + 2) % chips, chips - 1 - chip


class Spread:
    def __init__(self, peers, source, pick, sems, recvs, halved=False):
        me = lax.axis_index("blk")
        self.chips = peers // 2
        core, chip = me % 2, me // 2
        sibling = me + 1 - 2 * core
        self.halved = halved and self.chips == 4

        def copy(i, src, dst, to):
            return send(src, dst, sems.at[i], recvs.at[i], blk=to)

        self.first = [copy(0, source(chip), pick(me), sibling)]
        self.second, self.cross = [], []
        if self.halved:
            x, y, far = (2 * c + core for c in square(self.chips, chip))
            half = pick(me).shape[0] // 2
            low, high = pl.ds(0, half), pl.ds(half, half)
            for i, to in enumerate((x, y)):
                self.first.append(copy(1 + i, source(to // 2), pick(me), to))
                self.second.append(copy(3 + i, pick(to), pick(to), sibling))
            self.cross = [
                copy(5, pick(x).at[low], pick(x).at[low], y),
                copy(6, pick(y).at[high], pick(y).at[high], x),
            ]
            self.last = [
                copy(7 + i, pick(far).at[rows], pick(far).at[rows], sibling) for i, rows in enumerate((low, high))
            ]
            return
        for k in range(1, self.chips):
            to = (me + 2 * k) % peers
            self.first.append(copy(k, source(to // 2), pick(me), to))
            origin = pick((me + peers - 2 * k) % peers)
            self.second.append(copy(self.chips + k - 1, origin, origin, sibling))

    def start(self):
        for copy in self.first[1:] + self.first[:1]:
            copy.start()

    def forward(self):
        for i, (copy, onward) in enumerate(zip(self.first[1:], self.second)):
            copy.wait_recv()
            if self.halved:
                self.cross[i].start()
            onward.start()
        if self.halved:
            for copy, onward in zip(self.cross, self.last):
                copy.wait_recv()
                onward.start()

    def finish(self):
        for copy in self.first + self.cross:
            copy.wait_send()
        self.first[0].wait_recv()
        for copy in self.second + (self.last if self.halved else []):
            copy.wait()


class Line:
    def __init__(self, groups, pick, sems, recvs):
        self.groups, self.pick, self.sems, self.recvs = groups, pick, sems, recvs
        self.at = lax.axis_index("dp")

    def up(self, step, to, block):
        i = 2 * (step - 1)
        return send(self.pick(block), self.pick(block), self.sems.at[i], self.recvs.at[i], dp=to)

    def down(self, step, to, block):
        i = 2 * (step - 1) + 1
        return send(self.pick(block), self.pick(block), self.sems.at[i], self.recvs.at[i], dp=to)

    def start(self, step):
        at, n = self.at, self.groups

        @pl.when((at + 1 < n) & (at - (step - 1) >= 0))
        def _():
            self.up(step, at + 1, at - (step - 1)).start()

        @pl.when((at - 1 >= 0) & (at + (step - 1) < n))
        def _():
            self.down(step, at - 1, at + (step - 1)).start()

    def arrive(self, step, then=None):
        at, n = self.at, self.groups

        @pl.when(at - step >= 0)
        def _():
            self.up(step, at - 1, at - step).wait_recv()
            if then is not None:
                then(at - step).start()

        @pl.when(at + step < n)
        def _():
            self.down(step, at + 1, at + step).wait_recv()
            if then is not None:
                then(at + step).start()

    def finish(self, steps):
        at, n = self.at, self.groups
        for step in steps:

            @pl.when((at + 1 < n) & (at - (step - 1) >= 0))
            def _():
                self.up(step, at + 1, at - (step - 1)).wait_send()

            @pl.when((at - 1 >= 0) & (at + (step - 1) < n))
            def _():
                self.down(step, at - 1, at + (step - 1)).wait_send()


class LineSum:
    def __init__(self, groups, pick, up_got, dn_got, up_out, dn_out, sems, recvs, arrived=None, base=0):
        self.n, self.pick, self.arrived, self.base = groups, pick, arrived, base
        self.up_got, self.dn_got, self.up_out, self.dn_out = up_got, dn_got, up_out, dn_out
        self.sems, self.recvs = sems, recvs
        self.at = lax.axis_index("dp")

    @staticmethod
    def scratch(groups, *block, steps=None):
        hop = pltpu.VMEM((steps or groups - 1, *block), BF16)
        return [hop] * 4 + [pltpu.SemaphoreType.DMA((2 * groups,))] * 2

    def up(self, i, src, to):
        return send(src, self.up_got.at[i - self.base], self.sems.at[2 * i], self.recvs.at[2 * i], dp=to)

    def down(self, i, src, to):
        return send(src, self.dn_got.at[i - self.base], self.sems.at[2 * i + 1], self.recvs.at[2 * i + 1], dp=to)

    def add(self, out, one, other):
        def body(j, carry):
            out[j] = (one[j].astype(F32) + other[j].astype(F32)).astype(out.dtype)
            return carry

        lax.fori_loop(0, out.shape[0], body, 0)

    def step(self, i):
        at, n = self.at, self.n
        far = n - 1 - i

        @pl.when((at + far < n) & (at == 0))
        def _():
            self.up(i, self.pick(far), at + 1).start()

        @pl.when((at - far >= 0) & (at == n - 1))
        def _():
            self.down(i, self.pick(-far), at - 1).start()

        if i > 0:

            @pl.when((at + far < n) & (at > 0))
            def _():
                if self.arrived is None:
                    self.up(i - 1, self.up_out.at[max(i - 1 - self.base, 0)], at - 1).wait_recv()
                before = self.up_got.at[max(i - 1 - self.base, 0)] if self.arrived is None else self.arrived[0]
                self.add(self.up_out.at[i - self.base], self.pick(far), before)
                self.up(i, self.up_out.at[i - self.base], at + 1).start()

            @pl.when((at - far >= 0) & (at < n - 1))
            def _():
                if self.arrived is None:
                    self.down(i - 1, self.dn_out.at[max(i - 1 - self.base, 0)], at + 1).wait_recv()
                before = self.dn_got.at[max(i - 1 - self.base, 0)] if self.arrived is None else self.arrived[1]
                self.add(self.dn_out.at[i - self.base], self.pick(-far), before)
                self.down(i, self.dn_out.at[i - self.base], at - 1).start()

    def arrive(self, i, up, down):
        at, n = self.at, self.n
        far = n - 1 - i
        some_up, some_down = (at > 0) & (at - 1 + far < n), (at < n - 1) & (at + 1 - far >= 0)

        @pl.when(some_up)
        def _():
            self.up(i, self.up_out.at[i - self.base], at - 1).wait_recv()
            up[...] = self.up_got[i - self.base]

        @pl.when(some_down)
        def _():
            self.down(i, self.dn_out.at[i - self.base], at + 1).wait_recv()
            down[...] = self.dn_got[i - self.base]

        @pl.when(jnp.logical_not(some_up))
        def _():
            up[...] = jnp.zeros_like(up)

        @pl.when(jnp.logical_not(some_down))
        def _():
            down[...] = jnp.zeros_like(down)

    def total(self, out):
        at, n, i = self.at, self.n, self.n - 2

        @pl.when(at > 0)
        def _():
            self.up(i, self.up_out.at[i - self.base], at - 1).wait_recv()
            self.add(out, self.pick(0), self.up_got.at[i - self.base])

        @pl.when(at == 0)
        def _():
            self.down(i, self.dn_out.at[i - self.base], at + 1).wait_recv()
            self.add(out, self.pick(0), self.dn_got.at[i - self.base])

        @pl.when((at > 0) & (at < n - 1))
        def _():
            self.down(i, self.dn_out.at[i - self.base], at + 1).wait_recv()
            self.add(out, out, self.dn_got.at[i - self.base])

    def finish(self, steps=None):
        at, n = self.at, self.n
        for i in range(n - 1) if steps is None else steps:
            far = n - 1 - i

            @pl.when(at + far < n)
            def _():
                self.up(i, self.up_out.at[i - self.base], at + 1).wait_send()

            @pl.when(at - far >= 0)
            def _():
                self.down(i, self.dn_out.at[i - self.base], at - 1).wait_send()


class Reduce:
    def __init__(self, peers, part, half, mine, got, sems, recvs, place=None, halved=False, kept=None):
        me = lax.axis_index("blk")
        self.chips = peers // 2
        self.core, self.chip = me % 2, me // 2
        sibling = me + 1 - 2 * self.core
        self.part, self.half, self.mine, self.got, self.kept = part, half, mine, got, kept
        self.halved = halved and self.chips == 4

        def copy(i, src, dst, to):
            return send(src, dst, sems.at[i], recvs.at[i], blk=to)

        if self.halved:
            self.to = [self.chip, *square(self.chips, self.chip)]
        else:
            self.to = [(self.chip + k) % self.chips for k in range(self.chips)]
        self.inner = [copy(k, part.at[2 * to + 1 - self.core], half.at[k], sibling) for k, to in enumerate(self.to)]
        self.outer = []
        if self.halved:
            x, y, far = (2 * c + self.core for c in self.to[1:])
            middle = mine.shape[1] // 2
            self.low, self.high = pl.ds(0, middle), pl.ds(middle, middle)
            self.cross = [
                copy(6, mine.at[3, self.low], got.at[3, self.low], x),
                copy(7, mine.at[3, self.high], got.at[3, self.high], y),
            ]
            self.outer = [copy(4, mine.at[1], got.at[1], x), copy(5, mine.at[2], got.at[2], y)]
            return
        for k in range(1, self.chips):
            arrival = got.at[k] if place is None else place
            self.outer.append(copy(self.chips + k, mine.at[k], arrival, 2 * self.to[k] + self.core))

    def order(self):
        return list(range(self.chips - 1, -1, -1)) if self.halved else list(range(1, self.chips)) + [0]

    def start(self):
        for k in self.order():
            self.inner[k].start()

    def chip_sums(self):
        for k in self.order():
            self.inner[k].wait_recv()
            kept = self.part[2 * self.to[k] + self.core] if self.kept is None else self.kept[k]
            both_cores = kept.astype(F32) + self.half[k].astype(F32)
            self.mine[k] = both_cores.astype(BF16)
            if self.halved:
                if k == 3:
                    for copy in self.cross:
                        copy.start()
            elif k > 0:
                self.outer[k - 1].start()

    def pair(self):
        self.chip_sums()
        self.cross_sums()

    def cross_sums(self):
        if self.halved:
            for copy, rows, k in ((self.cross[0], self.low, 2), (self.cross[1], self.high, 1)):
                copy.wait_recv()
                summed = self.mine[k, rows].astype(F32) + self.got[3, rows].astype(F32)
                self.mine[k, rows] = summed.astype(BF16)
                self.outer[k - 1].start()

    def total(self):
        total = self.mine[0].astype(F32)
        for k, copy in enumerate(self.outer):
            copy.wait_recv()
            total = total + self.got[k + 1].astype(F32)
        return total

    def finish(self):
        for copy in self.inner + self.outer + (self.cross if self.halved else []):
            copy.wait_send()

    @staticmethod
    def scratch(peers, rows, width):
        block = pltpu.VMEM((peers // 2, rows, width), BF16)
        return [block, block, block, pltpu.SemaphoreType.DMA((peers,)), pltpu.SemaphoreType.DMA((peers,))]


def fanout(peers, source, dst, sems, recvs):
    me = lax.axis_index("blk")
    copies = []
    for k in range(1, peers):
        p = (me + k) % peers
        copies.append(send(source(p), dst(p), sems.at[k], recvs.at[k], blk=p))
    return copies


def attention_forward_kernel(
    groups, peers, heads, share, spans, span, doc_ref, on_ref, head_ref, x_all, w_ref, pieces_ref, dy_ref, ffn_ref,
    norm_all, dy_all, ext_ref, ffn_all, proj_ref, logit_ref,
    low_ref, att_ref, sum_ref, a1_ref, g_ref, y_ref, e0_ref, qp_ref, m_ref, kts_ref,
    kpt_ref, kt_ref, x_ref, norm_ref, keep_sem, x_sem, d_s, d_r, l_s, l_r,
):
    h = span
    scale = h ** -0.5
    slot, me = pl.program_id(0), lax.axis_index("blk")
    tall = 2 * span

    def dy_copies():
        keep = pltpu.make_async_copy(dy_ref, dy_all.at[me], keep_sem.at[0])
        return keep, Spread(peers, lambda c: dy_ref, lambda b: dy_all.at[b], d_s, d_r, True)

    at_dp = lax.axis_index("dp")
    ffn_line = Line(groups, lambda d: ffn_all.at[d], l_s, l_r)

    @pl.when(slot == 0)
    def _():
        own_ffn = pltpu.make_async_copy(ffn_ref, ffn_all.at[at_dp], keep_sem.at[1])
        own_ffn.start()
        loads = [
            pltpu.make_async_copy(x_all.at[pl.ds(i * tall, tall)], x_ref.at[pl.ds(i * tall, tall)], x_sem.at[i])
            for i in range(spans // 2)
        ]
        for copy in loads:
            copy.start()
        greet(peers, groups)
        keep, spread = dy_copies()
        keep.start()
        spread.start()
        own_ffn.wait()
        ffn_line.start(1)
        lanes_in, slab = peers * 128, peers * share
        source = lax.broadcasted_iota(jnp.int32, (lanes_in, slab), 0)
        target = lax.broadcasted_iota(jnp.int32, (lanes_in, slab), 1)
        place = (source // 128 * share + source % 128 == target) & (source % 128 < share)
        place = jnp.where(place, 1.0, 0.0).astype(BF16)
        for d in range(groups):
            pieces = jnp.concatenate([pieces_ref[d, b] for b in range(peers)], 1)
            ext_ref[:, d * slab : (d + 1) * slab] = dot(pieces, place).astype(BF16)
        gain = ext_ref[...].astype(F32)[heads : heads + 1]
        for i, copy in enumerate(loads):
            copy.wait()
            rows = pl.ds(i * tall, tall)
            norm_ref[rows, :] = rms_norm(x_ref[rows, :].astype(F32), gain).astype(BF16)
        pltpu.make_async_copy(norm_ref, norm_all, keep_sem.at[2]).start()

    def project(i, carry):
        rows = pl.ds(pl.multiple_of(i * tall, tall), tall)
        normed = norm_ref[rows, :]
        proj_ref[rows, :] = dot(normed, w_ref[...])
        every = dot(normed, ext_ref[...], NT)
        lane = lax.broadcasted_iota(jnp.int32, every.shape, 1)
        mine = jnp.sum(jnp.where(lane == head_ref[slot], every, 0.0), -1, keepdims=True)
        logit_ref[rows, :] = jnp.broadcast_to(mine, (tall, h))
        return carry

    lax.fori_loop(0, spans // 2, project, 0)
    r, c = rows_of(span), lanes(span)
    lower, strict, eye = c <= r, c < r, (c == r).astype(F32)
    at = [pl.ds(n * span, span) for n in range(spans)]
    group = 4
    for first in range(0, spans, group):
        members = range(first, min(first + group, spans))
        grams, betas, kept = [], [], []
        for n in members:
            q = proj_ref[at[n], 0:h]
            k = proj_ref[at[n], h : 2 * h]
            d = proj_ref[at[n], 3 * h : 4 * h]
            w = d * lax.rsqrt(jnp.sum(d * d, -1, keepdims=True) + EPSILON)
            qs, ks, ws = halves(q), halves(k), halves(w)
            z = dot3(both((qs, ws), 0), both((ws, ks), 0), NT)
            a1 = jnp.where(lower, z[:span, :span], 0.0)
            a1_ref[at[n], :] = a1
            b1 = jnp.where(strict, z[span:, span:], 0.0)
            grams.append(jnp.where(strict, z[span:, :span], 0.0))
            betas.append(2.0 / (1.0 + jnp.exp(-logit_ref[at[n], :])))
            kept.append((q, k, ws, halves(a1), halves(b1), z[:span, span:]))
        solved = inverses(grams, betas, span)
        for n, g, (q, k, ws, a1s, b1s, qk) in zip(members, solved, kept):
            g_ref[at[n], :] = g
            y = dot3(halves(g), both((ws, b1s), 1))
            y_ref[at[n], :] = y
            ys = halves(y)
            t = dot3(a1s, ys)
            u = dot3(ws, ys, TN)
            qp_ref[at[n], :] = (q - t[:, :h]).astype(BF16)
            local = (qk - t[:, h:]) * scale
            e0_ref[at[n], :] = jnp.where(lower, jnp.exp(local), 0.0)
            m_ref[at[n], :] = eye - u[:, :h]
            kpt_ref[:, at[n]] = k.T - u[:, h:]
    for n in range(spans):
        w = n * span
        e0 = e0_ref[at[n], :]
        total = jnp.sum(e0, -1, keepdims=True)
        numer = dot(e0.astype(BF16), proj_ref[at[n], 2 * h : 3 * h].astype(BF16))
        if n > 0:
            kt = kt_ref[:, :w]
            kts = halves(kt)
            kts_ref[0, n, :, :w] = kts[0]
            block = jnp.exp(dot(qp_ref[at[n], :], kts[0]) * scale)
            block = jnp.concatenate(
                [jnp.where(doc_ref[0, j] == doc_ref[0, n], block[:, j * span : (j + 1) * span], 0.0) for j in range(n)], 1
            )
            total = total + jnp.sum(block, -1, keepdims=True)
            numer = numer + dot(block.astype(BF16), proj_ref[:w, 2 * h : 3 * h].astype(BF16))
            if n < spans - 1:
                kt_ref[:, :w] = dot3(halves(m_ref[at[n], :]), kts)
        if n < spans - 1:
            kt_ref[:, at[n]] = kpt_ref[:, at[n]]
        attended = numer / total
        att_ref[at[n], :] = attended
        low_ref[at[n], :] = jnp.where(on_ref[slot] > 0, attended, 0.0).astype(BF16)
        sum_ref[at[n], :] = jnp.broadcast_to(total, (span, h))

    @pl.when(slot == 0)
    def _():
        dy_copies()[1].forward()
        ffn_line.arrive(1)
        ffn_line.start(2)

    @pl.when(slot == pl.num_programs(0) - 1)
    def _():
        keep, spread = dy_copies()
        for step in range(3, groups - 1):
            ffn_line.arrive(step - 1)
            ffn_line.start(step)
        spread.finish()
        keep.wait()
        pltpu.make_async_copy(norm_ref, norm_all, keep_sem.at[2]).wait()
        ffn_line.arrive(groups - 2)
        ffn_line.finish(range(1, groups - 1))


def attention_backward_kernel(
    groups, peers, own, shared, spans, span, doc_ref, on_ref, head_ref, outp_all, res_ref, gi_all, up_all, dn_all, gd_all, db_all, out_ref,
    proj_ref, logit_ref, att_ref, sum_ref, a1_ref, g_ref, y_ref, e0_ref, qp_ref, m_ref, kts_ref,
    dproj_ref, dlogit_ref, block_ref, rows_ref, dup_ref, ddn_ref,
    gkt_ref, dvt_ref, dqp_ref, dm_ref, dkpt_ref, ds_ref, datt_ref, half, mine, got, r_s, r_r, gi_ref, local,
    kept, up_ref, dn_ref, gd_ref, db_ref,
    ug, dg, uo, do, l_s, l_r, vg, wg, vo, wo, m_s, m_r,
):
    h = span
    scale = h ** -0.5
    r, c = rows_of(span), lanes(span)
    lower, strict, same = c <= r, c < r, c == r
    at = [pl.ds(n * span, span) for n in range(spans)]
    slot = pl.program_id(0)

    def reduce():
        return Reduce(peers, outp_all, half, mine, got, r_s, r_r, halved=True, kept=kept)

    place = {1: 0, -1: 1, 0: 2}
    line = LineSum(groups, lambda r: gi_ref.at[place[r]], ug, dg, uo, do, l_s, l_r, (up_ref, dn_ref), groups - 2)
    at_dp = line.at
    down = LineSum(groups, lambda r: gd_ref.at[at_dp + r], vg, wg, vo, wo, m_s, m_r)

    @pl.when(slot == 0)
    def _():
        core = lax.axis_index("blk") % 2
        sums = reduce()
        loads = fetch(
            [(gi_all.at[(at_dp + groups + r) % groups], gi_ref.at[i]) for r, i in place.items()]
            + [(up_all, up_ref), (dn_all, dn_ref), (gd_all, gd_ref), (db_all, db_ref)]
            + [(outp_all.at[2 * to + core], kept.at[k]) for k, to in enumerate(sums.to)],
            local,
        )
        greet(peers, groups)
        sums.start()
        for copy in loads[:5]:
            copy.wait()
        line.step(groups - 2)
        loads[5].wait()
        down.step(0)
        for copy in loads[6:]:
            copy.wait()

    which = jnp.where(slot < own, lax.axis_index("blk") % 2 * (own + shared) + slot, own)
    out_at = pl.multiple_of(which * h, 128)

    def pull_back(i, carry):
        rows = pl.ds(pl.multiple_of(i * 2 * span, span), 2 * span)
        datt_ref[rows, :] = dot(db_ref[rows, :], out_ref[pl.ds(out_at, h), :], NT)
        return carry

    lax.fori_loop(0, spans // 2, pull_back, 0)
    dvt_ref[...] = jnp.zeros_like(dvt_ref)
    for n in reversed(range(spans)):
        w = n * span
        last = n == spans - 1
        datt, total = jnp.where(on_ref[slot] > 0, datt_ref[at[n], :], 0.0), sum_ref[at[n], :]
        da = (datt / total).astype(BF16)
        delta = jnp.sum(datt * att_ref[at[n], :], -1, keepdims=True) / total
        e0 = e0_ref[at[n], :]
        mix = dot(da, proj_ref[at[n], 2 * h : 3 * h].astype(BF16), NT) - delta
        ds_ref[at[n], :] = (e0 * mix).astype(BF16).astype(F32) * scale
        dvt_ref[:, at[n]] += dot(da, e0.astype(BF16), TN)
        if n == 0:
            dqp_ref[at[n], :] = jnp.zeros((span, h), F32)
            dm_ref[at[n], :] = jnp.zeros((h, h), F32)
            dkpt_ref[:, at[n]] = gkt_ref[:, at[n]] if not last else jnp.zeros((h, span), F32)
            continue
        keys = kts_ref[0, n, :, :w]
        qp = qp_ref[at[n], :]
        block = jnp.exp(dot(qp, keys) * scale)
        block = jnp.concatenate(
            [jnp.where(doc_ref[0, j] == doc_ref[0, n], block[:, j * span : (j + 1) * span], 0.0) for j in range(n)], 1
        )
        wide = jnp.concatenate([delta] * n, 1)
        mix = dot(da, proj_ref[:w, 2 * h : 3 * h].astype(BF16), NT) - wide
        ds = (block * mix).astype(BF16)
        dqp_ref[at[n], :] = dot(ds, keys, NT) * scale
        pulled = dot(qp, ds, TN) * scale
        dvt_ref[:, :w] += dot(da, block.astype(BF16), TN)
        if last:
            dm_ref[at[n], :] = jnp.zeros((h, h), F32)
            dkpt_ref[:, at[n]] = jnp.zeros((h, span), F32)
            gkt_ref[:, :w] = pulled
        else:
            dkpt_ref[:, at[n]] = gkt_ref[:, at[n]]
            gs = halves(gkt_ref[:, :w])
            dm_ref[at[n], :] = dot(gs[0], keys, NT) + dot(gs[1], keys, NT)
            gkt_ref[:, :w] = pulled + dot3(halves(m_ref[at[n], :]), gs, TN)

    @pl.when(slot == 0)
    def _():
        reduce().pair()

    for n in range(spans):
        q = proj_ref[at[n], 0:h]
        k = proj_ref[at[n], h : 2 * h]
        d = proj_ref[at[n], 3 * h : 4 * h]
        inv = lax.rsqrt(jnp.sum(d * d, -1, keepdims=True) + EPSILON)
        w = d * inv
        beta = 2.0 / (1.0 + jnp.exp(-logit_ref[at[n], :]))
        qs, ks, ws = halves(q), halves(k), halves(w)
        dqp, ds, dkpt = dqp_ref[at[n], :], ds_ref[at[n], :], dkpt_ref[:, at[n]]
        ys = halves(y_ref[at[n], :])
        left = both((halves(dqp), halves(ds)), 1)
        mid = both((halves(dm_ref[at[n], :]), halves(dkpt)), 1)
        da1 = jnp.where(lower, -dot3(left, ys, NT), 0.0)
        dy = dot3(halves(a1_ref[at[n], :]), left, TN) + dot3(ws, mid)
        dx = -dot3(halves(g_ref[at[n], :]), halves(dy), TN)
        dl = -dot3(halves(dx), ys, NT)
        dw = dx[:, :h] - dot3(ys, mid, NT)
        pull = jnp.sum(jnp.where(same, dl, 0.0), -1, keepdims=True)
        dlogit = -pull * (1.0 - 0.5 * beta) / jnp.maximum(beta, 1e-30)
        before = jnp.where(slot == 0, 0.0, dlogit_ref[at[n], :].astype(F32))
        dlogit_ref[at[n], :] = jnp.where(c == head_ref[slot], dlogit, before).astype(BF16)
        dz = jnp.concatenate(
            [
                jnp.concatenate([da1, ds], 1),
                jnp.concatenate([jnp.where(strict, dl, 0.0), jnp.where(strict, dx[:, h:], 0.0)], 1),
            ],
            0,
        )
        dzs = halves(dz)
        dp = dot3(dzs, both((ws, ks), 0))
        dr = dot3(dzs, both((qs, ws), 0), TN)
        dw = dw + dp[span:] + dr[:span]
        dproj_ref[at[n], 0:h] = (dqp + dp[:span]).astype(BF16)
        dproj_ref[at[n], h : 2 * h] = (dkpt.T + dr[span:]).astype(BF16)
        dproj_ref[at[n], 2 * h : 3 * h] = dvt_ref[:, at[n]].T.astype(BF16)
        dproj_ref[at[n], 3 * h : 4 * h] = (inv * (dw - w * jnp.sum(dw * w, -1, keepdims=True))).astype(BF16)

    @pl.when(slot == 0)
    def _():
        for i in range(1, groups - 2):
            down.step(i)

    @pl.when(slot == pl.num_programs(0) - 1)
    def _():
        last = reduce()
        block_ref[...] = (res_ref[...] + last.total()).astype(BF16)
        last.finish()
        line.total(rows_ref)
        line.finish([groups - 2])
        down.arrive(groups - 3, dup_ref, ddn_ref)
        down.finish(range(groups - 2))


def head_specs(rows, h, spans, slots):
    mode = {"pipeline_mode": pl.Buffered(1)} if slots == 1 else {}
    one = pl.BlockSpec((rows, h), lambda s: (0, s), **mode)
    two = pl.BlockSpec((rows, 2 * h), lambda s: (0, s), **mode)
    four = pl.BlockSpec((rows, 4 * h), lambda s: (0, s), **mode)
    keys = pl.BlockSpec((1, spans, h, rows), lambda s: (s, 0, 0, 0), **mode)
    docs = pl.BlockSpec(memory_space=pltpu.SMEM)
    return one, two, four, keys, docs


def attention_forward(docs, on, my_heads, x_all, w, ext, dy, ffn, groups, peers, heads, slots, span):
    rows, width = x_all.shape
    spans, h = rows // span, span
    one, two, four, keys, smem = head_specs(rows, h, spans, slots)
    dma = pltpu.SemaphoreType.DMA
    vmem, hbm = pl.BlockSpec(memory_space=pltpu.VMEM), pl.BlockSpec(memory_space=pl.ANY)
    ext_rows = ext.shape[2]

    def full(columns, dtype=F32):
        return jax.ShapeDtypeStruct((rows, slots * columns), dtype)

    return pl.pallas_call(
        functools.partial(attention_forward_kernel, groups, peers, heads, width // (groups * peers), spans, span),
        grid=(slots,),
        in_specs=[smem, smem, smem, hbm, pl.BlockSpec((width, 4 * h), lambda s: (0, s)), vmem, vmem, vmem],
        out_specs=[
            hbm, hbm, pl.BlockSpec((ext_rows, width), lambda s: (0, 0)), hbm,
            four, one, one, one, one, one, one, two, one, one, one, keys,
        ],
        out_shape=[
            jax.ShapeDtypeStruct((rows, width), BF16), jax.ShapeDtypeStruct((peers, *dy.shape), BF16),
            jax.ShapeDtypeStruct((ext_rows, width), BF16), jax.ShapeDtypeStruct((groups, *ffn.shape), BF16),
            full(4 * h), full(h),
            full(h, BF16), full(h), full(h), full(h), full(h), full(2 * h), full(h), full(h, BF16), full(h),
            jax.ShapeDtypeStruct((slots, spans, h, rows), BF16),
        ],
        scratch_shapes=[
            pltpu.VMEM((h, rows), F32), pltpu.VMEM((h, rows), F32), pltpu.VMEM((rows, width), BF16),
            pltpu.VMEM((rows, width), BF16), dma((3,)), dma((spans // 2,)), dma((2 * peers,)), dma((2 * peers,)), dma((2 * groups,)), dma((2 * groups,)),
        ],
        compiler_params=pltpu.CompilerParams(
            collective_id=5, has_side_effects=True, vmem_limit_bytes=63 * 1024 * 1024
        ),
        name="attention_forward",
    )(docs, on, my_heads, x_all, w, ext, dy, ffn)


def attention_backward(
    docs, on, heads, outp, res, gi, up, dn, gd, db_all, out_rows, proj, logits, saved, groups, peers, own, shared, span
):
    rows = proj.shape[0]
    slots = own + shared
    spans, h = rows // span, span
    one, two, four, keys, smem = head_specs(rows, h, spans, slots)
    wide, tall = pltpu.VMEM((h, rows), F32), pltpu.VMEM((rows, h), F32)
    vmem, hbm = pl.BlockSpec(memory_space=pltpu.VMEM), pl.BlockSpec(memory_space=pl.ANY)
    block = pl.BlockSpec(gd.shape[1:], lambda s: (0, 0, 0))
    return pl.pallas_call(
        functools.partial(attention_backward_kernel, groups, peers, own, shared, spans, span),
        grid=(slots,),
        in_specs=[smem, smem, smem, hbm, vmem] + [hbm] * 5 + [vmem]
        + [four, one, one, one, one, one, two, one, one, one, keys],
        out_specs=[
            four, pl.BlockSpec((rows, h), lambda s: (0, 0)), pl.BlockSpec(res.shape, lambda s: (0, 0)),
            pl.BlockSpec(up.shape, lambda s: (0, 0, 0)), block, block,
        ],
        out_shape=[
            jax.ShapeDtypeStruct((rows, slots * 4 * h), BF16),
            jax.ShapeDtypeStruct((rows, h), BF16),
            jax.ShapeDtypeStruct(res.shape, BF16),
            jax.ShapeDtypeStruct(up.shape, BF16),
            jax.ShapeDtypeStruct(gd.shape[1:], BF16),
            jax.ShapeDtypeStruct(gd.shape[1:], BF16),
        ],
        scratch_shapes=[wide, wide, tall, tall, wide, tall, tall] + Reduce.scratch(peers, *res.shape)
        + [pltpu.VMEM((3, *up.shape), BF16), pltpu.SemaphoreType.DMA((7 + peers // 2,))]
        + [pltpu.VMEM((peers // 2, *res.shape), BF16)]
        + [pltpu.VMEM(x.shape, BF16) for x in (up, dn, gd, db_all)]
        + LineSum.scratch(groups, *up.shape, steps=1) + LineSum.scratch(groups, *gd.shape[1:], steps=groups - 2),
        compiler_params=pltpu.CompilerParams(
            collective_id=6, has_side_effects=True, vmem_limit_bytes=62 * 1024 * 1024
        ),
        name="attention_backward",
    )(docs, on, heads, outp, res, gi, up, dn, gd, db_all, out_rows, proj, logits, *saved)


def gather_kernel(
    groups, peers, heads, own, shared, aligned, attn_ref, gate_ref, tok_ref, out_ref, ext_ref,
    w_all, ffn_all, tok_all, out_all, ext_all, own_ref, mix_ref, ffn_ref, out_z,
    local, a_s, a_r, m_s, m_r, f_s, f_r, t_s, t_r, o_s, o_r, e_s, e_r, s_s, s_r,
    al_s, al_r, ml_s, ml_r, ol_s, ol_r, el_s, el_r,
):
    me, at = lax.axis_index("blk"), lax.axis_index("dp")
    core = me % 2
    sibling = me + 1 - 2 * core
    h = attn_ref.shape[1] // (4 * heads)
    width = 4 * h * heads // 4
    own_cols, quarter = own * 4 * h, shared * 2 * h
    units = gate_ref.shape[1] // (2 * groups * peers)
    for p in range(peers):
        first = (p // 2) * (2 * own + shared)
        for i in range(own):
            head = first + (p % 2) * (own + shared) + i
            for part in range(4):
                to = (4 * i + part) * h
                if head < heads:
                    own_ref[p, :, to : to + h] = attn_ref[:, part * width + head * h : part * width + (head + 1) * h]
                else:
                    own_ref[p, :, to : to + h] = jnp.zeros((own_ref.shape[1], h), BF16)
        for i in range(2 * shared):
            at_col = (2 * (p % 2) + i) * width + (first + own) * h
            mix_ref[p, :, i * h : (i + 1) * h] = attn_ref[:, at_col : at_col + h]

    def side(device):
        return pl.ds(pl.multiple_of(own_cols + quarter * (device % 2), 128), quarter)

    keeps = [
        pltpu.make_async_copy(ext_ref, ext_all.at[at, me], local.at[0]),
        pltpu.make_async_copy(out_ref, out_z.at[at], local.at[1]),
        pltpu.make_async_copy(own_ref.at[me], w_all.at[at, me, :, pl.ds(0, own_cols)], local.at[2]),
        pltpu.make_async_copy(tok_ref, tok_all.at[me], local.at[4]),
    ]
    if shared:
        keeps.append(pltpu.make_async_copy(mix_ref.at[me], w_all.at[at, me, :, side(me)], local.at[5]))
    for copy in keeps:
        copy.start()
    greet(peers, groups)
    moves = fanout(peers, lambda p: own_ref.at[p], lambda p: w_all.at[at, me, :, pl.ds(0, own_cols)], a_s, a_r)
    if shared:
        moves += fanout(peers, lambda p: mix_ref.at[p], lambda p: w_all.at[at, me, :, side(p)], m_s, m_r)
    exts = fanout(peers, lambda p: ext_ref, lambda p: ext_all.at[at, me], e_s, e_r)
    ffn = fanout(peers, lambda p: ffn_ref.at[p], lambda p: ffn_all.at[me], f_s, f_r)
    for copy in moves + exts:
        copy.start()
    out_line = Line(groups, lambda d: out_z.at[d], ol_s, ol_r)
    keeps[1].wait()
    out_line.start(1)
    for p in range(peers):
        for part in range(2):
            for d in range(groups):
                source = ((part * groups + d) * peers + p) * units
                to = (part * groups + d) * units
                ffn_ref[p, :, to : to + units] = gate_ref[:, source : source + units]
    own_ffn = pltpu.make_async_copy(ffn_ref.at[me], ffn_all.at[me], local.at[6])
    own_ffn.start()
    tok = Spread(peers, lambda c: tok_ref, lambda b: tok_all.at[b], t_s, t_r, True)
    if aligned:
        out = Spread(peers, lambda c: out_z.at[c], lambda b: out_all.at[b], o_s, o_r)
    else:
        out = Spread(peers, lambda c: out_z, lambda b: out_all.at[:, b], o_s, o_r)
    lines = [Line(groups, lambda d: w_all.at[d, :, :, pl.ds(0, own_cols)], al_s, al_r)]
    if shared:
        mix_line = Line(groups, lambda d: w_all.at[d, :, :, side(me)], ml_s, ml_r)
    ext_line = Line(groups, lambda d: ext_all.at[d], el_s, el_r)

    def across(d):
        block = w_all.at[d, :, :, side(me)]
        return send(block, block, s_s.at[d], s_r.at[d], blk=sibling)

    out_line.arrive(1)
    if groups > 2:
        out_line.start(2)
    for copy in moves:
        copy.wait_recv()
    for copy in keeps[2:3] + keeps[4:]:
        copy.wait()
    lines[0].start(1)
    if shared:
        mix_line.start(1)
        across(at).start()
    tok.start()
    for copy in exts:
        copy.wait_recv()
    keeps[0].wait()
    ext_line.start(1)
    for copy in ffn:
        copy.start()
    for step in range(3, groups):
        out_line.arrive(step - 1)
        out_line.start(step)
    if groups > 2:
        out_line.arrive(groups - 1)
    out.start()
    if aligned:
        mine = pltpu.make_async_copy(out_z.at[me // 2], out_all.at[me], local.at[7])
    else:
        mine = pltpu.make_async_copy(out_z, out_all.at[:, me], local.at[7])
    mine.start()
    for step in range(2, groups):
        lines[0].arrive(step - 1)
        lines[0].start(step)
        if shared:
            mix_line.arrive(step - 1, across)
            mix_line.start(step)
        ext_line.arrive(step - 1)
        ext_line.start(step)
        if step == 2:
            tok.forward()
    out.forward()
    lines[0].arrive(groups - 1)
    if shared:
        mix_line.arrive(groups - 1, across)
    ext_line.arrive(groups - 1)
    for copy in ffn:
        copy.wait_recv()
    for copy in moves + exts + ffn:
        copy.wait_send()
    for spread in (tok, out):
        spread.finish()
    lines[0].finish(range(1, groups))
    if shared:
        mix_line.finish(range(1, groups))
        for d in range(groups):
            across(d).wait()
    ext_line.finish(range(1, groups))
    out_line.finish(range(1, groups))
    mine.wait()
    keeps[3].wait()
    own_ffn.wait()


def gather_all(groups, peers, heads, own, shared, aligned, attn, gate, tok, out, ext):
    def shape(*dims):
        return jax.ShapeDtypeStruct(dims, BF16)

    dma = pltpu.SemaphoreType.DMA
    vmem, hbm = pl.BlockSpec(memory_space=pltpu.VMEM), pl.BlockSpec(memory_space=pl.ANY)
    share, h = attn.shape[0], attn.shape[1] // (4 * heads)
    own_cols, quarter = own * 4 * h, shared * 2 * h
    ffn = (peers, share, gate.shape[1] // peers)
    return pl.pallas_call(
        functools.partial(gather_kernel, groups, peers, heads, own, shared, aligned),
        in_specs=[vmem] * 5,
        out_specs=[hbm] * 5,
        out_shape=[
            shape(groups, peers, share, own_cols + 2 * quarter), shape(*ffn), shape(peers, *tok.shape),
            shape(peers, *out.shape) if aligned else shape(groups, peers, *out.shape),
            shape(groups, peers, *ext.shape),
        ],
        scratch_shapes=[
            pltpu.VMEM((peers, share, own_cols), BF16), pltpu.VMEM((peers, share, max(quarter, 128)), BF16),
            pltpu.VMEM(ffn, BF16), pltpu.VMEM((groups, *out.shape), BF16), dma((8,)),
        ]
        + [dma((2 * peers,))] * 12 + [dma((groups,))] * 2 + [dma((2 * groups,))] * 8,
        compiler_params=pltpu.CompilerParams(
            collective_id=1, has_side_effects=True, vmem_limit_bytes=63 * 1024 * 1024
        ),
        name="gather_all",
    )(attn, gate, tok, out, ext)


def branch_kernel(
    groups, peers, heads, own, shared, att_ref, out_ref, tok_ref, ext_ref, down_ref, ffn_ref, res_ref, n2_all, down_all, far_all,
    part, low, local, half, mine, got, r_s, r_r, n_s, n_r, dl_s, dl_r, h_s, h_r,
):
    me, at = lax.axis_index("blk"), lax.axis_index("dp")
    rows, width = tok_ref.shape
    own_down = pltpu.make_async_copy(down_ref, down_all.at[at], local.at[0])
    own_down.start()
    greet(peers, groups)
    down_line = Line(groups, lambda d: down_all.at[d], dl_s, dl_r)
    own_down.wait()
    down_line.start(1)

    def hop(i, block, to):
        return send(ffn_ref.at[block], far_all, h_s.at[i], h_r.at[i], dp=to)

    @pl.when(at == groups - 2)
    def _():
        hop(0, 0, at + 1).start()

    @pl.when(at == 1)
    def _():
        hop(1, groups - 1, at - 1).start()

    reduce = Reduce(peers, part, half, mine, got, r_s, r_r, halved=True)

    h = out_ref.shape[0] // (2 * own + shared)
    mine_rows = out_ref[pl.ds(pl.multiple_of(me % 2 * ((own + shared) * h), 128), own * h), :]
    if shared:
        mine_rows = jnp.concatenate([mine_rows, out_ref[own * h : (own + 1) * h, :]], 0)

    def fill(b):
        block = att_ref[pl.ds(pl.multiple_of(b * rows, rows), rows), :]
        part[b] = dot(block, mine_rows).astype(BF16)

    for k in reduce.order():
        fill(2 * reduce.to[k] + 1 - me % 2)
        reduce.inner[k].start()
    for k in reduce.order():
        fill(2 * reduce.to[k] + me % 2)
    reduce.pair()
    res_ref[...] = tok_ref[...].astype(F32) + reduce.total()
    low[...] = rms_norm(res_ref[...], ext_ref[...].astype(F32)[heads + 1 : heads + 2]).astype(BF16)
    keep = pltpu.make_async_copy(low, n2_all.at[me], local.at[1])
    keep.start()
    spread = Spread(peers, lambda c: low, lambda b: n2_all.at[b], n_s, n_r, True)
    spread.start()
    down_line.arrive(1)
    down_line.start(2)
    spread.forward()
    for step in range(3, groups):
        down_line.arrive(step - 1)
        down_line.start(step)
    spread.finish()
    down_line.arrive(groups - 1)
    reduce.finish()
    down_line.finish(range(1, groups))
    keep.wait()

    @pl.when(at == groups - 1)
    def _():
        hop(0, 0, at - 1).wait_recv()

    @pl.when(at == 0)
    def _():
        hop(1, groups - 1, at + 1).wait_recv()

    @pl.when(at == groups - 2)
    def _():
        hop(0, 0, at + 1).wait_send()

    @pl.when(at == 1)
    def _():
        hop(1, groups - 1, at - 1).wait_send()


def branch(groups, peers, heads, own, shared, att, out, tok, ext, down, ffn):
    rows, width = tok.shape
    dma = pltpu.SemaphoreType.DMA
    vmem, hbm = pl.BlockSpec(memory_space=pltpu.VMEM), pl.BlockSpec(memory_space=pl.ANY)
    return pl.pallas_call(
        functools.partial(branch_kernel, groups, peers, heads, own, shared),
        in_specs=[vmem] * 5 + [hbm],
        out_specs=[vmem, hbm, hbm, hbm],
        out_shape=[
            jax.ShapeDtypeStruct((rows, width), F32),
            jax.ShapeDtypeStruct((peers, rows, width), BF16),
            jax.ShapeDtypeStruct((groups, *down.shape), BF16),
            jax.ShapeDtypeStruct(ffn.shape[1:], BF16),
        ],
        scratch_shapes=[pltpu.VMEM((peers, rows, width), BF16), pltpu.VMEM((rows, width), BF16), dma((2,))]
        + Reduce.scratch(peers, rows, width)
        + [dma((2 * peers,)), dma((2 * peers,)), dma((2 * groups,)), dma((2 * groups,)), dma((2,)), dma((2,))],
        compiler_params=pltpu.CompilerParams(
            collective_id=2, has_side_effects=True, vmem_limit_bytes=63 * 1024 * 1024
        ),
        name="branch_and_norm",
    )(att, out, tok, ext, down, ffn)


def slab_order(groups, slab):
    if slab % 128:
        return list(range(groups))
    upper = lax.axis_index("dp") >= groups // 2
    return [jnp.where(upper, i, groups - 1 - i) for i in range(groups)]


def slab_of(ref, d, slab):
    if slab % 128:
        return ref[:, d * slab : (d + 1) * slab]
    return ref[:, pl.ds(pl.multiple_of(d * slab, 128), slab)]


def feed_forward_kernel(
    groups, peers, heads, n2_ref, ffn_all, far_all, down_all, dy_all, res_ref, ext_ref,
    dres_ref, db_all, outp_all, gd_all, gi_all, up_ref, dn_ref,
    w_ref, w_sem, down_ref, dy_ref, part, hidden, pulled, low, outp_ref, gd_ref, gi_ref, local, half, mine, got, r_s, r_r, n_s, n_r, ug, dg, uo, do, l_s, l_r,
):
    me = lax.axis_index("blk")
    rows, width = res_ref.shape
    cols = w_ref.shape[1]
    units = cols // 2
    share = gi_ref.shape[2]
    slab = peers * share
    at_dp = lax.axis_index("dp")
    loads = []
    for d in range(groups):
        gap = at_dp - d
        remote = (gap == groups - 1) | (gap == 1 - groups)
        into = w_ref.at[pl.ds(d * slab, slab)]
        loads.append(pltpu.make_async_copy(ffn_all.at[d], into, w_sem.at[d]))
        pl.when(remote)(pltpu.make_async_copy(far_all, into, w_sem.at[d]).start)
        pl.when(jnp.logical_not(remote))(loads[d].start)
    loads += [
        pltpu.make_async_copy(dy_all, dy_ref, w_sem.at[groups]),
        pltpu.make_async_copy(down_all, down_ref, w_sem.at[groups + 1]),
    ]
    for copy in loads[groups:]:
        copy.start()
    greet(peers, groups)
    for copy in loads:
        copy.wait()
    reduce = Reduce(peers, part, half, mine, got, r_s, r_r, halved=True)

    def block(ref, b, count=1):
        return ref.at[pl.ds(pl.multiple_of(b * rows, rows), count * rows)]

    for k in reduce.order():
        chip = reduce.to[k]
        normed = block(n2_ref, 2 * chip, 2)[...]
        gate_up = dot(normed, w_ref[...])
        gate, up = gate_up[:, :units], gate_up[:, units:]
        sig = 1.0 / (1.0 + jnp.exp(-gate))
        silu = gate * sig
        block(hidden, 2 * chip, 2)[...] = (silu * up).astype(BF16)
        dhidden = dot(block(dy_ref, 2 * chip, 2)[...], down_ref[...], NT)
        dgate = dhidden * up * (sig + silu * (1.0 - sig))
        both_pulled = jnp.concatenate([dgate, dhidden * silu], 1).astype(BF16)
        block(pulled, 2 * chip, 2)[...] = both_pulled
        pull = dot(both_pulled, w_ref[...], NT).astype(BF16)
        part[2 * chip] = pull[:rows]
        part[2 * chip + 1] = pull[rows:]
        reduce.inner[k].start()
    line = LineSum(groups, lambda r: gi_ref.at[line.at + r], ug, dg, uo, do, l_s, l_r)

    def chunk(d):
        gi_ref[d] = dot(slab_of(n2_ref, d, slab), pulled[...], TN).astype(BF16).reshape(peers, share, cols)

    order = slab_order(groups, slab)
    early = 1 if slab % 128 == 0 else groups
    for d in order[:early]:
        chunk(d)
    line.step(0)
    reduce.pair()
    for d in order[early:]:
        chunk(d)
    out_copies = [pltpu.make_async_copy(gi_ref, gi_all, local.at[1])]
    out_copies[0].start()
    dres_ref[...] = block(dy_ref, me)[...].astype(F32) + rms_pull(
        res_ref[...], ext_ref[...].astype(F32)[heads + 1 : heads + 2], reduce.total()
    )
    low[...] = dres_ref[...].astype(BF16)
    keep = pltpu.make_async_copy(low, db_all.at[me], local.at[0])
    keep.start()
    spread = Spread(peers, lambda c: low, lambda b: db_all.at[b], n_s, n_r, True)
    spread.start()
    gd_ref[...] = dot(hidden[...], dy_ref[...], TN).astype(BF16).reshape(gd_ref.shape)
    out_copies.append(pltpu.make_async_copy(gd_ref, gd_all, local.at[2]))
    out_copies[1].start()
    steps = range(max(groups - 2, 1))
    for i in steps[1:]:
        line.step(i)
    spread.forward()

    def out(i, carry):
        at = pl.ds(pl.multiple_of(i * 2 * rows, rows), 2 * rows)
        value = dot(hidden[at, :], down_ref[...]).astype(BF16)
        outp_ref[2 * i] = value[:rows]
        outp_ref[2 * i + 1] = value[rows:]
        return carry

    lax.fori_loop(0, peers // 2, out, 0)
    out_copies.append(pltpu.make_async_copy(outp_ref, outp_all, local.at[3]))
    out_copies[2].start()
    spread.finish()
    reduce.finish()
    line.arrive(steps[-1], up_ref, dn_ref)
    line.finish(steps)
    for copy in [keep] + out_copies:
        copy.wait()


def feed_forward(groups, peers, heads, n2_all, ffn, far, down, dy_all, res, ext):
    rows, width = res.shape
    tokens, cols = n2_all.shape[0], ffn.shape[2]
    share = width // (groups * peers)
    units = cols // (2 * groups)
    tall = 16 if units % 16 == 0 else units
    down_shape = (groups, units // tall, tall, width)
    dma = pltpu.SemaphoreType.DMA
    vmem, hbm = pl.BlockSpec(memory_space=pltpu.VMEM), pl.BlockSpec(memory_space=pl.ANY)

    def shape(*dims, dtype=BF16):
        return jax.ShapeDtypeStruct(dims, dtype)

    return pl.pallas_call(
        functools.partial(feed_forward_kernel, groups, peers, heads),
        in_specs=[vmem, hbm, hbm, hbm, hbm, vmem, vmem],
        out_specs=[vmem, hbm, hbm, hbm, hbm, vmem, vmem],
        out_shape=[
            shape(rows, width, dtype=F32), shape(peers, rows, width), shape(peers, rows, width),
            shape(*down_shape), shape(groups, peers, share, cols),
            shape(peers, share, cols), shape(peers, share, cols),
        ],
        scratch_shapes=[
            pltpu.VMEM((width, cols), BF16), dma((groups + 2,)),
            pltpu.VMEM(down.shape, BF16), pltpu.VMEM(dy_all.shape, BF16),
            pltpu.VMEM((peers, rows, width), BF16), pltpu.VMEM((tokens, cols // 2), BF16),
            pltpu.VMEM((tokens, cols), BF16), pltpu.VMEM((rows, width), BF16),
            pltpu.VMEM((peers, rows, width), BF16), pltpu.VMEM(down_shape, BF16),
            pltpu.VMEM((groups, peers, share, cols), BF16), dma((4,)),
        ]
        + Reduce.scratch(peers, rows, width)
        + [dma((2 * peers,)), dma((2 * peers,))]
        + LineSum.scratch(groups, peers, share, cols, steps=groups - 2),
        compiler_params=pltpu.CompilerParams(
            collective_id=3, has_side_effects=True, vmem_limit_bytes=62 * 1024 * 1024
        ),
        name="feed_forward",
    )(n2_all, ffn, far, down, dy_all, res, ext)


def final_kernel(
    groups, peers, heads, own, shared, aligned,
    norm_ref, dproj_ref, dlogit_ref, w_all, ext_ref, att_ref, db_all, ffn_all, tok_ref, dres_ref,
    gd_all, dup_ref, ddn_ref, wa_all, wb_ref, wf_all, ga_ref, gf_ref,
    dtok_ref, grad_ref, beta_out, gout_fin, ffn_out, down_fin, gain_out, gain_ffn_out,
    w_ref, db_ref, ffn_ref, gd_ref, wa_ref, wf_ref, f_sem, beta_fin,
    g_ref, beta_ref, part, half, mine, got, r_s, r_r,
    oug, odg, ouo, odo, ol_s, ol_r, own_fin, own_rows, w_s, w_r, ffn_rows, f_s, f_r,
    beta_got, beta_sum, b_s, b_r, bug, bdg, buo, bdo, bl_s, bl_r,
    vg, wg, vo, wo, m_s, m_r,
    *extra,
):
    me, at = lax.axis_index("blk"), lax.axis_index("dp")
    core, chip = me % 2, me // 2
    sibling = me + 1 - 2 * core
    rows, width = tok_ref.shape
    h = width // heads
    share = g_ref.shape[2]
    slab = peers * share
    own_cols, quarter = own * 4 * h, shared * 2 * h
    cols = own_cols + 2 * quarter
    extra = list(extra)
    if shared:
        mix_half, mix_sum, mug, mdg, muo, mdo, ml_s, ml_r, mix_fin, mix_rows, x_s, x_r, mw_s, mw_r = extra[:14]
        extra = extra[14:]
    if aligned:
        go_part, go_half, go_mine, go_all, g_s, g_r, gug, gdg, guo, gdo, gl_s, gl_r = extra
    loads = fetch(
        [(w_all, w_ref), (db_all, db_ref), (ffn_all, ffn_ref), (gd_all, gd_ref), (wa_all, wa_ref), (wf_all, wf_ref)], f_sem
    )
    greet(peers, groups)
    down = LineSum(groups, lambda r: gd_ref.at[at + r], vg, wg, vo, wo, m_s, m_r, (dup_ref, ddn_ref), groups - 2)
    own_line = LineSum(groups, lambda r: g_ref.at[at + r, :, :, pl.ds(0, own_cols)], oug, odg, ouo, odo, ol_s, ol_r)
    if shared:
        theirs = pl.ds(pl.multiple_of(own_cols + quarter * (1 - core), 128), quarter)
        ours = pl.ds(pl.multiple_of(own_cols + quarter * core, 128), quarter)
        mix = LineSum(groups, lambda r: mix_sum.at[at + r], mug, mdg, muo, mdo, ml_s, ml_r)

        def swap(d):
            return send(g_ref.at[d, :, :, theirs], mix_half.at[d], x_s.at[d], x_r.at[d], blk=sibling)

    order = slab_order(groups, slab)
    for i, d in enumerate(order):
        normed = slab_of(norm_ref, d, slab)
        g_ref[d] = dot(normed, dproj_ref[...], TN).astype(BF16).reshape(peers, share, cols)
        if i == (0 if slab % 128 == 0 else groups - 1):
            own_line.step(0)
        if shared:
            swap(d).start()
        beta_ref[d] = dot(normed, dlogit_ref[...], TN).astype(BF16).reshape(peers, share, 128)
    betas = fanout(peers, lambda p: beta_ref.at[:, p], lambda p: beta_got.at[me], b_s, b_r)
    ffn = fanout(peers, lambda p: ffn_ref.at[p], lambda p: ffn_rows.at[me], f_s, f_r)
    if shared:
        for i, d in enumerate(order):
            swap(d).wait_recv()

            def body(j, carry):
                mix_sum[d, j] = (g_ref[d, j, :, ours].astype(F32) + mix_half[d, j].astype(F32)).astype(BF16)
                return carry

            lax.fori_loop(0, peers, body, 0)
            if i == 0:
                mix.step(0)
    reduce = Reduce(peers, part, half, mine, got, r_s, r_r, halved=True)
    small = ext_ref[...].astype(F32)
    gain_row = small[heads : heads + 1]
    row = lax.broadcasted_iota(jnp.int32, small.shape, 0)
    small = jnp.where(row < heads, small, 0.0).astype(BF16)
    small = jnp.concatenate([small, jnp.zeros((128 - small.shape[0], width), BF16)], 0)

    def pull(k):
        to = 2 * reduce.to[k]
        two = pl.ds(pl.multiple_of(to * rows, rows), 2 * rows)
        value = (dot(dproj_ref[two, :], w_ref[...], NT) + dot(dlogit_ref[two, :], small)).astype(BF16)
        part[to] = value[:rows]
        part[to + 1] = value[rows:]
        reduce.inner[k].start()

    pulls = reduce.order()
    for copy in loads:
        copy.wait()
    pull(pulls[0])
    own_line.step(1)
    for k in pulls[1:]:
        pull(k)
    if shared:
        mix.step(1)
    reduce.chip_sums()
    for copy in betas:
        copy.start()
    if aligned:
        att = att_ref[...]
        mine_att, zero = att[:, : own * h], jnp.zeros((att.shape[0], own * h), BF16)
        wide = jnp.concatenate(
            [jnp.where(core == 0, mine_att, zero), att[:, own * h :], jnp.where(core == 1, mine_att, zero)], 1
        )
        tile = width // 3
        for j in range(0, width, tile):
            value = dot(wide, db_ref[:, j : j + tile], TN).astype(BF16)
            go_part[:, :, j : j + tile] = value.reshape(peers, share, tile)
        gout = Reduce(peers, go_part, go_half, go_mine, go_all, g_s, g_r, go_all.at[chip, 0])
        gout.start()
    reduce.cross_sums()
    sums = [own_line] + ([mix] if shared else [])
    for i in range(2, groups - 1):
        for item in sums:
            item.step(i)
    if aligned:
        gout.pair()
        go_all[chip, 0] = go_mine[0]
    for copy in ffn:
        copy.start()
    ffn_rows[me] = ffn_ref[me]
    beta_got[me] = beta_ref[:, me]
    for copy in betas:
        copy.wait_recv()
    summed = beta_got[0].astype(F32)
    for b in range(1, peers):
        summed = summed + beta_got[b].astype(F32)
    beta_sum[:, 0] = summed.astype(BF16)
    late = [LineSum(groups, lambda r: beta_sum.at[at + r], bug, bdg, buo, bdo, bl_s, bl_r)]
    if aligned:
        for copy in gout.outer:
            copy.wait_recv()
        late.append(LineSum(groups, lambda r: go_all.at[at + r], gug, gdg, guo, gdo, gl_s, gl_r))
    for item in late:
        item.step(0)
    own_line.total(own_fin)
    moves = fanout(peers, lambda p: own_fin.at[p], lambda p: own_rows.at[me], w_s, w_r)
    for copy in moves:
        copy.start()
    down.step(groups - 2)
    own_rows[me] = own_fin[me]
    if shared:
        mix.total(mix_fin)
        mix_moves = fanout(peers, lambda p: mix_fin.at[p], lambda p: mix_rows.at[me], mw_s, mw_r)
        for copy in mix_moves:
            copy.start()
        mix_rows[me] = mix_fin[me]
        moves += mix_moves
    for item in late:
        item.step(1)
    dtok_ref[...] = dres_ref[...] + rms_pull(tok_ref[...].astype(F32), gain_row, reduce.total())

    def row_sums(wide):
        high = wide.astype(BF16)
        low = (wide - high.astype(F32)).astype(BF16)
        ones = jnp.ones((8, wide.shape[1]), BF16)
        return (dot(ones, high, NT) + dot(ones, low, NT))[:1]

    for copy in ffn:
        copy.wait_recv()
    units = wf_ref.shape[1] // (2 * groups * peers)
    total = jnp.zeros((share, units), F32)
    for b in range(peers):
        for side in range(2):
            for d in range(groups):
                src = (side * groups + d) * units
                to = ((side * groups + d) * peers + b) * units
                value = ffn_rows[b, :, src : src + units].astype(F32)
                ffn_out[:, to : to + units] = value
                total = total + value * wf_ref[:, to : to + units].astype(F32)
    gain_ffn_out[...] = row_sums(total) / gf_ref[...].astype(F32)
    for i in range(2, groups - 1):
        for item in late:
            item.step(i)
    down.total(down_fin)
    late[0].total(beta_fin)
    for copy in moves:
        copy.wait_recv()
    beta_out[...] = beta_fin[0][:, :heads]
    gain = beta_fin[0] * wb_ref[...].astype(F32)
    hc = 2 * own + shared

    def put(acc, value, head, side):
        to = side * width + head * h
        value = value.astype(F32)
        grad_ref[:, to : to + h] = value
        return acc + value * wa_ref[:, to : to + h].astype(F32)

    for b in range(peers):
        for s in range(own):
            head = (b // 2) * hc + (b % 2) * (own + shared) + s
            if head < heads:
                for side in range(4):
                    gain = put(gain, own_rows[b, :, (4 * s + side) * h : (4 * s + side + 1) * h], head, side)
        if shared:
            for i in range(2):
                gain = put(gain, mix_rows[b, :, i * h : (i + 1) * h], (b // 2) * hc + own, 2 * (b % 2) + i)
    gain_out[...] = row_sums(gain) / ga_ref[...].astype(F32)
    if aligned:
        late[1].total(gout_fin)
    reduce.finish()
    for copy in betas + ffn + moves:
        copy.wait_send()
    if shared:
        for d in range(groups):
            swap(d).wait_send()
    if aligned:
        gout.finish()
    for item in sums + late:
        item.finish()
    down.finish([groups - 2])


def final_sums(groups, peers, heads, own, shared, aligned, *args):
    normed, dproj, dlogits, w, ext, att, db, ffn, tok = args[:9]
    gd, wa, wf = args[10], args[13], args[15]
    rows, width = tok.shape
    h, share = width // heads, wa.shape[0]
    own_cols, quarter, cols = own * 4 * h, shared * 2 * h, w.shape[1]
    dma = pltpu.SemaphoreType.DMA
    vmem = pl.BlockSpec(memory_space=pltpu.VMEM)

    def block(*dims):
        return pltpu.VMEM(dims, BF16)

    def shape(*dims, dtype=F32):
        return jax.ShapeDtypeStruct(dims, dtype)

    pair = [dma((peers,))] * 2
    large = (3, 6, 7, 10, 13, 15)
    scratch = [pltpu.VMEM(args[i].shape, args[i].dtype) for i in large] + [dma((len(large),)), pltpu.VMEM((1, share, 128), F32)]
    scratch += [block(groups, peers, share, cols), block(groups, peers, share, 128), block(peers, rows, width)]
    scratch += Reduce.scratch(peers, rows, width)
    scratch += LineSum.scratch(groups, peers, share, own_cols) + [block(peers, share, own_cols)] * 2 + pair
    scratch += [block(*ffn.shape)] + pair
    scratch += [block(peers, groups, share, 128), block(groups, 1, share, 128)] + pair
    scratch += LineSum.scratch(groups, 1, share, 128) + LineSum.scratch(groups, *gd.shape[1:], steps=1)
    if shared:
        scratch += [block(groups, peers, share, quarter)] * 2 + LineSum.scratch(groups, peers, share, quarter)
        scratch += [block(peers, share, quarter)] * 2 + [dma((groups,)), dma((groups,))] + pair
    if aligned:
        half = block(peers // 2, share, width)
        scratch += [block(peers, share, width), half, half, block(groups, 1, share, width)] + pair
        scratch += LineSum.scratch(groups, 1, share, width)
    return pl.pallas_call(
        functools.partial(final_kernel, groups, peers, heads, own, shared, aligned),
        in_specs=[pl.BlockSpec(memory_space=pl.ANY) if i in large else vmem for i in range(len(args))],
        out_specs=[vmem] * 8,
        out_shape=[
            shape(rows, width), shape(*wa.shape), shape(share, heads), shape(1, share, width), shape(*wf.shape),
            shape(*gd.shape[1:]), shape(1, share), shape(1, share),
        ],
        scratch_shapes=scratch,
        compiler_params=pltpu.CompilerParams(
            collective_id=4, has_side_effects=True, vmem_limit_bytes=63 * 1024 * 1024
        ),
        name="final_sums",
    )(*args)


def hand_over_kernel(*refs):
    count = (len(refs) - 2) // 3
    given, out, held, sems = refs[:count], refs[count : 2 * count], refs[2 * count : 3 * count], refs[3 * count :]
    loads = [pltpu.make_async_copy(given[i], held[i], sems[0].at[i]) for i in range(count)]
    stores = [pltpu.make_async_copy(held[i], out[i], sems[1].at[i]) for i in range(count)]
    for load in loads:
        load.start()
    for load, store in zip(loads, stores):
        load.wait()
        store.start()
    for store in stores:
        store.wait()


def hand_over(*results):
    dma = pltpu.SemaphoreType.DMA((len(results),))
    hbm = pl.BlockSpec(memory_space=pl.ANY)
    return pl.pallas_call(
        hand_over_kernel,
        in_specs=[hbm] * len(results),
        out_specs=[hbm] * len(results),
        out_shape=[jax.ShapeDtypeStruct(x.shape, x.dtype) for x in results],
        scratch_shapes=[pltpu.VMEM(x.shape, x.dtype) for x in results] + [dma, dma],
        compiler_params=pltpu.CompilerParams(vmem_limit_bytes=63 * 1024 * 1024),
        name="hand_over",
    )(*results)


def shards(
    tokens, cotangent, doc_table, gain_attn, attn_in, beta_proj, attn_out, gain_ffn, ffn_in, ffn_down
):
    rows, width = tokens.shape
    heads = beta_proj.shape[1]
    h = width // heads
    groups, peers = lax.axis_size("dp"), lax.axis_size("blk")
    chips = peers // 2
    hc = -(-heads // chips)
    own, shared = hc // 2, hc % 2
    slots, padded = own + shared, hc * chips
    own_cols, quarter = own * 4 * h, shared * 2 * h
    share, units = attn_in.shape[0], ffn_down.shape[0]
    aligned = chips == groups and padded == heads
    me = lax.axis_index("blk")
    chip, core = me // 2, me % 2
    ext = jnp.concatenate([beta_proj.T, gain_attn[None], gain_ffn[None]], 0)
    ext_rows = -(-(heads + 2) // 16) * 16
    ext = jnp.pad(ext, ((0, ext_rows - heads - 2), (0, 128 - share)))
    w2, ffn_part, x_all, out_all, ext_all = gather_all(
        groups, peers, heads, own, shared, aligned, attn_in, ffn_in, tokens, attn_out, ext
    )
    w2 = w2.reshape(width, -1)
    x_all = x_all.reshape(peers * rows, width)
    out_rows = out_all.reshape(-1, width)
    if not aligned:
        out_rows = jnp.pad(out_rows, ((0, (padded - heads) * h), (0, 0)))
        out_rows = lax.dynamic_slice_in_dim(out_rows, chip * hc * h, hc * h, 0)
    first = chip * hc + core * (own + shared)
    my_heads = jnp.stack([first + s for s in range(own)] + [chip * hc + own] * shared).astype(jnp.int32)
    on = jnp.stack([jnp.int32(1)] * own + [1 - core] * shared).astype(jnp.int32)
    normed, dy_all, ext_all, ffn_all, proj, logits, attended, *saved = attention_forward(
        doc_table, on, my_heads, x_all, w2, ext_all, cotangent, ffn_part,
        groups, peers, heads, slots, rows,
    )
    dy_all = dy_all.reshape(peers * rows, width)
    residual, normed_two_all, down_all, ffn_far = branch(
        groups, peers, heads, own, shared, attended, out_rows, tokens, ext_all, ffn_down, ffn_all
    )
    normed_two_all = normed_two_all.reshape(peers * rows, width)
    down_slab = down_all.reshape(-1, width)

    dresidual, dbranch_all, out_part, grad_down, grad_ffn, up, down = feed_forward(
        groups, peers, heads, normed_two_all, ffn_all.reshape(groups, peers * share, -1), ffn_far.reshape(peers * share, -1),
        down_slab, dy_all, residual, ext_all,
    )
    dbranch_all = dbranch_all.reshape(peers * rows, width)
    dproj, dlogits, block_out, grad_ffn, down_up, down_dn = attention_backward(
        doc_table, on, my_heads, out_part, residual, grad_ffn, up, down, grad_down, dbranch_all, out_rows,
        proj, logits, saved, groups, peers, own, shared, rows,
    )
    grad_tokens, grad_attn_in, grad_beta, grad_attn_out, grad_ffn_in, grad_down, grad_gain_attn, grad_gain_ffn = final_sums(
        groups, peers, heads, own, shared, aligned,
        normed, dproj, dlogits, w2, ext_all, attended, dbranch_all, grad_ffn, tokens, dresidual, grad_down, down_up, down_dn,
        attn_in, jnp.pad(beta_proj, ((0, 0), (0, 128 - heads))), ffn_in,
        gain_attn[None], gain_ffn[None],
    )
    if aligned:
        grad_attn_out = grad_attn_out[0]
    else:
        gout = dot(attended, dbranch_all, TN)
        first = chip * hc + core * (own + shared)
        whole = jnp.zeros((padded * h, width), F32)
        whole = lax.dynamic_update_slice_in_dim(whole, gout, first * h, 0)[: heads * h]
        grad_attn_out = lax.psum_scatter(whole, ("dp", "blk"), scatter_dimension=0, tiled=True)
    block_out, grad_tokens, grad_gain_attn, grad_attn_in, grad_beta, grad_attn_out, grad_gain_ffn, grad_ffn_in, grad_down = hand_over(
        block_out, grad_tokens, grad_gain_attn, grad_attn_in, grad_beta, grad_attn_out,
        grad_gain_ffn, grad_ffn_in, grad_down.reshape(units, width),
    )
    return (
        block_out, grad_tokens, grad_gain_attn[0], grad_attn_in, grad_beta, grad_attn_out,
        grad_gain_ffn[0], grad_ffn_in, grad_down,
    )


def solution(mesh):
    split, vector = P(("dp", "blk"), None), P(("dp", "blk"))
    in_specs = (split, split, P("dp", None), vector, split, split, split, vector, split, split)
    out_specs = (split, split, vector, split, split, split, vector, split, split)
    return jax.shard_map(shards, mesh=mesh, in_specs=in_specs, out_specs=out_specs, check_vma=False)
```

```python
import functools

import jax
import jax.numpy as jnp
from jax import lax
from jax.experimental import pallas as pl
from jax.experimental.pallas import tpu as pltpu
from jax.sharding import PartitionSpec as P

EPSILON = 1e-06
F32 = jnp.float32
BF16 = jnp.bfloat16

NN = (((1,), (0,)), ((), ()))
NT = (((1,), (1,)), ((), ()))
TN = (((0,), (0,)), ((), ()))


def dot(a, b, dims=NN):
    return lax.dot_general(a, b, dims, preferred_element_type=F32)


def halves(x):
    high = x.astype(BF16)
    return high, (x - high.astype(F32)).astype(BF16)


def dot3(a, b, dims=NN):
    (ah, al), (bh, bl) = a, b
    ka, kb = dims[0][0][0], dims[0][1][0]
    deep, wide = ah.shape[ka], bh.shape[1 - kb]
    if deep <= 128:
        left = jnp.concatenate([ah, al], ka)
        if wide <= 128:
            below = jnp.concatenate([bh, jnp.zeros_like(bh)], 1 - kb)
            both_parts = dot(left, jnp.concatenate([jnp.concatenate([bh, bl], 1 - kb), below], kb), dims)
            return both_parts[:, :wide] + both_parts[:, wide:]
        return dot(left, jnp.concatenate([bh, bh], kb), dims) + dot(ah, bl, dims)
    if wide <= 128:
        both_parts = dot(ah, jnp.concatenate([bh, bl], 1 - kb), dims)
        return both_parts[:, :wide] + (both_parts[:, wide:] + dot(al, bh, dims))
    return dot(ah, bh, dims) + (dot(ah, bl, dims) + dot(al, bh, dims))


def both(parts, axis):
    return tuple(jnp.concatenate(p, axis) for p in zip(*parts))


def rms_norm(values, gain):
    return values * lax.rsqrt(jnp.mean(values * values, axis=-1, keepdims=True) + EPSILON) * gain


def rms_pull(values, gain, grad):
    scale = lax.rsqrt(jnp.mean(values * values, axis=-1, keepdims=True) + EPSILON)
    inner = grad * gain
    along = jnp.mean(inner * values, axis=-1, keepdims=True)
    return scale * inner - values * (scale * scale * scale) * along


def lanes(n):
    return lax.broadcasted_iota(jnp.int32, (n, n), 1)


def rows_of(n):
    return lax.broadcasted_iota(jnp.int32, (n, n), 0)


def inverses(grams, betas, span):
    r, c = rows_of(span), lanes(span)
    eye = r == c
    outs = []
    pair = (c + 1 == r) & (r % 2 == 1)
    for gram, beta in zip(grams, betas):
        below = jnp.where(pair, gram, 0.0) * beta * beta.T
        outs.append(jnp.where(eye, beta, 0.0) - below)
    size = 2
    while size < span:
        part = (r // (2 * size) == c // (2 * size)) & ((r // size) % 2 == 1) & ((c // size) % 2 == 0)
        sides = [halves(x) for x in outs]
        steps = [dot3(halves(jnp.where(part, g, 0.0)), x) for g, x in zip(grams, sides)]
        outs = [x - dot3(s, halves(t)) for x, s, t in zip(outs, sides, steps)]
        size *= 2
    return outs


MESH = pl.DeviceIdType.MESH


def fetch(pairs, sems):
    copies = [pltpu.make_async_copy(src, dst, sems.at[i]) for i, (src, dst) in enumerate(pairs)]
    for copy in copies:
        copy.start()
    return copies


def send(src, dst, send_sem, recv_sem, **device):
    return pltpu.make_async_remote_copy(
        src_ref=src, dst_ref=dst, send_sem=send_sem, recv_sem=recv_sem, device_id=device, device_id_type=MESH
    )


def greet(peers, groups=0):
    barrier = pltpu.get_barrier_semaphore()
    me = lax.axis_index("blk")
    for k in range(1, peers):
        pl.semaphore_signal(barrier, inc=1, device_id={"blk": (me + k) % peers}, device_id_type=MESH)
    if groups:
        at = lax.axis_index("dp")

        @pl.when(at + 1 < groups)
        def _():
            pl.semaphore_signal(barrier, inc=1, device_id={"dp": at + 1}, device_id_type=MESH)

        @pl.when(at > 0)
        def _():
            pl.semaphore_signal(barrier, inc=1, device_id={"dp": at - 1}, device_id_type=MESH)

        @pl.when((at > 0) & (at + 1 < groups))
        def _():
            pl.semaphore_wait(barrier, peers + 1)

        @pl.when((at == 0) | (at + 1 == groups))
        def _():
            pl.semaphore_wait(barrier, peers)
    else:
        pl.semaphore_wait(barrier, peers - 1)


def square(chips, chip):
    return chip + 1 - 2 * (chip % 2), (chip + 2) % chips, chips - 1 - chip


class Spread:
    def __init__(self, peers, source, pick, sems, recvs, halved=False):
        me = lax.axis_index("blk")
        self.chips = peers // 2
        core, chip = me % 2, me // 2
        sibling = me + 1 - 2 * core
        self.halved = halved and self.chips == 4

        def copy(i, src, dst, to):
            return send(src, dst, sems.at[i], recvs.at[i], blk=to)

        self.first = [copy(0, source(chip), pick(me), sibling)]
        self.second, self.cross = [], []
        if self.halved:
            x, y, far = (2 * c + core for c in square(self.chips, chip))
            half = pick(me).shape[0] // 2
            low, high = pl.ds(0, half), pl.ds(half, half)
            for i, to in enumerate((x, y)):
                self.first.append(copy(1 + i, source(to // 2), pick(me), to))
                self.second.append(copy(3 + i, pick(to), pick(to), sibling))
            self.cross = [
                copy(5, pick(x).at[low], pick(x).at[low], y),
                copy(6, pick(y).at[high], pick(y).at[high], x),
            ]
            self.last = [
                copy(7 + i, pick(far).at[rows], pick(far).at[rows], sibling) for i, rows in enumerate((low, high))
            ]
            return
        for k in range(1, self.chips):
            to = (me + 2 * k) % peers
            self.first.append(copy(k, source(to // 2), pick(me), to))
            origin = pick((me + peers - 2 * k) % peers)
            self.second.append(copy(self.chips + k - 1, origin, origin, sibling))

    def start(self):
        for copy in self.first[1:] + self.first[:1]:
            copy.start()

    def forward(self):
        for i, (copy, onward) in enumerate(zip(self.first[1:], self.second)):
            copy.wait_recv()
            if self.halved:
                self.cross[i].start()
            onward.start()
        if self.halved:
            for copy, onward in zip(self.cross, self.last):
                copy.wait_recv()
                onward.start()

    def finish(self):
        for copy in self.first + self.cross:
            copy.wait_send()
        self.first[0].wait_recv()
        for copy in self.second + (self.last if self.halved else []):
            copy.wait()


class Line:
    def __init__(self, groups, pick, sems, recvs):
        self.groups, self.pick, self.sems, self.recvs = groups, pick, sems, recvs
        self.at = lax.axis_index("dp")

    def up(self, step, to, block):
        i = 2 * (step - 1)
        return send(self.pick(block), self.pick(block), self.sems.at[i], self.recvs.at[i], dp=to)

    def down(self, step, to, block):
        i = 2 * (step - 1) + 1
        return send(self.pick(block), self.pick(block), self.sems.at[i], self.recvs.at[i], dp=to)

    def start(self, step):
        at, n = self.at, self.groups

        @pl.when((at + 1 < n) & (at - (step - 1) >= 0))
        def _():
            self.up(step, at + 1, at - (step - 1)).start()

        @pl.when((at - 1 >= 0) & (at + (step - 1) < n))
        def _():
            self.down(step, at - 1, at + (step - 1)).start()

    def arrive(self, step, then=None):
        at, n = self.at, self.groups

        @pl.when(at - step >= 0)
        def _():
            self.up(step, at - 1, at - step).wait_recv()
            if then is not None:
                then(at - step).start()

        @pl.when(at + step < n)
        def _():
            self.down(step, at + 1, at + step).wait_recv()
            if then is not None:
                then(at + step).start()

    def finish(self, steps):
        at, n = self.at, self.groups
        for step in steps:

            @pl.when((at + 1 < n) & (at - (step - 1) >= 0))
            def _():
                self.up(step, at + 1, at - (step - 1)).wait_send()

            @pl.when((at - 1 >= 0) & (at + (step - 1) < n))
            def _():
                self.down(step, at - 1, at + (step - 1)).wait_send()


class LineSum:
    def __init__(self, groups, pick, up_got, dn_got, up_out, dn_out, sems, recvs, arrived=None, base=0):
        self.n, self.pick, self.arrived, self.base = groups, pick, arrived, base
        self.up_got, self.dn_got, self.up_out, self.dn_out = up_got, dn_got, up_out, dn_out
        self.sems, self.recvs = sems, recvs
        self.at = lax.axis_index("dp")

    @staticmethod
    def scratch(groups, *block, steps=None):
        hop = pltpu.VMEM((steps or groups - 1, *block), BF16)
        return [hop] * 4 + [pltpu.SemaphoreType.DMA((2 * groups,))] * 2

    def up(self, i, src, to):
        return send(src, self.up_got.at[i - self.base], self.sems.at[2 * i], self.recvs.at[2 * i], dp=to)

    def down(self, i, src, to):
        return send(src, self.dn_got.at[i - self.base], self.sems.at[2 * i + 1], self.recvs.at[2 * i + 1], dp=to)

    def add(self, out, one, other):
        def body(j, carry):
            out[j] = (one[j].astype(F32) + other[j].astype(F32)).astype(out.dtype)
            return carry

        lax.fori_loop(0, out.shape[0], body, 0)

    def step(self, i):
        at, n = self.at, self.n
        far = n - 1 - i

        @pl.when((at + far < n) & (at == 0))
        def _():
            self.up(i, self.pick(far), at + 1).start()

        @pl.when((at - far >= 0) & (at == n - 1))
        def _():
            self.down(i, self.pick(-far), at - 1).start()

        if i > 0:

            @pl.when((at + far < n) & (at > 0))
            def _():
                if self.arrived is None:
                    self.up(i - 1, self.up_out.at[max(i - 1 - self.base, 0)], at - 1).wait_recv()
                before = self.up_got.at[max(i - 1 - self.base, 0)] if self.arrived is None else self.arrived[0]
                self.add(self.up_out.at[i - self.base], self.pick(far), before)
                self.up(i, self.up_out.at[i - self.base], at + 1).start()

            @pl.when((at - far >= 0) & (at < n - 1))
            def _():
                if self.arrived is None:
                    self.down(i - 1, self.dn_out.at[max(i - 1 - self.base, 0)], at + 1).wait_recv()
                before = self.dn_got.at[max(i - 1 - self.base, 0)] if self.arrived is None else self.arrived[1]
                self.add(self.dn_out.at[i - self.base], self.pick(-far), before)
                self.down(i, self.dn_out.at[i - self.base], at - 1).start()

    def arrive(self, i, up, down):
        at, n = self.at, self.n
        far = n - 1 - i
        some_up, some_down = (at > 0) & (at - 1 + far < n), (at < n - 1) & (at + 1 - far >= 0)

        @pl.when(some_up)
        def _():
            self.up(i, self.up_out.at[i - self.base], at - 1).wait_recv()
            up[...] = self.up_got[i - self.base]

        @pl.when(some_down)
        def _():
            self.down(i, self.dn_out.at[i - self.base], at + 1).wait_recv()
            down[...] = self.dn_got[i - self.base]

        @pl.when(jnp.logical_not(some_up))
        def _():
            up[...] = jnp.zeros_like(up)

        @pl.when(jnp.logical_not(some_down))
        def _():
            down[...] = jnp.zeros_like(down)

    def total(self, out):
        at, n, i = self.at, self.n, self.n - 2

        @pl.when(at > 0)
        def _():
            self.up(i, self.up_out.at[i - self.base], at - 1).wait_recv()
            self.add(out, self.pick(0), self.up_got.at[i - self.base])

        @pl.when(at == 0)
        def _():
            self.down(i, self.dn_out.at[i - self.base], at + 1).wait_recv()
            self.add(out, self.pick(0), self.dn_got.at[i - self.base])

        @pl.when((at > 0) & (at < n - 1))
        def _():
            self.down(i, self.dn_out.at[i - self.base], at + 1).wait_recv()
            self.add(out, out, self.dn_got.at[i - self.base])

    def finish(self, steps=None):
        at, n = self.at, self.n
        for i in range(n - 1) if steps is None else steps:
            far = n - 1 - i

            @pl.when(at + far < n)
            def _():
                self.up(i, self.up_out.at[i - self.base], at + 1).wait_send()

            @pl.when(at - far >= 0)
            def _():
                self.down(i, self.dn_out.at[i - self.base], at - 1).wait_send()


class Reduce:
    def __init__(self, peers, part, half, mine, got, sems, recvs, place=None, halved=False, kept=None):
        me = lax.axis_index("blk")
        self.chips = peers // 2
        self.core, self.chip = me % 2, me // 2
        sibling = me + 1 - 2 * self.core
        self.part, self.half, self.mine, self.got, self.kept = part, half, mine, got, kept
        self.halved = halved and self.chips == 4

        def copy(i, src, dst, to):
            return send(src, dst, sems.at[i], recvs.at[i], blk=to)

        if self.halved:
            self.to = [self.chip, *square(self.chips, self.chip)]
        else:
            self.to = [(self.chip + k) % self.chips for k in range(self.chips)]
        self.inner = [copy(k, part.at[2 * to + 1 - self.core], half.at[k], sibling) for k, to in enumerate(self.to)]
        self.outer = []
        if self.halved:
            x, y, far = (2 * c + self.core for c in self.to[1:])
            middle = mine.shape[1] // 2
            self.low, self.high = pl.ds(0, middle), pl.ds(middle, middle)
            self.cross = [
                copy(6, mine.at[3, self.low], got.at[3, self.low], x),
                copy(7, mine.at[3, self.high], got.at[3, self.high], y),
            ]
            self.outer = [copy(4, mine.at[1], got.at[1], x), copy(5, mine.at[2], got.at[2], y)]
            return
        for k in range(1, self.chips):
            arrival = got.at[k] if place is None else place
            self.outer.append(copy(self.chips + k, mine.at[k], arrival, 2 * self.to[k] + self.core))

    def order(self):
        return list(range(self.chips - 1, -1, -1)) if self.halved else list(range(1, self.chips)) + [0]

    def start(self):
        for k in self.order():
            self.inner[k].start()

    def chip_sums(self):
        for k in self.order():
            self.inner[k].wait_recv()
            kept = self.part[2 * self.to[k] + self.core] if self.kept is None else self.kept[k]
            both_cores = kept.astype(F32) + self.half[k].astype(F32)
            self.mine[k] = both_cores.astype(BF16)
            if self.halved:
                if k == 3:
                    for copy in self.cross:
                        copy.start()
            elif k > 0:
                self.outer[k - 1].start()

    def pair(self):
        self.chip_sums()
        self.cross_sums()

    def cross_sums(self):
        if self.halved:
            for copy, rows, k in ((self.cross[0], self.low, 2), (self.cross[1], self.high, 1)):
                copy.wait_recv()
                summed = self.mine[k, rows].astype(F32) + self.got[3, rows].astype(F32)
                self.mine[k, rows] = summed.astype(BF16)
                self.outer[k - 1].start()

    def total(self):
        total = self.mine[0].astype(F32)
        for k, copy in enumerate(self.outer):
            copy.wait_recv()
            total = total + self.got[k + 1].astype(F32)
        return total

    def finish(self):
        for copy in self.inner + self.outer + (self.cross if self.halved else []):
            copy.wait_send()

    @staticmethod
    def scratch(peers, rows, width):
        block = pltpu.VMEM((peers // 2, rows, width), BF16)
        return [block, block, block, pltpu.SemaphoreType.DMA((peers,)), pltpu.SemaphoreType.DMA((peers,))]


def fanout(peers, source, dst, sems, recvs):
    me = lax.axis_index("blk")
    copies = []
    for k in range(1, peers):
        p = (me + k) % peers
        copies.append(send(source(p), dst(p), sems.at[k], recvs.at[k], blk=p))
    return copies


def attention_forward_kernel(
    groups, peers, heads, share, spans, span, doc_ref, on_ref, head_ref, x_all, w_ref, pieces_ref, dy_ref, ffn_ref,
    norm_all, dy_all, ext_ref, ffn_all, proj_ref, logit_ref,
    low_ref, att_ref, sum_ref, a1_ref, g_ref, y_ref, e0_ref, qp_ref, m_ref, kts_ref,
    kpt_ref, kt_ref, x_ref, norm_ref, keep_sem, x_sem, d_s, d_r, l_s, l_r,
):
    h = span
    scale = h ** -0.5
    slot, me = pl.program_id(0), lax.axis_index("blk")
    tall = 2 * span

    def dy_copies():
        keep = pltpu.make_async_copy(dy_ref, dy_all.at[me], keep_sem.at[0])
        return keep, Spread(peers, lambda c: dy_ref, lambda b: dy_all.at[b], d_s, d_r, True)

    at_dp = lax.axis_index("dp")
    ffn_line = Line(groups, lambda d: ffn_all.at[d], l_s, l_r)

    @pl.when(slot == 0)
    def _():
        own_ffn = pltpu.make_async_copy(ffn_ref, ffn_all.at[at_dp], keep_sem.at[1])
        own_ffn.start()
        loads = [
            pltpu.make_async_copy(x_all.at[pl.ds(i * tall, tall)], x_ref.at[pl.ds(i * tall, tall)], x_sem.at[i])
            for i in range(spans // 2)
        ]
        for copy in loads:
            copy.start()
        greet(peers, groups)
        keep, spread = dy_copies()
        keep.start()
        spread.start()
        own_ffn.wait()
        ffn_line.start(1)
        lanes_in, slab = peers * 128, peers * share
        source = lax.broadcasted_iota(jnp.int32, (lanes_in, slab), 0)
        target = lax.broadcasted_iota(jnp.int32, (lanes_in, slab), 1)
        place = (source // 128 * share + source % 128 == target) & (source % 128 < share)
        place = jnp.where(place, 1.0, 0.0).astype(BF16)
        for d in range(groups):
            pieces = jnp.concatenate([pieces_ref[d, b] for b in range(peers)], 1)
            ext_ref[:, d * slab : (d + 1) * slab] = dot(pieces, place).astype(BF16)
        gain = ext_ref[...].astype(F32)[heads : heads + 1]
        for i, copy in enumerate(loads):
            copy.wait()
            rows = pl.ds(i * tall, tall)
            norm_ref[rows, :] = rms_norm(x_ref[rows, :].astype(F32), gain).astype(BF16)
        pltpu.make_async_copy(norm_ref, norm_all, keep_sem.at[2]).start()

    def project(i, carry):
        rows = pl.ds(pl.multiple_of(i * tall, tall), tall)
        normed = norm_ref[rows, :]
        proj_ref[rows, :] = dot(normed, w_ref[...])
        every = dot(normed, ext_ref[...], NT)
        lane = lax.broadcasted_iota(jnp.int32, every.shape, 1)
        mine = jnp.sum(jnp.where(lane == head_ref[slot], every, 0.0), -1, keepdims=True)
        logit_ref[rows, :] = jnp.broadcast_to(mine, (tall, h))
        return carry

    lax.fori_loop(0, spans // 2, project, 0)
    r, c = rows_of(span), lanes(span)
    lower, strict, eye = c <= r, c < r, (c == r).astype(F32)
    at = [pl.ds(n * span, span) for n in range(spans)]
    group = 4
    for first in range(0, spans, group):
        members = range(first, min(first + group, spans))
        grams, betas, kept = [], [], []
        for n in members:
            q = proj_ref[at[n], 0:h]
            k = proj_ref[at[n], h : 2 * h]
            d = proj_ref[at[n], 3 * h : 4 * h]
            w = d * lax.rsqrt(jnp.sum(d * d, -1, keepdims=True) + EPSILON)
            qs, ks, ws = halves(q), halves(k), halves(w)
            z = dot3(both((qs, ws), 0), both((ws, ks), 0), NT)
            a1 = jnp.where(lower, z[:span, :span], 0.0)
            a1_ref[at[n], :] = a1
            b1 = jnp.where(strict, z[span:, span:], 0.0)
            grams.append(jnp.where(strict, z[span:, :span], 0.0))
            betas.append(2.0 / (1.0 + jnp.exp(-logit_ref[at[n], :])))
            kept.append((q, k, ws, halves(a1), halves(b1), z[:span, span:]))
        solved = inverses(grams, betas, span)
        for n, g, (q, k, ws, a1s, b1s, qk) in zip(members, solved, kept):
            g_ref[at[n], :] = g
            y = dot3(halves(g), both((ws, b1s), 1))
            y_ref[at[n], :] = y
            ys = halves(y)
            t = dot3(a1s, ys)
            u = dot3(ws, ys, TN)
            qp_ref[at[n], :] = (q - t[:, :h]).astype(BF16)
            local = (qk - t[:, h:]) * scale
            e0_ref[at[n], :] = jnp.where(lower, jnp.exp(local), 0.0)
            m_ref[at[n], :] = eye - u[:, :h]
            kpt_ref[:, at[n]] = k.T - u[:, h:]
    for n in range(spans):
        w = n * span
        e0 = e0_ref[at[n], :]
        total = jnp.sum(e0, -1, keepdims=True)
        numer = dot(e0.astype(BF16), proj_ref[at[n], 2 * h : 3 * h].astype(BF16))
        if n > 0:
            kt = kt_ref[:, :w]
            kts = halves(kt)
            kts_ref[0, n, :, :w] = kts[0]
            block = jnp.exp(dot(qp_ref[at[n], :], kts[0]) * scale)
            block = jnp.concatenate(
                [jnp.where(doc_ref[0, j] == doc_ref[0, n], block[:, j * span : (j + 1) * span], 0.0) for j in range(n)], 1
            )
            total = total + jnp.sum(block, -1, keepdims=True)
            numer = numer + dot(block.astype(BF16), proj_ref[:w, 2 * h : 3 * h].astype(BF16))
            if n < spans - 1:
                kt_ref[:, :w] = dot3(halves(m_ref[at[n], :]), kts)
        if n < spans - 1:
            kt_ref[:, at[n]] = kpt_ref[:, at[n]]
        attended = numer / total
        att_ref[at[n], :] = attended
        low_ref[at[n], :] = jnp.where(on_ref[slot] > 0, attended, 0.0).astype(BF16)
        sum_ref[at[n], :] = jnp.broadcast_to(total, (span, h))

    @pl.when(slot == 0)
    def _():
        dy_copies()[1].forward()
        ffn_line.arrive(1)
        ffn_line.start(2)

    @pl.when(slot == pl.num_programs(0) - 1)
    def _():
        keep, spread = dy_copies()
        for step in range(3, groups - 1):
            ffn_line.arrive(step - 1)
            ffn_line.start(step)
        spread.finish()
        keep.wait()
        pltpu.make_async_copy(norm_ref, norm_all, keep_sem.at[2]).wait()
        ffn_line.arrive(groups - 2)
        ffn_line.finish(range(1, groups - 1))


def attention_backward_kernel(
    groups, peers, own, shared, spans, span, doc_ref, on_ref, head_ref, outp_all, res_ref, gi_all, up_all, dn_all, gd_all, db_all, out_ref,
    proj_ref, logit_ref, att_ref, sum_ref, a1_ref, g_ref, y_ref, e0_ref, qp_ref, m_ref, kts_ref,
    dproj_ref, dlogit_ref, block_ref, rows_ref, dup_ref, ddn_ref,
    gkt_ref, dvt_ref, dqp_ref, dm_ref, dkpt_ref, ds_ref, datt_ref, half, mine, got, r_s, r_r, gi_ref, local,
    kept, up_ref, dn_ref, gd_ref, db_ref,
    ug, dg, uo, do, l_s, l_r, vg, wg, vo, wo, m_s, m_r,
):
    h = span
    scale = h ** -0.5
    r, c = rows_of(span), lanes(span)
    lower, strict, same = c <= r, c < r, c == r
    at = [pl.ds(n * span, span) for n in range(spans)]
    slot = pl.program_id(0)

    def reduce():
        return Reduce(peers, outp_all, half, mine, got, r_s, r_r, halved=True, kept=kept)

    place = {1: 0, -1: 1, 0: 2}
    line = LineSum(groups, lambda r: gi_ref.at[place[r]], ug, dg, uo, do, l_s, l_r, (up_ref, dn_ref), groups - 2)
    at_dp = line.at
    down = LineSum(groups, lambda r: gd_ref.at[at_dp + r], vg, wg, vo, wo, m_s, m_r)

    @pl.when(slot == 0)
    def _():
        core = lax.axis_index("blk") % 2
        sums = reduce()
        loads = fetch(
            [(gi_all.at[(at_dp + groups + r) % groups], gi_ref.at[i]) for r, i in place.items()]
            + [(up_all, up_ref), (dn_all, dn_ref), (gd_all, gd_ref), (db_all, db_ref)]
            + [(outp_all.at[2 * to + core], kept.at[k]) for k, to in enumerate(sums.to)],
            local,
        )
        greet(peers, groups)
        sums.start()
        for copy in loads[:5]:
            copy.wait()
        line.step(groups - 2)
        loads[5].wait()
        down.step(0)
        for copy in loads[6:]:
            copy.wait()

    which = jnp.where(slot < own, lax.axis_index("blk") % 2 * (own + shared) + slot, own)
    out_at = pl.multiple_of(which * h, 128)

    def pull_back(i, carry):
        rows = pl.ds(pl.multiple_of(i * 2 * span, span), 2 * span)
        datt_ref[rows, :] = dot(db_ref[rows, :], out_ref[pl.ds(out_at, h), :], NT)
        return carry

    lax.fori_loop(0, spans // 2, pull_back, 0)
    dvt_ref[...] = jnp.zeros_like(dvt_ref)
    for n in reversed(range(spans)):
        w = n * span
        last = n == spans - 1
        datt, total = jnp.where(on_ref[slot] > 0, datt_ref[at[n], :], 0.0), sum_ref[at[n], :]
        da = (datt / total).astype(BF16)
        delta = jnp.sum(datt * att_ref[at[n], :], -1, keepdims=True) / total
        e0 = e0_ref[at[n], :]
        mix = dot(da, proj_ref[at[n], 2 * h : 3 * h].astype(BF16), NT) - delta
        ds_ref[at[n], :] = (e0 * mix).astype(BF16).astype(F32) * scale
        dvt_ref[:, at[n]] += dot(da, e0.astype(BF16), TN)
        if n == 0:
            dqp_ref[at[n], :] = jnp.zeros((span, h), F32)
            dm_ref[at[n], :] = jnp.zeros((h, h), F32)
            dkpt_ref[:, at[n]] = gkt_ref[:, at[n]] if not last else jnp.zeros((h, span), F32)
            continue
        keys = kts_ref[0, n, :, :w]
        qp = qp_ref[at[n], :]
        block = jnp.exp(dot(qp, keys) * scale)
        block = jnp.concatenate(
            [jnp.where(doc_ref[0, j] == doc_ref[0, n], block[:, j * span : (j + 1) * span], 0.0) for j in range(n)], 1
        )
        wide = jnp.concatenate([delta] * n, 1)
        mix = dot(da, proj_ref[:w, 2 * h : 3 * h].astype(BF16), NT) - wide
        ds = (block * mix).astype(BF16)
        dqp_ref[at[n], :] = dot(ds, keys, NT) * scale
        pulled = dot(qp, ds, TN) * scale
        dvt_ref[:, :w] += dot(da, block.astype(BF16), TN)
        if last:
            dm_ref[at[n], :] = jnp.zeros((h, h), F32)
            dkpt_ref[:, at[n]] = jnp.zeros((h, span), F32)
            gkt_ref[:, :w] = pulled
        else:
            dkpt_ref[:, at[n]] = gkt_ref[:, at[n]]
            gs = halves(gkt_ref[:, :w])
            dm_ref[at[n], :] = dot(gs[0], keys, NT) + dot(gs[1], keys, NT)
            gkt_ref[:, :w] = pulled + dot3(halves(m_ref[at[n], :]), gs, TN)

    @pl.when(slot == 0)
    def _():
        reduce().pair()

    for n in range(spans):
        q = proj_ref[at[n], 0:h]
        k = proj_ref[at[n], h : 2 * h]
        d = proj_ref[at[n], 3 * h : 4 * h]
        inv = lax.rsqrt(jnp.sum(d * d, -1, keepdims=True) + EPSILON)
        w = d * inv
        beta = 2.0 / (1.0 + jnp.exp(-logit_ref[at[n], :]))
        qs, ks, ws = halves(q), halves(k), halves(w)
        dqp, ds, dkpt = dqp_ref[at[n], :], ds_ref[at[n], :], dkpt_ref[:, at[n]]
        ys = halves(y_ref[at[n], :])
        left = both((halves(dqp), halves(ds)), 1)
        mid = both((halves(dm_ref[at[n], :]), halves(dkpt)), 1)
        da1 = jnp.where(lower, -dot3(left, ys, NT), 0.0)
        dy = dot3(halves(a1_ref[at[n], :]), left, TN) + dot3(ws, mid)
        dx = -dot3(halves(g_ref[at[n], :]), halves(dy), TN)
        dl = -dot3(halves(dx), ys, NT)
        dw = dx[:, :h] - dot3(ys, mid, NT)
        pull = jnp.sum(jnp.where(same, dl, 0.0), -1, keepdims=True)
        dlogit = -pull * (1.0 - 0.5 * beta) / jnp.maximum(beta, 1e-30)
        before = jnp.where(slot == 0, 0.0, dlogit_ref[at[n], :].astype(F32))
        dlogit_ref[at[n], :] = jnp.where(c == head_ref[slot], dlogit, before).astype(BF16)
        dz = jnp.concatenate(
            [
                jnp.concatenate([da1, ds], 1),
                jnp.concatenate([jnp.where(strict, dl, 0.0), jnp.where(strict, dx[:, h:], 0.0)], 1),
            ],
            0,
        )
        dzs = halves(dz)
        dp = dot3(dzs, both((ws, ks), 0))
        dr = dot3(dzs, both((qs, ws), 0), TN)
        dw = dw + dp[span:] + dr[:span]
        dproj_ref[at[n], 0:h] = (dqp + dp[:span]).astype(BF16)
        dproj_ref[at[n], h : 2 * h] = (dkpt.T + dr[span:]).astype(BF16)
        dproj_ref[at[n], 2 * h : 3 * h] = dvt_ref[:, at[n]].T.astype(BF16)
        dproj_ref[at[n], 3 * h : 4 * h] = (inv * (dw - w * jnp.sum(dw * w, -1, keepdims=True))).astype(BF16)

    @pl.when(slot == 0)
    def _():
        for i in range(1, groups - 2):
            down.step(i)

    @pl.when(slot == pl.num_programs(0) - 1)
    def _():
        last = reduce()
        block_ref[...] = (res_ref[...] + last.total()).astype(BF16)
        last.finish()
        line.total(rows_ref)
        line.finish([groups - 2])
        down.arrive(groups - 3, dup_ref, ddn_ref)
        down.finish(range(groups - 2))


def head_specs(rows, h, spans, slots):
    mode = {"pipeline_mode": pl.Buffered(1)} if slots == 1 else {}
    one = pl.BlockSpec((rows, h), lambda s: (0, s), **mode)
    two = pl.BlockSpec((rows, 2 * h), lambda s: (0, s), **mode)
    four = pl.BlockSpec((rows, 4 * h), lambda s: (0, s), **mode)
    keys = pl.BlockSpec((1, spans, h, rows), lambda s: (s, 0, 0, 0), **mode)
    docs = pl.BlockSpec(memory_space=pltpu.SMEM)
    return one, two, four, keys, docs


def attention_forward(docs, on, my_heads, x_all, w, ext, dy, ffn, groups, peers, heads, slots, span):
    rows, width = x_all.shape
    spans, h = rows // span, span
    one, two, four, keys, smem = head_specs(rows, h, spans, slots)
    dma = pltpu.SemaphoreType.DMA
    vmem, hbm = pl.BlockSpec(memory_space=pltpu.VMEM), pl.BlockSpec(memory_space=pl.ANY)
    ext_rows = ext.shape[2]

    def full(columns, dtype=F32):
        return jax.ShapeDtypeStruct((rows, slots * columns), dtype)

    return pl.pallas_call(
        functools.partial(attention_forward_kernel, groups, peers, heads, width // (groups * peers), spans, span),
        grid=(slots,),
        in_specs=[smem, smem, smem, hbm, pl.BlockSpec((width, 4 * h), lambda s: (0, s)), vmem, vmem, vmem],
        out_specs=[
            hbm, hbm, pl.BlockSpec((ext_rows, width), lambda s: (0, 0)), hbm,
            four, one, one, one, one, one, one, two, one, one, one, keys,
        ],
        out_shape=[
            jax.ShapeDtypeStruct((rows, width), BF16), jax.ShapeDtypeStruct((peers, *dy.shape), BF16),
            jax.ShapeDtypeStruct((ext_rows, width), BF16), jax.ShapeDtypeStruct((groups, *ffn.shape), BF16),
            full(4 * h), full(h),
            full(h, BF16), full(h), full(h), full(h), full(h), full(2 * h), full(h), full(h, BF16), full(h),
            jax.ShapeDtypeStruct((slots, spans, h, rows), BF16),
        ],
        scratch_shapes=[
            pltpu.VMEM((h, rows), F32), pltpu.VMEM((h, rows), F32), pltpu.VMEM((rows, width), BF16),
            pltpu.VMEM((rows, width), BF16), dma((3,)), dma((spans // 2,)), dma((2 * peers,)), dma((2 * peers,)), dma((2 * groups,)), dma((2 * groups,)),
        ],
        compiler_params=pltpu.CompilerParams(
            collective_id=5, has_side_effects=True, vmem_limit_bytes=63 * 1024 * 1024
        ),
        name="attention_forward",
    )(docs, on, my_heads, x_all, w, ext, dy, ffn)


def attention_backward(
    docs, on, heads, outp, res, gi, up, dn, gd, db_all, out_rows, proj, logits, saved, groups, peers, own, shared, span
):
    rows = proj.shape[0]
    slots = own + shared
    spans, h = rows // span, span
    one, two, four, keys, smem = head_specs(rows, h, spans, slots)
    wide, tall = pltpu.VMEM((h, rows), F32), pltpu.VMEM((rows, h), F32)
    vmem, hbm = pl.BlockSpec(memory_space=pltpu.VMEM), pl.BlockSpec(memory_space=pl.ANY)
    block = pl.BlockSpec(gd.shape[1:], lambda s: (0, 0, 0))
    return pl.pallas_call(
        functools.partial(attention_backward_kernel, groups, peers, own, shared, spans, span),
        grid=(slots,),
        in_specs=[smem, smem, smem, hbm, vmem] + [hbm] * 5 + [vmem]
        + [four, one, one, one, one, one, two, one, one, one, keys],
        out_specs=[
            four, pl.BlockSpec((rows, h), lambda s: (0, 0)), pl.BlockSpec(res.shape, lambda s: (0, 0)),
            pl.BlockSpec(up.shape, lambda s: (0, 0, 0)), block, block,
        ],
        out_shape=[
            jax.ShapeDtypeStruct((rows, slots * 4 * h), BF16),
            jax.ShapeDtypeStruct((rows, h), BF16),
            jax.ShapeDtypeStruct(res.shape, BF16),
            jax.ShapeDtypeStruct(up.shape, BF16),
            jax.ShapeDtypeStruct(gd.shape[1:], BF16),
            jax.ShapeDtypeStruct(gd.shape[1:], BF16),
        ],
        scratch_shapes=[wide, wide, tall, tall, wide, tall, tall] + Reduce.scratch(peers, *res.shape)
        + [pltpu.VMEM((3, *up.shape), BF16), pltpu.SemaphoreType.DMA((7 + peers // 2,))]
        + [pltpu.VMEM((peers // 2, *res.shape), BF16)]
        + [pltpu.VMEM(x.shape, BF16) for x in (up, dn, gd, db_all)]
        + LineSum.scratch(groups, *up.shape, steps=1) + LineSum.scratch(groups, *gd.shape[1:], steps=groups - 2),
        compiler_params=pltpu.CompilerParams(
            collective_id=6, has_side_effects=True, vmem_limit_bytes=62 * 1024 * 1024
        ),
        name="attention_backward",
    )(docs, on, heads, outp, res, gi, up, dn, gd, db_all, out_rows, proj, logits, *saved)


def gather_kernel(
    groups, peers, heads, own, shared, aligned, attn_ref, gate_ref, tok_ref, out_ref, ext_ref, down_ref,
    w_all, ffn_all, tok_all, out_all, ext_all, down_all, own_ref, mix_ref, ffn_ref, out_z,
    local, a_s, a_r, m_s, m_r, f_s, f_r, t_s, t_r, o_s, o_r, e_s, e_r, s_s, s_r,
    al_s, al_r, ml_s, ml_r, ol_s, ol_r, el_s, el_r, dl_s, dl_r,
):
    me, at = lax.axis_index("blk"), lax.axis_index("dp")
    core = me % 2
    sibling = me + 1 - 2 * core
    h = attn_ref.shape[1] // (4 * heads)
    width = 4 * h * heads // 4
    own_cols, quarter = own * 4 * h, shared * 2 * h
    units = gate_ref.shape[1] // (2 * groups * peers)
    for p in range(peers):
        first = (p // 2) * (2 * own + shared)
        for i in range(own):
            head = first + (p % 2) * (own + shared) + i
            for part in range(4):
                to = (4 * i + part) * h
                if head < heads:
                    own_ref[p, :, to : to + h] = attn_ref[:, part * width + head * h : part * width + (head + 1) * h]
                else:
                    own_ref[p, :, to : to + h] = jnp.zeros((own_ref.shape[1], h), BF16)
        for i in range(2 * shared):
            at_col = (2 * (p % 2) + i) * width + (first + own) * h
            mix_ref[p, :, i * h : (i + 1) * h] = attn_ref[:, at_col : at_col + h]

    def side(device):
        return pl.ds(pl.multiple_of(own_cols + quarter * (device % 2), 128), quarter)

    keeps = [
        pltpu.make_async_copy(ext_ref, ext_all.at[at, me], local.at[0]),
        pltpu.make_async_copy(out_ref, out_z.at[at], local.at[1]),
        pltpu.make_async_copy(own_ref.at[me], w_all.at[at, me, :, pl.ds(0, own_cols)], local.at[2]),
        pltpu.make_async_copy(tok_ref, tok_all.at[me], local.at[4]),
    ]
    if shared:
        keeps.append(pltpu.make_async_copy(mix_ref.at[me], w_all.at[at, me, :, side(me)], local.at[3]))
    own_down = pltpu.make_async_copy(down_ref, down_all.at[at], local.at[5])
    own_down.start()
    for copy in keeps:
        copy.start()
    greet(peers, groups)
    moves = fanout(peers, lambda p: own_ref.at[p], lambda p: w_all.at[at, me, :, pl.ds(0, own_cols)], a_s, a_r)
    if shared:
        moves += fanout(peers, lambda p: mix_ref.at[p], lambda p: w_all.at[at, me, :, side(p)], m_s, m_r)
    exts = fanout(peers, lambda p: ext_ref, lambda p: ext_all.at[at, me], e_s, e_r)
    ffn = fanout(peers, lambda p: ffn_ref.at[p], lambda p: ffn_all.at[me], f_s, f_r)
    for copy in moves + exts:
        copy.start()
    out_line = Line(groups, lambda d: out_z.at[d], ol_s, ol_r)
    keeps[1].wait()
    out_line.start(1)
    down_line = Line(groups, lambda d: down_all.at[d], dl_s, dl_r)
    own_down.wait()
    down_line.start(1)
    for p in range(peers):
        for part in range(2):
            for d in range(groups):
                source = ((part * groups + d) * peers + p) * units
                to = (part * groups + d) * units
                ffn_ref[p, :, to : to + units] = gate_ref[:, source : source + units]
    own_ffn = pltpu.make_async_copy(ffn_ref.at[me], ffn_all.at[me], local.at[6])
    own_ffn.start()
    tok = Spread(peers, lambda c: tok_ref, lambda b: tok_all.at[b], t_s, t_r, True)
    if aligned:
        out = Spread(peers, lambda c: out_z.at[c], lambda b: out_all.at[b], o_s, o_r)
    else:
        out = Spread(peers, lambda c: out_z, lambda b: out_all.at[:, b], o_s, o_r)
    lines = [Line(groups, lambda d: w_all.at[d, :, :, pl.ds(0, own_cols)], al_s, al_r)]
    if shared:
        mix_line = Line(groups, lambda d: w_all.at[d, :, :, side(me)], ml_s, ml_r)
    ext_line = Line(groups, lambda d: ext_all.at[d], el_s, el_r)

    def across(d):
        block = w_all.at[d, :, :, side(me)]
        return send(block, block, s_s.at[d], s_r.at[d], blk=sibling)

    out_line.arrive(1)
    if groups > 2:
        out_line.start(2)
    for copy in moves:
        copy.wait_recv()
    for copy in keeps[2:3] + keeps[4:]:
        copy.wait()
    lines[0].start(1)
    if shared:
        mix_line.start(1)
        across(at).start()
    tok.start()
    for copy in exts:
        copy.wait_recv()
    keeps[0].wait()
    ext_line.start(1)
    for copy in ffn:
        copy.start()
    for step in range(3, groups):
        out_line.arrive(step - 1)
        out_line.start(step)
    if groups > 2:
        out_line.arrive(groups - 1)
    out.start()
    if aligned:
        mine = pltpu.make_async_copy(out_z.at[me // 2], out_all.at[me], local.at[7])
    else:
        mine = pltpu.make_async_copy(out_z, out_all.at[:, me], local.at[7])
    mine.start()
    for step in range(2, groups):
        lines[0].arrive(step - 1)
        lines[0].start(step)
        if shared:
            mix_line.arrive(step - 1, across)
            mix_line.start(step)
        ext_line.arrive(step - 1)
        ext_line.start(step)
        if step == 2:
            tok.forward()
    out.forward()
    lines[0].arrive(groups - 1)
    if shared:
        mix_line.arrive(groups - 1, across)
    ext_line.arrive(groups - 1)
    down_line.arrive(1)
    down_line.finish([1])
    for copy in ffn:
        copy.wait_recv()
    for copy in moves + exts + ffn:
        copy.wait_send()
    for spread in (tok, out):
        spread.finish()
    lines[0].finish(range(1, groups))
    if shared:
        mix_line.finish(range(1, groups))
        for d in range(groups):
            across(d).wait()
    ext_line.finish(range(1, groups))
    out_line.finish(range(1, groups))
    mine.wait()
    keeps[3].wait()
    own_ffn.wait()


def gather_all(groups, peers, heads, own, shared, aligned, attn, gate, tok, out, ext, down):
    def shape(*dims):
        return jax.ShapeDtypeStruct(dims, BF16)

    dma = pltpu.SemaphoreType.DMA
    vmem, hbm = pl.BlockSpec(memory_space=pltpu.VMEM), pl.BlockSpec(memory_space=pl.ANY)
    share, h = attn.shape[0], attn.shape[1] // (4 * heads)
    own_cols, quarter = own * 4 * h, shared * 2 * h
    ffn = (peers, share, gate.shape[1] // peers)
    return pl.pallas_call(
        functools.partial(gather_kernel, groups, peers, heads, own, shared, aligned),
        in_specs=[vmem] * 6,
        out_specs=[hbm] * 6,
        out_shape=[
            shape(groups, peers, share, own_cols + 2 * quarter), shape(*ffn), shape(peers, *tok.shape),
            shape(peers, *out.shape) if aligned else shape(groups, peers, *out.shape),
            shape(groups, peers, *ext.shape), shape(groups, *down.shape),
        ],
        scratch_shapes=[
            pltpu.VMEM((peers, share, own_cols), BF16), pltpu.VMEM((peers, share, max(quarter, 128)), BF16),
            pltpu.VMEM(ffn, BF16), pltpu.VMEM((groups, *out.shape), BF16), dma((8,)),
        ]
        + [dma((2 * peers,))] * 12 + [dma((groups,))] * 2 + [dma((2 * groups,))] * 10,
        compiler_params=pltpu.CompilerParams(
            collective_id=1, has_side_effects=True, vmem_limit_bytes=63 * 1024 * 1024
        ),
        name="gather_all",
    )(attn, gate, tok, out, ext, down)


def branch_kernel(
    groups, peers, heads, own, shared, att_ref, out_ref, tok_ref, ext_ref, down_in, ffn_ref, res_ref, n2_all, down_all, far_all,
    part, low, local, half, mine, got, r_s, r_r, n_s, n_r, dl_s, dl_r, h_s, h_r,
):
    me, at = lax.axis_index("blk"), lax.axis_index("dp")
    rows, width = tok_ref.shape
    greet(peers, groups)
    down_line = Line(groups, lambda d: down_all.at[d], dl_s, dl_r)
    down_line.start(2)

    def hop(i, block, to):
        return send(ffn_ref.at[block], far_all, h_s.at[i], h_r.at[i], dp=to)

    @pl.when(at == groups - 2)
    def _():
        hop(0, 0, at + 1).start()

    @pl.when(at == 1)
    def _():
        hop(1, groups - 1, at - 1).start()

    reduce = Reduce(peers, part, half, mine, got, r_s, r_r, halved=True)

    h = out_ref.shape[0] // (2 * own + shared)
    mine_rows = out_ref[pl.ds(pl.multiple_of(me % 2 * ((own + shared) * h), 128), own * h), :]
    if shared:
        mine_rows = jnp.concatenate([mine_rows, out_ref[own * h : (own + 1) * h, :]], 0)

    def fill(b):
        block = att_ref[pl.ds(pl.multiple_of(b * rows, rows), rows), :]
        part[b] = dot(block, mine_rows).astype(BF16)

    for k in reduce.order():
        fill(2 * reduce.to[k] + 1 - me % 2)
        reduce.inner[k].start()
    for k in reduce.order():
        fill(2 * reduce.to[k] + me % 2)
    reduce.pair()
    res_ref[...] = tok_ref[...].astype(F32) + reduce.total()
    low[...] = rms_norm(res_ref[...], ext_ref[...].astype(F32)[heads + 1 : heads + 2]).astype(BF16)
    keep = pltpu.make_async_copy(low, n2_all.at[me], local.at[1])
    keep.start()
    spread = Spread(peers, lambda c: low, lambda b: n2_all.at[b], n_s, n_r, True)
    spread.start()
    for step in range(3, groups):
        down_line.arrive(step - 1)
        down_line.start(step)
    spread.forward()
    down_line.arrive(groups - 1)
    spread.finish()
    reduce.finish()
    down_line.finish(range(2, groups))
    keep.wait()

    @pl.when(at == groups - 1)
    def _():
        hop(0, 0, at - 1).wait_recv()

    @pl.when(at == 0)
    def _():
        hop(1, groups - 1, at + 1).wait_recv()

    @pl.when(at == groups - 2)
    def _():
        hop(0, 0, at + 1).wait_send()

    @pl.when(at == 1)
    def _():
        hop(1, groups - 1, at - 1).wait_send()


def branch(groups, peers, heads, own, shared, att, out, tok, ext, down, ffn):
    rows, width = tok.shape
    dma = pltpu.SemaphoreType.DMA
    vmem, hbm = pl.BlockSpec(memory_space=pltpu.VMEM), pl.BlockSpec(memory_space=pl.ANY)
    return pl.pallas_call(
        functools.partial(branch_kernel, groups, peers, heads, own, shared),
        in_specs=[vmem] * 4 + [hbm, hbm],
        out_specs=[vmem, hbm, hbm, hbm],
        input_output_aliases={4: 2},
        out_shape=[
            jax.ShapeDtypeStruct((rows, width), F32),
            jax.ShapeDtypeStruct((peers, rows, width), BF16),
            jax.ShapeDtypeStruct(down.shape, BF16),
            jax.ShapeDtypeStruct(ffn.shape[1:], BF16),
        ],
        scratch_shapes=[pltpu.VMEM((peers, rows, width), BF16), pltpu.VMEM((rows, width), BF16), dma((2,))]
        + Reduce.scratch(peers, rows, width)
        + [dma((2 * peers,)), dma((2 * peers,)), dma((2 * groups,)), dma((2 * groups,)), dma((2,)), dma((2,))],
        compiler_params=pltpu.CompilerParams(
            collective_id=2, has_side_effects=True, vmem_limit_bytes=63 * 1024 * 1024
        ),
        name="branch_and_norm",
    )(att, out, tok, ext, down, ffn)


def slab_order(groups, slab):
    if slab % 128:
        return list(range(groups))
    upper = lax.axis_index("dp") >= groups // 2
    return [jnp.where(upper, i, groups - 1 - i) for i in range(groups)]


def slab_of(ref, d, slab):
    if slab % 128:
        return ref[:, d * slab : (d + 1) * slab]
    return ref[:, pl.ds(pl.multiple_of(d * slab, 128), slab)]


def feed_forward_kernel(
    groups, peers, heads, n2_ref, ffn_all, far_all, down_all, dy_all, res_ref, ext_ref,
    dres_ref, db_all, outp_all, gd_all, gi_all, up_ref, dn_ref,
    w_ref, w_sem, down_ref, dy_ref, part, hidden, pulled, low, outp_ref, gd_ref, gi_ref, local, half, mine, got, r_s, r_r, n_s, n_r, ug, dg, uo, do, l_s, l_r,
):
    me = lax.axis_index("blk")
    rows, width = res_ref.shape
    cols = w_ref.shape[1]
    units = cols // 2
    share = gi_ref.shape[2]
    slab = peers * share
    at_dp = lax.axis_index("dp")
    loads = []
    for d in range(groups):
        gap = at_dp - d
        remote = (gap == groups - 1) | (gap == 1 - groups)
        into = w_ref.at[pl.ds(d * slab, slab)]
        loads.append(pltpu.make_async_copy(ffn_all.at[d], into, w_sem.at[d]))
        pl.when(remote)(pltpu.make_async_copy(far_all, into, w_sem.at[d]).start)
        pl.when(jnp.logical_not(remote))(loads[d].start)
    loads += [
        pltpu.make_async_copy(dy_all, dy_ref, w_sem.at[groups]),
        pltpu.make_async_copy(down_all, down_ref, w_sem.at[groups + 1]),
    ]
    for copy in loads[groups:]:
        copy.start()
    greet(peers, groups)
    for copy in loads:
        copy.wait()
    reduce = Reduce(peers, part, half, mine, got, r_s, r_r, halved=True)

    def block(ref, b, count=1):
        return ref.at[pl.ds(pl.multiple_of(b * rows, rows), count * rows)]

    for k in reduce.order():
        chip = reduce.to[k]
        normed = block(n2_ref, 2 * chip, 2)[...]
        gate_up = dot(normed, w_ref[...])
        gate, up = gate_up[:, :units], gate_up[:, units:]
        sig = 1.0 / (1.0 + jnp.exp(-gate))
        silu = gate * sig
        block(hidden, 2 * chip, 2)[...] = (silu * up).astype(BF16)
        dhidden = dot(block(dy_ref, 2 * chip, 2)[...], down_ref[...], NT)
        dgate = dhidden * up * (sig + silu * (1.0 - sig))
        both_pulled = jnp.concatenate([dgate, dhidden * silu], 1).astype(BF16)
        block(pulled, 2 * chip, 2)[...] = both_pulled
        pull = dot(both_pulled, w_ref[...], NT).astype(BF16)
        part[2 * chip] = pull[:rows]
        part[2 * chip + 1] = pull[rows:]
        reduce.inner[k].start()
    line = LineSum(groups, lambda r: gi_ref.at[line.at + r], ug, dg, uo, do, l_s, l_r)

    def chunk(d):
        gi_ref[d] = dot(slab_of(n2_ref, d, slab), pulled[...], TN).astype(BF16).reshape(peers, share, cols)

    order = slab_order(groups, slab)
    early = 1 if slab % 128 == 0 else groups
    for d in order[:early]:
        chunk(d)
    line.step(0)
    reduce.pair()
    for d in order[early:]:
        chunk(d)
    out_copies = [pltpu.make_async_copy(gi_ref, gi_all, local.at[1])]
    out_copies[0].start()
    dres_ref[...] = block(dy_ref, me)[...].astype(F32) + rms_pull(
        res_ref[...], ext_ref[...].astype(F32)[heads + 1 : heads + 2], reduce.total()
    )
    low[...] = dres_ref[...].astype(BF16)
    keep = pltpu.make_async_copy(low, db_all.at[me], local.at[0])
    keep.start()
    spread = Spread(peers, lambda c: low, lambda b: db_all.at[b], n_s, n_r, True)
    spread.start()
    gd_ref[...] = dot(hidden[...], dy_ref[...], TN).astype(BF16).reshape(gd_ref.shape)
    out_copies.append(pltpu.make_async_copy(gd_ref, gd_all, local.at[2]))
    out_copies[1].start()
    steps = range(max(groups - 2, 1))
    for i in steps[1:]:
        line.step(i)
    spread.forward()

    def out(i, carry):
        at = pl.ds(pl.multiple_of(i * 2 * rows, rows), 2 * rows)
        value = dot(hidden[at, :], down_ref[...]).astype(BF16)
        outp_ref[2 * i] = value[:rows]
        outp_ref[2 * i + 1] = value[rows:]
        return carry

    lax.fori_loop(0, peers // 2, out, 0)
    out_copies.append(pltpu.make_async_copy(outp_ref, outp_all, local.at[3]))
    out_copies[2].start()
    spread.finish()
    reduce.finish()
    line.arrive(steps[-1], up_ref, dn_ref)
    line.finish(steps)
    for copy in [keep] + out_copies:
        copy.wait()


def feed_forward(groups, peers, heads, n2_all, ffn, far, down, dy_all, res, ext):
    rows, width = res.shape
    tokens, cols = n2_all.shape[0], ffn.shape[2]
    share = width // (groups * peers)
    units = cols // (2 * groups)
    tall = 16 if units % 16 == 0 else units
    down_shape = (groups, units // tall, tall, width)
    dma = pltpu.SemaphoreType.DMA
    vmem, hbm = pl.BlockSpec(memory_space=pltpu.VMEM), pl.BlockSpec(memory_space=pl.ANY)

    def shape(*dims, dtype=BF16):
        return jax.ShapeDtypeStruct(dims, dtype)

    return pl.pallas_call(
        functools.partial(feed_forward_kernel, groups, peers, heads),
        in_specs=[vmem, hbm, hbm, hbm, hbm, vmem, vmem],
        out_specs=[vmem, hbm, hbm, hbm, hbm, vmem, vmem],
        out_shape=[
            shape(rows, width, dtype=F32), shape(peers, rows, width), shape(peers, rows, width),
            shape(*down_shape), shape(groups, peers, share, cols),
            shape(peers, share, cols), shape(peers, share, cols),
        ],
        scratch_shapes=[
            pltpu.VMEM((width, cols), BF16), dma((groups + 2,)),
            pltpu.VMEM(down.shape, BF16), pltpu.VMEM(dy_all.shape, BF16),
            pltpu.VMEM((peers, rows, width), BF16), pltpu.VMEM((tokens, cols // 2), BF16),
            pltpu.VMEM((tokens, cols), BF16), pltpu.VMEM((rows, width), BF16),
            pltpu.VMEM((peers, rows, width), BF16), pltpu.VMEM(down_shape, BF16),
            pltpu.VMEM((groups, peers, share, cols), BF16), dma((4,)),
        ]
        + Reduce.scratch(peers, rows, width)
        + [dma((2 * peers,)), dma((2 * peers,))]
        + LineSum.scratch(groups, peers, share, cols, steps=groups - 2),
        compiler_params=pltpu.CompilerParams(
            collective_id=3, has_side_effects=True, vmem_limit_bytes=62 * 1024 * 1024
        ),
        name="feed_forward",
    )(n2_all, ffn, far, down, dy_all, res, ext)


def final_kernel(
    groups, peers, heads, own, shared, aligned,
    norm_ref, dproj_ref, dlogit_ref, w_all, ext_ref, att_ref, db_all, ffn_all, tok_ref, dres_ref,
    gd_all, dup_ref, ddn_ref, wa_all, wb_ref, wf_all, ga_ref, gf_ref,
    dtok_ref, grad_ref, beta_out, gout_fin, ffn_out, down_fin, gain_out, gain_ffn_out,
    w_ref, db_ref, ffn_ref, gd_ref, wa_ref, wf_ref, f_sem, beta_fin,
    g_ref, beta_ref, part, half, mine, got, r_s, r_r,
    oug, odg, ouo, odo, ol_s, ol_r, own_fin, own_rows, w_s, w_r, ffn_rows, f_s, f_r,
    beta_got, beta_sum, b_s, b_r, bug, bdg, buo, bdo, bl_s, bl_r,
    vg, wg, vo, wo, m_s, m_r,
    *extra,
):
    me, at = lax.axis_index("blk"), lax.axis_index("dp")
    core, chip = me % 2, me // 2
    sibling = me + 1 - 2 * core
    rows, width = tok_ref.shape
    h = width // heads
    share = g_ref.shape[2]
    slab = peers * share
    own_cols, quarter = own * 4 * h, shared * 2 * h
    cols = own_cols + 2 * quarter
    extra = list(extra)
    if shared:
        mix_half, mix_sum, mug, mdg, muo, mdo, ml_s, ml_r, mix_fin, mix_rows, x_s, x_r, mw_s, mw_r = extra[:14]
        extra = extra[14:]
    if aligned:
        go_part, go_half, go_mine, go_all, g_s, g_r, gug, gdg, guo, gdo, gl_s, gl_r = extra
    loads = fetch(
        [(w_all, w_ref), (db_all, db_ref), (ffn_all, ffn_ref), (gd_all, gd_ref), (wa_all, wa_ref), (wf_all, wf_ref)], f_sem
    )
    greet(peers, groups)
    down = LineSum(groups, lambda r: gd_ref.at[at + r], vg, wg, vo, wo, m_s, m_r, (dup_ref, ddn_ref), groups - 2)
    own_line = LineSum(groups, lambda r: g_ref.at[at + r, :, :, pl.ds(0, own_cols)], oug, odg, ouo, odo, ol_s, ol_r)
    if shared:
        theirs = pl.ds(pl.multiple_of(own_cols + quarter * (1 - core), 128), quarter)
        ours = pl.ds(pl.multiple_of(own_cols + quarter * core, 128), quarter)
        mix = LineSum(groups, lambda r: mix_sum.at[at + r], mug, mdg, muo, mdo, ml_s, ml_r)

        def swap(d):
            return send(g_ref.at[d, :, :, theirs], mix_half.at[d], x_s.at[d], x_r.at[d], blk=sibling)

    order = slab_order(groups, slab)
    for i, d in enumerate(order):
        normed = slab_of(norm_ref, d, slab)
        g_ref[d] = dot(normed, dproj_ref[...], TN).astype(BF16).reshape(peers, share, cols)
        if i == (0 if slab % 128 == 0 else groups - 1):
            own_line.step(0)
        if shared:
            swap(d).start()
        beta_ref[d] = dot(normed, dlogit_ref[...], TN).astype(BF16).reshape(peers, share, 128)
    betas = fanout(peers, lambda p: beta_ref.at[:, p], lambda p: beta_got.at[me], b_s, b_r)
    ffn = fanout(peers, lambda p: ffn_ref.at[p], lambda p: ffn_rows.at[me], f_s, f_r)
    if shared:
        for i, d in enumerate(order):
            swap(d).wait_recv()

            def body(j, carry):
                mix_sum[d, j] = (g_ref[d, j, :, ours].astype(F32) + mix_half[d, j].astype(F32)).astype(BF16)
                return carry

            lax.fori_loop(0, peers, body, 0)
            if i == 0:
                mix.step(0)
    reduce = Reduce(peers, part, half, mine, got, r_s, r_r, halved=True)
    small = ext_ref[...].astype(F32)
    gain_row = small[heads : heads + 1]
    row = lax.broadcasted_iota(jnp.int32, small.shape, 0)
    small = jnp.where(row < heads, small, 0.0).astype(BF16)
    small = jnp.concatenate([small, jnp.zeros((128 - small.shape[0], width), BF16)], 0)

    def pull(k):
        to = 2 * reduce.to[k]
        two = pl.ds(pl.multiple_of(to * rows, rows), 2 * rows)
        value = (dot(dproj_ref[two, :], w_ref[...], NT) + dot(dlogit_ref[two, :], small)).astype(BF16)
        part[to] = value[:rows]
        part[to + 1] = value[rows:]
        reduce.inner[k].start()

    pulls = reduce.order()
    for copy in loads:
        copy.wait()
    pull(pulls[0])
    own_line.step(1)
    for k in pulls[1:]:
        pull(k)
    if shared:
        mix.step(1)
    reduce.chip_sums()
    for copy in betas:
        copy.start()
    if aligned:
        att = att_ref[...]
        mine_att, zero = att[:, : own * h], jnp.zeros((att.shape[0], own * h), BF16)
        wide = jnp.concatenate(
            [jnp.where(core == 0, mine_att, zero), att[:, own * h :], jnp.where(core == 1, mine_att, zero)], 1
        )
        tile = width // 3
        for j in range(0, width, tile):
            value = dot(wide, db_ref[:, j : j + tile], TN).astype(BF16)
            go_part[:, :, j : j + tile] = value.reshape(peers, share, tile)
        gout = Reduce(peers, go_part, go_half, go_mine, go_all, g_s, g_r, go_all.at[chip, 0])
        gout.start()
    reduce.cross_sums()
    sums = [own_line] + ([mix] if shared else [])
    for i in range(2, groups - 1):
        for item in sums:
            item.step(i)
    if aligned:
        gout.pair()
        go_all[chip, 0] = go_mine[0]
    for copy in ffn:
        copy.start()
    ffn_rows[me] = ffn_ref[me]
    beta_got[me] = beta_ref[:, me]
    for copy in betas:
        copy.wait_recv()
    summed = beta_got[0].astype(F32)
    for b in range(1, peers):
        summed = summed + beta_got[b].astype(F32)
    beta_sum[:, 0] = summed.astype(BF16)
    late = [LineSum(groups, lambda r: beta_sum.at[at + r], bug, bdg, buo, bdo, bl_s, bl_r)]
    if aligned:
        for copy in gout.outer:
            copy.wait_recv()
        late.append(LineSum(groups, lambda r: go_all.at[at + r], gug, gdg, guo, gdo, gl_s, gl_r))
    for item in late:
        item.step(0)
    own_line.total(own_fin)
    moves = fanout(peers, lambda p: own_fin.at[p], lambda p: own_rows.at[me], w_s, w_r)
    for copy in moves:
        copy.start()
    down.step(groups - 2)
    own_rows[me] = own_fin[me]
    if shared:
        mix.total(mix_fin)
        mix_moves = fanout(peers, lambda p: mix_fin.at[p], lambda p: mix_rows.at[me], mw_s, mw_r)
        for copy in mix_moves:
            copy.start()
        mix_rows[me] = mix_fin[me]
        moves += mix_moves
    for item in late:
        item.step(1)
    dtok_ref[...] = dres_ref[...] + rms_pull(tok_ref[...].astype(F32), gain_row, reduce.total())

    def row_sums(wide):
        high = wide.astype(BF16)
        low = (wide - high.astype(F32)).astype(BF16)
        ones = jnp.ones((8, wide.shape[1]), BF16)
        return (dot(ones, high, NT) + dot(ones, low, NT))[:1]

    for copy in ffn:
        copy.wait_recv()
    units = wf_ref.shape[1] // (2 * groups * peers)
    total = jnp.zeros((share, units), F32)
    for b in range(peers):
        for side in range(2):
            for d in range(groups):
                src = (side * groups + d) * units
                to = ((side * groups + d) * peers + b) * units
                value = ffn_rows[b, :, src : src + units].astype(F32)
                ffn_out[:, to : to + units] = value
                total = total + value * wf_ref[:, to : to + units].astype(F32)
    gain_ffn_out[...] = row_sums(total) / gf_ref[...].astype(F32)
    for i in range(2, groups - 1):
        for item in late:
            item.step(i)
    down.total(down_fin)
    late[0].total(beta_fin)
    for copy in moves:
        copy.wait_recv()
    beta_out[...] = jnp.concatenate([beta_fin[0], jnp.zeros((128 - share, 128), F32)], 0).T[:heads, :share]
    gain = beta_fin[0] * wb_ref[...].astype(F32)
    hc = 2 * own + shared

    def put(acc, value, head, side):
        to = side * width + head * h
        value = value.astype(F32)
        grad_ref[:, to : to + h] = value
        return acc + value * wa_ref[:, to : to + h].astype(F32)

    for b in range(peers):
        for s in range(own):
            head = (b // 2) * hc + (b % 2) * (own + shared) + s
            if head < heads:
                for side in range(4):
                    gain = put(gain, own_rows[b, :, (4 * s + side) * h : (4 * s + side + 1) * h], head, side)
        if shared:
            for i in range(2):
                gain = put(gain, mix_rows[b, :, i * h : (i + 1) * h], (b // 2) * hc + own, 2 * (b % 2) + i)
    gain_out[...] = row_sums(gain) / ga_ref[...].astype(F32)
    if aligned:
        late[1].total(gout_fin)
    reduce.finish()
    for copy in betas + ffn + moves:
        copy.wait_send()
    if shared:
        for d in range(groups):
            swap(d).wait_send()
    if aligned:
        gout.finish()
    for item in sums + late:
        item.finish()
    down.finish([groups - 2])


def final_sums(groups, peers, heads, own, shared, aligned, *args):
    normed, dproj, dlogits, w, ext, att, db, ffn, tok = args[:9]
    gd, wa, wf = args[10], args[13], args[15]
    rows, width = tok.shape
    h, share = width // heads, wa.shape[0]
    own_cols, quarter, cols = own * 4 * h, shared * 2 * h, w.shape[1]
    dma = pltpu.SemaphoreType.DMA
    vmem = pl.BlockSpec(memory_space=pltpu.VMEM)

    def block(*dims):
        return pltpu.VMEM(dims, BF16)

    def shape(*dims, dtype=F32):
        return jax.ShapeDtypeStruct(dims, dtype)

    pair = [dma((peers,))] * 2
    large = (3, 6, 7, 10, 13, 15)
    scratch = [pltpu.VMEM(args[i].shape, args[i].dtype) for i in large] + [dma((len(large),)), pltpu.VMEM((1, share, 128), F32)]
    scratch += [block(groups, peers, share, cols), block(groups, peers, share, 128), block(peers, rows, width)]
    scratch += Reduce.scratch(peers, rows, width)
    scratch += LineSum.scratch(groups, peers, share, own_cols) + [block(peers, share, own_cols)] * 2 + pair
    scratch += [block(*ffn.shape)] + pair
    scratch += [block(peers, groups, share, 128), block(groups, 1, share, 128)] + pair
    scratch += LineSum.scratch(groups, 1, share, 128) + LineSum.scratch(groups, *gd.shape[1:], steps=1)
    if shared:
        scratch += [block(groups, peers, share, quarter)] * 2 + LineSum.scratch(groups, peers, share, quarter)
        scratch += [block(peers, share, quarter)] * 2 + [dma((groups,)), dma((groups,))] + pair
    if aligned:
        half = block(peers // 2, share, width)
        scratch += [block(peers, share, width), half, half, block(groups, 1, share, width)] + pair
        scratch += LineSum.scratch(groups, 1, share, width)
    return pl.pallas_call(
        functools.partial(final_kernel, groups, peers, heads, own, shared, aligned),
        in_specs=[pl.BlockSpec(memory_space=pl.ANY) if i in large else vmem for i in range(len(args))],
        out_specs=[vmem] * 8,
        out_shape=[
            shape(rows, width), shape(*wa.shape), shape(heads, share), shape(1, share, width), shape(*wf.shape),
            shape(*gd.shape[1:]), shape(1, share), shape(1, share),
        ],
        scratch_shapes=scratch,
        compiler_params=pltpu.CompilerParams(
            collective_id=4, has_side_effects=True, vmem_limit_bytes=63 * 1024 * 1024
        ),
        name="final_sums",
    )(*args)


def hand_over_kernel(*refs):
    count = (len(refs) - 2) // 3
    given, out, held, sems = refs[:count], refs[count : 2 * count], refs[2 * count : 3 * count], refs[3 * count :]
    loads = [pltpu.make_async_copy(given[i], held[i], sems[0].at[i]) for i in range(count)]
    stores = [pltpu.make_async_copy(held[i], out[i], sems[1].at[i]) for i in range(count)]
    for load in loads:
        load.start()
    for load, store in zip(loads, stores):
        load.wait()
        store.start()
    for store in stores:
        store.wait()


def hand_over(*results):
    dma = pltpu.SemaphoreType.DMA((len(results),))
    hbm = pl.BlockSpec(memory_space=pl.ANY)
    return pl.pallas_call(
        hand_over_kernel,
        in_specs=[hbm] * len(results),
        out_specs=[hbm] * len(results),
        out_shape=[jax.ShapeDtypeStruct(x.shape, x.dtype) for x in results],
        scratch_shapes=[pltpu.VMEM(x.shape, x.dtype) for x in results] + [dma, dma],
        compiler_params=pltpu.CompilerParams(vmem_limit_bytes=63 * 1024 * 1024),
        name="hand_over",
    )(*results)


def shards(
    tokens, cotangent, doc_table, gain_attn, attn_in, beta_proj, attn_out, gain_ffn, ffn_in, ffn_down
):
    rows, width = tokens.shape
    heads = beta_proj.shape[1]
    h = width // heads
    groups, peers = lax.axis_size("dp"), lax.axis_size("blk")
    chips = peers // 2
    hc = -(-heads // chips)
    own, shared = hc // 2, hc % 2
    slots, padded = own + shared, hc * chips
    own_cols, quarter = own * 4 * h, shared * 2 * h
    share, units = attn_in.shape[0], ffn_down.shape[0]
    aligned = chips == groups and padded == heads
    me = lax.axis_index("blk")
    chip, core = me // 2, me % 2
    ext = jnp.concatenate([beta_proj.T, gain_attn[None], gain_ffn[None]], 0)
    ext_rows = -(-(heads + 2) // 16) * 16
    ext = jnp.pad(ext, ((0, ext_rows - heads - 2), (0, 128 - share)))
    w2, ffn_part, x_all, out_all, ext_all, down_part = gather_all(
        groups, peers, heads, own, shared, aligned, attn_in, ffn_in, tokens, attn_out, ext, ffn_down
    )
    w2 = w2.reshape(width, -1)
    x_all = x_all.reshape(peers * rows, width)
    out_rows = out_all.reshape(-1, width)
    if not aligned:
        out_rows = jnp.pad(out_rows, ((0, (padded - heads) * h), (0, 0)))
        out_rows = lax.dynamic_slice_in_dim(out_rows, chip * hc * h, hc * h, 0)
    first = chip * hc + core * (own + shared)
    my_heads = jnp.stack([first + s for s in range(own)] + [chip * hc + own] * shared).astype(jnp.int32)
    on = jnp.stack([jnp.int32(1)] * own + [1 - core] * shared).astype(jnp.int32)
    normed, dy_all, ext_all, ffn_all, proj, logits, attended, *saved = attention_forward(
        doc_table, on, my_heads, x_all, w2, ext_all, cotangent, ffn_part,
        groups, peers, heads, slots, rows,
    )
    dy_all = dy_all.reshape(peers * rows, width)
    residual, normed_two_all, down_all, ffn_far = branch(
        groups, peers, heads, own, shared, attended, out_rows, tokens, ext_all, down_part, ffn_all
    )
    normed_two_all = normed_two_all.reshape(peers * rows, width)
    down_slab = down_all.reshape(-1, width)

    dresidual, dbranch_all, out_part, grad_down, grad_ffn, up, down = feed_forward(
        groups, peers, heads, normed_two_all, ffn_all.reshape(groups, peers * share, -1), ffn_far.reshape(peers * share, -1),
        down_slab, dy_all, residual, ext_all,
    )
    dbranch_all = dbranch_all.reshape(peers * rows, width)
    dproj, dlogits, block_out, grad_ffn, down_up, down_dn = attention_backward(
        doc_table, on, my_heads, out_part, residual, grad_ffn, up, down, grad_down, dbranch_all, out_rows,
        proj, logits, saved, groups, peers, own, shared, rows,
    )
    grad_tokens, grad_attn_in, grad_beta, grad_attn_out, grad_ffn_in, grad_down, grad_gain_attn, grad_gain_ffn = final_sums(
        groups, peers, heads, own, shared, aligned,
        normed, dproj, dlogits, w2, ext_all, attended, dbranch_all, grad_ffn, tokens, dresidual, grad_down, down_up, down_dn,
        attn_in, jnp.pad(beta_proj, ((0, 0), (0, 128 - heads))), ffn_in,
        gain_attn[None], gain_ffn[None],
    )
    if aligned:
        grad_attn_out = grad_attn_out[0]
    else:
        gout = dot(attended, dbranch_all, TN)
        first = chip * hc + core * (own + shared)
        whole = jnp.zeros((padded * h, width), F32)
        whole = lax.dynamic_update_slice_in_dim(whole, gout, first * h, 0)[: heads * h]
        grad_attn_out = lax.psum_scatter(whole, ("dp", "blk"), scatter_dimension=0, tiled=True)
    block_out, grad_tokens, grad_gain_attn, grad_attn_in, grad_beta, grad_attn_out, grad_gain_ffn, grad_ffn_in, grad_down = hand_over(
        block_out, grad_tokens, grad_gain_attn, grad_attn_in, grad_beta, grad_attn_out,
        grad_gain_ffn, grad_ffn_in, grad_down.reshape(units, width),
    )
    return (
        block_out, grad_tokens, grad_gain_attn[0], grad_attn_in, grad_beta.T, grad_attn_out,
        grad_gain_ffn[0], grad_ffn_in, grad_down,
    )


def solution(mesh):
    split, vector = P(("dp", "blk"), None), P(("dp", "blk"))
    in_specs = (split, split, P("dp", None), vector, split, split, split, vector, split, split)
    out_specs = (split, split, vector, split, split, split, vector, split, split)
    return jax.shard_map(shards, mesh=mesh, in_specs=in_specs, out_specs=out_specs, check_vma=False)
```
